128 devices in a mesh: rep: 2 (over y_hi), shard: 64 (over x, y_lo, z, core).
Axes of the slice: x: 4, y: 4 (y_hi: 2, y_lo: 2; y = y_hi * 2 + y_lo), z: 4, core: 2. Of those that a mesh axis runs over, the one named last changes fastest.
Arguments:
- layer_in: bfloat16 [2, 2, 4096, 2048], P(None, 'rep', 'shard'), may hold values from -6 to 6
- cotangent: bfloat16 [2, 2, 4096, 2048], P(None, 'rep', 'shard'), may hold values from -6 to 6
- segment_ids: int32 [2, 2, 4096], P(None, 'rep', 'shard'), may hold values from 0 to 4095, as said below
- norm_gain: float32 [2048], P('shard'), may hold values from 0.5 to 1.5
- in_weight: bfloat16 [2048, 8512], P('shard'), may hold values from -0.125 to 0.125
- conv_weight: float32 [4, 4352], P(None, 'shard'), may hold values from -3 to 3
- conv_bias: float32 [4352], P('shard'), may hold values from -0.5 to 0.5
- dt_bias: float32 [64], P('shard'), may hold values from -7 to -5
- a_log: float32 [64], P('shard')
- skip_gain: float32 [64], P('shard'), may hold values from 0.5 to 1.5
- out_gain: float32 [4096], P('shard'), may hold values from 0.5 to 1.5
- out_weight: bfloat16 [4096, 2048], P('shard'), may hold values from -0.09375 to 0.09375
Outputs:
- layer_out: bfloat16 [2, 2, 4096, 2048], P(None, 'rep', 'shard')
- grad_layer_in: bfloat16 [2, 2, 4096, 2048], P(None, 'rep', 'shard')
- grad_norm_gain: float32 [2048], P('shard')
- grad_in_weight: float32 [2048, 8512], P('shard')
- grad_conv_weight: float32 [4, 4352], P(None, 'shard')
- grad_conv_bias: float32 [4352], P('shard')
- grad_dt_bias: float32 [64], P('shard')
- grad_a_log: float32 [64], P('shard')
- grad_skip_gain: float32 [64], P('shard')
- grad_out_gain: float32 [4096], P('shard')
- grad_out_weight: float32 [4096, 2048], P('shard')
The draws below stay inside these ranges and needn't reach their ends.
Inputs may be any that keep to these rules, and one draw needn't show every extreme that they name: `segment_ids`: along each sequence the numbers never fall and start at 0; they rise by at most 1 from one token to the next, except that the last token of every sequence is a document of its own numbered 4096 - 1. In each sequence position of the 2 micro-batches, one micro-batch holds a document that begins within the first 64 tokens and ends within the last 64.
All inputs are finite; a program needn't handle non-finite values.
Results may differ from the reference program's by a relative error of at most 0.0066.
Values may be sent and summed in bfloat16 or wider, within the bound.
A program may use at most 768 MiB of HBM per device.

```python
import math
import jax
import jax.numpy as jnp
from jax import lax

D = 2048
INNER = 4096
NH = 64
HEADDIM = 64
STATE = 128
MICRO = 2
MB_TOK = 64
CONV = 4352
PROJ = 8512
SEQUENCES = 2
LENGTH = 4096


def draw_segment_ids(key, part):
    key = jax.random.fold_in(key, 11)
    key_len, key_scale, key_pick, key_first, key_last = jax.random.split(key, 5)
    full_shape = (MICRO, SEQUENCES, LENGTH)
    scales = jax.random.randint(key_scale, full_shape, 0, 11)
    spans = jax.random.randint(key_len, full_shape, 0, 1 << 30)
    lengths = 1 + spans % jnp.left_shift(2, scales)
    ends = jnp.cumsum(lengths, axis=-1)

    def mark_row(row_ends):
        return jnp.zeros((LENGTH,), jnp.int32).at[row_ends].set(1, mode='drop')
    marks = jax.vmap(jax.vmap(mark_row))(ends)
    chosen = jax.random.randint(key_pick, (SEQUENCES,), 0, MICRO)
    first = jax.random.randint(key_first, (SEQUENCES,), 1, MB_TOK)
    last = jax.random.randint(key_last, (SEQUENCES,), LENGTH - MB_TOK, LENGTH - 1)
    positions = jnp.arange(LENGTH)[None, None, :]
    picked = (jnp.arange(MICRO)[:, None] == chosen[None, :])[:, :, None]
    inside = (positions > first[None, :, None]) & (positions <= last[None, :, None])
    edges = (positions == first[None, :, None]) | (positions == last[None, :, None] + 1)
    marks = jnp.where(picked & inside, 0, jnp.where(picked & edges, 1, marks))
    numbers = jnp.cumsum(marks, axis=-1).astype(jnp.int32)
    return jnp.where(positions == LENGTH - 1, LENGTH - 1, numbers).astype(jnp.int32)


def draw_a_log(key, part):
    key = jax.random.fold_in(key, 23)
    rate_low = 20.0 / LENGTH
    rate_high = 8.0
    unit = jax.random.uniform(key, (NH,), jnp.float32)
    return (jnp.log(rate_low) + unit * (jnp.log(rate_high) - jnp.log(rate_low))).astype(jnp.float32)


def steps_of(rng, extent, cuts, low, high):
    factor_of, own = 1.0, jax.random.fold_in(rng, 6)
    for axis_at, parts in cuts:
        draws = jnp.exp(jax.random.uniform(jax.random.fold_in(own, axis_at), (parts,), jnp.float32, low / len(cuts), high / len(cuts)))
        factor_of = factor_of * jnp.repeat(draws, extent[axis_at] // parts).reshape([-1 if axis == axis_at else 1 for axis in range(len(extent))])
    return factor_of


def centred(rng, extent, scale, bound, cuts=(), kind=jnp.bfloat16):
    values = scale * jax.random.normal(rng, extent, jnp.float32)
    if cuts:
        values = values * steps_of(rng, extent, cuts, -0.22, 0.18)
    return jnp.clip(values, -bound, bound).astype(kind)


def setup_inputs(seed: int = 0) -> dict:
    keys = jax.random.split(jax.random.key(seed), 13)
    return {
        "layer_in": centred(keys[0], (MICRO, SEQUENCES, LENGTH, D), 1.0, 6.0, ((1, 2), (2, 64))),
        "cotangent": centred(keys[1], (MICRO, SEQUENCES, LENGTH, D), 1.0, 6.0, ((1, 2), (2, 64))),
        "segment_ids": draw_segment_ids(jax.random.fold_in(keys[12], 71), 0),
        "norm_gain": jnp.clip(1.0 + 0.1 * jax.random.normal(keys[3], (D,), jnp.float32), 0.5, 1.5),
        "in_weight": centred(keys[4], (D, PROJ), D ** -0.5, 0.125, ((0, 64),)),
        "conv_weight": centred(keys[5], (4, CONV), 4 ** -0.5, 3.0, ((1, 64),), jnp.float32),
        "conv_bias": jnp.clip(jax.random.uniform(keys[6], (CONV,), jnp.float32, -0.5, 0.5) * steps_of(keys[6], (CONV,), ((0, 64),), -0.4, 0.0), -0.5, 0.5),
        "dt_bias": jnp.clip(-7.0 + 2.0 * jax.random.uniform(keys[7], (NH,), jnp.float32) ** steps_of(keys[7], (NH,), ((0, 64),), -0.2, 0.2), -7.0, -5.0),
        "a_log": draw_a_log(jax.random.fold_in(keys[12], 71), 0),
        "skip_gain": jnp.clip(0.5 + 1.0 * jax.random.uniform(keys[9], (NH,), jnp.float32) ** steps_of(keys[9], (NH,), ((0, 64),), -0.2, 0.2), 0.5, 1.5),
        "out_gain": jnp.clip(1.0 + 0.1 * jax.random.normal(keys[10], (INNER,), jnp.float32), 0.5, 1.5),
        "out_weight": centred(keys[11], (INNER, D), INNER ** -0.5, 0.09375, ((0, 64),)),
    }


@jax.custom_vjp
def low(v):
    return lax.optimization_barrier(v.astype(jnp.bfloat16)).astype(jnp.float32)

@jax.custom_vjp
def low_back(v):
    return v

def low_keep(v):
    return (low(v), None)

def low_pass(kept, grad):
    return (grad,)

def back_keep(v):
    return (v, None)

def back_low(kept, grad):
    return (low(grad),)
low.defvjp(low_keep, low_pass)
low_back.defvjp(back_keep, back_low)
EPS = 1e-05
HIGH = lax.Precision.HIGHEST

def rms_scale(values, gain):
    return values * lax.rsqrt(lax.optimization_barrier(jnp.mean(values * values, axis=-1, keepdims=True)) + EPS) * gain

def causal_conv(xbc, seg_ids, conv_weight, conv_bias):
    count = xbc.shape[0]
    padded = jnp.concatenate([jnp.zeros((3, xbc.shape[1]), xbc.dtype), xbc], 0)
    seg_pad = jnp.concatenate([jnp.full((3,), -1, jnp.int32), seg_ids.astype(jnp.int32)])
    total = jnp.zeros_like(xbc) + conv_bias[None, :]
    for tap in range(4):
        same = (seg_pad[tap:tap + count] == seg_ids).astype(xbc.dtype)
        total = total + conv_weight[tap][None, :] * padded[tap:tap + count] * same[:, None]
    return total

def ssd_block(carry, pieces):
    state, prev_seg, rate = carry
    inputs, b_rows, c_rows, delta, seg_ids = pieces
    count = seg_ids.shape[0]
    positions = jnp.arange(count)
    keep = ((seg_ids[:, None] == seg_ids[None, :]) & (positions[:, None] >= positions[None, :]))[:, :, None]
    cumul = jnp.cumsum(delta * rate[None, :], axis=0)
    spread = jnp.where(keep, jnp.exp(jnp.where(keep, cumul[:, None, :] - cumul[None, :, :], 0.0)), 0.0)
    scores = jnp.einsum('tn,sn->ts', c_rows, b_rows, precision=HIGH)
    driven = delta[:, :, None] * inputs
    inner_part = jnp.einsum('tsh,shp->thp', scores[:, :, None] * spread, driven, precision=HIGH)
    carry_on = (seg_ids == prev_seg).astype(inputs.dtype)
    carried = jnp.einsum('tn,hpn->thp', c_rows, state, precision=HIGH) * (jnp.exp(cumul) * carry_on[:, None])[:, :, None]
    last = seg_ids[count - 1]
    to_end = (seg_ids == last).astype(inputs.dtype)
    weight_end = jnp.exp(cumul[count - 1][None, :] - cumul) * to_end[:, None]
    joined = (last == prev_seg).astype(inputs.dtype)
    new_state = state * (jnp.exp(cumul[count - 1]) * joined)[:, None, None]
    new_state = new_state + jnp.einsum('sh,shp,sn->hpn', weight_end, driven, b_rows, precision=HIGH)
    return ((new_state, last, rate), inner_part + carried)

def layer_sequence(params, hidden, seg_ids):
    norm_gain, in_weight, conv_weight, conv_bias, dt_bias, a_log, skip_gain, out_gain, out_weight = params
    count = hidden.shape[0]
    block = math.gcd(count, 256)
    blocks = count // block
    normed = low(rms_scale(hidden, norm_gain))
    proj = low_back(jnp.dot(normed, in_weight, precision=HIGH))
    gate_part = proj[:, :INNER]
    xbc = low(proj[:, INNER:INNER + CONV])
    dt_raw = proj[:, INNER + CONV:]
    acts = jax.nn.silu(causal_conv(xbc, seg_ids, conv_weight, conv_bias))
    inputs = acts[:, :INNER].reshape(count, NH, HEADDIM)
    b_rows = acts[:, INNER:INNER + STATE]
    c_rows = acts[:, INNER + STATE:]
    delta = jax.nn.softplus(dt_raw + dt_bias[None, :])
    rate = -jnp.exp(a_log)
    start = (jnp.zeros((NH, HEADDIM, STATE), hidden.dtype), jnp.array(-1, jnp.int32), rate)
    pieces = (inputs.reshape(blocks, block, NH, HEADDIM), b_rows.reshape(blocks, block, STATE), c_rows.reshape(blocks, block, STATE), delta.reshape(blocks, block, NH), seg_ids.astype(jnp.int32).reshape(blocks, block))
    _, mixed = lax.scan(jax.checkpoint(ssd_block), start, pieces)
    mixed = mixed.reshape(count, NH, HEADDIM) + skip_gain[None, :, None] * inputs
    gated = mixed.reshape(count, INNER) * jax.nn.silu(gate_part)
    normed_out = low(rms_scale(gated, out_gain))
    return hidden + jnp.dot(normed_out, out_weight, precision=HIGH)

def reference(layer_in, cotangent, segment_ids, norm_gain, in_weight, conv_weight, conv_bias, dt_bias, a_log, skip_gain, out_gain, out_weight):
    params = tuple((item.astype(jnp.float32) for item in (norm_gain, in_weight, conv_weight, conv_bias, dt_bias, a_log, skip_gain, out_gain, out_weight)))
    flat_in = layer_in.astype(jnp.float32).reshape(MICRO * SEQUENCES, LENGTH, D)
    flat_seg = segment_ids.astype(jnp.int32).reshape(MICRO * SEQUENCES, LENGTH)
    flat_cot = cotangent.astype(jnp.float32).reshape(MICRO * SEQUENCES, LENGTH, D)
    one_sequence = jax.checkpoint(layer_sequence)

    def forward(weights, hidden_all):

        def per_row(pair):
            return one_sequence(weights, pair[0], pair[1])
        return lax.map(per_row, (hidden_all, flat_seg))
    result, pullback = jax.vjp(forward, params, flat_in)
    grad_params, grad_hidden = pullback(flat_cot)
    layer_out = result.astype(jnp.bfloat16).reshape(MICRO, SEQUENCES, LENGTH, D)
    grad_layer_in = grad_hidden.astype(jnp.bfloat16).reshape(MICRO, SEQUENCES, LENGTH, D)
    return (layer_out, grad_layer_in, grad_params[0], grad_params[1], grad_params[2], grad_params[3], grad_params[4], grad_params[5], grad_params[6], grad_params[7], grad_params[8])
```

```python
import functools

import jax
import jax.numpy as jnp
from jax import lax
from jax.experimental import pallas as pl
from jax.experimental.pallas import tpu as pltpu
from jax.sharding import Mesh, PartitionSpec as P

EPS = 1e-05
INNER = 4096
MICRO = 2
CONV = 4352
F32 = jnp.float32
BF16 = jnp.bfloat16
AXES = ("rep", "x", "y", "z", "c")
SEQ = ("x", "y", "z", "c")
GROUPS = 8
TOK = 512
Q = 128
CH = TOK // Q

MESH = pl.DeviceIdType.MESH
ANY = pl.BlockSpec(memory_space=pl.ANY)
VM = pl.BlockSpec(memory_space=pltpu.VMEM)


class Net:
    def __init__(self, send, recv):
        self.send, self.recv, self.used, self.open = send, recv, 0, []
        self.keys = {}
        self.rep, self.x, self.y, self.z, self.c = (lax.axis_index(a) for a in AXES)
        self.ring = 2 * self.rep + self.y
        self.g = 2 * self.x + self.y
        self.m = 2 * self.z + self.c

    def at(self, dx=0, dy=0, dz=0, dc=0):
        ring = lax.rem(self.ring + dy, 4)
        return (ring // 2, lax.rem(self.x + dx, 4), lax.rem(ring, 2), lax.rem(self.z + dz, 4), lax.rem(self.c + dc, 2))

    def pair(self):
        return (self.rep, self.x, 1 - self.y, self.z, self.c)

    def group(self, d):
        g = lax.rem(self.g + d, 8)
        return (self.rep, g // 2, lax.rem(g, 2), self.z, self.c)

    def member(self, dz, dc):
        return 2 * lax.rem(self.z + dz, 4) + lax.rem(self.c + dc, 2)

    def push(self, src, dst, where):
        i = self.used
        self.used += 1
        copy = pltpu.make_async_remote_copy(
            src_ref=src, dst_ref=dst, send_sem=self.send.at[i], recv_sem=self.recv.at[i], device_id=where, device_id_type=MESH
        )
        copy.start()
        self.open.append(copy)
        return copy

    def copy(self, key, src, dst, where):
        i = self.keys.setdefault(key, len(self.keys))
        return pltpu.make_async_remote_copy(
            src_ref=src, dst_ref=dst, send_sem=self.send.at[i], recv_sem=self.recv.at[i], device_id=where, device_id_type=MESH
        )

    def behind(self, d):
        return 2 * lax.rem(self.x + 4 - d, 4) + self.y

    def local(self, src, dst):
        i = self.used
        self.used += 1
        copy = pltpu.make_async_copy(src, dst, self.recv.at[i])
        copy.start()
        return copy

    def meet(self, peers):
        barrier = pltpu.get_barrier_semaphore()
        for peer in peers:
            pl.semaphore_signal(barrier, inc=1, device_id=peer, device_id_type=MESH)
        pl.semaphore_wait(barrier, len(peers))

    def finish(self):
        for copy in self.open:
            copy.wait_send()


OTHERS = [(dz, dc) for dz in (0, 1, 3, 2) for dc in (0, 1) if (dz, dc) != (0, 0)]
ZS = (0, 1, 3, 2)
XS = (1, 3, 2)


def call(kernel, name, cid, outs, ins, spaces_in, spaces_out, sems, scratch=(), cost=1 << 20):
    return pl.pallas_call(
        kernel,
        name=name,
        out_shape=outs,
        in_specs=spaces_in,
        out_specs=spaces_out,
        scratch_shapes=[*scratch, pltpu.SemaphoreType.DMA((sems,)), pltpu.SemaphoreType.DMA((sems,))],
        compiler_params=pltpu.CompilerParams(collective_id=cid, has_side_effects=True, vmem_limit_bytes=60 << 20),
        cost_estimate=pl.CostEstimate(flops=0, bytes_accessed=cost, transcendentals=0),
    )(*ins)


def sds(shape, dtype):
    return jax.ShapeDtypeStruct(shape, dtype)


def gather_kernel(hid, wsend, small, hid_all, w_in, small_all, halo, send, recv):
    n = Net(send, recv)
    g, m, z, c, y = n.g, n.m, n.z, n.c, n.y
    n.meet(
        [n.at(dz=a, dc=b) for a, b in OTHERS] + [n.at(dx=d) for d in XS] + [n.at(dy=1), n.at(dy=3), n.group(1), n.group(7)]
    )
    own = [n.local(wsend.at[m], w_in.at[g, m]), n.local(small, small_all.at[g, m]), n.local(hid, hid_all.at[m])]
    w_cp, s_cp = {}, {}
    for a, b in OTHERS:
        w_cp[a, b] = n.push(wsend.at[n.member(a, b)], w_in.at[g, m], n.at(dz=a, dc=b))
        s_cp[a, b] = n.push(small, small_all.at[g, m], n.at(dz=a, dc=b))
    last = []

    def along_y(ref, group, pick):
        for half, dy in ((0, 1), (1, 3)):
            part = pick(ref, group, half)
            last.append(n.push(part, part, n.at(dy=dy)))

    def w_half(k):
        first = 2 * lax.rem(z + 4 - ZS[k], 4)
        return lambda ref, group, half: ref.at[group, pl.ds(first, 2), pl.ds(16 * half, 16)]

    x_cp = {}
    for cp in own:
        cp.wait()
    for k, a in enumerate(ZS):
        for b in (0, 1):
            if (a, b) != (0, 0):
                w_cp[a, b].wait_recv()
        block = w_in.at[g, pl.ds(2 * lax.rem(z + 4 - a, 4), 2)]
        for d in XS:
            x_cp[k, d] = n.push(block, block, n.at(dx=d))
        along_y(w_in, g, w_half(k))
    h_cp = {a: n.push(hid, hid_all.at[m], n.at(dz=a)) for a in (1, 3, 2)}
    h_sib = n.push(hid, hid_all.at[m], n.at(dc=1))
    for a, b in OTHERS:
        s_cp[a, b].wait_recv()
    s_x = {d: n.push(small_all.at[g], small_all.at[g], n.at(dx=d)) for d in XS}
    last.append(n.push(small_all.at[g], small_all.at[g], n.pair()))
    for d in XS:
        other = 2 * lax.rem(n.x + 4 - d, 4) + y
        for k in range(4):
            x_cp[k, d].wait_recv()
            along_y(w_in, other, w_half(k))
        s_x[d].wait_recv()
        last.append(n.push(small_all.at[other], small_all.at[other], n.pair()))
        h_cp[d].wait_recv()
        theirs = hid_all.at[2 * lax.rem(z + 4 - d, 4) + c]
        last.append(n.push(theirs, theirs, n.at(dc=1)))
    h_sib.wait_recv()
    for cp in last:
        cp.wait_recv()
    edge = n.push(hid_all.at[7, :, pl.ds(48, 16)], halo, n.group(1))
    edge.wait_recv()
    n.finish()


def gather(hid, wsend, small):
    outs = [sds((8, 2, 64, 2048), BF16), sds((8, 8, 32, 1408), BF16), sds((8, 8, 8, 128), F32), sds((2, 16, 2048), BF16)]
    return call(gather_kernel, "gather", 0, outs, (hid, wsend, small), [VM] * 3, [ANY] * 4, 112)


def states_out(n, block, everyone):
    n.local(block, everyone.at[n.g]).wait()
    own = everyone.at[n.g]
    ahead = {d: n.push(own, own, n.at(dx=d)) for d in XS}
    last = []

    def along_y(group):
        last.append(n.push(everyone.at[group], everyone.at[group], n.pair()))

    along_y(n.g)

    def rest():
        for d in XS:
            ahead[d].wait_recv()
            along_y(2 * lax.rem(n.x + 4 - d, 4) + n.y)
        for cp in last:
            cp.wait_recv()

    return rest


def sums_kernel(mine, everyone, send, recv):
    n = Net(send, recv)
    n.meet([n.at(dz=a, dc=b) for a, b in OTHERS])
    everyone[n.m] = mine[...]
    for a, b in OTHERS:
        n.push(mine, everyone.at[n.m], n.at(dz=a, dc=b))
    for cp in n.open:
        cp.wait_recv()
    n.finish()


def member_gather(mine, name, cid):
    return call(sums_kernel, name, cid, sds((8, *mine.shape), mine.dtype), (mine,), [VM], VM, 16)


def a2a_kernel(mine, edge, theirs, edge_next, send, recv):
    n = Net(send, recv)
    n.meet([n.at(dz=a, dc=b) for a, b in OTHERS] + [n.group(1), n.group(7)])
    theirs[n.m] = mine[n.m]
    for a, b in OTHERS:
        n.push(mine.at[n.member(a, b)], theirs.at[n.m], n.at(dz=a, dc=b))
    n.push(edge, edge_next, n.group(7))
    for cp in n.open:
        cp.wait_recv()
    n.finish()


def bc_swap(mine, edge):
    return call(a2a_kernel, "bc_swap", 3, [sds(mine.shape, mine.dtype), sds(edge.shape, edge.dtype)], (mine, edge), [VM] * 2, [VM] * 2, 16)


def edge_kernel(edge, edge_next, send, recv):
    n = Net(send, recv)
    n.meet([n.group(1), n.group(7)])
    n.push(edge, edge_next, n.group(7)).wait_recv()
    n.finish()


def edge_back(edge):
    return call(edge_kernel, "edge", 6, sds(edge.shape, edge.dtype), (edge,), [VM], VM, 2)


def tokens_begin(n, part, near):
    return [n.push(part.at[2 * lax.rem(n.z + d, 4) + 1 - n.c], near.at[d], n.at(dc=1)) for d in (1, 3, 2, 0)]


def tokens_middle(n, part, near, both, far, begun):
    away = []
    for cp, d in zip(begun, (1, 3, 2, 0)):
        cp.wait_recv()
        at = 2 * lax.rem(n.z + d, 4) + n.c
        for i in range(2):
            both[d, i] = (part[at, i].astype(F32) + near[d, i].astype(F32)).astype(BF16)
        if d:
            away.append(n.push(both.at[d], far.at[d - 1], n.at(dz=d)))
    return away


def tokens_end(both, far, out, away):
    for cp in away:
        cp.wait_recv()
    for i in range(2):
        out[i] = both[0, i].astype(F32) + far[0, i].astype(F32) + far[1, i].astype(F32) + far[2, i].astype(F32)


TOKEN_SCRATCH = [pltpu.VMEM((4, 2, 64, 2048), jnp.bfloat16), pltpu.VMEM((4, 2, 64, 2048), jnp.bfloat16), pltpu.VMEM((3, 2, 64, 2048), jnp.bfloat16)]


def backward_kernel(starts, part, starts_all, total, near, both, far, send, recv):
    n = Net(send, recv)
    n.meet([n.at(dz=a) for a in (1, 3, 2)] + [n.at(dc=1)] + [n.at(dx=d) for d in XS] + [n.pair()])
    rest = states_out(n, starts, starts_all)
    begun = tokens_begin(n, part, near)
    away = tokens_middle(n, part, near, both, far, begun)
    rest()
    tokens_end(both, far, total, away)
    n.finish()


def backward_states(starts, part):
    outs = [sds((8, *starts.shape), BF16), sds((2, 64, 2048), F32)]
    return call(backward_kernel, "states_backward", 4, outs, (starts, part), [VM, VM], [ANY, VM], 32, TOKEN_SCRATCH)


MA = 5


def add4(a, b):
    return a.astype(F32) + b[0].astype(F32) + b[1].astype(F32) + b[2].astype(F32)


def final_kernel(gw, go, part, small, gi, g_out, total, small_all, near, both, far, a1, a2, b1, b2, b3, pa, pb, oc, oa1, oa2, ob1, ob2, ob3, opa, opb, final, s1, s2, sx, sy, send, recv):
    n = Net(send, recv)
    x, y, z, c, rep, ring = n.x, n.y, n.z, n.c, n.rep, n.ring
    n.meet([n.at(dz=a, dc=b) for a, b in OTHERS] + [n.at(dx=d) for d in XS] + [n.at(dy=d) for d in XS])
    MB = 8 - MA

    swap = n.push(go.at[:, 1 - c], oc.at[pl.ds(4 * c, 4)], n.at(dc=1))
    for k in range(4):
        oc[4 * c + k] = go[k, c]
    begun = tokens_begin(n, part, near)
    A1 = {d: n.push(gw.at[pl.ds(2 * lax.rem(x + d, 4), 2), pl.ds(0, MA)], a1.at[d - 1], n.at(dx=d)) for d in XS}
    B1 = {}
    for d in XS:
        to = lax.rem(ring + d, 4)
        for k in range(4):
            B1[d, k] = n.push(gw.at[2 * k + lax.rem(to, 2), pl.ds(MA, MB), pl.ds(16 * (to // 2), 16)], b1.at[d - 1, k], n.at(dy=d))
    S1 = {d: n.push(small, s1.at[d - 1], n.at(dx=d)) for d in XS}
    away = tokens_middle(n, part, near, both, far, begun)
    swap.wait_recv()
    OA1 = {d: n.push(oc.at[pl.ds(2 * lax.rem(x + d, 4), 2), pl.ds(0, 32)], oa1.at[d - 1], n.at(dx=d)) for d in XS}
    OB1 = {}
    for d in XS:
        to = lax.rem(ring + d, 4)
        for k in range(4):
            OB1[d, k] = n.push(oc.at[2 * k + lax.rem(to, 2), pl.ds(32 + 16 * (to // 2), 16)], ob1.at[d - 1, k], n.at(dy=d))
    for d in XS:
        S1[d].wait_recv()
    sx[...] = small[...] + s1[0] + s1[1] + s1[2]
    S2 = {d: n.push(sx, s2.at[d - 1], n.at(dy=d)) for d in XS}
    for d in XS:
        for k in range(4):
            B1[d, k].wait_recv()
    for k in range(4):
        pb[k] = add4(gw[2 * k + y, pl.ds(MA, MB), pl.ds(16 * rep, 16)], b1[:, k]).astype(BF16)
    B2 = {d: n.push(pb.at[lax.rem(x + d, 4)], b2.at[d - 1], n.at(dx=d)) for d in XS}
    for d in XS:
        A1[d].wait_recv()
    for h in range(2):
        for k in range(MA):
            pa[h, k] = add4(gw[2 * x + h, k], a1[:, h, k]).astype(BF16)
    A2 = {d: n.push(pa.at[lax.rem(ring + d, 2)], a2.at[d - 1], n.at(dy=d)) for d in XS}
    for d in XS:
        for k in range(4):
            OB1[d, k].wait_recv()
    for k in range(4):
        opb[k] = add4(oc[2 * k + y, pl.ds(32 + 16 * rep, 16)], ob1[:, k]).astype(BF16)
    OB2 = {d: n.push(opb.at[lax.rem(x + d, 4)], ob2.at[d - 1], n.at(dx=d)) for d in XS}
    for d in XS:
        OA1[d].wait_recv()
    for h in range(2):
        opa[h] = add4(oc[2 * x + h, pl.ds(0, 32)], oa1[:, h]).astype(BF16)
    OA2 = {d: n.push(opa.at[lax.rem(ring + d, 2)], oa2.at[d - 1], n.at(dy=d)) for d in XS}
    for d in XS:
        S2[d].wait_recv()
    sy[...] = sx[...] + s2[0] + s2[1] + s2[2]
    small_all[n.m] = sy[...]
    S3 = [n.push(sy, small_all.at[n.m], n.at(dz=a, dc=b)) for a, b in OTHERS]
    for d in XS:
        B2[d].wait_recv()
    final[pl.ds(MA, MB), pl.ds(16 * rep, 16)] = add4(pb[x], b2).astype(BF16)
    mineb = final.at[pl.ds(MA, MB), pl.ds(16 * rep, 16)]
    B3 = n.push(mineb, mineb, n.at(dy=2))
    for d in XS:
        OB2[d].wait_recv()
    ob3[rep] = add4(opb[x], ob2)
    OB3 = n.push(ob3.at[rep], ob3.at[rep], n.at(dy=2))
    for d in XS:
        A2[d].wait_recv()
    for k in range(MA):
        final[k] = add4(pa[y, k], a2[:, k]).astype(BF16)
    B3.wait_recv()
    gi[n.m] = final[n.m]
    F = [n.push(final.at[n.member(a, b)], gi.at[n.m], n.at(dz=a, dc=b)) for a, b in OTHERS]
    for d in XS:
        OA2[d].wait_recv()
    g_out[pl.ds(0, 32)] = add4(opa[y], oa2)
    OB3.wait_recv()
    g_out[pl.ds(32, 16)] = ob3[0]
    g_out[pl.ds(48, 16)] = ob3[1]
    tokens_end(both, far, total, away)
    for cp in F + S3:
        cp.wait_recv()
    n.finish()


def final_exchange(gw, go, part, small):
    w = gw.shape[-1]
    MB = 8 - MA
    outs = [sds((8, 32, w), BF16), sds((64, 2048), F32), sds((2, 64, 2048), F32), sds((8, *small.shape), F32)]
    V = lambda *s: pltpu.VMEM(s, BF16)
    scratch = TOKEN_SCRATCH + [
        V(3, 2, MA, 32, w), V(3, MA, 32, w), V(3, 4, MB, 16, w), V(3, MB, 16, w), V(16, 128), V(2, MA, 32, w), V(4, MB, 16, w),
        V(8, 64, 2048), V(3, 2, 32, 2048), V(3, 32, 2048), V(3, 4, 16, 2048), V(3, 16, 2048), pltpu.VMEM((2, 16, 2048), F32), V(2, 32, 2048), V(4, 16, 2048),
        V(8, 32, w), pltpu.VMEM((3, *small.shape), F32), pltpu.VMEM((3, *small.shape), F32), pltpu.VMEM(small.shape, F32), pltpu.VMEM(small.shape, F32),
    ]
    return call(final_kernel, "gradients", 5, outs, (gw, go, part, small), [VM] * 4, [VM] * 4, 128, scratch)


NN = (((1,), (0,)), ((), ()))
NT = (((1,), (1,)), ((), ()))
TN = (((0,), (0,)), ((), ()))
TT = (((0,), (1,)), ((), ()))


def bdot(a, b, dims=NN):
    return lax.dot_general(a, b, dims, preferred_element_type=F32)


def parts(v, count):
    out = []
    for _ in range(count):
        p = v.astype(BF16)
        out.append(p)
        v = v - p.astype(F32)
    return out


def left_parts(v, w, count, dims=NN):
    return sum(bdot(p, w, dims) for p in parts(v, count))


def right_parts(w, v, count, dims=NN):
    return sum(bdot(w, p, dims) for p in parts(v, count))


def iota(shape, dim):
    return lax.broadcasted_iota(jnp.int32, shape, dim)


def spread_matrix():
    return (iota((128, 512), 0) == iota((128, 512), 1) // 64).astype(BF16)


def heads_of(v, eh):
    return left_parts(v, eh, 2)


def sums_of(v, eh):
    return left_parts(v, eh, 2, NT)


def lower_matrix():
    return (iota((Q, Q), 0) >= iota((Q, Q), 1)).astype(BF16)


def sigmoid(v):
    return 1.0 / (1.0 + jnp.exp(-v))


def softplus(v):
    return jnp.maximum(v, 0.0) + jnp.log1p(jnp.exp(-jnp.abs(v)))


def row_scale(h):
    return lax.rsqrt(jnp.mean(h * h, axis=-1, keepdims=True) + EPS)


def decays(L, flags):
    E = jnp.exp(L) * flags[:, 3:4]
    W = jnp.exp(L[Q - 1 : Q] - L) * flags[:, 4:5]
    return E, W


def wave_kernel(
    hid, halo, gain, w, conv, hp, flags, segrow, og, cot, outw, coef,
    normed, gate, pre, ext, delta, logs, mixed, carried, states, sums, dno, endlog, cot_all, w_out,
    proj_s, pre_s, gate_s, delta_s, logs_s, sloc, inner, dno_s, state, total, tail, ends, cot_s, w_o, w_s, send, recv, done,
):
    t = pl.program_id(0)
    c = lax.rem(t, CH)
    at = lax.rem(t, 8)
    micro = at // CH
    eh = spread_matrix()
    n = Net(send, recv)
    g, m, core = n.g, n.m, n.c

    def cot_z(a):
        return n.copy(("cot", a), cot_s.at[m], cot_s.at[m], n.at(dz=a))

    def cot_near():
        return n.copy("near", cot_s.at[m], cot_s.at[m], n.at(dc=1))

    def cot_on(a):
        theirs = cot_s.at[2 * lax.rem(n.z + 4 - a, 4) + core]
        return n.copy(("on", a), theirs, theirs, n.at(dc=1))

    def out_x(d):
        return n.copy(("ox", d), w_o.at[g], w_o.at[g], n.at(dx=d))

    def out_y(d, half):
        part = w_o.at[n.behind(d), pl.ds(32 * half, 32)]
        return n.copy(("oy", d, half), part, part, n.at(dy=3 if half else 1))

    def out_swap():
        return n.copy("swap", w_o.at[pl.ds(4 * (1 - core), 4)], w_s.at[:, core], n.at(dc=1))

    def end_x(i, d):
        return n.copy(("ex", i, d), ends.at[g, i], ends.at[g, i], n.at(dx=d))

    def end_y(i, d):
        part = ends.at[n.behind(d), i]
        return n.copy(("ey", i, d), part, part, n.pair())

    ALLX = (0,) + XS
    out_copies = [pltpu.make_async_copy(cot_s, cot_all, done.at[0]), pltpu.make_async_copy(w_s, w_out, done.at[1])]

    @pl.when(t == 0)
    def _():
        n.meet([n.at(dz=a) for a in (1, 3, 2)] + [n.at(dc=1)] + [n.at(dx=d) for d in XS] + [n.at(dy=1), n.at(dy=3)])
        cot_s[m] = cot[...]
        w_o[g] = outw[...]
        for d in XS:
            out_x(d).start()
        for half in (0, 1):
            out_y(0, half).start()
        for a in (1, 3, 2):
            cot_z(a).start()
        cot_near().start()

    @pl.when((t < 8) & (c == 0))
    def _():
        h = hid[...].reshape(TOK, 2048).astype(F32)
        nb = (h * row_scale(h) * gain[...]).astype(BF16)
        normed[...] = nb.reshape(8, 1, 64, 2048)
        e = halo[0].astype(F32)
        eb = (e * row_scale(e) * gain[...]).astype(BF16)
        proj_s[...] = bdot(jnp.concatenate([eb, nb], 0), w[...])
        tail[0:8] = proj_s[8:16, 512:1280].astype(BF16).astype(F32)
        state[...] = jnp.zeros_like(state)
        total[...] = jnp.zeros_like(total)

    @pl.when(t < 8)
    def _():
        rows = pl.ds(pl.multiple_of(16 + Q * c, 16), Q)
        f = flags[...]
        gt = proj_s[rows, 0:512]
        gate[...] = gt
        gate_s[at] = gt
        xbc = proj_s[rows, 512:1280].astype(BF16).astype(F32)
        tail[8:] = xbc
        acc = conv[4:5] + conv[3:4] * xbc
        for k in range(3):
            acc = acc + conv[k : k + 1] * tail[5 + k : 5 + k + Q] * f[:, k : k + 1]
        pre[...] = acc
        pre_s[at] = acc
        ext[0] = tail[...]
        d = softplus(proj_s[rows, 1280:1408] + hp[0:1])
        delta[...] = d
        delta_s[at] = d
        L = right_parts(lower_matrix(), d * hp[1:2], 3)
        logs[...] = L
        logs_s[at] = L
        E, W = decays(L, f)
        x = acc[:, :512]
        X = x * sigmoid(x)
        b = acc[:, 512:640]
        B = (b * sigmoid(b)).astype(BF16)
        S = right_parts(B, heads_of(W * d, eh) * X, 2, TN)
        sloc[at] = S
        both = heads_of(jnp.concatenate([E[Q - 8 :], L[Q - 8 :]], 0), eh)
        new = both[7:8] * state[...] + S
        state[...] = new
        tail[0:8] = tail[Q : Q + 8]
        lt = total[...] + L[Q - 1 : Q]
        total[...] = lt

        @pl.when(c == CH - 1)
        def _():
            ends[g, micro, 0:128] = new.astype(BF16)
            p = parts(jnp.broadcast_to(heads_of(jnp.broadcast_to(lt, (8, 128)), eh)[0:1], (16, 512)), 3)
            r = iota((16, 512), 0)
            ends[g, micro, 128:144] = jnp.where(r == 0, p[0], jnp.where(r == 1, p[1], jnp.where(r == 2, p[2], jnp.zeros_like(p[0]))))

    for i, when in ((0, CH - 1), (1, 2 * CH - 1)):

        @pl.when(t == when)
        def _(i=i):
            for d in XS:
                end_x(i, d).start()
            end_y(i, 0).start()

    @pl.when(t == 4)
    def _():
        for d in XS:
            out_x(d).wait_recv()
            for half in (0, 1):
                out_y(d, half).start()

    for i, when in ((0, 6), (1, 11)):

        @pl.when(t == when)
        def _(i=i):
            for d in XS:
                end_x(i, d).wait_recv()
                end_y(i, d).start()

    @pl.when(t == 8)
    def _():
        for d in ALLX:
            for half in (0, 1):
                out_y(d, half).wait_recv()
        out_swap().start()
        for k in range(4):
            w_s[k, core] = w_o[4 * core + k]
        for a in (1, 3, 2):
            cot_z(a).wait_recv()
            cot_on(a).start()

    @pl.when((t >= 8) & (t < 16))
    def _():
        L = logs_s[at]
        a = pre_s[at]
        X, B, C = activations(a)
        U = (heads_of(delta_s[at], eh) * X).astype(BF16)
        psi = bdot(C, B, NT)
        keep = same_mask(flags[...], segrow[0])
        LT = L.T
        for j in range(4):
            u = pair_halves(U[:, 128 * j : 128 * j + 128])
            y = jnp.zeros((Q, 128), F32)
            for e in range(2):
                h = 2 * j + e
                K = jnp.where(keep, jnp.exp(L[:, h : h + 1] - LT[h : h + 1]), 0.0)
                y = y + bdot((psi * K).astype(BF16), u[e])
            inner[at, :, 128 * j : 128 * j + 128] = y

    @pl.when(t == 16)
    def _():
        out_swap().wait_recv()
        cot_near().wait_recv()
        for a in (1, 3, 2):
            cot_on(a).wait_recv()
        for cp in out_copies:
            cp.start()
        for i in (0, 1):
            for d in ALLX:
                end_y(i, d).wait_recv()
        for q in range(8):
            for i in range(2):
                endlog[q, i] = ends[q, i, 128:144]

    @pl.when((t >= 16) & (c == 0))
    def _():
        dno_s[...] = bdot(cot_s[:, micro].reshape(TOK, 2048), w_s[...].reshape(512, 2048), NT)
        state[...] = entering(ends, coef, 0, micro)

    @pl.when(t >= 16)
    def _():
        f = flags[...]
        E, _ = decays(logs_s[at], f)
        a = pre_s[at]
        X, _, C = activations(a)
        more = heads_of(jnp.concatenate([E, jnp.broadcast_to(hp[2:3], (8, 128))], 0), eh)
        Ex, skip = more[:Q], more[Q : Q + 1]
        S = state[...]
        states[0, 0] = S
        Yc = Ex * bdot(C, S.astype(BF16))
        carried[...] = Yc
        mix = inner[at] + Yc + skip * X
        mixed[...] = mix
        after = Ex[Q - 1 : Q] * S + sloc[at]
        state[...] = after
        states[0, 1] = after
        gt = gate_s[at]
        gated = mix * (gt * sigmoid(gt))
        dn = dno_s[pl.ds(pl.multiple_of(Q * c, Q), Q)]
        dno[...] = dn
        ones = jnp.ones((8, 512), BF16)
        sums[0, 0:8] = right_parts(ones, gated * gated, 2, NT)
        sums[0, 8:16] = right_parts(ones, dn * og[...] * gated, 2, NT)

    @pl.when(t == 23)
    def _():
        for cp in out_copies:
            cp.wait()
        for a in (1, 3, 2):
            cot_z(a).wait_send()
            cot_on(a).wait_send()
        cot_near().wait_send()
        out_swap().wait_send()
        for d in XS:
            out_x(d).wait_send()
        for d in ALLX:
            for half in (0, 1):
                out_y(d, half).wait_send()
        for i in (0, 1):
            for d in XS:
                end_x(i, d).wait_send()
            for d in ALLX:
                end_y(i, d).wait_send()


def tile(width, at=lambda t: t):
    return pl.BlockSpec((Q, width), lambda t: (at(t), 0))


def whole(*shape):
    return pl.BlockSpec(shape, lambda t: (0,) * len(shape))


def plain(kernel, name, outs, ins, spaces_in, spaces_out, scratch=(), flops=1 << 30):
    return pl.pallas_call(
        kernel,
        name=name,
        grid=(MICRO * CH,),
        out_shape=outs,
        in_specs=spaces_in,
        out_specs=spaces_out,
        scratch_shapes=list(scratch),
        compiler_params=pltpu.CompilerParams(vmem_limit_bytes=56 << 20),
        cost_estimate=pl.CostEstimate(flops=flops, bytes_accessed=16 << 20, transcendentals=0),
    )(*ins)


T = MICRO * TOK
HID = pl.BlockSpec((2, 1, 64, 2048), lambda t: (t % CH, t // CH, 0, 0))


def agblock(width, at=lambda t: t):
    return pl.BlockSpec((2, 1, 64, width), lambda t: (at(t) % CH, at(t) // CH, 0, 0))


def wave(hid, halo, gain, w, conv, hp, flags, segrow, og, cot, outw, coef):
    outs = [
        sds((8, 2, 64, 2048), BF16), sds((T, 512), F32), sds((T, 768), F32), sds((8, Q + 8, 768), F32), sds((T, 128), F32), sds((T, 128), F32),
        sds((T, 512), F32), sds((T, 512), F32), sds((8, 2, 128, 512), F32), sds((8, 16, 128), F32), sds((T, 512), F32), sds((8, 2, 16, 512), BF16), sds((8, 2, 64, 2048), BF16), sds((4, 2, 64, 2048), BF16),
    ]
    first = lambda t: jnp.minimum(t, 7)
    last = lambda t: jnp.maximum(t - 16, 0)
    ring = lambda t: t % 8
    micro = pl.BlockSpec((8, 1, 64, 2048), lambda t: (0, first(t) // CH, 0, 0))
    V = lambda *shape: pltpu.VMEM(shape, F32)
    return pl.pallas_call(
        wave_kernel,
        name="wave",
        grid=(24,),
        out_shape=outs,
        in_specs=[
            micro, pl.BlockSpec((1, 16, 2048), lambda t: (first(t) // CH, 0, 0)), whole(1, 2048), whole(2048, 1408), whole(8, 768), whole(8, 128), tile(128, ring), blk(1, 128, ring), whole(1, 512),
            whole(2, 64, 2048), whole(64, 2048), SMEM,
        ],
        out_specs=[
            micro, tile(512, first), tile(768, first), blk(Q + 8, 768, first), tile(128, first), tile(128, first),
            tile(512, last), tile(512, last), pl.BlockSpec((1, 2, 128, 512), lambda t: (last(t), 0, 0, 0)), blk(16, 128, last), tile(512, last), whole(8, 2, 16, 512), ANY, ANY,
        ],
        scratch_shapes=[
            V(TOK + 16, 1408), V(8, Q, 768), V(8, Q, 512), V(8, Q, 128), V(8, Q, 128), V(8, 128, 512), V(8, Q, 512), V(TOK, 512), V(128, 512), V(1, 128), V(Q + 8, 768),
            pltpu.VMEM((8, 2, 144, 512), BF16), pltpu.VMEM((8, 2, 64, 2048), BF16), pltpu.VMEM((8, 64, 2048), BF16), pltpu.VMEM((4, 2, 64, 2048), BF16),
            pltpu.SemaphoreType.DMA((48,)), pltpu.SemaphoreType.DMA((48,)), pltpu.SemaphoreType.DMA((2,)),
        ],
        compiler_params=pltpu.CompilerParams(collective_id=1, has_side_effects=True, vmem_limit_bytes=60 << 20),
        cost_estimate=pl.CostEstimate(flops=8 << 30, bytes_accessed=32 << 20, transcendentals=0),
    )(hid, halo, gain, w, conv, hp, flags, segrow, og, cot, outw, coef)


def entering(everyone, coef, direction, micro, logs=None):
    total = jnp.zeros((128, 512), F32)
    at = 0 if everyone.shape[1] == 1 else micro
    rows = [(everyone[q, at, 128:144] if logs is None else logs[q, 0]).astype(F32) for q in range(8)]
    lt = [v[0:1] + v[1:2] + v[2:3] for v in rows]
    for q in range(8):
        log = sum(coef[80 * direction + 8 * q + r] * lt[r] for r in range(8))
        total = total + jnp.exp(log) * coef[80 * direction + 64 + 8 * micro + q] * everyone[q, at, 0:128].astype(F32)
    return total


def same_mask(flags, segrow):
    return (flags[:, 5:6] == segrow) & (iota((Q, Q), 0) >= iota((Q, Q), 1))


def activations(pre):
    a = pre * sigmoid(pre)
    return a[:, :512], a[:, 512:640].astype(BF16), a[:, 640:768].astype(BF16)


def pair_halves(v):
    low_half = iota(v.shape, 1) < 64
    zero = jnp.zeros_like(v)
    return jnp.where(low_half, v, zero), jnp.where(low_half, zero, v)


def blk(a, b, at=lambda t: t):
    return pl.BlockSpec((1, a, b), lambda t: (at(t), 0, 0))


SMEM = pl.BlockSpec(memory_space=pltpu.SMEM)


def column(row):
    return jnp.concatenate([jnp.broadcast_to(row, (128, 128)).T] * 4, 1)


def out_kernel(mixed, gate, dno, sums, pre, logs, flags, og, hp, nout, dmix, dgate, tloc, starts, small, state):
    t = pl.program_id(0)
    c = CH - 1 - lax.rem(t, CH)
    eh = spread_matrix()

    @pl.when(c == CH - 1)
    def _():
        state[...] = jnp.zeros_like(state)

    @pl.when(t == 0)
    def _():
        small[...] = jnp.zeros_like(small)

    tot = sums[0, 0]
    for q in range(1, 8):
        tot = tot + sums[q, 0]
    r = column(lax.rsqrt(tot[0:1] / INNER + EPS))
    s2 = column(tot[8:9] / INNER)
    gt = gate[...]
    s = sigmoid(gt)
    sg = gt * s
    mix = mixed[...]
    gated = mix * sg
    dn = dno[...]
    n0 = gated * r
    nout[...] = (n0 * og[...]).astype(BF16).reshape(2, 1, 64, 512)
    d_gated = r * (dn * og[...] - n0 * r * s2)
    dm = d_gated * sg
    dmix[...] = dm
    dgate[...] = (d_gated * mix * (s * (1.0 + gt * (1.0 - s)))).astype(BF16)
    x = pre[:, :512]
    X = x * sigmoid(x)
    cc = pre[:, 640:768]
    C = (cc * sigmoid(cc)).astype(BF16)
    small[0:1] += jnp.sum(dn * n0, 0, keepdims=True)
    small[1:2] += jnp.sum(X * dm, 0, keepdims=True)
    E, _ = decays(logs[...], flags[...])
    Ex = heads_of(E, eh)
    G = right_parts(C, Ex * dm, 2, TN)
    tloc[0] = G
    new = Ex[Q - 1 : Q] * state[...] + G
    state[...] = new

    @pl.when(c == 0)
    def _():
        starts[0] = new.astype(BF16)


def back_at(t):
    return (t // CH) * CH + (CH - 1 - t % CH)


def out_call(mixed, gate, dno, sums, pre, logs, flags, og, hp):
    outs = [sds((8, 2, 64, 512), BF16), sds((T, 512), F32), sds((T, 512), BF16), sds((8, 128, 512), F32), sds((2, 128, 512), BF16), sds((8, 512), F32)]
    b = back_at
    return plain(
        out_kernel, "out", outs, (mixed, gate, dno, sums, pre, logs, flags, og, hp),
        [tile(512, b), tile(512, b), tile(512, b), pl.BlockSpec((8, 1, 16, 128), lambda t: (0, back_at(t), 0, 0)), tile(768, b), tile(128, b), tile(128, b), whole(1, 512), whole(8, 128)],
        [agblock(512, b), tile(512, b), tile(512, b), blk(128, 512, b), blk(128, 512, lambda t: t // CH), whole(8, 512)],
        [pltpu.VMEM((128, 512), F32)],
    )


def back_kernel(pre, delta, logs, flags, segrow, mixed, carried, dmix, states, tloc, starts, ends, hp, coef, dpre, dbc, ddt, small, state):
    t = pl.program_id(0)
    c = CH - 1 - lax.rem(t, CH)
    eh = spread_matrix()

    @pl.when(c == CH - 1)
    def _():
        state[...] = entering(starts, coef, 1, t // CH, ends)

    @pl.when(t == 0)
    def _():
        small[...] = jnp.zeros_like(small)

    L = logs[...]
    f = flags[...]
    d = delta[...]
    E, W = decays(L, f)
    p = pre[...]
    s = sigmoid(p)
    X = p[:, :512] * s[:, :512]
    B = (p[:, 512:640] * s[:, 512:640]).astype(BF16)
    C = (p[:, 640:] * s[:, 640:]).astype(BF16)
    more = heads_of(jnp.concatenate([E, W, d, jnp.broadcast_to(hp[2:3], (8, 128))], 0), eh)
    Ex, Wx, dx, skip = more[:Q], more[Q : 2 * Q], more[2 * Q : 3 * Q], more[3 * Q : 3 * Q + 1]
    U = dx * X
    Ub = U.astype(BF16)
    dm = dmix[...]
    dmb = dm.astype(BF16)
    Yc = carried[...]
    Yi = mixed[...] - Yc - skip * X
    G = state[...]
    Gb = G.astype(BF16)
    psi = bdot(C, B, NT)
    keep = same_mask(f, segrow[0])
    LT = L.T
    dpsi = jnp.zeros((Q, Q), F32)
    cols = []
    for j in range(4):
        js = slice(128 * j, 128 * j + 128)
        u = pair_halves(Ub[:, js])
        y = pair_halves(dmb[:, js])
        acc = jnp.zeros((Q, 128), F32)
        for e in range(2):
            h = 2 * j + e
            K = jnp.where(keep, jnp.exp(L[:, h : h + 1] - LT[h : h + 1]), 0.0)
            acc = acc + bdot((psi * K).astype(BF16), y[e], TN)
            dpsi = dpsi + bdot(y[e], u[e], NT) * K
        cols.append(acc)
    dUi = jnp.concatenate(cols, 1)
    dUc = Wx * bdot(B, Gb)
    dU = dUi + dUc
    S0, S1 = states[0, 0], states[0, 1]
    dpb = dpsi.astype(BF16)
    dbc[0:128] = (bdot(C, dpb, TN) + bdot(Gb, (Wx * U).astype(BF16), NT)).astype(BF16)
    dbc[128:256] = (bdot(B, dpb, TT) + bdot(S0.astype(BF16), (Ex * dm).astype(BF16), NT)).astype(BF16)
    dL = sums_of(dmb.astype(F32) * Yi + dm * Yc - Ub.astype(F32) * dUi - U * dUc, eh)
    end = sums_of(jnp.broadcast_to(jnp.sum(G * S1, 0, keepdims=True), (8, 512)), eh)[0:1]
    upper = (iota((Q, Q), 0) <= iota((Q, Q), 1)).astype(BF16)
    dstep = right_parts(upper, dL, 3) + end
    rate = hp[1:2]
    dd = sums_of(dU * X, eh) + dstep * rate
    dr = dd * (1.0 - jnp.exp(-d))
    ddt[...] = dr.astype(BF16)
    small[0:1] += jnp.sum(dr, 0, keepdims=True)
    small[1:2] += jnp.sum(dstep * d * rate, 0, keepdims=True)
    sx = s[:, :512]
    dpre[...] = (dx * dU + skip * dm) * (sx * (1.0 + p[:, :512] * (1.0 - sx)))
    state[...] = Ex[Q - 1 : Q] * G + tloc[0]


def back_call(pre, delta, logs, flags, segrow, mixed, carried, dmix, states, tloc, starts, ends, hp, coef):
    outs = [sds((T, 512), F32), sds((256, T), BF16), sds((T, 128), BF16), sds((8, 128), F32)]
    b = back_at
    return plain(
        back_kernel, "back", outs, (pre, delta, logs, flags, segrow, mixed, carried, dmix, states, tloc, starts, ends, hp, coef),
        [tile(768, b), tile(128, b), tile(128, b), tile(128, b), blk(1, 128, b), tile(512, b), tile(512, b), tile(512, b), pl.BlockSpec((1, 2, 128, 512), lambda t: (back_at(t), 0, 0, 0)), blk(128, 512, b), pl.BlockSpec((8, 1, 128, 512), lambda t: (0, t // CH, 0, 0)), pl.BlockSpec((8, 1, 16, 512), lambda t: (0, t // CH, 0, 0)), whole(8, 128), SMEM],
        [tile(512, b), pl.BlockSpec((256, Q), lambda t: (0, back_at(t))), tile(128, b), whole(8, 128)],
        [pltpu.VMEM((128, 512), F32)],
    )


def pick_matrix(rows, start, count, shift, dtype=BF16):
    r, l = iota((rows, 128), 0), iota((rows, 128), 1)
    return ((r - start == l - shift) & (l >= shift) & (l < shift + count)).astype(dtype)


def bc_kernel(parts_in, pre, where, dpre):
    total = parts_in[0].astype(F32)
    for q in range(1, 8):
        total = total + parts_in[q].astype(F32)
    eye = pick_matrix(32, 0, 32, 0)
    d = left_parts(total, eye, 2, TN)
    p = left_parts(pre[:, 512:768], pick_matrix(256, 32 * where[0], 32, 0), 3)
    s = sigmoid(p)
    dpre[...] = d * (s * (1.0 + p * (1.0 - s)))


def bc_call(parts_in, pre, where):
    return plain(
        bc_kernel, "bc", sds((T, 128), F32), (parts_in, pre, where),
        [pl.BlockSpec((8, 32, Q), lambda t: (0, 0, t)), tile(768), SMEM], tile(128),
    )


def conv_back_kernel(dpre, dbc, nextx, nextbc, ext, flags, fnext, conv, ddt, dgate, where, w_b, hid, dproj, small, dn, gnorm, ahead, e, rows):
    t = pl.program_id(0)
    c = CH - 1 - lax.rem(t, CH)

    @pl.when(c == CH - 1)
    def _():
        ahead[Q:, 0:512] = nextx[0]
        ahead[Q:, 512:640] = nextbc[0]

    @pl.when(t == 0)
    def _():
        small[...] = jnp.zeros_like(small)

    pick = pick_matrix(256, 32 * where[0], 32, 0)
    ahead[0:Q, 0:512] = dpre[...]
    ahead[0:Q, 512:640] = dbc[...]
    dp = ahead[0:Q]
    cw = jnp.concatenate([conv[:, 0:512], left_parts(conv[:, 512:768], pick, 3)], 1)
    e[:, 0:512] = ext[0, :, 0:512]
    e[:, 512:640] = bdot(ext[0, :, 512:768].astype(BF16), pick)
    f, fn = flags[...], fnext[...]
    dx = cw[3:4] * dp
    small[3:4] += jnp.sum(dp * e[8 : 8 + Q], 0, keepdims=True)
    small[4:5] += jnp.sum(dp, 0, keepdims=True)
    for k in range(3):
        small[k : k + 1] += jnp.sum(dp * e[5 + k : 5 + k + Q] * f[:, k : k + 1], 0, keepdims=True)
        dx = dx + cw[k : k + 1] * ahead[3 - k : 3 - k + Q] * fn[:, k : k + 1]
    moved = bdot(ddt[...], pick_matrix(128, 0, 8, 32))
    full = jnp.concatenate([dgate[...], dx[:, 0:512].astype(BF16), (dx[:, 512:640] + moved).astype(BF16)], 1)
    dproj[...] = full.reshape(2, 1, 64, 1152)
    rows[pl.ds(pl.multiple_of(Q * c, Q), Q)] = full
    ahead[Q:] = ahead[0:8]

    @pl.when(c == 0)
    def _():
        d = bdot(rows[...], w_b[...], NT)
        dn[...] = d.astype(BF16).reshape(8, 1, 64, 2048)
        h = hid[...].reshape(TOK, 2048).astype(F32)
        part = jnp.sum(d * (h * row_scale(h)), 0, keepdims=True)

        @pl.when(t < CH)
        def _():
            gnorm[...] = part

        @pl.when(t >= CH)
        def _():
            gnorm[...] += part


def conv_back_call(dpre, dbc, nextx, nextbc, ext, flags, fnext, conv, ddt, dgate, where, w_b, hid):
    b = back_at
    micro = lambda t: t // CH
    return plain(
        conv_back_kernel, "conv_back", [sds((8, 2, 64, 1152), BF16), sds((8, 640), F32), sds((8, 2, 64, 2048), BF16), sds((1, 2048), F32)], (dpre, dbc, nextx, nextbc, ext, flags, fnext, conv, ddt, dgate, where, w_b, hid),
        [tile(512, b), tile(128, b), blk(8, 512, micro), blk(8, 128, micro), blk(Q + 8, 768, b), tile(128, b), tile(128, b), whole(8, 768), tile(128, b), tile(512, b), SMEM, whole(2048, 1152), pl.BlockSpec((8, 1, 64, 2048), lambda t: (0, t // CH, 0, 0))],
        [agblock(1152, b), whole(8, 640), pl.BlockSpec((8, 1, 64, 2048), lambda t: (0, t // CH, 0, 0)), whole(1, 2048)],
        [pltpu.VMEM((Q + 8, 640), F32)] * 2 + [pltpu.VMEM((TOK, 1152), BF16)],
    )


def strips(v, zi, ci):
    r = v.shape[0]
    return lax.dynamic_slice(v.reshape(r, 2, 4, 4, 128), (0, ci, 0, zi, 0), (r, 1, 4, 1, 128)).reshape(r, 512)


def from_members(v):
    r = v.shape[1]
    return v.reshape(4, 2, r, 4, 128).transpose(2, 1, 3, 0, 4).reshape(r, 4096)


def from_heads(v):
    r = v.shape[1]
    return v.reshape(4, 2, r, 4, 2).transpose(2, 1, 3, 0, 4).reshape(r, 64)


def from_rows(v):
    return v.transpose(1, 0, 2).reshape(v.shape[1], 256)


def to_members(v):
    r = v.shape[0]
    return v.reshape(r, 2, 4, 4, 128).transpose(3, 1, 0, 2, 4).reshape(8, r, 512)


def xdot(a, b, dims=NN):
    return lax.dot_general(a, b, dims, preferred_element_type=F32)


def per_device(layer_in, cotangent, segment_ids, norm_gain, in_weight, conv_weight, conv_bias, dt_bias, a_log, skip_gain, out_gain, out_weight):
    xi, yi, zi, ci = (lax.axis_index(a) for a in SEQ)
    g = 2 * xi + yi
    m = 2 * zi + ci
    where = m.astype(jnp.int32).reshape(1)
    pack = jnp.concatenate([segment_ids[:, 0].astype(F32).reshape(-1), norm_gain, conv_weight.reshape(-1), conv_bias, dt_bias, a_log, skip_gain, out_gain, jnp.zeros((1024 - 567,), F32)]).reshape(8, 128)
    bc = jnp.broadcast_to(in_weight[None, :, 8192:8448], (8, 32, 256))
    dt_w = in_weight[:, 8448:].reshape(32, 2, 4, 4, 2).transpose(3, 1, 0, 2, 4).reshape(8, 32, 8)
    w_send = jnp.concatenate([to_members(in_weight[:, :4096]), to_members(in_weight[:, 4096:8192]), bc, dt_w, jnp.zeros((8, 32, 120), BF16)], 2)
    hid_all, w_in, small_all, halo = gather(layer_in[:, 0], w_send, pack)
    w_in = w_in.reshape(2048, 1408)
    full = small_all.reshape(64, 1024)
    seg_full = full[:, :128].reshape(64, 2, 64).transpose(1, 0, 2).reshape(2, 4096)
    full = full[:, 128:]
    norm_full = full[:, :32].reshape(1, 2048)
    conv_full = full[:, 32:372].reshape(64, 5, 68).transpose(1, 0, 2).reshape(5, CONV)
    conv = jnp.concatenate([strips(conv_full[:, :INNER], zi, ci), conv_full[:, INNER:]], 1)
    conv = jnp.pad(conv, ((0, 3), (0, 0)))
    hv = lax.dynamic_slice(full[:, 372:439].reshape(2, 4, 4, 2, 67), (ci, 0, zi, 0, 0), (1, 4, 1, 2, 67)).reshape(8, 67)
    og = hv[:, 3:].reshape(1, 512)
    hp = jnp.pad(jnp.stack([hv[:, 0], -jnp.exp(hv[:, 1]), hv[:, 2]]), ((0, 5), (0, 120)))

    padded = jnp.concatenate([jnp.full((MICRO, 8), -1.0, F32), seg_full, jnp.full((MICRO, 8), -2.0, F32)], 1)
    near = lax.dynamic_slice(padded, (0, g * TOK), (MICRO, TOK + 16))
    own = near[:, 8 : 8 + TOK]
    chunked = own.reshape(MICRO, CH, Q)
    before = jnp.concatenate([near[:, 7:8], chunked[:, :-1, -1]], 1)[:, :, None]
    lanes = [(near[:, 5 + k : 5 + k + TOK] == own).astype(F32).reshape(T) for k in range(3)]
    lanes += [(chunked == before).astype(F32).reshape(T), (chunked == chunked[:, :, -1:]).astype(F32).reshape(T), own.reshape(T)]
    flags = jnp.pad(jnp.stack(lanes, 1), ((0, 0), (0, 122)))
    fnext = jnp.pad(jnp.stack([(near[:, 11 - k : 11 - k + TOK] == own).astype(F32).reshape(T) for k in range(3)], 1), ((0, 0), (0, 125)))
    segrow = own.reshape(8, 1, Q)
    lasts = seg_full.reshape(MICRO, GROUPS, TOK)[:, :, -1]
    idx = jnp.arange(GROUPS)
    q, r = idx[:, None], idx[None, :]
    last_before = jnp.sum(jnp.where(idx == g - 1, lasts, 0.0), 1, keepdims=True)
    last_own = jnp.sum(jnp.where(idx == g, lasts, 0.0), 1, keepdims=True)
    ok_before = (idx < g) & (lasts == last_before)
    ok_after = (idx > g) & (jnp.roll(lasts, 1, axis=1) == last_own)
    coef = jnp.concatenate([((r > q) & (r < g)).astype(F32), ok_before.astype(F32), ((r > g) & (r < q)).astype(F32), ok_after.astype(F32)], 0).reshape(160)

    normed, gate, pre, ext, delta, logs, mixed, carried, states, sums, dno, ends_all, cot, w_out = wave(hid_all, halo, norm_full, w_in, conv, hp, flags, segrow, og, cotangent[:, 0], out_weight, coef)
    sums_all = member_gather(sums, "norm_sums", 2)
    nout, dmix, dgate, tloc, starts, small_o = out_call(mixed, gate, dno, sums_all, pre, logs, flags, og, hp)
    nout = nout.reshape(T, 512)
    branch = xdot(nout, w_out.reshape(512, 2048)).astype(BF16).reshape(8, 2, 64, 2048)
    g_wout = xdot(nout, cot.reshape(T, 2048), TN).astype(BF16).reshape(4, 2, 64, 2048)
    starts_all, own_branch = backward_states(starts, branch)
    dpre, dbc, ddt, small_b = back_call(pre, delta, logs, flags, segrow, mixed, carried, dmix, states, tloc, starts_all, ends_all, hp, coef)
    bc_all, nextx = bc_swap(dbc.reshape(8, 32, T), dpre.reshape(MICRO, TOK, 512)[:, :8])
    dpre_bc = bc_call(bc_all, pre, where)
    nextbc = edge_back(dpre_bc.reshape(MICRO, TOK, 128)[:, :8])
    tail = xdot(w_in[:, 1024:1280], pick_matrix(256, 32 * m, 32, 0)) + xdot(w_in[:, 1280:1408], pick_matrix(128, 0, 8, 32))
    w_b = jnp.concatenate([w_in[:, :1024], tail.astype(BF16)], 1)
    dproj, small_c, d_normed, g_norm = conv_back_call(dpre, dpre_bc, nextx, nextbc, ext, flags, fnext, conv, ddt, dgate, where, w_b, hid_all)
    gw = xdot(normed.reshape(T, 2048), dproj.reshape(T, 1152), TN).astype(BF16).reshape(8, 8, 32, 1152)
    g_skip = small_o[1].reshape(8, 64).sum(1)
    heads_g = jnp.pad(jnp.concatenate([small_b[0, :8], small_b[1, :8], g_skip]), (0, 128 - 24))
    small = jnp.concatenate([g_norm[0], small_c[:5].reshape(-1), small_o[0], heads_g, jnp.zeros((256,), F32)]).reshape(48, 128)
    gi, g_out, own_dn, small_sum = final_exchange(gw, g_wout, d_normed, small)
    gi = gi.astype(F32)
    hid_o = layer_in[:, 0].astype(F32)
    layer_out = (hid_o + own_branch).astype(BF16)
    ro = row_scale(hid_o)
    dg = own_dn * norm_full
    d_hid = ro * dg - hid_o * (ro * ro * ro) * jnp.mean(dg * hid_o, -1, keepdims=True)
    grad_in = (cotangent[:, 0].astype(F32) + d_hid).astype(BF16)
    g_in = jnp.concatenate([from_members(gi[:, :, :512]), from_members(gi[:, :, 512:1024]), from_rows(gi[:, :, 1024:1056]), from_heads(gi[:, :, 1056:1064])], 1)
    at = 8 * g + m
    g_norm = lax.dynamic_slice(small_sum[:, :16].sum(0).reshape(64, 32), (at, 0), (1, 32)).reshape(32)
    conv_s = small_sum[:, 16:41].reshape(8, 5, 640)
    conv_s = jnp.concatenate([from_members(conv_s[:, :, :512]), from_rows(conv_s[:, :, 512:544])], 1)
    conv_s = lax.dynamic_slice(conv_s, (0, 68 * at), (5, 68))
    og_s = from_members(small_sum[:, 41:45].reshape(8, 1, 512))[0]
    og_s = lax.dynamic_slice(og_s, (64 * at,), (64,))
    hd_s = from_heads(small_sum[:, 45, :24].reshape(8, 3, 8))
    hd_s = lax.dynamic_slice(hd_s, (0, at), (3, 1))
    return (layer_out[:, None], grad_in[:, None], g_norm, g_in, conv_s[:4], conv_s[4], hd_s[0], hd_s[1], hd_s[2], og_s, g_out)


def solution(mesh):
    fine = Mesh(mesh.devices.reshape(2, 4, 2, 4, 2), AXES)
    tok = P(None, "rep", SEQ, None)
    return jax.shard_map(
        per_device,
        mesh=fine,
        in_specs=(tok, tok, P(None, "rep", SEQ), P(SEQ), P(SEQ, None), P(None, SEQ), P(SEQ), P(SEQ), P(SEQ), P(SEQ), P(SEQ), P(SEQ, None)),
        out_specs=(tok, tok, P(SEQ), P(SEQ, None), P(None, SEQ), P(SEQ), P(SEQ), P(SEQ), P(SEQ), P(SEQ), P(SEQ, None)),
        check_vma=False,
    )
```

```python
import functools

import jax
import jax.numpy as jnp
from jax import lax
from jax.experimental import pallas as pl
from jax.experimental.pallas import tpu as pltpu
from jax.sharding import Mesh, PartitionSpec as P

EPS = 1e-05
INNER = 4096
MICRO = 2
CONV = 4352
F32 = jnp.float32
BF16 = jnp.bfloat16
AXES = ("rep", "x", "y", "z", "c")
SEQ = ("x", "y", "z", "c")
GROUPS = 8
TOK = 512
Q = 128
CH = TOK // Q

MESH = pl.DeviceIdType.MESH
ANY = pl.BlockSpec(memory_space=pl.ANY)
VM = pl.BlockSpec(memory_space=pltpu.VMEM)


class Net:
    def __init__(self, send, recv):
        self.send, self.recv, self.used, self.open = send, recv, 0, []
        self.keys = {}
        self.rep, self.x, self.y, self.z, self.c = (lax.axis_index(a) for a in AXES)
        self.ring = 2 * self.rep + self.y
        self.g = 2 * self.x + self.y
        self.m = 2 * self.z + self.c

    def at(self, dx=0, dy=0, dz=0, dc=0):
        ring = lax.rem(self.ring + dy, 4)
        return (ring // 2, lax.rem(self.x + dx, 4), lax.rem(ring, 2), lax.rem(self.z + dz, 4), lax.rem(self.c + dc, 2))

    def pair(self):
        return (self.rep, self.x, 1 - self.y, self.z, self.c)

    def group(self, d):
        g = lax.rem(self.g + d, 8)
        return (self.rep, g // 2, lax.rem(g, 2), self.z, self.c)

    def member(self, dz, dc):
        return 2 * lax.rem(self.z + dz, 4) + lax.rem(self.c + dc, 2)

    def push(self, src, dst, where):
        i = self.used
        self.used += 1
        copy = pltpu.make_async_remote_copy(
            src_ref=src, dst_ref=dst, send_sem=self.send.at[i], recv_sem=self.recv.at[i], device_id=where, device_id_type=MESH
        )
        copy.start()
        self.open.append(copy)
        return copy

    def copy(self, key, src, dst, where):
        i = self.keys.setdefault(key, len(self.keys))
        return pltpu.make_async_remote_copy(
            src_ref=src, dst_ref=dst, send_sem=self.send.at[i], recv_sem=self.recv.at[i], device_id=where, device_id_type=MESH
        )

    def behind(self, d):
        return 2 * lax.rem(self.x + 4 - d, 4) + self.y

    def local(self, src, dst):
        i = self.used
        self.used += 1
        copy = pltpu.make_async_copy(src, dst, self.recv.at[i])
        copy.start()
        return copy

    def meet(self, peers):
        barrier = pltpu.get_barrier_semaphore()
        for peer in peers:
            pl.semaphore_signal(barrier, inc=1, device_id=peer, device_id_type=MESH)
        pl.semaphore_wait(barrier, len(peers))

    def finish(self):
        for copy in self.open:
            copy.wait_send()


OTHERS = [(dz, dc) for dz in (0, 1, 3, 2) for dc in (0, 1) if (dz, dc) != (0, 0)]
ZS = (0, 1, 3, 2)
XS = (1, 3, 2)


def call(kernel, name, cid, outs, ins, spaces_in, spaces_out, sems, scratch=(), cost=1 << 20):
    return pl.pallas_call(
        kernel,
        name=name,
        out_shape=outs,
        in_specs=spaces_in,
        out_specs=spaces_out,
        scratch_shapes=[*scratch, pltpu.SemaphoreType.DMA((sems,)), pltpu.SemaphoreType.DMA((sems,))],
        compiler_params=pltpu.CompilerParams(collective_id=cid, has_side_effects=True, vmem_limit_bytes=60 << 20),
        cost_estimate=pl.CostEstimate(flops=0, bytes_accessed=cost, transcendentals=0),
    )(*ins)


def sds(shape, dtype):
    return jax.ShapeDtypeStruct(shape, dtype)


def gather_kernel(hid, wsend, small, hid_all, w_in, small_all, halo, send, recv):
    n = Net(send, recv)
    g, m, z, c, y = n.g, n.m, n.z, n.c, n.y
    n.meet(
        [n.at(dz=a, dc=b) for a, b in OTHERS] + [n.at(dx=d) for d in XS] + [n.at(dy=1), n.at(dy=3), n.group(1), n.group(7)]
    )
    own = [n.local(wsend.at[m], w_in.at[g, m]), n.local(small, small_all.at[g, m]), n.local(hid, hid_all.at[m])]
    w_cp, s_cp = {}, {}
    for a, b in OTHERS:
        w_cp[a, b] = n.push(wsend.at[n.member(a, b)], w_in.at[g, m], n.at(dz=a, dc=b))
        s_cp[a, b] = n.push(small, small_all.at[g, m], n.at(dz=a, dc=b))
    last = []

    def along_y(ref, group, pick):
        for half, dy in ((0, 1), (1, 3)):
            part = pick(ref, group, half)
            last.append(n.push(part, part, n.at(dy=dy)))

    def w_half(k):
        first = 2 * lax.rem(z + 4 - ZS[k], 4)
        return lambda ref, group, half: ref.at[group, pl.ds(first, 2), pl.ds(16 * half, 16)]

    x_cp = {}
    for cp in own:
        cp.wait()

    def issue(k):
        for b in (0, 1):
            if (ZS[k], b) != (0, 0):
                w_cp[ZS[k], b].wait_recv()
        block = w_in.at[g, pl.ds(2 * lax.rem(z + 4 - ZS[k], 4), 2)]
        for d in XS:
            x_cp[k, d] = n.push(block, block, n.at(dx=d))
        along_y(w_in, g, w_half(k))

    issue(0)
    issue(1)
    h_cp = {a: n.push(hid, hid_all.at[m], n.at(dz=a)) for a in (1, 3, 2)}
    h_sib = n.push(hid, hid_all.at[m], n.at(dc=1))
    for k in range(4):
        for d in XS:
            x_cp[k, d].wait_recv()
            along_y(w_in, 2 * lax.rem(n.x + 4 - d, 4) + y, w_half(k))
        if k < 2:
            issue(k + 2)
    for a, b in OTHERS:
        s_cp[a, b].wait_recv()
    s_x = {d: n.push(small_all.at[g], small_all.at[g], n.at(dx=d)) for d in XS}
    last.append(n.push(small_all.at[g], small_all.at[g], n.pair()))
    for d in XS:
        other = 2 * lax.rem(n.x + 4 - d, 4) + y
        s_x[d].wait_recv()
        last.append(n.push(small_all.at[other], small_all.at[other], n.pair()))
        h_cp[d].wait_recv()
        theirs = hid_all.at[2 * lax.rem(z + 4 - d, 4) + c]
        last.append(n.push(theirs, theirs, n.at(dc=1)))
    h_sib.wait_recv()
    for cp in last:
        cp.wait_recv()
    edge = n.push(hid_all.at[7, :, pl.ds(48, 16)], halo, n.group(1))
    edge.wait_recv()
    n.finish()


def gather(hid, wsend, small):
    outs = [sds((8, 2, 64, 2048), BF16), sds((8, 8, 32, 1408), BF16), sds((8, 8, 8, 128), F32), sds((2, 16, 2048), BF16)]
    return call(gather_kernel, "gather", 0, outs, (hid, wsend, small), [VM] * 3, [ANY] * 4, 112)


def states_out(n, block, everyone):
    n.local(block, everyone.at[n.g]).wait()
    own = everyone.at[n.g]
    ahead = {d: n.push(own, own, n.at(dx=d)) for d in XS}
    last = []

    def along_y(group):
        last.append(n.push(everyone.at[group], everyone.at[group], n.pair()))

    along_y(n.g)

    def rest():
        for d in XS:
            ahead[d].wait_recv()
            along_y(2 * lax.rem(n.x + 4 - d, 4) + n.y)
        for cp in last:
            cp.wait_recv()

    return rest


def sums_kernel(mine, everyone, send, recv):
    n = Net(send, recv)
    n.meet([n.at(dz=a, dc=b) for a, b in OTHERS])
    everyone[n.m] = mine[...]
    for a, b in OTHERS:
        n.push(mine, everyone.at[n.m], n.at(dz=a, dc=b))
    for cp in n.open:
        cp.wait_recv()
    n.finish()


def member_gather(mine, name, cid):
    return call(sums_kernel, name, cid, sds((8, *mine.shape), mine.dtype), (mine,), [VM], VM, 16)


def tokens_begin(n, part, near):
    return [n.push(part.at[2 * lax.rem(n.z + d, 4) + 1 - n.c], near.at[d], n.at(dc=1)) for d in (1, 3, 2, 0)]


def tokens_middle(n, part, near, both, far, begun):
    away = []
    for cp, d in zip(begun, (1, 3, 2, 0)):
        cp.wait_recv()
        at = 2 * lax.rem(n.z + d, 4) + n.c
        for i in range(2):
            both[d, i] = (part[at, i].astype(F32) + near[d, i].astype(F32)).astype(BF16)
        if d:
            away.append(n.push(both.at[d], far.at[d - 1], n.at(dz=d)))
    return away


def tokens_end(both, far, out, away):
    for cp in away:
        cp.wait_recv()
    for i in range(2):
        out[i] = both[0, i].astype(F32) + far[0, i].astype(F32) + far[1, i].astype(F32) + far[2, i].astype(F32)


TOKEN_SCRATCH = [pltpu.VMEM((4, 2, 64, 2048), jnp.bfloat16), pltpu.VMEM((4, 2, 64, 2048), jnp.bfloat16), pltpu.VMEM((3, 2, 64, 2048), jnp.bfloat16)]


def backward_kernel(starts, part, starts_all, total, near, both, far, send, recv):
    n = Net(send, recv)
    n.meet([n.at(dz=a) for a in (1, 3, 2)] + [n.at(dc=1)] + [n.at(dx=d) for d in XS] + [n.pair()])
    rest = states_out(n, starts, starts_all)
    begun = tokens_begin(n, part, near)
    away = tokens_middle(n, part, near, both, far, begun)
    rest()
    tokens_end(both, far, total, away)
    n.finish()


def backward_states(starts, part):
    outs = [sds((8, *starts.shape), BF16), sds((2, 64, 2048), F32)]
    return call(backward_kernel, "states_backward", 4, outs, (starts, part), [VM, VM], [ANY, VM], 32, TOKEN_SCRATCH)


def add4(a, b):
    return a.astype(F32) + b[0].astype(F32) + b[1].astype(F32) + b[2].astype(F32)


NN = (((1,), (0,)), ((), ()))
NT = (((1,), (1,)), ((), ()))
TN = (((0,), (0,)), ((), ()))
TT = (((0,), (1,)), ((), ()))


def bdot(a, b, dims=NN):
    return lax.dot_general(a, b, dims, preferred_element_type=F32)


def parts(v, count):
    out = []
    for _ in range(count):
        p = v.astype(BF16)
        out.append(p)
        v = v - p.astype(F32)
    return out


def left_parts(v, w, count, dims=NN):
    return sum(bdot(p, w, dims) for p in parts(v, count))


def right_parts(w, v, count, dims=NN):
    return sum(bdot(w, p, dims) for p in parts(v, count))


def iota(shape, dim):
    return lax.broadcasted_iota(jnp.int32, shape, dim)


def spread_matrix():
    return (iota((128, 512), 0) == iota((128, 512), 1) // 64).astype(BF16)


def heads_of(v, eh):
    return left_parts(v, eh, 2)


def sums_of(v, eh):
    return left_parts(v, eh, 2, NT)


def lower_matrix():
    return (iota((Q, Q), 0) >= iota((Q, Q), 1)).astype(BF16)


def sigmoid(v):
    return 1.0 / (1.0 + jnp.exp(-v))


def softplus(v):
    return jnp.maximum(v, 0.0) + jnp.log1p(jnp.exp(-jnp.abs(v)))


def row_scale(h):
    return lax.rsqrt(jnp.mean(h * h, axis=-1, keepdims=True) + EPS)


def decays(L, flags):
    E = jnp.exp(L) * flags[:, 3:4]
    W = jnp.exp(L[Q - 1 : Q] - L) * flags[:, 4:5]
    return E, W


def wave_kernel(
    hid, halo, gain, w, conv, hp, flags, segrow, og, cot, outw, coef,
    normed, gate, pre, ext, delta, logs, mixed, carried, states, sums, dno, endlog, cot_all, w_out,
    proj_s, pre_s, gate_s, delta_s, logs_s, sloc, inner, dno_s, state, total, tail, ends, cot_s, w_o, w_s, send, recv, done,
):
    t = pl.program_id(0)
    c = lax.rem(t, CH)
    at = lax.rem(t, 8)
    micro = at // CH
    eh = spread_matrix()
    n = Net(send, recv)
    g, m, core = n.g, n.m, n.c

    def cot_z(a):
        return n.copy(("cot", a), cot_s.at[m], cot_s.at[m], n.at(dz=a))

    def cot_near():
        return n.copy("near", cot_s.at[m], cot_s.at[m], n.at(dc=1))

    def cot_on(a):
        theirs = cot_s.at[2 * lax.rem(n.z + 4 - a, 4) + core]
        return n.copy(("on", a), theirs, theirs, n.at(dc=1))

    def out_x(d):
        return n.copy(("ox", d), w_o.at[g], w_o.at[g], n.at(dx=d))

    def out_y(d, half):
        part = w_o.at[n.behind(d), pl.ds(32 * half, 32)]
        return n.copy(("oy", d, half), part, part, n.at(dy=3 if half else 1))

    def out_swap():
        return n.copy("swap", w_o.at[pl.ds(4 * (1 - core), 4)], w_s.at[:, core], n.at(dc=1))

    def end_x(i, d):
        return n.copy(("ex", i, d), ends.at[g, i], ends.at[g, i], n.at(dx=d))

    def end_y(i, d):
        part = ends.at[n.behind(d), i]
        return n.copy(("ey", i, d), part, part, n.pair())

    ALLX = (0,) + XS
    out_copies = [pltpu.make_async_copy(cot_s, cot_all, done.at[0]), pltpu.make_async_copy(w_s, w_out, done.at[1])]

    @pl.when(t == 0)
    def _():
        n.meet([n.at(dz=a) for a in (1, 3, 2)] + [n.at(dc=1)] + [n.at(dx=d) for d in XS] + [n.at(dy=1), n.at(dy=3)])
        cot_s[m] = cot[...]
        w_o[g] = outw[...]
        for d in XS:
            out_x(d).start()
        for half in (0, 1):
            out_y(0, half).start()
        for a in (1, 3, 2):
            cot_z(a).start()
        cot_near().start()

    @pl.when((t < 8) & (c == 0))
    def _():
        h = hid[...].reshape(TOK, 2048).astype(F32)
        nb = (h * row_scale(h) * gain[...]).astype(BF16)
        normed[...] = nb.reshape(8, 1, 64, 2048)
        e = halo[0].astype(F32)
        eb = (e * row_scale(e) * gain[...]).astype(BF16)
        proj_s[...] = bdot(jnp.concatenate([eb, nb], 0), w[...])
        tail[0:8] = proj_s[8:16, 512:1280].astype(BF16).astype(F32)
        state[...] = jnp.zeros_like(state)
        total[...] = jnp.zeros_like(total)

    @pl.when(t < 8)
    def _():
        rows = pl.ds(pl.multiple_of(16 + Q * c, 16), Q)
        f = flags[...]
        gt = proj_s[rows, 0:512]
        gate[...] = gt
        gate_s[at] = gt
        xbc = proj_s[rows, 512:1280].astype(BF16).astype(F32)
        tail[8:] = xbc
        acc = conv[4:5] + conv[3:4] * xbc
        for k in range(3):
            acc = acc + conv[k : k + 1] * tail[5 + k : 5 + k + Q] * f[:, k : k + 1]
        pre[...] = acc
        pre_s[at] = acc
        ext[0] = tail[...].astype(BF16)
        d = softplus(proj_s[rows, 1280:1408] + hp[0:1])
        delta[...] = d
        delta_s[at] = d
        L = right_parts(lower_matrix(), d * hp[1:2], 3)
        logs[...] = L
        logs_s[at] = L
        E, W = decays(L, f)
        x = acc[:, :512]
        X = x * sigmoid(x)
        b = acc[:, 512:640]
        B = (b * sigmoid(b)).astype(BF16)
        S = right_parts(B, heads_of(W * d, eh) * X, 2, TN)
        sloc[at] = S
        both = heads_of(jnp.concatenate([E[Q - 8 :], L[Q - 8 :]], 0), eh)
        new = both[7:8] * state[...] + S
        state[...] = new
        tail[0:8] = tail[Q : Q + 8]
        lt = total[...] + L[Q - 1 : Q]
        total[...] = lt

        @pl.when(c == CH - 1)
        def _():
            ends[g, micro, 0:128] = new.astype(BF16)
            p = parts(jnp.broadcast_to(heads_of(jnp.broadcast_to(lt, (8, 128)), eh)[0:1], (16, 512)), 3)
            r = iota((16, 512), 0)
            ends[g, micro, 128:144] = jnp.where(r == 0, p[0], jnp.where(r == 1, p[1], jnp.where(r == 2, p[2], jnp.zeros_like(p[0]))))

    for i, when in ((0, CH - 1), (1, 2 * CH - 1)):

        @pl.when(t == when)
        def _(i=i):
            for d in XS:
                end_x(i, d).start()
            end_y(i, 0).start()

    @pl.when(t == 4)
    def _():
        for d in XS:
            out_x(d).wait_recv()
            for half in (0, 1):
                out_y(d, half).start()

    for i, when in ((0, 6), (1, 11)):

        @pl.when(t == when)
        def _(i=i):
            for d in XS:
                end_x(i, d).wait_recv()
                end_y(i, d).start()

    @pl.when(t == 8)
    def _():
        for d in ALLX:
            for half in (0, 1):
                out_y(d, half).wait_recv()
        out_swap().start()
        for k in range(4):
            w_s[k, core] = w_o[4 * core + k]
        for a in (1, 3, 2):
            cot_z(a).wait_recv()
            cot_on(a).start()

    @pl.when((t >= 8) & (t < 16))
    def _():
        L = logs_s[at]
        a = pre_s[at]
        X, B, C = activations(a)
        U = (heads_of(delta_s[at], eh) * X).astype(BF16)
        psi = bdot(C, B, NT)
        keep = same_mask(flags[...], segrow[0])
        LT = L.T
        for j in range(4):
            u = pair_halves(U[:, 128 * j : 128 * j + 128])
            y = jnp.zeros((Q, 128), F32)
            for e in range(2):
                h = 2 * j + e
                K = jnp.where(keep, jnp.exp(L[:, h : h + 1] - LT[h : h + 1]), 0.0)
                y = y + bdot((psi * K).astype(BF16), u[e])
            inner[at, :, 128 * j : 128 * j + 128] = y

    @pl.when(t == 16)
    def _():
        out_swap().wait_recv()
        cot_near().wait_recv()
        for a in (1, 3, 2):
            cot_on(a).wait_recv()
        for cp in out_copies:
            cp.start()
        for i in (0, 1):
            for d in ALLX:
                end_y(i, d).wait_recv()
        for q in range(8):
            for i in range(2):
                endlog[q, i] = ends[q, i, 128:144]

    @pl.when((t >= 16) & (c == 0))
    def _():
        dno_s[...] = bdot(cot_s[:, micro].reshape(TOK, 2048), w_s[...].reshape(512, 2048), NT)
        state[...] = entering(ends, coef, 0, micro)

    @pl.when(t >= 16)
    def _():
        f = flags[...]
        E, _ = decays(logs_s[at], f)
        a = pre_s[at]
        X, _, C = activations(a)
        more = heads_of(jnp.concatenate([E, jnp.broadcast_to(hp[2:3], (8, 128))], 0), eh)
        Ex, skip = more[:Q], more[Q : Q + 1]
        S = state[...]
        states[0, 0] = S
        Yc = Ex * bdot(C, S.astype(BF16))
        carried[...] = Yc
        mix = inner[at] + Yc + skip * X
        mixed[...] = mix
        after = Ex[Q - 1 : Q] * S + sloc[at]
        state[...] = after
        states[0, 1] = after
        gt = gate_s[at]
        gated = mix * (gt * sigmoid(gt))
        dn = dno_s[pl.ds(pl.multiple_of(Q * c, Q), Q)]
        dno[...] = dn
        ones = jnp.ones((8, 512), BF16)
        sums[0, 0:8] = right_parts(ones, gated * gated, 2, NT)
        sums[0, 8:16] = right_parts(ones, dn * og[...] * gated, 2, NT)

    @pl.when(t == 23)
    def _():
        for cp in out_copies:
            cp.wait()
        for a in (1, 3, 2):
            cot_z(a).wait_send()
            cot_on(a).wait_send()
        cot_near().wait_send()
        out_swap().wait_send()
        for d in XS:
            out_x(d).wait_send()
        for d in ALLX:
            for half in (0, 1):
                out_y(d, half).wait_send()
        for i in (0, 1):
            for d in XS:
                end_x(i, d).wait_send()
            for d in ALLX:
                end_y(i, d).wait_send()


def tile(width, at=lambda t: t):
    return pl.BlockSpec((Q, width), lambda t: (at(t), 0))


def whole(*shape):
    return pl.BlockSpec(shape, lambda t: (0,) * len(shape))


def plain(kernel, name, outs, ins, spaces_in, spaces_out, scratch=(), flops=1 << 30):
    return pl.pallas_call(
        kernel,
        name=name,
        grid=(MICRO * CH,),
        out_shape=outs,
        in_specs=spaces_in,
        out_specs=spaces_out,
        scratch_shapes=list(scratch),
        compiler_params=pltpu.CompilerParams(vmem_limit_bytes=56 << 20),
        cost_estimate=pl.CostEstimate(flops=flops, bytes_accessed=16 << 20, transcendentals=0),
    )(*ins)


T = MICRO * TOK
HID = pl.BlockSpec((2, 1, 64, 2048), lambda t: (t % CH, t // CH, 0, 0))


def agblock(width, at=lambda t: t):
    return pl.BlockSpec((2, 1, 64, width), lambda t: (at(t) % CH, at(t) // CH, 0, 0))


def wave(hid, halo, gain, w, conv, hp, flags, segrow, og, cot, outw, coef):
    outs = [
        sds((8, 2, 64, 2048), BF16), sds((T, 512), F32), sds((T, 768), F32), sds((8, Q + 8, 768), BF16), sds((T, 128), F32), sds((T, 128), F32),
        sds((T, 512), F32), sds((T, 512), F32), sds((8, 2, 128, 512), F32), sds((8, 16, 128), F32), sds((T, 512), F32), sds((8, 2, 16, 512), BF16), sds((8, 2, 64, 2048), BF16), sds((4, 2, 64, 2048), BF16),
    ]
    first = lambda t: jnp.minimum(t, 7)
    last = lambda t: jnp.maximum(t - 16, 0)
    ring = lambda t: t % 8
    micro = pl.BlockSpec((8, 1, 64, 2048), lambda t: (0, first(t) // CH, 0, 0))
    V = lambda *shape: pltpu.VMEM(shape, F32)
    return pl.pallas_call(
        wave_kernel,
        name="wave",
        grid=(24,),
        out_shape=outs,
        in_specs=[
            micro, pl.BlockSpec((1, 16, 2048), lambda t: (first(t) // CH, 0, 0)), whole(1, 2048), whole(2048, 1408), whole(8, 768), whole(8, 128), tile(128, ring), blk(1, 128, ring), whole(1, 512),
            whole(2, 64, 2048), whole(64, 2048), SMEM,
        ],
        out_specs=[
            micro, tile(512, first), tile(768, first), blk(Q + 8, 768, first), tile(128, first), tile(128, first),
            tile(512, last), tile(512, last), pl.BlockSpec((1, 2, 128, 512), lambda t: (last(t), 0, 0, 0)), blk(16, 128, last), tile(512, last), whole(8, 2, 16, 512), ANY, ANY,
        ],
        scratch_shapes=[
            V(TOK + 16, 1408), V(8, Q, 768), V(8, Q, 512), V(8, Q, 128), V(8, Q, 128), V(8, 128, 512), V(8, Q, 512), V(TOK, 512), V(128, 512), V(1, 128), V(Q + 8, 768),
            pltpu.VMEM((8, 2, 144, 512), BF16), pltpu.VMEM((8, 2, 64, 2048), BF16), pltpu.VMEM((8, 64, 2048), BF16), pltpu.VMEM((4, 2, 64, 2048), BF16),
            pltpu.SemaphoreType.DMA((48,)), pltpu.SemaphoreType.DMA((48,)), pltpu.SemaphoreType.DMA((2,)),
        ],
        compiler_params=pltpu.CompilerParams(collective_id=1, has_side_effects=True, vmem_limit_bytes=60 << 20),
        cost_estimate=pl.CostEstimate(flops=8 << 30, bytes_accessed=32 << 20, transcendentals=0),
    )(hid, halo, gain, w, conv, hp, flags, segrow, og, cot, outw, coef)


def entering(everyone, coef, direction, micro, logs=None):
    total = jnp.zeros((128, 512), F32)
    at = 0 if everyone.shape[1] == 1 else micro
    rows = [(everyone[q, at, 128:144] if logs is None else logs[q, 0]).astype(F32) for q in range(8)]
    lt = [v[0:1] + v[1:2] + v[2:3] for v in rows]
    for q in range(8):
        log = sum(coef[80 * direction + 8 * q + r] * lt[r] for r in range(8))
        total = total + jnp.exp(log) * coef[80 * direction + 64 + 8 * micro + q] * everyone[q, at, 0:128].astype(F32)
    return total


def same_mask(flags, segrow):
    return (flags[:, 5:6] == segrow) & (iota((Q, Q), 0) >= iota((Q, Q), 1))


def activations(pre):
    a = pre * sigmoid(pre)
    return a[:, :512], a[:, 512:640].astype(BF16), a[:, 640:768].astype(BF16)


def pair_halves(v):
    low_half = iota(v.shape, 1) < 64
    zero = jnp.zeros_like(v)
    return jnp.where(low_half, v, zero), jnp.where(low_half, zero, v)


def blk(a, b, at=lambda t: t):
    return pl.BlockSpec((1, a, b), lambda t: (at(t), 0, 0))


SMEM = pl.BlockSpec(memory_space=pltpu.SMEM)


def column(row):
    return jnp.concatenate([jnp.broadcast_to(row, (128, 128)).T] * 4, 1)


def out_kernel(mixed, gate, dno, sums, pre, logs, flags, og, hp, nout, dmix, dgate, tloc, starts, small, state):
    t = pl.program_id(0)
    c = CH - 1 - lax.rem(t, CH)
    eh = spread_matrix()

    @pl.when(c == CH - 1)
    def _():
        state[...] = jnp.zeros_like(state)

    @pl.when(t == 0)
    def _():
        small[...] = jnp.zeros_like(small)

    tot = sums[0, 0]
    for q in range(1, 8):
        tot = tot + sums[q, 0]
    r = column(lax.rsqrt(tot[0:1] / INNER + EPS))
    s2 = column(tot[8:9] / INNER)
    gt = gate[...]
    s = sigmoid(gt)
    sg = gt * s
    mix = mixed[...]
    gated = mix * sg
    dn = dno[...]
    n0 = gated * r
    nout[...] = (n0 * og[...]).astype(BF16).reshape(2, 1, 64, 512)
    d_gated = r * (dn * og[...] - n0 * r * s2)
    dm = d_gated * sg
    dmix[...] = dm
    dgate[...] = (d_gated * mix * (s * (1.0 + gt * (1.0 - s)))).astype(BF16)
    x = pre[:, :512]
    X = x * sigmoid(x)
    cc = pre[:, 640:768]
    C = (cc * sigmoid(cc)).astype(BF16)
    small[0:1] += jnp.sum(dn * n0, 0, keepdims=True)
    small[1:2] += jnp.sum(X * dm, 0, keepdims=True)
    E, _ = decays(logs[...], flags[...])
    Ex = heads_of(E, eh)
    G = right_parts(C, Ex * dm, 2, TN)
    tloc[0] = G
    new = Ex[Q - 1 : Q] * state[...] + G
    state[...] = new

    @pl.when(c == 0)
    def _():
        starts[0] = new.astype(BF16)


def back_at(t):
    return (t // CH) * CH + (CH - 1 - t % CH)


def out_call(mixed, gate, dno, sums, pre, logs, flags, og, hp):
    outs = [sds((8, 2, 64, 512), BF16), sds((T, 512), F32), sds((T, 512), BF16), sds((8, 128, 512), F32), sds((2, 128, 512), BF16), sds((8, 512), F32)]
    b = back_at
    return plain(
        out_kernel, "out", outs, (mixed, gate, dno, sums, pre, logs, flags, og, hp),
        [tile(512, b), tile(512, b), tile(512, b), pl.BlockSpec((8, 1, 16, 128), lambda t: (0, back_at(t), 0, 0)), tile(768, b), tile(128, b), tile(128, b), whole(1, 512), whole(8, 128)],
        [agblock(512, b), tile(512, b), tile(512, b), blk(128, 512, b), blk(128, 512, lambda t: t // CH), whole(8, 512)],
        [pltpu.VMEM((128, 512), F32)],
    )


def back_kernel(pre, delta, logs, flags, segrow, mixed, carried, dmix, states, tloc, starts, ends, hp, coef, dpre, dbc, ddt, small, state):
    t = pl.program_id(0)
    c = CH - 1 - lax.rem(t, CH)
    eh = spread_matrix()

    @pl.when(c == CH - 1)
    def _():
        state[...] = entering(starts, coef, 1, t // CH, ends)

    @pl.when(t == 0)
    def _():
        small[...] = jnp.zeros_like(small)

    L = logs[...]
    f = flags[...]
    d = delta[...]
    E, W = decays(L, f)
    p = pre[...]
    s = sigmoid(p)
    X = p[:, :512] * s[:, :512]
    B = (p[:, 512:640] * s[:, 512:640]).astype(BF16)
    C = (p[:, 640:] * s[:, 640:]).astype(BF16)
    more = heads_of(jnp.concatenate([E, W, d, jnp.broadcast_to(hp[2:3], (8, 128))], 0), eh)
    Ex, Wx, dx, skip = more[:Q], more[Q : 2 * Q], more[2 * Q : 3 * Q], more[3 * Q : 3 * Q + 1]
    U = dx * X
    Ub = U.astype(BF16)
    dm = dmix[...]
    dmb = dm.astype(BF16)
    Yc = carried[...]
    Yi = mixed[...] - Yc - skip * X
    G = state[...]
    Gb = G.astype(BF16)
    psi = bdot(C, B, NT)
    keep = same_mask(f, segrow[0])
    LT = L.T
    dpsi = jnp.zeros((Q, Q), F32)
    cols = []
    for j in range(4):
        js = slice(128 * j, 128 * j + 128)
        u = pair_halves(Ub[:, js])
        y = pair_halves(dmb[:, js])
        acc = jnp.zeros((Q, 128), F32)
        for e in range(2):
            h = 2 * j + e
            K = jnp.where(keep, jnp.exp(L[:, h : h + 1] - LT[h : h + 1]), 0.0)
            acc = acc + bdot((psi * K).astype(BF16), y[e], TN)
            dpsi = dpsi + bdot(y[e], u[e], NT) * K
        cols.append(acc)
    dUi = jnp.concatenate(cols, 1)
    dUc = Wx * bdot(B, Gb)
    dU = dUi + dUc
    S0, S1 = states[0, 0], states[0, 1]
    dpb = dpsi.astype(BF16)
    dbc[0:128] = (bdot(C, dpb, TN) + bdot(Gb, (Wx * U).astype(BF16), NT)).astype(BF16)
    dbc[128:256] = (bdot(B, dpb, TT) + bdot(S0.astype(BF16), (Ex * dm).astype(BF16), NT)).astype(BF16)
    dL = sums_of(dmb.astype(F32) * Yi + dm * Yc - Ub.astype(F32) * dUi - U * dUc, eh)
    end = sums_of(jnp.broadcast_to(jnp.sum(G * S1, 0, keepdims=True), (8, 512)), eh)[0:1]
    upper = (iota((Q, Q), 0) <= iota((Q, Q), 1)).astype(BF16)
    dstep = right_parts(upper, dL, 3) + end
    rate = hp[1:2]
    dd = sums_of(dU * X, eh) + dstep * rate
    dr = dd * (1.0 - jnp.exp(-d))
    ddt[...] = dr.astype(BF16)
    small[0:1] += jnp.sum(dr, 0, keepdims=True)
    small[1:2] += jnp.sum(dstep * d * rate, 0, keepdims=True)
    sx = s[:, :512]
    dpre[...] = (dx * dU + skip * dm) * (sx * (1.0 + p[:, :512] * (1.0 - sx)))
    state[...] = Ex[Q - 1 : Q] * G + tloc[0]


def back_call(pre, delta, logs, flags, segrow, mixed, carried, dmix, states, tloc, starts, ends, hp, coef):
    outs = [sds((T, 512), F32), sds((256, T), BF16), sds((T, 128), BF16), sds((8, 128), F32)]
    b = back_at
    return plain(
        back_kernel, "back", outs, (pre, delta, logs, flags, segrow, mixed, carried, dmix, states, tloc, starts, ends, hp, coef),
        [tile(768, b), tile(128, b), tile(128, b), tile(128, b), blk(1, 128, b), tile(512, b), tile(512, b), tile(512, b), pl.BlockSpec((1, 2, 128, 512), lambda t: (back_at(t), 0, 0, 0)), blk(128, 512, b), pl.BlockSpec((8, 1, 128, 512), lambda t: (0, t // CH, 0, 0)), pl.BlockSpec((8, 1, 16, 512), lambda t: (0, t // CH, 0, 0)), whole(8, 128), SMEM],
        [tile(512, b), pl.BlockSpec((256, Q), lambda t: (0, back_at(t))), tile(128, b), whole(8, 128)],
        [pltpu.VMEM((128, 512), F32)],
    )


def pick_matrix(rows, start, count, shift, dtype=BF16):
    r, l = iota((rows, 128), 0), iota((rows, 128), 1)
    return ((r - start == l - shift) & (l >= shift) & (l < shift + count)).astype(dtype)


class Reduce:
    def __init__(self, n, key, a, b, a1, a2, pa, b1, b2, pb, b3):
        self.n, self.key, self.a, self.b = n, key, a, b
        self.a1, self.a2, self.pa, self.b1, self.b2, self.pb, self.b3 = a1, a2, pa, b1, b2, pb, b3
        self.half = a.shape[1] // 2

    def group(self, d, f):
        n = self.n
        return 2 * lax.rem(n.x + d, 4) + lax.rem(n.y + f, 2)

    def first_a(self, d, f):
        return self.n.copy((self.key, "a1", d, f), self.a.at[self.group(d, f)], self.a1.at[d - 1, f], self.n.at(dx=d))

    def first_b(self, d, e):
        n = self.n
        rep = lax.rem(n.ring + e, 4) // 2
        rows = pl.ds(pl.multiple_of(self.half * rep, self.half), self.half)
        return n.copy((self.key, "b1", d, e), self.b.at[self.group(d, e % 2), rows], self.b1.at[e - 1, lax.rem(n.x + d, 4)], n.at(dy=e))

    def send(self, d, f):
        for e in (1, 3) if f else (2,):
            self.first_b(d, e).start()
        if d:
            self.first_a(d, f).start()

    def second_a(self, e):
        return self.n.copy((self.key, "a2", e), self.pa.at[e % 2], self.a2.at[e - 1], self.n.at(dy=e))

    def second_b(self, d):
        return self.n.copy((self.key, "b2", d), self.pb.at[lax.rem(self.n.x + d, 4)], self.b2.at[d - 1], self.n.at(dx=d))

    def third_b(self):
        return self.n.copy((self.key, "b3"), self.b3.at[self.n.rep], self.b3.at[self.n.rep], self.n.at(dy=2))

    def middle_a(self, f):
        for d in XS:
            self.first_a(d, f).wait_recv()
        self.pa[f] = add4(self.a[self.group(0, f)], self.a1[:, f]).astype(BF16)
        for e in (1, 3) if f else (2,):
            self.second_a(e).start()

    def middle_b(self):
        n = self.n
        rows = pl.ds(pl.multiple_of(self.half * n.rep, self.half), self.half)
        for d in (2, 1, 3, 0):
            for e in XS:
                self.first_b(d, e).wait_recv()
            k = lax.rem(n.x + d, 4)
            self.pb[k] = add4(self.b[2 * k + n.y, rows], self.b1[:, k]).astype(BF16)
            if d:
                self.second_b(d).start()

    def last_b(self):
        for d in XS:
            self.second_b(d).wait_recv()
        self.b3[self.n.rep] = add4(self.pb[self.n.x], self.b2).astype(self.b3.dtype)
        self.third_b().start()

    def last_a(self):
        for e in XS:
            self.second_a(e).wait_recv()
        return add4(self.pa[0], self.a2)

    def finish(self):
        for d in XS:
            for f in (0, 1):
                self.first_a(d, f).wait_send()
            self.second_b(d).wait_send()
        for e in XS:
            for d in range(4):
                self.first_b(d, e).wait_send()
            self.second_a(e).wait_send()
        self.third_b().wait_send()


CA = 640
CB = 1152 - CA


def tail_kernel(
    go, dbc, edge_x, dpre, pre, ext, flags, fnext, conv, ddt, dgate, w, hid, normed, small_o, small_b,
    gi, g_out, total, small_all,
    bc_s, ex_s, eb_src, eb_s, dps, pre_s, ext_s, fl_s, fn_s, ddt_s, dg_s, w_s, hid_s, nm_s, wt, e_s, dproj, part, near, far, conv_acc, gnorm,
    s0, s1, s2, sx, ga, gb, ga1, ga2, gpa, gb1, gb2, gpb, gb3, oa, ob, oa1, oa2, opa, ob1, ob2, opb, ob3, oin, final, send, recv, load,
):
    n = Net(send, recv)
    x, y, z, c, m = n.x, n.y, n.z, n.c, n.m
    loads = {}

    def fetch(key, src, dst):
        loads[key] = pltpu.make_async_copy(src, dst, load.at[len(loads)])
        loads[key].start()

    fetch("pre", pre.at[:, :, pl.ds(512, 256)], pre_s)
    fetch("w", w, w_s)
    fetch("dpre", dpre, dps.at[:, pl.ds(0, TOK), pl.ds(0, 512)])
    fetch("ext", ext, ext_s)
    fetch("flags", flags, fl_s)
    fetch("fnext", fnext, fn_s)
    fetch("ddt", ddt, ddt_s)
    fetch("dgate", dgate, dg_s)
    fetch("hid", hid, hid_s)
    fetch("normed", normed, nm_s)
    n.meet([n.at(dz=a, dc=b) for a, b in OTHERS] + [n.at(dx=d) for d in XS] + [n.at(dy=d) for d in XS] + [n.group(1), n.group(7)])

    def bc_copy(a, b):
        return n.copy(("bc", a, b), dbc.at[n.member(a, b)], bc_s.at[m], n.at(dz=a, dc=b))

    edge1 = n.copy("edge1", edge_x, ex_s, n.group(7))
    edge2 = n.copy("edge2", eb_src, eb_s, n.group(7))
    swap = n.copy("swap", go.at[:, 1 - c], oin, n.at(dc=1))

    def near_copy(d, i):
        return n.copy(("near", d, i), part.at[2 * lax.rem(z + d, 4) + 1 - c, i], near.at[d, i], n.at(dc=1))

    def far_copy(d, i):
        return n.copy(("far", d, i), near.at[d, i], far.at[d - 1, i], n.at(dz=d))

    def small_x(d):
        return n.copy(("sx", d), s0, s1.at[d - 1], n.at(dx=d))

    def small_y(d):
        return n.copy(("sy", d), sx, s2.at[d - 1], n.at(dy=d))

    def small_m(a, b):
        return n.copy(("sm", a, b), small_all.at[m], small_all.at[m], n.at(dz=a, dc=b))

    def rows_copy(a, b):
        return n.copy(("rows", a, b), final.at[n.member(a, b)], gi.at[m], n.at(dz=a, dc=b))

    W = Reduce(n, "w", ga, gb, ga1, ga2, gpa, gb1, gb2, gpb, gb3)
    O = Reduce(n, "o", oa, ob, oa1, oa2, opa, ob1, ob2, opb, ob3)

    for a, b in OTHERS:
        bc_copy(a, b).start()
    edge1.start()
    swap.start()
    bc_s[m] = dbc[m]
    pick = pick_matrix(256, 32 * m, 32, 0)
    loads["w"].wait()
    wt[...] = (bdot(w_s[:, 1024:1280], pick) + bdot(w_s[:, 1280:1408], pick_matrix(128, 0, 8, 32))).astype(BF16)
    cw = jnp.concatenate([conv[:, 0:512], left_parts(conv[:, 512:768], pick, 3)], 1)
    for k in range(4):
        oa[4 * c + k] = go[k, c, :, 0:1024]
        ob[4 * c + k] = go[k, c, :, 1024:2048]
    swap.wait_recv()
    for k in range(4):
        oa[4 * (1 - c) + k] = oin[k, :, 0:1024]
        ob[4 * (1 - c) + k] = oin[k, :, 1024:2048]
    for d in (2, 1, 3, 0):
        for f in (1, 0):
            O.send(d, f)

    for key in ("pre", "dpre"):
        loads[key].wait()
    for a, b in OTHERS:
        bc_copy(a, b).wait_recv()
    eye = pick_matrix(32, 0, 32, 0)

    def bc_chunk(i, k):
        t = CH * i + k
        tot = bc_s[0, :, Q * t : Q * t + Q].astype(F32)
        for q in range(1, 8):
            tot = tot + bc_s[q, :, Q * t : Q * t + Q].astype(F32)
        d = left_parts(tot, eye, 2, TN)
        p = left_parts(pre_s[t], pick, 2)
        s = sigmoid(p)
        dps[i, Q * k : Q * k + Q, 512:640] = d * (s * (1.0 + p * (1.0 - s)))

    for i in range(MICRO):
        bc_chunk(i, 0)
        eb_src[i] = dps[i, 0:8, 512:640]
    edge2.start()
    for i in range(MICRO):
        for k in range(1, CH):
            bc_chunk(i, k)
    for key in ("ext", "flags", "fnext", "ddt", "dgate"):
        loads[key].wait()
    conv_acc[...] = jnp.zeros_like(conv_acc)
    pick_dt = pick_matrix(128, 0, 8, 32)

    def conv_chunk(i, k):
        t = CH * i + k
        e_s[:, 0:512] = ext_s[t, :, 0:512].astype(F32)
        e_s[:, 512:640] = bdot(ext_s[t, :, 512:768], pick)
        f, fn = fl_s[t], fn_s[t]
        dp = dps[i, Q * k : Q * k + Q]
        dx = cw[3:4] * dp
        conv_acc[3:4] += jnp.sum(dp * e_s[8 : 8 + Q], 0, keepdims=True)
        conv_acc[4:5] += jnp.sum(dp, 0, keepdims=True)
        for j in range(3):
            conv_acc[j : j + 1] += jnp.sum(dp * e_s[5 + j : 5 + j + Q] * f[:, j : j + 1], 0, keepdims=True)
            dx = dx + cw[j : j + 1] * dps[i, Q * k + 3 - j : Q * k + 3 - j + Q] * fn[:, j : j + 1]
        rows = slice(Q * k, Q * k + Q)
        dproj[i, rows, 0:512] = dg_s[t]
        dproj[i, rows, 512:1024] = dx[:, 0:512].astype(BF16)
        dproj[i, rows, 1024:1152] = (dx[:, 512:640] + bdot(ddt_s[t], pick_dt)).astype(BF16)

    for i in range(MICRO):
        for k in range(CH - 1):
            conv_chunk(i, k)
    edge1.wait_recv()
    edge2.wait_recv()
    for i in range(MICRO):
        dps[i, TOK : TOK + 8, 0:512] = ex_s[i]
        dps[i, TOK : TOK + 8, 512:640] = eb_s[i]
        conv_chunk(i, CH - 1)

    loads["hid"].wait()
    for i in range(MICRO):
        h = hid_s[:, i].reshape(TOK, 2048).astype(F32)
        scale = row_scale(h)
        main, rest = dproj[i, :, 0:1024], dproj[i, :, 1024:1152]

        def tile_of(j, carry, i=i, scale=scale, main=main, rest=rest):
            at = pl.ds(pl.multiple_of(256 * j, 256), 256)
            d = bdot(main, w_s[at, 0:1024], NT) + bdot(rest, wt[at], NT)
            part[:, i, :, at] = d.astype(BF16).reshape(8, 64, 256)
            hv = hid_s[:, i, :, at].reshape(TOK, 256).astype(F32)
            s = jnp.sum(d * (hv * scale), 0, keepdims=True)
            gnorm[0:1, at] = s if i == 0 else gnorm[0:1, at] + s
            return carry

        lax.fori_loop(0, 8, tile_of, 0)
        for d in (1, 3, 2, 0):
            near_copy(d, i).start()
    for r in range(16):
        s0[r : r + 1] = gnorm[0:1, 128 * r : 128 * r + 128]
    for k in range(5):
        for r in range(5):
            s0[16 + 5 * k + r : 17 + 5 * k + r] = conv_acc[k : k + 1, 128 * r : 128 * r + 128]
    for r in range(4):
        s0[41 + r : 42 + r] = small_o[0:1, 128 * r : 128 * r + 128]
    s0[45:47] = small_b[0:2]
    s0[47:48] = sums_of(small_o[...], spread_matrix())[1:2]
    for d in XS:
        small_x(d).start()

    loads["normed"].wait()
    for d in (2, 1, 3, 0):
        for f in (1, 0):
            q = W.group(d, f)
            at = pl.ds(pl.multiple_of(256 * q, 256), 256)
            v = sum(bdot(nm_s[:, i, :, at].reshape(TOK, 256), dproj[i], TN) for i in range(MICRO))
            ga[q] = v[:, 0:CA].astype(BF16)
            gb[q] = v[:, CA:].astype(BF16)
            W.send(d, f)
    O.middle_a(1)
    O.middle_a(0)
    O.middle_b()
    for i in range(MICRO):
        for d in (1, 3, 2, 0):
            near_copy(d, i).wait_recv()
            at = 2 * lax.rem(z + d, 4) + c
            near[d, i] = (part[at, i].astype(F32) + near[d, i].astype(F32)).astype(BF16)
            if d:
                far_copy(d, i).start()
    for d in XS:
        small_x(d).wait_recv()
    sx[...] = s0[...] + s1[0] + s1[1] + s1[2]
    for d in XS:
        small_y(d).start()
    W.middle_a(1)
    W.middle_a(0)
    W.middle_b()
    O.last_b()
    for d in XS:
        small_y(d).wait_recv()
    small_all[m] = sx[...] + s2[0] + s2[1] + s2[2]
    for a, b in OTHERS:
        small_m(a, b).start()
    g_out[:, 0:1024] = O.last_a()
    O.third_b().wait_recv()
    for h in range(2):
        g_out[32 * h : 32 * h + 32, 1024:2048] = ob3[h]
    for i in range(MICRO):
        for d in XS:
            far_copy(d, i).wait_recv()
        total[i] = near[0, i].astype(F32) + far[0, i].astype(F32) + far[1, i].astype(F32) + far[2, i].astype(F32)
    W.last_b()
    final[:, :, 0:CA] = W.last_a().astype(BF16).reshape(8, 32, CA)
    W.third_b().wait_recv()
    for h in range(2):
        final[4 * h : 4 * h + 4, :, CA:] = gb3[h].reshape(4, 32, CB)
    for a, b in OTHERS:
        rows_copy(a, b).start()
    gi[m] = final[m]
    for a, b in OTHERS:
        rows_copy(a, b).wait_recv()
        small_m(a, b).wait_recv()
    W.finish()
    O.finish()
    for a, b in OTHERS:
        bc_copy(a, b).wait_send()
        rows_copy(a, b).wait_send()
        small_m(a, b).wait_send()
    for d in XS:
        small_x(d).wait_send()
        small_y(d).wait_send()
        for i in range(MICRO):
            far_copy(d, i).wait_send()
    for d in range(4):
        for i in range(MICRO):
            near_copy(d, i).wait_send()
    edge1.wait_send()
    edge2.wait_send()
    swap.wait_send()


def tail_call(go, dbc, edge_x, dpre, pre, ext, flags, fnext, conv, ddt, dgate, w, hid, normed, small_o, small_b):
    outs = [sds((8, 32, 1152), BF16), sds((64, 2048), F32), sds((2, 64, 2048), F32), sds((8, 48, 128), F32)]
    V = lambda *s: pltpu.VMEM(s, BF16)
    R = lambda *s: pltpu.VMEM(s, F32)
    scratch = [
        V(8, 32, T), R(2, 8, 512), R(2, 8, 128), R(2, 8, 128), R(2, TOK + 8, 640), R(8, Q, 256), V(8, Q + 8, 768), R(8, Q, 128), R(8, Q, 128), V(8, Q, 128), V(8, Q, 512), V(2048, 1408),
        V(8, 2, 64, 2048), V(8, 2, 64, 2048), V(2048, 128), R(Q + 8, 640), V(2, TOK, 1152), V(8, 2, 64, 2048), V(4, 2, 64, 2048), V(3, 2, 64, 2048), R(8, 640), R(8, 2048),
        R(48, 128), R(3, 48, 128), R(3, 48, 128), R(48, 128),
        V(8, 256, CA), V(8, 256, CB), V(3, 2, 256, CA), V(3, 256, CA), V(2, 256, CA), V(3, 4, 128, CB), V(3, 128, CB), V(4, 128, CB), V(2, 128, CB),
        V(8, 64, 1024), V(8, 64, 1024), V(3, 2, 64, 1024), V(3, 64, 1024), V(2, 64, 1024), V(3, 4, 32, 1024), V(3, 32, 1024), V(4, 32, 1024), R(2, 32, 1024), V(4, 64, 2048),
        V(8, 32, 1152),
    ]
    return pl.pallas_call(
        tail_kernel,
        name="tail",
        out_shape=outs,
        in_specs=[VM, VM, VM] + [ANY] * 5 + [VM] + [ANY] * 5 + [VM] * 2,
        out_specs=[VM] * 4,
        scratch_shapes=[*scratch, pltpu.SemaphoreType.DMA((112,)), pltpu.SemaphoreType.DMA((112,)), pltpu.SemaphoreType.DMA((10,))],
        compiler_params=pltpu.CompilerParams(collective_id=5, has_side_effects=True, vmem_limit_bytes=62 << 20),
        cost_estimate=pl.CostEstimate(flops=8 << 30, bytes_accessed=32 << 20, transcendentals=0),
    )(go, dbc, edge_x, dpre, pre, ext, flags, fnext, conv, ddt, dgate, w, hid, normed, small_o, small_b)


def strips(v, zi, ci):
    r = v.shape[0]
    return lax.dynamic_slice(v.reshape(r, 2, 4, 4, 128), (0, ci, 0, zi, 0), (r, 1, 4, 1, 128)).reshape(r, 512)


def from_members(v):
    r = v.shape[1]
    return v.reshape(4, 2, r, 4, 128).transpose(2, 1, 3, 0, 4).reshape(r, 4096)


def from_heads(v):
    r = v.shape[1]
    return v.reshape(4, 2, r, 4, 2).transpose(2, 1, 3, 0, 4).reshape(r, 64)


def from_rows(v):
    return v.transpose(1, 0, 2).reshape(v.shape[1], 256)


def to_members(v):
    r = v.shape[0]
    return v.reshape(r, 2, 4, 4, 128).transpose(3, 1, 0, 2, 4).reshape(8, r, 512)


def xdot(a, b, dims=NN):
    return lax.dot_general(a, b, dims, preferred_element_type=F32)


def per_device(layer_in, cotangent, segment_ids, norm_gain, in_weight, conv_weight, conv_bias, dt_bias, a_log, skip_gain, out_gain, out_weight):
    xi, yi, zi, ci = (lax.axis_index(a) for a in SEQ)
    g = 2 * xi + yi
    m = 2 * zi + ci
    pack = jnp.concatenate([segment_ids[:, 0].astype(F32).reshape(-1), norm_gain, conv_weight.reshape(-1), conv_bias, dt_bias, a_log, skip_gain, out_gain, jnp.zeros((1024 - 567,), F32)]).reshape(8, 128)
    bc = jnp.broadcast_to(in_weight[None, :, 8192:8448], (8, 32, 256))
    dt_w = in_weight[:, 8448:].reshape(32, 2, 4, 4, 2).transpose(3, 1, 0, 2, 4).reshape(8, 32, 8)
    w_send = jnp.concatenate([to_members(in_weight[:, :4096]), to_members(in_weight[:, 4096:8192]), bc, dt_w, jnp.zeros((8, 32, 120), BF16)], 2)
    hid_all, w_in, small_all, halo = gather(layer_in[:, 0], w_send, pack)
    w_in = w_in.reshape(2048, 1408)
    full = small_all.reshape(64, 1024)
    seg_full = full[:, :128].reshape(64, 2, 64).transpose(1, 0, 2).reshape(2, 4096)
    full = full[:, 128:]
    norm_full = full[:, :32].reshape(1, 2048)
    conv_full = full[:, 32:372].reshape(64, 5, 68).transpose(1, 0, 2).reshape(5, CONV)
    conv = jnp.concatenate([strips(conv_full[:, :INNER], zi, ci), conv_full[:, INNER:]], 1)
    conv = jnp.pad(conv, ((0, 3), (0, 0)))
    hv = lax.dynamic_slice(full[:, 372:439].reshape(2, 4, 4, 2, 67), (ci, 0, zi, 0, 0), (1, 4, 1, 2, 67)).reshape(8, 67)
    og = hv[:, 3:].reshape(1, 512)
    hp = jnp.pad(jnp.stack([hv[:, 0], -jnp.exp(hv[:, 1]), hv[:, 2]]), ((0, 5), (0, 120)))

    padded = jnp.concatenate([jnp.full((MICRO, 8), -1.0, F32), seg_full, jnp.full((MICRO, 8), -2.0, F32)], 1)
    near = lax.dynamic_slice(padded, (0, g * TOK), (MICRO, TOK + 16))
    own = near[:, 8 : 8 + TOK]
    chunked = own.reshape(MICRO, CH, Q)
    before = jnp.concatenate([near[:, 7:8], chunked[:, :-1, -1]], 1)[:, :, None]
    lanes = [(near[:, 5 + k : 5 + k + TOK] == own).astype(F32).reshape(T) for k in range(3)]
    lanes += [(chunked == before).astype(F32).reshape(T), (chunked == chunked[:, :, -1:]).astype(F32).reshape(T), own.reshape(T)]
    flags = jnp.pad(jnp.stack(lanes, 1), ((0, 0), (0, 122)))
    fnext = jnp.pad(jnp.stack([(near[:, 11 - k : 11 - k + TOK] == own).astype(F32).reshape(T) for k in range(3)], 1), ((0, 0), (0, 125)))
    segrow = own.reshape(8, 1, Q)
    lasts = seg_full.reshape(MICRO, GROUPS, TOK)[:, :, -1]
    idx = jnp.arange(GROUPS)
    q, r = idx[:, None], idx[None, :]
    last_before = jnp.sum(jnp.where(idx == g - 1, lasts, 0.0), 1, keepdims=True)
    last_own = jnp.sum(jnp.where(idx == g, lasts, 0.0), 1, keepdims=True)
    ok_before = (idx < g) & (lasts == last_before)
    ok_after = (idx > g) & (jnp.roll(lasts, 1, axis=1) == last_own)
    coef = jnp.concatenate([((r > q) & (r < g)).astype(F32), ok_before.astype(F32), ((r > g) & (r < q)).astype(F32), ok_after.astype(F32)], 0).reshape(160)

    normed, gate, pre, ext, delta, logs, mixed, carried, states, sums, dno, ends_all, cot, w_out = wave(hid_all, halo, norm_full, w_in, conv, hp, flags, segrow, og, cotangent[:, 0], out_weight, coef)
    sums_all = member_gather(sums, "norm_sums", 2)
    nout, dmix, dgate, tloc, starts, small_o = out_call(mixed, gate, dno, sums_all, pre, logs, flags, og, hp)
    nout = nout.reshape(T, 512)
    branch = xdot(nout, w_out.reshape(512, 2048)).astype(BF16).reshape(8, 2, 64, 2048)
    g_wout = xdot(nout, cot.reshape(T, 2048), TN).astype(BF16).reshape(4, 2, 64, 2048)
    starts_all, own_branch = backward_states(starts, branch)
    dpre, dbc, ddt, small_b = back_call(pre, delta, logs, flags, segrow, mixed, carried, dmix, states, tloc, starts_all, ends_all, hp, coef)
    split = lambda v: v.reshape(8, Q, v.shape[-1])
    edge_x = dpre.reshape(MICRO, TOK, 512)[:, :8]
    gi, g_out, own_dn, small_sum = tail_call(
        g_wout, dbc.reshape(8, 32, T), edge_x, dpre.reshape(MICRO, TOK, 512), split(pre), ext, split(flags), split(fnext), conv, split(ddt), split(dgate), w_in, hid_all, normed, small_o, small_b
    )
    gi = gi.astype(F32)
    hid_o = layer_in[:, 0].astype(F32)
    layer_out = (hid_o + own_branch).astype(BF16)
    ro = row_scale(hid_o)
    dg = own_dn * norm_full
    d_hid = ro * dg - hid_o * (ro * ro * ro) * jnp.mean(dg * hid_o, -1, keepdims=True)
    grad_in = (cotangent[:, 0].astype(F32) + d_hid).astype(BF16)
    g_in = jnp.concatenate([from_members(gi[:, :, :512]), from_members(gi[:, :, 512:1024]), from_rows(gi[:, :, 1024:1056]), from_heads(gi[:, :, 1056:1064])], 1)
    at = 8 * g + m
    g_norm = lax.dynamic_slice(small_sum[:, :16].sum(0).reshape(64, 32), (at, 0), (1, 32)).reshape(32)
    conv_s = small_sum[:, 16:41].reshape(8, 5, 640)
    conv_s = jnp.concatenate([from_members(conv_s[:, :, :512]), from_rows(conv_s[:, :, 512:544])], 1)
    conv_s = lax.dynamic_slice(conv_s, (0, 68 * at), (5, 68))
    og_s = from_members(small_sum[:, 41:45].reshape(8, 1, 512))[0]
    og_s = lax.dynamic_slice(og_s, (64 * at,), (64,))
    hd_s = from_heads(small_sum[:, 45:48, :8])
    hd_s = lax.dynamic_slice(hd_s, (0, at), (3, 1))
    return (layer_out[:, None], grad_in[:, None], g_norm, g_in, conv_s[:4], conv_s[4], hd_s[0], hd_s[1], hd_s[2], og_s, g_out)


def solution(mesh):
    fine = Mesh(mesh.devices.reshape(2, 4, 2, 4, 2), AXES)
    tok = P(None, "rep", SEQ, None)
    return jax.shard_map(
        per_device,
        mesh=fine,
        in_specs=(tok, tok, P(None, "rep", SEQ), P(SEQ), P(SEQ, None), P(None, SEQ), P(SEQ), P(SEQ), P(SEQ), P(SEQ), P(SEQ), P(SEQ, None)),
        out_specs=(tok, tok, P(SEQ), P(SEQ, None), P(None, SEQ), P(SEQ), P(SEQ), P(SEQ), P(SEQ), P(SEQ), P(SEQ, None)),
        check_vma=False,
    )
```

```python
import functools

import jax
import jax.numpy as jnp
from jax import lax
from jax.experimental import pallas as pl
from jax.experimental.pallas import tpu as pltpu
from jax.sharding import Mesh, PartitionSpec as P

EPS = 1e-05
INNER = 4096
MICRO = 2
CONV = 4352
F32 = jnp.float32
BF16 = jnp.bfloat16
AXES = ("rep", "x", "y", "z", "c")
SEQ = ("x", "y", "z", "c")
GROUPS = 8
TOK = 512
Q = 128
CH = TOK // Q

MESH = pl.DeviceIdType.MESH
ANY = pl.BlockSpec(memory_space=pl.ANY)
VM = pl.BlockSpec(memory_space=pltpu.VMEM)


class Net:
    def __init__(self, send, recv):
        self.send, self.recv, self.used, self.open = send, recv, 0, []
        self.keys = {}
        self.rep, self.x, self.y, self.z, self.c = (lax.axis_index(a) for a in AXES)
        self.ring = 2 * self.rep + self.y
        self.g = 2 * self.x + self.y
        self.m = 2 * self.z + self.c

    def at(self, dx=0, dy=0, dz=0, dc=0):
        ring = lax.rem(self.ring + dy, 4)
        return (ring // 2, lax.rem(self.x + dx, 4), lax.rem(ring, 2), lax.rem(self.z + dz, 4), lax.rem(self.c + dc, 2))

    def pair(self):
        return (self.rep, self.x, 1 - self.y, self.z, self.c)

    def across(self, dx):
        return (self.rep, lax.rem(self.x + dx, 4), 1 - self.y, self.z, self.c)

    def group(self, d):
        g = lax.rem(self.g + d, 8)
        return (self.rep, g // 2, lax.rem(g, 2), self.z, self.c)

    def member(self, dz, dc):
        return 2 * lax.rem(self.z + dz, 4) + lax.rem(self.c + dc, 2)

    def push(self, src, dst, where):
        i = self.used
        self.used += 1
        copy = pltpu.make_async_remote_copy(
            src_ref=src, dst_ref=dst, send_sem=self.send.at[i], recv_sem=self.recv.at[i], device_id=where, device_id_type=MESH
        )
        copy.start()
        self.open.append(copy)
        return copy

    def copy(self, key, src, dst, where):
        i = self.keys.setdefault(key, len(self.keys))
        return pltpu.make_async_remote_copy(
            src_ref=src, dst_ref=dst, send_sem=self.send.at[i], recv_sem=self.recv.at[i], device_id=where, device_id_type=MESH
        )

    def behind(self, d):
        return 2 * lax.rem(self.x + 4 - d, 4) + self.y

    def local(self, src, dst):
        i = self.used
        self.used += 1
        copy = pltpu.make_async_copy(src, dst, self.recv.at[i])
        copy.start()
        return copy

    def meet(self, peers):
        barrier = pltpu.get_barrier_semaphore()
        for peer in peers:
            pl.semaphore_signal(barrier, inc=1, device_id=peer, device_id_type=MESH)
        pl.semaphore_wait(barrier, len(peers))

    def finish(self):
        for copy in self.open:
            copy.wait_send()


OTHERS = [(dz, dc) for dz in (0, 1, 3, 2) for dc in (0, 1) if (dz, dc) != (0, 0)]
ZS = (0, 1, 3, 2)
XS = (1, 3, 2)


def call(kernel, name, cid, outs, ins, spaces_in, spaces_out, sems, scratch=(), cost=1 << 20):
    return pl.pallas_call(
        kernel,
        name=name,
        out_shape=outs,
        in_specs=spaces_in,
        out_specs=spaces_out,
        scratch_shapes=[*scratch, pltpu.SemaphoreType.DMA((sems,)), pltpu.SemaphoreType.DMA((sems,))],
        compiler_params=pltpu.CompilerParams(collective_id=cid, has_side_effects=True, vmem_limit_bytes=60 << 20),
        cost_estimate=pl.CostEstimate(flops=0, bytes_accessed=cost, transcendentals=0),
    )(*ins)


def sds(shape, dtype):
    return jax.ShapeDtypeStruct(shape, dtype)


def gather_kernel(hid, wsend, small, hid_all, w_in, small_all, halo, send, recv):
    n = Net(send, recv)
    g, m, z, c, y = n.g, n.m, n.z, n.c, n.y
    n.meet(
        [n.at(dz=a, dc=b) for a, b in OTHERS] + [n.at(dx=d) for d in XS] + [n.at(dy=1), n.at(dy=3), n.group(1), n.group(7)]
    )
    own = [n.local(wsend.at[m], w_in.at[g, m]), n.local(small, small_all.at[g, m]), n.local(hid, hid_all.at[m])]
    w_cp, s_cp = {}, {}
    for a, b in OTHERS:
        w_cp[a, b] = n.push(wsend.at[n.member(a, b)], w_in.at[g, m], n.at(dz=a, dc=b))
        s_cp[a, b] = n.push(small, small_all.at[g, m], n.at(dz=a, dc=b))
    last = []

    def along_y(ref, group, pick):
        for half, dy in ((0, 1), (1, 3)):
            part = pick(ref, group, half)
            last.append(n.push(part, part, n.at(dy=dy)))

    def w_half(k):
        first = 2 * lax.rem(z + 4 - ZS[k], 4)
        return lambda ref, group, half: ref.at[group, pl.ds(first, 2), pl.ds(16 * half, 16)]

    x_cp = {}
    for cp in own:
        cp.wait()

    def issue(k):
        for b in (0, 1):
            if (ZS[k], b) != (0, 0):
                w_cp[ZS[k], b].wait_recv()
        block = w_in.at[g, pl.ds(2 * lax.rem(z + 4 - ZS[k], 4), 2)]
        for d in XS:
            x_cp[k, d] = n.push(block, block, n.at(dx=d))
        along_y(w_in, g, w_half(k))

    issue(0)
    issue(1)
    h_cp = {a: n.push(hid, hid_all.at[m], n.at(dz=a)) for a in (1, 3, 2)}
    h_sib = n.push(hid, hid_all.at[m], n.at(dc=1))
    for k in range(4):
        for d in XS:
            x_cp[k, d].wait_recv()
            along_y(w_in, 2 * lax.rem(n.x + 4 - d, 4) + y, w_half(k))
        if k < 2:
            issue(k + 2)
    for a, b in OTHERS:
        s_cp[a, b].wait_recv()
    s_x = {d: n.push(small_all.at[g], small_all.at[g], n.at(dx=d)) for d in XS}
    last.append(n.push(small_all.at[g], small_all.at[g], n.pair()))
    for d in XS:
        other = 2 * lax.rem(n.x + 4 - d, 4) + y
        s_x[d].wait_recv()
        last.append(n.push(small_all.at[other], small_all.at[other], n.pair()))
        h_cp[d].wait_recv()
        theirs = hid_all.at[2 * lax.rem(z + 4 - d, 4) + c]
        last.append(n.push(theirs, theirs, n.at(dc=1)))
    h_sib.wait_recv()
    for cp in last:
        cp.wait_recv()
    edge = n.push(hid_all.at[7, :, pl.ds(48, 16)], halo, n.group(1))
    edge.wait_recv()
    n.finish()


def gather(hid, wsend, small):
    outs = [sds((8, 2, 64, 2048), BF16), sds((8, 8, 32, 1408), BF16), sds((8, 8, 8, 128), F32), sds((2, 16, 2048), BF16)]
    return call(gather_kernel, "gather", 0, outs, (hid, wsend, small), [VM] * 3, [ANY] * 4, 112)


def add4(a, b):
    return a.astype(F32) + b[0].astype(F32) + b[1].astype(F32) + b[2].astype(F32)


NN = (((1,), (0,)), ((), ()))
NT = (((1,), (1,)), ((), ()))
TN = (((0,), (0,)), ((), ()))
TT = (((0,), (1,)), ((), ()))


def bdot(a, b, dims=NN):
    return lax.dot_general(a, b, dims, preferred_element_type=F32)


def parts(v, count):
    out = []
    for _ in range(count):
        p = v.astype(BF16)
        out.append(p)
        v = v - p.astype(F32)
    return out


def left_parts(v, w, count, dims=NN):
    return sum(bdot(p, w, dims) for p in parts(v, count))


def right_parts(w, v, count, dims=NN):
    return sum(bdot(w, p, dims) for p in parts(v, count))


def iota(shape, dim):
    return lax.broadcasted_iota(jnp.int32, shape, dim)


def spread_matrix():
    return (iota((128, 512), 0) == iota((128, 512), 1) // 64).astype(BF16)


def heads_of(v, eh):
    return left_parts(v, eh, 2)


def sums_of(v, eh):
    return left_parts(v, eh, 2, NT)


def lower_matrix():
    return (iota((Q, Q), 0) >= iota((Q, Q), 1)).astype(BF16)


def sigmoid(v):
    return 1.0 / (1.0 + jnp.exp(-v))


def softplus(v):
    return jnp.maximum(v, 0.0) + jnp.log1p(jnp.exp(-jnp.abs(v)))


def row_scale(h):
    return lax.rsqrt(jnp.mean(h * h, axis=-1, keepdims=True) + EPS)


def decays(L, flags):
    E = jnp.exp(L) * flags[:, 3:4]
    W = jnp.exp(L[Q - 1 : Q] - L) * flags[:, 4:5]
    return E, W


def wave_kernel(
    hid, halo, gain, w, conv, hp, flags, segrow, og, cot, outw, coef,
    normed, gate, pre, ext, delta, logs, mixed, carried, states, sums, dno, endlog, cot_all, w_out,
    sums_s, log_s, rsend, rrecv, proj_s, pre_s, gate_s, delta_s, logs_s, sloc, inner, dno_s, state, total, tail, ends, cot_s, w_o, w_s, send, recv, done,
):
    t = pl.program_id(0)
    c = lax.rem(t, CH)
    at = lax.rem(t, 8)
    micro = at // CH
    eh = spread_matrix()
    n = Net(send, recv)
    g, m, core = n.g, n.m, n.c

    def cot_z(a):
        return n.copy(("cot", a), cot_s.at[m], cot_s.at[m], n.at(dz=a))

    def cot_near():
        return n.copy("near", cot_s.at[m], cot_s.at[m], n.at(dc=1))

    def cot_on(a):
        theirs = cot_s.at[2 * lax.rem(n.z + 4 - a, 4) + core]
        return n.copy(("on", a), theirs, theirs, n.at(dc=1))

    def out_x(d):
        return n.copy(("ox", d), w_o.at[g], w_o.at[g], n.at(dx=d))

    def out_y(d, half):
        part = w_o.at[n.behind(d), pl.ds(32 * half, 32)]
        return n.copy(("oy", d, half), part, part, n.at(dy=3 if half else 1))

    def out_swap():
        return n.copy("swap", w_o.at[pl.ds(4 * (1 - core), 4)], w_s.at[:, core], n.at(dc=1))

    def end_x(i, d):
        return n.copy(("ex", i, d), ends.at[g, i], ends.at[g, i], n.at(dx=d))

    def part_y(i):
        return n.copy(("r", i), rsend.at[i], rrecv.at[i], n.pair())

    def log_x(i, d):
        return n.copy(("lx", i, d), log_s.at[g, i], log_s.at[g, i], n.at(dx=d))

    def log_y(i, d):
        return n.copy(("ly", i, d), log_s.at[g, i], log_s.at[g, i], n.across(d))

    def sum_copy(i, a, b):
        mine = sums_s.at[m, pl.ds(CH * i, CH)]
        return n.copy(("sum", i, a, b), mine, mine, n.at(dz=a, dc=b))

    ALLX = (0,) + XS
    out_copies = [pltpu.make_async_copy(cot_s, cot_all, done.at[0]), pltpu.make_async_copy(w_s, w_out, done.at[1])]

    @pl.when(t == 0)
    def _():
        n.meet([n.at(dz=a, dc=b) for a, b in OTHERS] + [n.at(dx=d) for d in XS] + [n.at(dy=1), n.at(dy=3)] + [n.across(d) for d in ALLX])
        cot_s[m] = cot[...]
        w_o[g] = outw[...]
        for d in XS:
            out_x(d).start()
        for half in (0, 1):
            out_y(0, half).start()
        for a in (1, 3, 2):
            cot_z(a).start()
        cot_near().start()

    @pl.when((t < 8) & (c == 0))
    def _():
        h = hid[...].reshape(TOK, 2048).astype(F32)
        nb = (h * row_scale(h) * gain[...]).astype(BF16)
        normed[...] = nb.reshape(8, 1, 64, 2048)
        e = halo[0].astype(F32)
        eb = (e * row_scale(e) * gain[...]).astype(BF16)
        proj_s[...] = bdot(jnp.concatenate([eb, nb], 0), w[...])
        tail[0:8] = proj_s[8:16, 512:1280].astype(BF16).astype(F32)
        state[...] = jnp.zeros_like(state)
        total[...] = jnp.zeros_like(total)

    @pl.when(t < 8)
    def _():
        rows = pl.ds(pl.multiple_of(16 + Q * c, 16), Q)
        f = flags[...]
        gt = proj_s[rows, 0:512]
        gate[...] = gt
        gate_s[at] = gt
        xbc = proj_s[rows, 512:1280].astype(BF16).astype(F32)
        tail[8:] = xbc
        acc = conv[4:5] + conv[3:4] * xbc
        for k in range(3):
            acc = acc + conv[k : k + 1] * tail[5 + k : 5 + k + Q] * f[:, k : k + 1]
        pre[...] = acc
        pre_s[at] = acc
        ext[0] = tail[...].astype(BF16)
        d = softplus(proj_s[rows, 1280:1408] + hp[0:1])
        delta[...] = d
        delta_s[at] = d
        L = right_parts(lower_matrix(), d * hp[1:2], 3)
        logs[...] = L
        logs_s[at] = L
        E, W = decays(L, f)
        x = acc[:, :512]
        X = x * sigmoid(x)
        b = acc[:, 512:640]
        B = (b * sigmoid(b)).astype(BF16)
        S = right_parts(B, heads_of(W * d, eh) * X, 2, TN)
        sloc[at] = S
        both = heads_of(jnp.concatenate([E[Q - 8 :], L[Q - 8 :]], 0), eh)
        new = both[7:8] * state[...] + S
        state[...] = new
        tail[0:8] = tail[Q : Q + 8]
        lt = total[...] + L[Q - 1 : Q]
        total[...] = lt

        @pl.when(c == CH - 1)
        def _():
            ends[g, micro] = new.astype(BF16)
            p = parts(jnp.broadcast_to(heads_of(jnp.broadcast_to(lt, (8, 128)), eh)[0:1], (16, 512)), 3)
            r = iota((16, 512), 0)
            log_s[g, micro] = jnp.where(r == 0, p[0], jnp.where(r == 1, p[1], jnp.where(r == 2, p[2], jnp.zeros_like(p[0]))))

    for i, when in ((0, CH - 1), (1, 2 * CH - 1)):

        @pl.when(t == when)
        def _(i=i):
            for d in XS:
                log_x(i, d).start()
            for d in ALLX:
                log_y(i, d).start()
            for d in XS:
                end_x(i, d).start()

    @pl.when(t == 4)
    def _():
        for d in XS:
            out_x(d).wait_recv()
            for half in (0, 1):
                out_y(d, half).start()

    for i, when in ((0, 6), (1, 11)):

        @pl.when(t == when)
        def _(i=i):
            for d in XS:
                log_x(i, d).wait_recv()
            for d in ALLX:
                log_y(i, d).wait_recv()
            for d in XS:
                end_x(i, d).wait_recv()
            rsend[i] = entering(ends, log_s, coef, 1, 0, i, n.y).astype(BF16)
            part_y(i).start()

    @pl.when(t == 8)
    def _():
        for d in ALLX:
            for half in (0, 1):
                out_y(d, half).wait_recv()
        out_swap().start()
        for k in range(4):
            w_s[k, core] = w_o[4 * core + k]
        for a in (1, 3, 2):
            cot_z(a).wait_recv()
            cot_on(a).start()

    @pl.when((t >= 8) & (t < 16))
    def _():
        L = logs_s[at]
        a = pre_s[at]
        X, B, C = activations(a)
        U = (heads_of(delta_s[at], eh) * X).astype(BF16)
        psi = bdot(C, B, NT)
        keep = same_mask(flags[...], segrow[0])
        LT = L.T
        for j in range(4):
            u = pair_halves(U[:, 128 * j : 128 * j + 128])
            y = jnp.zeros((Q, 128), F32)
            for e in range(2):
                h = 2 * j + e
                K = jnp.where(keep, jnp.exp(L[:, h : h + 1] - LT[h : h + 1]), 0.0)
                y = y + bdot((psi * K).astype(BF16), u[e])
            inner[at, :, 128 * j : 128 * j + 128] = y

    @pl.when(t == 16)
    def _():
        out_swap().wait_recv()
        cot_near().wait_recv()
        for a in (1, 3, 2):
            cot_on(a).wait_recv()
        for cp in out_copies:
            cp.start()
        for i in (0, 1):
            part_y(i).wait_recv()
        endlog[...] = log_s[...]

    @pl.when((t >= 16) & (c == 0))
    def _():
        dno_s[...] = bdot(cot_s[:, micro].reshape(TOK, 2048), w_s[...].reshape(512, 2048), NT)
        state[...] = entering(ends, log_s, coef, 0, 0, micro, n.y) + rrecv[micro].astype(F32)

    @pl.when(t >= 16)
    def _():
        f = flags[...]
        E, _ = decays(logs_s[at], f)
        a = pre_s[at]
        X, _, C = activations(a)
        more = heads_of(jnp.concatenate([E, jnp.broadcast_to(hp[2:3], (8, 128))], 0), eh)
        Ex, skip = more[:Q], more[Q : Q + 1]
        S = state[...]
        states[0, 0] = S
        Yc = Ex * bdot(C, S.astype(BF16))
        carried[...] = Yc
        mix = inner[at] + Yc + skip * X
        mixed[...] = mix
        after = Ex[Q - 1 : Q] * S + sloc[at]
        state[...] = after
        states[0, 1] = after
        gt = gate_s[at]
        gated = mix * (gt * sigmoid(gt))
        dn = dno_s[pl.ds(pl.multiple_of(Q * c, Q), Q)]
        dno[...] = dn
        ones = jnp.ones((8, 512), BF16)
        sums_s[m, at, 0:8] = right_parts(ones, gated * gated, 2, NT)
        sums_s[m, at, 8:16] = right_parts(ones, dn * og[...] * gated, 2, NT)

    for i, when in ((0, 19), (1, 23)):

        @pl.when(t == when)
        def _(i=i):
            for a, b in OTHERS:
                sum_copy(i, a, b).start()

    @pl.when(t == 23)
    def _():
        for cp in out_copies:
            cp.wait()
        for i in (0, 1):
            for a, b in OTHERS:
                sum_copy(i, a, b).wait_recv()
        sums[...] = sums_s[...]
        for a in (1, 3, 2):
            cot_z(a).wait_send()
            cot_on(a).wait_send()
        cot_near().wait_send()
        out_swap().wait_send()
        for d in XS:
            out_x(d).wait_send()
        for d in ALLX:
            for half in (0, 1):
                out_y(d, half).wait_send()
        for i in (0, 1):
            part_y(i).wait_send()
            for d in XS:
                end_x(i, d).wait_send()
                log_x(i, d).wait_send()
            for d in ALLX:
                log_y(i, d).wait_send()
            for a, b in OTHERS:
                sum_copy(i, a, b).wait_send()


def tile(width, at=lambda t: t):
    return pl.BlockSpec((Q, width), lambda t: (at(t), 0))


def whole(*shape):
    return pl.BlockSpec(shape, lambda t: (0,) * len(shape))


def plain(kernel, name, outs, ins, spaces_in, spaces_out, scratch=(), flops=1 << 30):
    return pl.pallas_call(
        kernel,
        name=name,
        grid=(MICRO * CH,),
        out_shape=outs,
        in_specs=spaces_in,
        out_specs=spaces_out,
        scratch_shapes=list(scratch),
        compiler_params=pltpu.CompilerParams(vmem_limit_bytes=56 << 20),
        cost_estimate=pl.CostEstimate(flops=flops, bytes_accessed=16 << 20, transcendentals=0),
    )(*ins)


T = MICRO * TOK
HID = pl.BlockSpec((2, 1, 64, 2048), lambda t: (t % CH, t // CH, 0, 0))


def agblock(width, at=lambda t: t):
    return pl.BlockSpec((2, 1, 64, width), lambda t: (at(t) % CH, at(t) // CH, 0, 0))


def wave(hid, halo, gain, w, conv, hp, flags, segrow, og, cot, outw, coef):
    outs = [
        sds((8, 2, 64, 2048), BF16), sds((T, 512), F32), sds((T, 768), F32), sds((8, Q + 8, 768), BF16), sds((T, 128), F32), sds((T, 128), F32),
        sds((T, 512), F32), sds((T, 512), F32), sds((8, 2, 128, 512), F32), sds((8, 8, 16, 128), F32), sds((T, 512), F32), sds((8, 2, 16, 512), BF16), sds((8, 2, 64, 2048), BF16), sds((4, 2, 64, 2048), BF16),
    ]
    first = lambda t: jnp.minimum(t, 7)
    last = lambda t: jnp.maximum(t - 16, 0)
    ring = lambda t: t % 8
    micro = pl.BlockSpec((8, 1, 64, 2048), lambda t: (0, first(t) // CH, 0, 0))
    V = lambda *shape: pltpu.VMEM(shape, F32)
    return pl.pallas_call(
        wave_kernel,
        name="wave",
        grid=(24,),
        out_shape=outs,
        in_specs=[
            micro, pl.BlockSpec((1, 16, 2048), lambda t: (first(t) // CH, 0, 0)), whole(1, 2048), whole(2048, 1408), whole(8, 768), whole(8, 128), tile(128, ring), blk(1, 128, ring), whole(1, 512),
            whole(2, 64, 2048), whole(64, 2048), SMEM,
        ],
        out_specs=[
            micro, tile(512, first), tile(768, first), blk(Q + 8, 768, first), tile(128, first), tile(128, first),
            tile(512, last), tile(512, last), pl.BlockSpec((1, 2, 128, 512), lambda t: (last(t), 0, 0, 0)), whole(8, 8, 16, 128), tile(512, last), whole(8, 2, 16, 512), ANY, ANY,
        ],
        scratch_shapes=[
            V(8, 8, 16, 128), pltpu.VMEM((8, 2, 16, 512), BF16), pltpu.VMEM((2, 128, 512), BF16), pltpu.VMEM((2, 128, 512), BF16), V(TOK + 16, 1408), V(8, Q, 768), V(8, Q, 512), V(8, Q, 128), V(8, Q, 128), V(8, 128, 512), V(8, Q, 512), V(TOK, 512), V(128, 512), V(1, 128), V(Q + 8, 768),
            pltpu.VMEM((8, 2, 128, 512), BF16), pltpu.VMEM((8, 2, 64, 2048), BF16), pltpu.VMEM((8, 64, 2048), BF16), pltpu.VMEM((4, 2, 64, 2048), BF16),
            pltpu.SemaphoreType.DMA((64,)), pltpu.SemaphoreType.DMA((64,)), pltpu.SemaphoreType.DMA((2,)),
        ],
        compiler_params=pltpu.CompilerParams(collective_id=1, has_side_effects=True, vmem_limit_bytes=60 << 20),
        cost_estimate=pl.CostEstimate(flops=8 << 30, bytes_accessed=32 << 20, transcendentals=0),
    )(hid, halo, gain, w, conv, hp, flags, segrow, og, cot, outw, coef)


def entering(everyone, logs, coef, target, direction, micro, y):
    total = jnp.zeros((128, 512), F32)
    rows = [logs[q, micro].astype(F32) for q in range(8)]
    lt = [v[0:1] + v[1:2] + v[2:3] for v in rows]
    base = 160 * target + 80 * direction
    for k in range(4):
        q = 2 * k + y
        log = sum(coef[base + 8 * q + r] * lt[r] for r in range(8))
        total = total + jnp.exp(log) * coef[base + 64 + 8 * micro + q] * everyone[q, micro].astype(F32)
    return total


def same_mask(flags, segrow):
    return (flags[:, 5:6] == segrow) & (iota((Q, Q), 0) >= iota((Q, Q), 1))


def activations(pre):
    a = pre * sigmoid(pre)
    return a[:, :512], a[:, 512:640].astype(BF16), a[:, 640:768].astype(BF16)


def pair_halves(v):
    low_half = iota(v.shape, 1) < 64
    zero = jnp.zeros_like(v)
    return jnp.where(low_half, v, zero), jnp.where(low_half, zero, v)


def blk(a, b, at=lambda t: t):
    return pl.BlockSpec((1, a, b), lambda t: (at(t), 0, 0))


SMEM = pl.BlockSpec(memory_space=pltpu.SMEM)


def column(row):
    return jnp.concatenate([jnp.broadcast_to(row, (128, 128)).T] * 4, 1)


def back_at(t):
    return (t // CH) * CH + (CH - 1 - t % CH)


def pick_matrix(rows, start, count, shift, dtype=BF16):
    r, l = iota((rows, 128), 0), iota((rows, 128), 1)
    return ((r - start == l - shift) & (l >= shift) & (l < shift + count)).astype(dtype)


class Reduce:
    def __init__(self, n, key, a, b, a1, a2, pa, b1, b2, pb, b3):
        self.n, self.key, self.a, self.b = n, key, a, b
        self.a1, self.a2, self.pa, self.b1, self.b2, self.pb, self.b3 = a1, a2, pa, b1, b2, pb, b3
        self.half = a.shape[1] // 2

    def group(self, d, f):
        n = self.n
        return 2 * lax.rem(n.x + d, 4) + lax.rem(n.y + f, 2)

    def first_a(self, d, f):
        return self.n.copy((self.key, "a1", d, f), self.a.at[self.group(d, f)], self.a1.at[d - 1, f], self.n.at(dx=d))

    def first_b(self, d, e):
        n = self.n
        rep = lax.rem(n.ring + e, 4) // 2
        rows = pl.ds(pl.multiple_of(self.half * rep, self.half), self.half)
        return n.copy((self.key, "b1", d, e), self.b.at[self.group(d, e % 2), rows], self.b1.at[e - 1, lax.rem(n.x + d, 4)], n.at(dy=e))

    def send_a(self, d, f):
        if d:
            self.first_a(d, f).start()

    def send_b(self, d, f):
        for e in (1, 3) if f else (2,):
            self.first_b(d, e).start()

    def second_a(self, e):
        return self.n.copy((self.key, "a2", e), self.pa.at[e % 2], self.a2.at[e - 1], self.n.at(dy=e))

    def second_b(self, d):
        return self.n.copy((self.key, "b2", d), self.pb.at[lax.rem(self.n.x + d, 4)], self.b2.at[d - 1], self.n.at(dx=d))

    def third_b(self):
        return self.n.copy((self.key, "b3"), self.b3.at[self.n.rep], self.b3.at[self.n.rep], self.n.at(dy=2))

    def middle_a(self, f):
        for d in XS:
            self.first_a(d, f).wait_recv()
        self.pa[f] = add4(self.a[self.group(0, f)], self.a1[:, f]).astype(BF16)
        for e in (1, 3) if f else (2,):
            self.second_a(e).start()

    def middle_b(self):
        n = self.n
        rows = pl.ds(pl.multiple_of(self.half * n.rep, self.half), self.half)
        for d in (2, 1, 3, 0):
            for e in XS:
                self.first_b(d, e).wait_recv()
            k = lax.rem(n.x + d, 4)
            self.pb[k] = add4(self.b[2 * k + n.y, rows], self.b1[:, k]).astype(BF16)
            if d:
                self.second_b(d).start()

    def last_b(self):
        for d in XS:
            self.second_b(d).wait_recv()
        self.b3[self.n.rep] = add4(self.pb[self.n.x], self.b2).astype(self.b3.dtype)
        self.third_b().start()

    def last_a(self):
        for e in XS:
            self.second_a(e).wait_recv()
        return add4(self.pa[0], self.a2)

    def finish(self):
        for d in XS:
            for f in (0, 1):
                self.first_a(d, f).wait_send()
            self.second_b(d).wait_send()
        for e in XS:
            for d in range(4):
                self.first_b(d, e).wait_send()
            self.second_a(e).wait_send()
        self.third_b().wait_send()


def back_wave_kernel(
    mixed, carried, states, gate, dno, sums, pre, delta, logs, flags, segrow, og, hp, wout, cot, endlog, coef,
    dgate, dpre, dbc, ddt, small_o, small_b, total, g_out,
    nout, dmix, tloc, inner, dbi, starts, rsend, rrecv, cot_s, part, near, far, gsw, oa, ob, oa1, oa2, opa, ob1, ob2, opb, ob3, oin, state, send, recv, load,
):
    t = pl.program_id(0)
    at = back_at(lax.rem(t, 8))
    micro = at // CH
    c = lax.rem(at, CH)
    eh = spread_matrix()
    n = Net(send, recv)
    g, m, core, z = n.g, n.m, n.c, n.z
    O = Reduce(n, "o", oa, ob, oa1, oa2, opa, ob1, ob2, opb, ob3)
    bring = pltpu.make_async_copy(cot, cot_s, load.at[0])
    swap = n.copy("swap", gsw.at[:, 1 - core], oin, n.at(dc=1))

    def start_x(i, d):
        return n.copy(("sx", i, d), starts.at[g, i], starts.at[g, i], n.at(dx=d))

    def part_y(i):
        return n.copy(("r", i), rsend.at[i], rrecv.at[i], n.pair())

    def near_copy(d, i):
        return n.copy(("near", d, i), part.at[2 * lax.rem(z + d, 4) + 1 - core, i], near.at[d, i], n.at(dc=1))

    def far_copy(d, i):
        return n.copy(("far", d, i), near.at[d, i], far.at[d - 1, i], n.at(dz=d))

    @pl.when(t == 0)
    def _():
        bring.start()
        n.meet([n.at(dz=a) for a in (1, 3, 2)] + [n.at(dc=1)] + [n.at(dx=d) for d in XS] + [n.at(dy=d) for d in XS])
        small_o[...] = jnp.zeros_like(small_o)
        small_b[...] = jnp.zeros_like(small_b)

    @pl.when((t < 8) & (c == CH - 1))
    def _():
        state[...] = jnp.zeros_like(state)

    @pl.when(t < 8)
    def _():
        tot = sums[0, 0]
        for q in range(1, 8):
            tot = tot + sums[q, 0]
        r = column(lax.rsqrt(tot[0:1] / INNER + EPS))
        s2 = column(tot[8:9] / INNER)
        gt = gate[...]
        s = sigmoid(gt)
        sg = gt * s
        mix = mixed[...]
        gated = mix * sg
        dn = dno[...]
        n0 = gated * r
        nb = (n0 * og[...]).astype(BF16)
        nout[micro, pl.ds(pl.multiple_of(Q * c, Q), Q)] = nb
        d_gated = r * (dn * og[...] - n0 * r * s2)
        dm = d_gated * sg
        dmix[at] = dm
        dgate[...] = (d_gated * mix * (s * (1.0 + gt * (1.0 - s)))).astype(BF16)
        x = pre[:, :512]
        X = x * sigmoid(x)
        cc = pre[:, 640:768]
        C = (cc * sigmoid(cc)).astype(BF16)
        small_o[0:1] += jnp.sum(dn * n0, 0, keepdims=True)
        small_o[1:2] += jnp.sum(X * dm, 0, keepdims=True)
        E, _ = decays(logs[...], flags[...])
        Ex = heads_of(E, eh)
        G = right_parts(C, Ex * dm, 2, TN)
        tloc[at] = G
        new = Ex[Q - 1 : Q] * state[...] + G
        state[...] = new

        @pl.when(c == 0)
        def _():
            starts[g, micro] = new.astype(BF16)

    for i, when in ((0, 3), (1, 7)):

        @pl.when(t == when)
        def _(i=i):
            for d in XS:
                start_x(i, d).start()
            part[:, i] = bdot(nout[i], wout[...]).astype(BF16).reshape(8, 64, 2048)
            for d in (1, 3, 2, 0):
                near_copy(d, i).start()

    @pl.when(t == 8)
    def _():
        bring.wait()

        def columns(j, carry):
            to = pl.ds(pl.multiple_of(256 * j, 256), 256)
            v = sum(bdot(nout[i], cot_s[:, i, :, to].reshape(TOK, 256), TN) for i in range(MICRO))
            gsw[:, :, :, to] = v.astype(BF16).reshape(4, 2, 64, 256)
            return carry

        lax.fori_loop(0, 8, columns, 0)
        swap.start()
        for k in range(4):
            oa[4 * core + k] = gsw[k, core, :, 0:1024]
            ob[4 * core + k] = gsw[k, core, :, 1024:2048]

    for i, when in ((0, 9), (1, 12)):

        @pl.when(t == when)
        def _(i=i):
            for d in XS:
                start_x(i, d).wait_recv()
            rsend[i] = entering(starts, endlog, coef, 1, 1, i, n.y).astype(BF16)
            part_y(i).start()
            for d in (1, 3, 2, 0):
                near_copy(d, i).wait_recv()
                there = 2 * lax.rem(z + d, 4) + core
                near[d, i] = (part[there, i].astype(F32) + near[d, i].astype(F32)).astype(BF16)
                if d:
                    far_copy(d, i).start()

    @pl.when(t == 10)
    def _():
        swap.wait_recv()
        for k in range(4):
            oa[4 * (1 - core) + k] = oin[k, :, 0:1024]
            ob[4 * (1 - core) + k] = oin[k, :, 1024:2048]
        for d in (2, 1, 3, 0):
            for f in (1, 0):
                O.send_a(d, f)
                O.send_b(d, f)

    @pl.when((t >= 8) & (t < 16))
    def _():
        L = logs[...]
        f = flags[...]
        E, _ = decays(L, f)
        X, B, C = activations(pre[...])
        more = heads_of(jnp.concatenate([E, delta[...]], 0), eh)
        Ex, dx = more[:Q], more[Q:]
        Ub = (dx * X).astype(BF16)
        dm = dmix[at]
        dmb = dm.astype(BF16)
        psi = bdot(C, B, NT)
        keep = same_mask(f, segrow[0])
        LT = L.T
        dpsi = jnp.zeros((Q, Q), F32)
        for j in range(4):
            js = slice(128 * j, 128 * j + 128)
            u = pair_halves(Ub[:, js])
            y = pair_halves(dmb[:, js])
            acc = jnp.zeros((Q, 128), F32)
            for e in range(2):
                h = 2 * j + e
                K = jnp.where(keep, jnp.exp(L[:, h : h + 1] - LT[h : h + 1]), 0.0)
                acc = acc + bdot((psi * K).astype(BF16), y[e], TN)
                dpsi = dpsi + bdot(y[e], u[e], NT) * K
            inner[at, :, js] = acc
        dpb = dpsi.astype(BF16)
        dbi[at, 0:128] = bdot(C, dpb, TN)
        dbi[at, 128:256] = bdot(B, dpb, TT) + bdot(states[0, 0].astype(BF16), (Ex * dm).astype(BF16), NT)

    @pl.when(t == 16)
    def _():
        for i in (0, 1):
            part_y(i).wait_recv()

    @pl.when((t >= 16) & (c == CH - 1))
    def _():
        state[...] = entering(starts, endlog, coef, 0, 1, micro, n.y) + rrecv[micro].astype(F32)

    @pl.when(t >= 16)
    def _():
        L = logs[...]
        d = delta[...]
        E, W = decays(L, flags[...])
        p = pre[:, 0:512]
        s = sigmoid(p)
        X = p * s
        bb = pre[:, 512:640]
        B = (bb * sigmoid(bb)).astype(BF16)
        more = heads_of(jnp.concatenate([E[Q - 8 :], W, d, jnp.broadcast_to(hp[2:3], (8, 128))], 0), eh)
        Elast, Wx, dx, skip = more[7:8], more[8 : 8 + Q], more[8 + Q : 8 + 2 * Q], more[8 + 2 * Q : 9 + 2 * Q]
        U = dx * X
        dm = dmix[at]
        Yc = carried[...]
        Yi = mixed[...] - Yc - skip * X
        G = state[...]
        Gb = G.astype(BF16)
        dUi = inner[at]
        dUc = Wx * bdot(B, Gb)
        dU = dUi + dUc
        dbc[0:128] = (dbi[at, 0:128] + bdot(Gb, (Wx * U).astype(BF16), NT)).astype(BF16)
        dbc[128:256] = dbi[at, 128:256].astype(BF16)
        dL = sums_of(dm.astype(BF16).astype(F32) * Yi + dm * Yc - U.astype(BF16).astype(F32) * dUi - U * dUc, eh)
        end = sums_of(jnp.broadcast_to(jnp.sum(G * states[0, 1], 0, keepdims=True), (8, 512)), eh)[0:1]
        upper = (iota((Q, Q), 0) <= iota((Q, Q), 1)).astype(BF16)
        dstep = right_parts(upper, dL, 3) + end
        rate = hp[1:2]
        dr = (sums_of(dU * X, eh) + dstep * rate) * (1.0 - jnp.exp(-d))
        ddt[...] = dr.astype(BF16)
        small_b[0:1] += jnp.sum(dr, 0, keepdims=True)
        small_b[1:2] += jnp.sum(dstep * d * rate, 0, keepdims=True)
        dpre[...] = (dx * dU + skip * dm) * (s * (1.0 + p * (1.0 - s)))
        state[...] = Elast * G + tloc[at]

    @pl.when(t == 19)
    def _():
        O.middle_a(1)
        O.middle_a(0)
        O.middle_b()

    @pl.when(t == 22)
    def _():
        O.last_b()

    @pl.when(t == 23)
    def _():
        g_out[:, 0:1024] = O.last_a()
        for i in range(MICRO):
            for d in XS:
                far_copy(d, i).wait_recv()
            total[i] = near[0, i].astype(F32) + far[0, i].astype(F32) + far[1, i].astype(F32) + far[2, i].astype(F32)
        O.third_b().wait_recv()
        for h in range(2):
            g_out[32 * h : 32 * h + 32, 1024:2048] = ob3[h]
        O.finish()
        swap.wait_send()
        for i in range(MICRO):
            part_y(i).wait_send()
            for d in XS:
                start_x(i, d).wait_send()
                far_copy(d, i).wait_send()
            for d in range(4):
                near_copy(d, i).wait_send()


def back_wave(mixed, carried, states, gate, dno, sums, pre, delta, logs, flags, segrow, og, hp, wout, cot, endlog, coef):
    outs = [
        sds((T, 512), BF16), sds((T, 512), F32), sds((256, T), BF16), sds((T, 128), BF16), sds((8, 512), F32), sds((8, 128), F32), sds((2, 64, 2048), F32), sds((64, 2048), F32),
    ]
    b = lambda t: back_at(t % 8)
    first = lambda t: back_at(jnp.minimum(t, 7))
    last = lambda t: back_at(jnp.maximum(t - 16, 0))
    V = lambda *s: pltpu.VMEM(s, BF16)
    R = lambda *s: pltpu.VMEM(s, F32)
    return pl.pallas_call(
        back_wave_kernel,
        name="back_wave",
        grid=(24,),
        out_shape=outs,
        in_specs=[
            tile(512, b), tile(512, b), pl.BlockSpec((1, 2, 128, 512), lambda t: (b(t), 0, 0, 0)), tile(512, first), tile(512, first), pl.BlockSpec((8, 1, 16, 128), lambda t: (0, first(t), 0, 0)),
            tile(768, b), tile(128, b), tile(128, b), tile(128, b), blk(1, 128, b), whole(1, 512), whole(8, 128), whole(512, 2048), ANY, whole(8, 2, 16, 512), SMEM,
        ],
        out_specs=[
            tile(512, first), tile(512, last), pl.BlockSpec((256, Q), lambda t: (0, last(t))), tile(128, last), whole(8, 512), whole(8, 128), whole(2, 64, 2048), whole(64, 2048),
        ],
        scratch_shapes=[
            V(2, TOK, 512), R(8, Q, 512), R(8, 128, 512), R(8, Q, 512), R(8, 256, 128), V(8, 2, 128, 512), V(2, 128, 512), V(2, 128, 512), V(8, 2, 64, 2048), V(8, 2, 64, 2048),
            V(4, 2, 64, 2048), V(3, 2, 64, 2048), V(4, 2, 64, 2048),
            V(8, 64, 1024), V(8, 64, 1024), V(3, 2, 64, 1024), V(3, 64, 1024), V(2, 64, 1024), V(3, 4, 32, 1024), V(3, 32, 1024), V(4, 32, 1024), R(2, 32, 1024), V(4, 64, 2048), R(128, 512),
            pltpu.SemaphoreType.DMA((56,)), pltpu.SemaphoreType.DMA((56,)), pltpu.SemaphoreType.DMA((1,)),
        ],
        compiler_params=pltpu.CompilerParams(collective_id=4, has_side_effects=True, vmem_limit_bytes=62 << 20),
        cost_estimate=pl.CostEstimate(flops=8 << 30, bytes_accessed=32 << 20, transcendentals=0),
    )(mixed, carried, states, gate, dno, sums, pre, delta, logs, flags, segrow, og, hp, wout, cot, endlog, coef)


CA = 640
CB = 1152 - CA


def tail_kernel(
    dbc, edge_x, dpre, pre, ext, flags, fnext, conv, ddt, dgate, w, hid, normed, small_o, small_b,
    gi, total, small_all,
    bc_s, ex_s, eb_src, eb_s, dps, pre_s, ext_s, fl_s, fn_s, ddt_s, dg_s, w_s, hid_s, nm_s, wt, e_s, dproj, part, near, far, conv_acc, gnorm,
    s0, s1, s2, sx, ga, gb, ga1, ga2, gpa, gb1, gb2, gpb, gb3, final, send, recv, load,
):
    n = Net(send, recv)
    x, y, z, c, m = n.x, n.y, n.z, n.c, n.m
    loads = {}

    def fetch(key, src, dst):
        loads[key] = pltpu.make_async_copy(src, dst, load.at[len(loads)])
        loads[key].start()

    fetch("normed", normed, nm_s)
    fetch("dgate", dgate, dg_s)
    fetch("pre", pre.at[:, :, pl.ds(512, 256)], pre_s)
    fetch("w", w, w_s)
    fetch("dpre", dpre, dps.at[:, pl.ds(0, TOK), pl.ds(0, 512)])
    fetch("ext", ext, ext_s)
    fetch("flags", flags, fl_s)
    fetch("fnext", fnext, fn_s)
    fetch("ddt", ddt, ddt_s)
    fetch("hid", hid, hid_s)
    n.meet([n.at(dz=a, dc=b) for a, b in OTHERS] + [n.at(dx=d) for d in XS] + [n.at(dy=d) for d in XS] + [n.group(1), n.group(7)])

    def bc_copy(a, b):
        return n.copy(("bc", a, b), dbc.at[n.member(a, b)], bc_s.at[m], n.at(dz=a, dc=b))

    edge1 = n.copy("edge1", edge_x, ex_s, n.group(7))
    edge2 = n.copy("edge2", eb_src, eb_s, n.group(7))

    def near_copy(d, i):
        return n.copy(("near", d, i), part.at[2 * lax.rem(z + d, 4) + 1 - c, i], near.at[d, i], n.at(dc=1))

    def far_copy(d, i):
        return n.copy(("far", d, i), near.at[d, i], far.at[d - 1, i], n.at(dz=d))

    def small_x(d):
        return n.copy(("sx", d), s0, s1.at[d - 1], n.at(dx=d))

    def small_y(d):
        return n.copy(("sy", d), sx, s2.at[d - 1], n.at(dy=d))

    def small_m(a, b):
        return n.copy(("sm", a, b), small_all.at[m], small_all.at[m], n.at(dz=a, dc=b))

    def rows_copy(a, b):
        return n.copy(("rows", a, b), final.at[n.member(a, b)], gi.at[m], n.at(dz=a, dc=b))

    W = Reduce(n, "w", ga, gb, ga1, ga2, gpa, gb1, gb2, gpb, gb3)

    for a, b in OTHERS:
        bc_copy(a, b).start()
    edge1.start()
    bc_s[m] = dbc[m]

    def weight_tile(q, right):
        rows = pl.ds(pl.multiple_of(256 * q, 256), 256)
        return sum(bdot(nm_s[:, i, :, rows].reshape(TOK, 256), right[i], TN) for i in range(MICRO)).astype(BF16)

    loads["normed"].wait()
    loads["dgate"].wait()
    for d in (2, 1, 3, 0):
        for f in (1, 0):
            q = W.group(d, f)
            gb[q] = weight_tile(q, dg_s)
            W.send_b(d, f)
    pick = pick_matrix(256, 32 * m, 32, 0)
    loads["w"].wait()
    wt[...] = (bdot(w_s[:, 1024:1280], pick) + bdot(w_s[:, 1280:1408], pick_matrix(128, 0, 8, 32))).astype(BF16)
    cw = jnp.concatenate([conv[:, 0:512], left_parts(conv[:, 512:768], pick, 3)], 1)
    for key in ("pre", "dpre"):
        loads[key].wait()
    for a, b in OTHERS:
        bc_copy(a, b).wait_recv()
    eye = pick_matrix(32, 0, 32, 0)

    def bc_chunk(i, k):
        t = CH * i + k
        tot = bc_s[0, :, Q * t : Q * t + Q].astype(F32)
        for q in range(1, 8):
            tot = tot + bc_s[q, :, Q * t : Q * t + Q].astype(F32)
        d = left_parts(tot, eye, 2, TN)
        p = left_parts(pre_s[t], pick, 2)
        s = sigmoid(p)
        dps[i, Q * k : Q * k + Q, 512:640] = d * (s * (1.0 + p * (1.0 - s)))

    for i in range(MICRO):
        bc_chunk(i, 0)
        eb_src[i] = dps[i, 0:8, 512:640]
    edge2.start()
    for i in range(MICRO):
        for k in range(1, CH):
            bc_chunk(i, k)
    for key in ("ext", "flags", "fnext", "ddt"):
        loads[key].wait()
    conv_acc[...] = jnp.zeros_like(conv_acc)
    pick_dt = pick_matrix(128, 0, 8, 32)

    def conv_chunk(i, k):
        t = CH * i + k
        e_s[:, 0:512] = ext_s[t, :, 0:512].astype(F32)
        e_s[:, 512:640] = bdot(ext_s[t, :, 512:768], pick)
        f, fn = fl_s[t], fn_s[t]
        dp = dps[i, Q * k : Q * k + Q]
        dx = cw[3:4] * dp
        conv_acc[3:4] += jnp.sum(dp * e_s[8 : 8 + Q], 0, keepdims=True)
        conv_acc[4:5] += jnp.sum(dp, 0, keepdims=True)
        for j in range(3):
            conv_acc[j : j + 1] += jnp.sum(dp * e_s[5 + j : 5 + j + Q] * f[:, j : j + 1], 0, keepdims=True)
            dx = dx + cw[j : j + 1] * dps[i, Q * k + 3 - j : Q * k + 3 - j + Q] * fn[:, j : j + 1]
        rows = slice(Q * k, Q * k + Q)
        dproj[i, rows, 0:512] = dx[:, 0:512].astype(BF16)
        dproj[i, rows, 512:640] = (dx[:, 512:640] + bdot(ddt_s[t], pick_dt)).astype(BF16)

    for i in range(MICRO):
        for k in range(CH - 1):
            conv_chunk(i, k)
    edge1.wait_recv()
    edge2.wait_recv()
    for i in range(MICRO):
        dps[i, TOK : TOK + 8, 0:512] = ex_s[i]
        dps[i, TOK : TOK + 8, 512:640] = eb_s[i]
        conv_chunk(i, CH - 1)

    for d in (2, 1, 3, 0):
        for f in (1, 0):
            q = W.group(d, f)
            ga[q] = weight_tile(q, dproj)
            W.send_a(d, f)

    loads["hid"].wait()
    for i in range(MICRO):
        h = hid_s[:, i].reshape(TOK, 2048).astype(F32)
        scale = row_scale(h)
        first, main, rest = dg_s[i], dproj[i, :, 0:512], dproj[i, :, 512:640]

        def tile_of(j, carry, i=i, scale=scale, first=first, main=main, rest=rest):
            at = pl.ds(pl.multiple_of(256 * j, 256), 256)
            d = bdot(first, w_s[at, 0:512], NT) + bdot(main, w_s[at, 512:1024], NT) + bdot(rest, wt[at], NT)
            part[:, i, :, at] = d.astype(BF16).reshape(8, 64, 256)
            hv = hid_s[:, i, :, at].reshape(TOK, 256).astype(F32)
            s = jnp.sum(d * (hv * scale), 0, keepdims=True)
            gnorm[0:1, at] = s if i == 0 else gnorm[0:1, at] + s
            return carry

        lax.fori_loop(0, 8, tile_of, 0)
        for d in (1, 3, 2, 0):
            near_copy(d, i).start()
    for r in range(16):
        s0[r : r + 1] = gnorm[0:1, 128 * r : 128 * r + 128]
    for k in range(5):
        for r in range(5):
            s0[16 + 5 * k + r : 17 + 5 * k + r] = conv_acc[k : k + 1, 128 * r : 128 * r + 128]
    for r in range(4):
        s0[41 + r : 42 + r] = small_o[0:1, 128 * r : 128 * r + 128]
    s0[45:47] = small_b[0:2]
    s0[47:48] = sums_of(small_o[...], spread_matrix())[1:2]
    for d in XS:
        small_x(d).start()

    for i in range(MICRO):
        for d in (1, 3, 2, 0):
            near_copy(d, i).wait_recv()
            at = 2 * lax.rem(z + d, 4) + c
            near[d, i] = (part[at, i].astype(F32) + near[d, i].astype(F32)).astype(BF16)
            if d:
                far_copy(d, i).start()
    for d in XS:
        small_x(d).wait_recv()
    sx[...] = s0[...] + s1[0] + s1[1] + s1[2]
    for d in XS:
        small_y(d).start()
    W.middle_b()
    W.middle_a(1)
    W.middle_a(0)
    W.last_b()
    for d in XS:
        small_y(d).wait_recv()
    small_all[m] = sx[...] + s2[0] + s2[1] + s2[2]
    for a, b in OTHERS:
        small_m(a, b).start()
    for i in range(MICRO):
        for d in XS:
            far_copy(d, i).wait_recv()
        total[i] = near[0, i].astype(F32) + far[0, i].astype(F32) + far[1, i].astype(F32) + far[2, i].astype(F32)
    W.third_b().wait_recv()
    for h in range(2):
        final[4 * h : 4 * h + 4, :, 0:CB] = gb3[h].reshape(4, 32, CB)
    final[:, :, CB:] = W.last_a().astype(BF16).reshape(8, 32, CA)
    for a, b in OTHERS:
        rows_copy(a, b).start()
    gi[m] = final[m]
    for a, b in OTHERS:
        rows_copy(a, b).wait_recv()
        small_m(a, b).wait_recv()
    W.finish()
    for a, b in OTHERS:
        bc_copy(a, b).wait_send()
        rows_copy(a, b).wait_send()
        small_m(a, b).wait_send()
    for d in XS:
        small_x(d).wait_send()
        small_y(d).wait_send()
        for i in range(MICRO):
            far_copy(d, i).wait_send()
    for d in range(4):
        for i in range(MICRO):
            near_copy(d, i).wait_send()
    edge1.wait_send()
    edge2.wait_send()


def tail_call(dbc, edge_x, dpre, pre, ext, flags, fnext, conv, ddt, dgate, w, hid, normed, small_o, small_b):
    outs = [sds((8, 32, 1152), BF16), sds((2, 64, 2048), F32), sds((8, 48, 128), F32)]
    V = lambda *s: pltpu.VMEM(s, BF16)
    R = lambda *s: pltpu.VMEM(s, F32)
    scratch = [
        V(8, 32, T), R(2, 8, 512), R(2, 8, 128), R(2, 8, 128), R(2, TOK + 8, 640), R(8, Q, 256), V(8, Q + 8, 768), R(8, Q, 128), R(8, Q, 128), V(8, Q, 128), V(2, TOK, 512), V(2048, 1408),
        V(8, 2, 64, 2048), V(8, 2, 64, 2048), V(2048, 128), R(Q + 8, 640), V(2, TOK, 640), V(8, 2, 64, 2048), V(4, 2, 64, 2048), V(3, 2, 64, 2048), R(8, 640), R(8, 2048),
        R(48, 128), R(3, 48, 128), R(3, 48, 128), R(48, 128),
        V(8, 256, CA), V(8, 256, CB), V(3, 2, 256, CA), V(3, 256, CA), V(2, 256, CA), V(3, 4, 128, CB), V(3, 128, CB), V(4, 128, CB), V(2, 128, CB),
        V(8, 32, 1152),
    ]
    return pl.pallas_call(
        tail_kernel,
        name="tail",
        out_shape=outs,
        in_specs=[VM, VM] + [ANY] * 5 + [VM] + [ANY] * 5 + [VM] * 2,
        out_specs=[VM] * 3,
        scratch_shapes=[*scratch, pltpu.SemaphoreType.DMA((112,)), pltpu.SemaphoreType.DMA((112,)), pltpu.SemaphoreType.DMA((10,))],
        compiler_params=pltpu.CompilerParams(collective_id=5, has_side_effects=True, vmem_limit_bytes=62 << 20),
        cost_estimate=pl.CostEstimate(flops=8 << 30, bytes_accessed=32 << 20, transcendentals=0),
    )(dbc, edge_x, dpre, pre, ext, flags, fnext, conv, ddt, dgate, w, hid, normed, small_o, small_b)


def strips(v, zi, ci):
    r = v.shape[0]
    return lax.dynamic_slice(v.reshape(r, 2, 4, 4, 128), (0, ci, 0, zi, 0), (r, 1, 4, 1, 128)).reshape(r, 512)


def from_members(v):
    r = v.shape[1]
    return v.reshape(4, 2, r, 4, 128).transpose(2, 1, 3, 0, 4).reshape(r, 4096)


def from_heads(v):
    r = v.shape[1]
    return v.reshape(4, 2, r, 4, 2).transpose(2, 1, 3, 0, 4).reshape(r, 64)


def from_rows(v):
    return v.transpose(1, 0, 2).reshape(v.shape[1], 256)


def to_members(v):
    r = v.shape[0]
    return v.reshape(r, 2, 4, 4, 128).transpose(3, 1, 0, 2, 4).reshape(8, r, 512)


def xdot(a, b, dims=NN):
    return lax.dot_general(a, b, dims, preferred_element_type=F32)


def per_device(layer_in, cotangent, segment_ids, norm_gain, in_weight, conv_weight, conv_bias, dt_bias, a_log, skip_gain, out_gain, out_weight):
    xi, yi, zi, ci = (lax.axis_index(a) for a in SEQ)
    g = 2 * xi + yi
    m = 2 * zi + ci
    pack = jnp.concatenate([segment_ids[:, 0].astype(F32).reshape(-1), norm_gain, conv_weight.reshape(-1), conv_bias, dt_bias, a_log, skip_gain, out_gain, jnp.zeros((1024 - 567,), F32)]).reshape(8, 128)
    bc = jnp.broadcast_to(in_weight[None, :, 8192:8448], (8, 32, 256))
    dt_w = in_weight[:, 8448:].reshape(32, 2, 4, 4, 2).transpose(3, 1, 0, 2, 4).reshape(8, 32, 8)
    w_send = jnp.concatenate([to_members(in_weight[:, :4096]), to_members(in_weight[:, 4096:8192]), bc, dt_w, jnp.zeros((8, 32, 120), BF16)], 2)
    hid_all, w_in, small_all, halo = gather(layer_in[:, 0], w_send, pack)
    w_in = w_in.reshape(2048, 1408)
    full = small_all.reshape(64, 1024)
    seg_full = full[:, :128].reshape(64, 2, 64).transpose(1, 0, 2).reshape(2, 4096)
    full = full[:, 128:]
    norm_full = full[:, :32].reshape(1, 2048)
    conv_full = full[:, 32:372].reshape(64, 5, 68).transpose(1, 0, 2).reshape(5, CONV)
    conv = jnp.concatenate([strips(conv_full[:, :INNER], zi, ci), conv_full[:, INNER:]], 1)
    conv = jnp.pad(conv, ((0, 3), (0, 0)))
    hv = lax.dynamic_slice(full[:, 372:439].reshape(2, 4, 4, 2, 67), (ci, 0, zi, 0, 0), (1, 4, 1, 2, 67)).reshape(8, 67)
    og = hv[:, 3:].reshape(1, 512)
    hp = jnp.pad(jnp.stack([hv[:, 0], -jnp.exp(hv[:, 1]), hv[:, 2]]), ((0, 5), (0, 120)))

    padded = jnp.concatenate([jnp.full((MICRO, 8), -1.0, F32), seg_full, jnp.full((MICRO, 8), -2.0, F32)], 1)
    near = lax.dynamic_slice(padded, (0, g * TOK), (MICRO, TOK + 16))
    own = near[:, 8 : 8 + TOK]
    chunked = own.reshape(MICRO, CH, Q)
    before = jnp.concatenate([near[:, 7:8], chunked[:, :-1, -1]], 1)[:, :, None]
    lanes = [(near[:, 5 + k : 5 + k + TOK] == own).astype(F32).reshape(T) for k in range(3)]
    lanes += [(chunked == before).astype(F32).reshape(T), (chunked == chunked[:, :, -1:]).astype(F32).reshape(T), own.reshape(T)]
    flags = jnp.pad(jnp.stack(lanes, 1), ((0, 0), (0, 122)))
    fnext = jnp.pad(jnp.stack([(near[:, 11 - k : 11 - k + TOK] == own).astype(F32).reshape(T) for k in range(3)], 1), ((0, 0), (0, 125)))
    segrow = own.reshape(8, 1, Q)
    lasts = seg_full.reshape(MICRO, GROUPS, TOK)[:, :, -1]
    idx = jnp.arange(GROUPS)
    q, r = idx[:, None], idx[None, :]
    tables = []
    for target in (g, 2 * xi + 1 - yi):
        last_before = jnp.sum(jnp.where(idx == target - 1, lasts, 0.0), 1, keepdims=True)
        last_own = jnp.sum(jnp.where(idx == target, lasts, 0.0), 1, keepdims=True)
        ok_before = (idx < target) & (lasts == last_before)
        ok_after = (idx > target) & (jnp.roll(lasts, 1, axis=1) == last_own)
        tables += [(r > q) & (r < target), ok_before, (r > target) & (r < q), ok_after]
    coef = jnp.concatenate([v.astype(F32) for v in tables], 0).reshape(320)

    normed, gate, pre, ext, delta, logs, mixed, carried, states, sums, dno, ends_all, cot, w_out = wave(hid_all, halo, norm_full, w_in, conv, hp, flags, segrow, og, cotangent[:, 0], out_weight, coef)
    dgate, dpre, dbc, ddt, small_o, small_b, own_branch, g_out = back_wave(
        mixed, carried, states, gate, dno, sums, pre, delta, logs, flags, segrow, og, hp, w_out.reshape(512, 2048), cot, ends_all, coef
    )
    split = lambda v: v.reshape(8, Q, v.shape[-1])
    by_micro = lambda v: v.reshape(MICRO, TOK, v.shape[-1])
    gi, own_dn, small_sum = tail_call(
        dbc.reshape(8, 32, T), by_micro(dpre)[:, :8], by_micro(dpre), split(pre), ext, split(flags), split(fnext), conv, split(ddt), by_micro(dgate), w_in, hid_all, normed, small_o, small_b
    )
    gi = gi.astype(F32)
    hid_o = layer_in[:, 0].astype(F32)
    layer_out = (hid_o + own_branch).astype(BF16)
    ro = row_scale(hid_o)
    dg = own_dn * norm_full
    d_hid = ro * dg - hid_o * (ro * ro * ro) * jnp.mean(dg * hid_o, -1, keepdims=True)
    grad_in = (cotangent[:, 0].astype(F32) + d_hid).astype(BF16)
    g_in = jnp.concatenate([from_members(gi[:, :, :512]), from_members(gi[:, :, 512:1024]), from_rows(gi[:, :, 1024:1056]), from_heads(gi[:, :, 1056:1064])], 1)
    at = 8 * g + m
    g_norm = lax.dynamic_slice(small_sum[:, :16].sum(0).reshape(64, 32), (at, 0), (1, 32)).reshape(32)
    conv_s = small_sum[:, 16:41].reshape(8, 5, 640)
    conv_s = jnp.concatenate([from_members(conv_s[:, :, :512]), from_rows(conv_s[:, :, 512:544])], 1)
    conv_s = lax.dynamic_slice(conv_s, (0, 68 * at), (5, 68))
    og_s = from_members(small_sum[:, 41:45].reshape(8, 1, 512))[0]
    og_s = lax.dynamic_slice(og_s, (64 * at,), (64,))
    hd_s = from_heads(small_sum[:, 45:48, :8])
    hd_s = lax.dynamic_slice(hd_s, (0, at), (3, 1))
    return (layer_out[:, None], grad_in[:, None], g_norm, g_in, conv_s[:4], conv_s[4], hd_s[0], hd_s[1], hd_s[2], og_s, g_out)


def solution(mesh):
    fine = Mesh(mesh.devices.reshape(2, 4, 2, 4, 2), AXES)
    tok = P(None, "rep", SEQ, None)
    return jax.shard_map(
        per_device,
        mesh=fine,
        in_specs=(tok, tok, P(None, "rep", SEQ), P(SEQ), P(SEQ, None), P(None, SEQ), P(SEQ), P(SEQ), P(SEQ), P(SEQ), P(SEQ), P(SEQ, None)),
        out_specs=(tok, tok, P(SEQ), P(SEQ, None), P(None, SEQ), P(SEQ), P(SEQ), P(SEQ), P(SEQ), P(SEQ), P(SEQ, None)),
        check_vma=False,
    )
```

```python
import functools

import jax
import jax.numpy as jnp
from jax import lax
from jax.experimental import pallas as pl
from jax.experimental.pallas import tpu as pltpu
from jax.sharding import Mesh, PartitionSpec as P

EPS = 1e-05
INNER = 4096
MICRO = 2
CONV = 4352
F32 = jnp.float32
BF16 = jnp.bfloat16
AXES = ("rep", "x", "y", "z", "c")
SEQ = ("x", "y", "z", "c")
GROUPS = 8
TOK = 512
Q = 128
CH = TOK // Q

MESH = pl.DeviceIdType.MESH
ANY = pl.BlockSpec(memory_space=pl.ANY)
VM = pl.BlockSpec(memory_space=pltpu.VMEM)


class Net:
    def __init__(self, send, recv):
        self.send, self.recv, self.used, self.open = send, recv, 0, []
        self.keys = {}
        self.rep, self.x, self.y, self.z, self.c = (lax.axis_index(a) for a in AXES)
        self.ring = 2 * self.rep + self.y
        self.g = 2 * self.x + self.y
        self.m = 2 * self.z + self.c

    def at(self, dx=0, dy=0, dz=0, dc=0):
        ring = lax.rem(self.ring + dy, 4)
        return (ring // 2, lax.rem(self.x + dx, 4), lax.rem(ring, 2), lax.rem(self.z + dz, 4), lax.rem(self.c + dc, 2))

    def pair(self):
        return (self.rep, self.x, 1 - self.y, self.z, self.c)

    def across(self, dx):
        return (self.rep, lax.rem(self.x + dx, 4), 1 - self.y, self.z, self.c)

    def group(self, d):
        g = lax.rem(self.g + d, 8)
        return (self.rep, g // 2, lax.rem(g, 2), self.z, self.c)

    def member(self, dz, dc):
        return 2 * lax.rem(self.z + dz, 4) + lax.rem(self.c + dc, 2)

    def push(self, src, dst, where):
        i = self.used
        self.used += 1
        copy = pltpu.make_async_remote_copy(
            src_ref=src, dst_ref=dst, send_sem=self.send.at[i], recv_sem=self.recv.at[i], device_id=where, device_id_type=MESH
        )
        copy.start()
        self.open.append(copy)
        return copy

    def copy(self, key, src, dst, where):
        i = self.keys.setdefault(key, len(self.keys))
        return pltpu.make_async_remote_copy(
            src_ref=src, dst_ref=dst, send_sem=self.send.at[i], recv_sem=self.recv.at[i], device_id=where, device_id_type=MESH
        )

    def behind(self, d):
        return 2 * lax.rem(self.x + 4 - d, 4) + self.y

    def local(self, src, dst):
        i = self.used
        self.used += 1
        copy = pltpu.make_async_copy(src, dst, self.recv.at[i])
        copy.start()
        return copy

    def meet(self, peers):
        barrier = pltpu.get_barrier_semaphore()
        for peer in peers:
            pl.semaphore_signal(barrier, inc=1, device_id=peer, device_id_type=MESH)
        pl.semaphore_wait(barrier, len(peers))

    def finish(self):
        for copy in self.open:
            copy.wait_send()


OTHERS = [(dz, dc) for dz in (0, 1, 3, 2) for dc in (0, 1) if (dz, dc) != (0, 0)]
ZS = (0, 1, 3, 2)
XS = (1, 3, 2)
ORDER = [(d, f) for d in (2, 1, 3, 0) for f in (1, 0)]


def call(kernel, name, cid, outs, ins, spaces_in, spaces_out, sems, scratch=(), cost=1 << 20):
    return pl.pallas_call(
        kernel,
        name=name,
        out_shape=outs,
        in_specs=spaces_in,
        out_specs=spaces_out,
        scratch_shapes=[*scratch, pltpu.SemaphoreType.DMA((sems,)), pltpu.SemaphoreType.DMA((sems,))],
        compiler_params=pltpu.CompilerParams(collective_id=cid, has_side_effects=True, vmem_limit_bytes=60 << 20),
        cost_estimate=pl.CostEstimate(flops=0, bytes_accessed=cost, transcendentals=0),
    )(*ins)


def sds(shape, dtype):
    return jax.ShapeDtypeStruct(shape, dtype)


def gather_kernel(hid, wsend, small, hid_all, w_in, small_all, halo, send, recv):
    n = Net(send, recv)
    g, m, z, c, y = n.g, n.m, n.z, n.c, n.y
    n.meet(
        [n.at(dz=a, dc=b) for a, b in OTHERS] + [n.at(dx=d) for d in XS] + [n.at(dy=1), n.at(dy=3), n.group(1), n.group(7)]
    )
    own = [n.local(wsend.at[m], w_in.at[g, m]), n.local(small, small_all.at[g, m]), n.local(hid, hid_all.at[m])]
    w_cp, s_cp = {}, {}
    for a, b in OTHERS:
        w_cp[a, b] = n.push(wsend.at[n.member(a, b)], w_in.at[g, m], n.at(dz=a, dc=b))
        s_cp[a, b] = n.push(small, small_all.at[g, m], n.at(dz=a, dc=b))
    last = []

    def along_y(ref, group, pick):
        for half, dy in ((0, 1), (1, 3)):
            part = pick(ref, group, half)
            last.append(n.push(part, part, n.at(dy=dy)))

    def w_half(k):
        first = 2 * lax.rem(z + 4 - ZS[k], 4)
        return lambda ref, group, half: ref.at[group, pl.ds(first, 2), pl.ds(16 * half, 16)]

    x_cp = {}
    for cp in own:
        cp.wait()

    def issue(k):
        for b in (0, 1):
            if (ZS[k], b) != (0, 0):
                w_cp[ZS[k], b].wait_recv()
        block = w_in.at[g, pl.ds(2 * lax.rem(z + 4 - ZS[k], 4), 2)]
        for d in XS:
            x_cp[k, d] = n.push(block, block, n.at(dx=d))
        along_y(w_in, g, w_half(k))

    issue(0)
    issue(1)
    h_cp = {a: n.push(hid, hid_all.at[m], n.at(dz=a)) for a in (1, 3, 2)}
    h_sib = n.push(hid, hid_all.at[m], n.at(dc=1))
    for k in range(4):
        for d in XS:
            x_cp[k, d].wait_recv()
            along_y(w_in, 2 * lax.rem(n.x + 4 - d, 4) + y, w_half(k))
        if k < 2:
            issue(k + 2)
    for a, b in OTHERS:
        s_cp[a, b].wait_recv()
    s_x = {d: n.push(small_all.at[g], small_all.at[g], n.at(dx=d)) for d in XS}
    last.append(n.push(small_all.at[g], small_all.at[g], n.pair()))
    for d in XS:
        other = 2 * lax.rem(n.x + 4 - d, 4) + y
        s_x[d].wait_recv()
        last.append(n.push(small_all.at[other], small_all.at[other], n.pair()))
        h_cp[d].wait_recv()
        theirs = hid_all.at[2 * lax.rem(z + 4 - d, 4) + c]
        last.append(n.push(theirs, theirs, n.at(dc=1)))
    h_sib.wait_recv()
    for cp in last:
        cp.wait_recv()
    edge = n.push(hid_all.at[7, :, pl.ds(48, 16)], halo, n.group(1))
    edge.wait_recv()
    n.finish()


def gather(hid, wsend, small):
    outs = [sds((8, 2, 64, 2048), BF16), sds((8, 8, 32, 1408), BF16), sds((8, 8, 8, 128), F32), sds((2, 16, 2048), BF16)]
    return call(gather_kernel, "gather", 0, outs, (hid, wsend, small), [VM] * 3, [ANY] * 4, 112)


def add4(a, b):
    return a.astype(F32) + b[0].astype(F32) + b[1].astype(F32) + b[2].astype(F32)


NN = (((1,), (0,)), ((), ()))
NT = (((1,), (1,)), ((), ()))
TN = (((0,), (0,)), ((), ()))
TT = (((0,), (1,)), ((), ()))


def bdot(a, b, dims=NN):
    return lax.dot_general(a, b, dims, preferred_element_type=F32)


def parts(v, count):
    out = []
    for _ in range(count):
        p = v.astype(BF16)
        out.append(p)
        v = v - p.astype(F32)
    return out


def left_parts(v, w, count, dims=NN):
    return sum(bdot(p, w, dims) for p in parts(v, count))


def right_parts(w, v, count, dims=NN):
    return sum(bdot(w, p, dims) for p in parts(v, count))


def iota(shape, dim):
    return lax.broadcasted_iota(jnp.int32, shape, dim)


def spread_matrix():
    return (iota((128, 512), 0) == iota((128, 512), 1) // 64).astype(BF16)


def heads_of(v, eh):
    return left_parts(v, eh, 2)


def sums_of(v, eh):
    return left_parts(v, eh, 2, NT)


def lower_matrix():
    return (iota((Q, Q), 0) >= iota((Q, Q), 1)).astype(BF16)


def sigmoid(v):
    return 1.0 / (1.0 + jnp.exp(-v))


def softplus(v):
    return jnp.maximum(v, 0.0) + jnp.log1p(jnp.exp(-jnp.abs(v)))


def row_scale(h):
    return lax.rsqrt(jnp.mean(h * h, axis=-1, keepdims=True) + EPS)


def decays(L, flags):
    E = jnp.exp(L) * flags[:, 3:4]
    W = jnp.exp(L[Q - 1 : Q] - L) * flags[:, 4:5]
    return E, W


def wave_kernel(
    hid, halo, gain, w, conv, hp, flags, segrow, og, cot, outw, coef,
    normed, gate, pre, ext, delta, logs, mixed, carried, states, sums, dno, endlog, cot_all, w_out,
    sums_s, log_s, rsend, rrecv, proj_s, pre_s, gate_s, delta_s, logs_s, sloc, inner, dno_s, state, total, tail, ends, cot_s, w_o, w_s, send, recv, done,
):
    t = pl.program_id(0)
    c = lax.rem(t, CH)
    at = lax.rem(t, 8)
    micro = at // CH
    eh = spread_matrix()
    n = Net(send, recv)
    g, m, core = n.g, n.m, n.c

    def cot_z(a):
        return n.copy(("cot", a), cot_s.at[m], cot_s.at[m], n.at(dz=a))

    def cot_near():
        return n.copy("near", cot_s.at[m], cot_s.at[m], n.at(dc=1))

    def cot_on(a):
        theirs = cot_s.at[2 * lax.rem(n.z + 4 - a, 4) + core]
        return n.copy(("on", a), theirs, theirs, n.at(dc=1))

    def out_x(d):
        return n.copy(("ox", d), w_o.at[g], w_o.at[g], n.at(dx=d))

    def out_y(d, half):
        part = w_o.at[n.behind(d), pl.ds(32 * half, 32)]
        return n.copy(("oy", d, half), part, part, n.at(dy=3 if half else 1))

    def out_swap():
        return n.copy("swap", w_o.at[pl.ds(4 * (1 - core), 4)], w_s.at[:, core], n.at(dc=1))

    def end_x(i, d):
        return n.copy(("ex", i, d), ends.at[g, i], ends.at[g, i], n.at(dx=d))

    def part_y(i):
        return n.copy(("r", i), rsend.at[i], rrecv.at[i], n.pair())

    def log_x(i, d):
        return n.copy(("lx", i, d), log_s.at[g, i], log_s.at[g, i], n.at(dx=d))

    def log_y(i, d):
        return n.copy(("ly", i, d), log_s.at[g, i], log_s.at[g, i], n.across(d))

    def sum_copy(i, a, b):
        mine = sums_s.at[m, pl.ds(CH * i, CH)]
        return n.copy(("sum", i, a, b), mine, mine, n.at(dz=a, dc=b))

    ALLX = (0,) + XS
    out_copies = [pltpu.make_async_copy(cot_s, cot_all, done.at[0]), pltpu.make_async_copy(w_s, w_out, done.at[1])]

    @pl.when(t == 0)
    def _():
        n.meet([n.at(dz=a, dc=b) for a, b in OTHERS] + [n.at(dx=d) for d in XS] + [n.at(dy=1), n.at(dy=3)] + [n.across(d) for d in ALLX])
        cot_s[m] = cot[...]
        w_o[g] = outw[...]
        for d in XS:
            out_x(d).start()
        for half in (0, 1):
            out_y(0, half).start()
        for a in (1, 3, 2):
            cot_z(a).start()
        cot_near().start()

    @pl.when((t < 8) & (c == 0))
    def _():
        h = hid[...].reshape(TOK, 2048).astype(F32)
        nb = (h * row_scale(h) * gain[...]).astype(BF16)
        normed[...] = nb.reshape(8, 1, 64, 2048)
        e = halo[0].astype(F32)
        eb = (e * row_scale(e) * gain[...]).astype(BF16)
        proj_s[...] = bdot(jnp.concatenate([eb, nb], 0), w[...])
        tail[0:8] = proj_s[8:16, 512:1280].astype(BF16).astype(F32)
        state[...] = jnp.zeros_like(state)
        total[...] = jnp.zeros_like(total)

    @pl.when(t < 8)
    def _():
        rows = pl.ds(pl.multiple_of(16 + Q * c, 16), Q)
        f = flags[...]
        gt = proj_s[rows, 0:512]
        gate[...] = gt
        gate_s[at] = gt
        xbc = proj_s[rows, 512:1280].astype(BF16).astype(F32)
        tail[8:] = xbc
        acc = conv[4:5] + conv[3:4] * xbc
        for k in range(3):
            acc = acc + conv[k : k + 1] * tail[5 + k : 5 + k + Q] * f[:, k : k + 1]
        pre[...] = acc
        pre_s[at] = acc
        ext[0] = tail[...].astype(BF16)
        d = softplus(proj_s[rows, 1280:1408] + hp[0:1])
        delta[...] = d
        delta_s[at] = d
        L = right_parts(lower_matrix(), d * hp[1:2], 3)
        logs[...] = L
        logs_s[at] = L
        E, W = decays(L, f)
        x = acc[:, :512]
        X = x * sigmoid(x)
        b = acc[:, 512:640]
        B = (b * sigmoid(b)).astype(BF16)
        S = right_parts(B, heads_of(W * d, eh) * X, 2, TN)
        sloc[at] = S
        both = heads_of(jnp.concatenate([E[Q - 8 :], L[Q - 8 :]], 0), eh)
        new = both[7:8] * state[...] + S
        state[...] = new
        tail[0:8] = tail[Q : Q + 8]
        lt = total[...] + L[Q - 1 : Q]
        total[...] = lt

        @pl.when(c == CH - 1)
        def _():
            ends[g, micro] = new.astype(BF16)
            p = parts(jnp.broadcast_to(heads_of(jnp.broadcast_to(lt, (8, 128)), eh)[0:1], (16, 512)), 3)
            r = iota((16, 512), 0)
            log_s[g, micro] = jnp.where(r == 0, p[0], jnp.where(r == 1, p[1], jnp.where(r == 2, p[2], jnp.zeros_like(p[0]))))

    for i, when in ((0, CH - 1), (1, 2 * CH - 1)):

        @pl.when(t == when)
        def _(i=i):
            for d in XS:
                log_x(i, d).start()
            for d in ALLX:
                log_y(i, d).start()
            for d in XS:
                end_x(i, d).start()

    @pl.when(t == 4)
    def _():
        for d in XS:
            out_x(d).wait_recv()
            for half in (0, 1):
                out_y(d, half).start()

    for i, when in ((0, 6), (1, 11)):

        @pl.when(t == when)
        def _(i=i):
            for d in XS:
                log_x(i, d).wait_recv()
            for d in ALLX:
                log_y(i, d).wait_recv()
            for d in XS:
                end_x(i, d).wait_recv()
            rsend[i] = entering(ends, log_s, coef, 1, 0, i, n.y).astype(BF16)
            part_y(i).start()

    @pl.when(t == 8)
    def _():
        for d in ALLX:
            for half in (0, 1):
                out_y(d, half).wait_recv()
        out_swap().start()
        for k in range(4):
            w_s[k, core] = w_o[4 * core + k]
        for a in (1, 3, 2):
            cot_z(a).wait_recv()
            cot_on(a).start()

    @pl.when((t >= 8) & (t < 16))
    def _():
        L = logs_s[at]
        a = pre_s[at]
        X, B, C = activations(a)
        U = (heads_of(delta_s[at], eh) * X).astype(BF16)
        psi = bdot(C, B, NT)
        keep = same_mask(flags[...], segrow[0])
        LT = L.T
        for j in range(4):
            u = pair_halves(U[:, 128 * j : 128 * j + 128])
            y = jnp.zeros((Q, 128), F32)
            for e in range(2):
                h = 2 * j + e
                K = jnp.where(keep, jnp.exp(L[:, h : h + 1] - LT[h : h + 1]), 0.0)
                y = y + bdot((psi * K).astype(BF16), u[e])
            inner[at, :, 128 * j : 128 * j + 128] = y

    @pl.when(t == 16)
    def _():
        out_swap().wait_recv()
        cot_near().wait_recv()
        for a in (1, 3, 2):
            cot_on(a).wait_recv()
        for cp in out_copies:
            cp.start()
        for i in (0, 1):
            part_y(i).wait_recv()
        endlog[...] = log_s[...]

    @pl.when((t >= 16) & (c == 0))
    def _():
        dno_s[...] = bdot(cot_s[:, micro].reshape(TOK, 2048), w_s[...].reshape(512, 2048), NT)
        state[...] = entering(ends, log_s, coef, 0, 0, micro, n.y) + rrecv[micro].astype(F32)

    @pl.when(t >= 16)
    def _():
        f = flags[...]
        E, _ = decays(logs_s[at], f)
        a = pre_s[at]
        X, _, C = activations(a)
        more = heads_of(jnp.concatenate([E, jnp.broadcast_to(hp[2:3], (8, 128))], 0), eh)
        Ex, skip = more[:Q], more[Q : Q + 1]
        S = state[...]
        states[0, 0] = S
        Yc = Ex * bdot(C, S.astype(BF16))
        carried[...] = Yc
        mix = inner[at] + Yc + skip * X
        mixed[...] = mix
        after = Ex[Q - 1 : Q] * S + sloc[at]
        state[...] = after
        states[0, 1] = after
        gt = gate_s[at]
        gated = mix * (gt * sigmoid(gt))
        dn = dno_s[pl.ds(pl.multiple_of(Q * c, Q), Q)]
        dno[...] = dn
        ones = jnp.ones((8, 512), BF16)
        sums_s[m, at, 0:8] = right_parts(ones, gated * gated, 2, NT)
        sums_s[m, at, 8:16] = right_parts(ones, dn * og[...] * gated, 2, NT)

    for i, when in ((0, 19), (1, 23)):

        @pl.when(t == when)
        def _(i=i):
            for a, b in OTHERS:
                sum_copy(i, a, b).start()

    @pl.when(t == 23)
    def _():
        for cp in out_copies:
            cp.wait()
        for i in (0, 1):
            for a, b in OTHERS:
                sum_copy(i, a, b).wait_recv()
        sums[...] = sums_s[...]
        for a in (1, 3, 2):
            cot_z(a).wait_send()
            cot_on(a).wait_send()
        cot_near().wait_send()
        out_swap().wait_send()
        for d in XS:
            out_x(d).wait_send()
        for d in ALLX:
            for half in (0, 1):
                out_y(d, half).wait_send()
        for i in (0, 1):
            part_y(i).wait_send()
            for d in XS:
                end_x(i, d).wait_send()
                log_x(i, d).wait_send()
            for d in ALLX:
                log_y(i, d).wait_send()
            for a, b in OTHERS:
                sum_copy(i, a, b).wait_send()


def tile(width, at=lambda t: t):
    return pl.BlockSpec((Q, width), lambda t: (at(t), 0))


def whole(*shape):
    return pl.BlockSpec(shape, lambda t: (0,) * len(shape))


def plain(kernel, name, outs, ins, spaces_in, spaces_out, scratch=(), flops=1 << 30):
    return pl.pallas_call(
        kernel,
        name=name,
        grid=(MICRO * CH,),
        out_shape=outs,
        in_specs=spaces_in,
        out_specs=spaces_out,
        scratch_shapes=list(scratch),
        compiler_params=pltpu.CompilerParams(vmem_limit_bytes=56 << 20),
        cost_estimate=pl.CostEstimate(flops=flops, bytes_accessed=16 << 20, transcendentals=0),
    )(*ins)


T = MICRO * TOK
HID = pl.BlockSpec((2, 1, 64, 2048), lambda t: (t % CH, t // CH, 0, 0))


def agblock(width, at=lambda t: t):
    return pl.BlockSpec((2, 1, 64, width), lambda t: (at(t) % CH, at(t) // CH, 0, 0))


def wave(hid, halo, gain, w, conv, hp, flags, segrow, og, cot, outw, coef):
    outs = [
        sds((8, 2, 64, 2048), BF16), sds((T, 512), F32), sds((T, 768), F32), sds((8, Q + 8, 768), BF16), sds((T, 128), F32), sds((T, 128), F32),
        sds((T, 512), F32), sds((T, 512), F32), sds((8, 2, 128, 512), F32), sds((8, 8, 16, 128), F32), sds((T, 512), F32), sds((8, 2, 16, 512), BF16), sds((8, 2, 64, 2048), BF16), sds((4, 2, 64, 2048), BF16),
    ]
    first = lambda t: jnp.minimum(t, 7)
    last = lambda t: jnp.maximum(t - 16, 0)
    ring = lambda t: t % 8
    micro = pl.BlockSpec((8, 1, 64, 2048), lambda t: (0, first(t) // CH, 0, 0))
    V = lambda *shape: pltpu.VMEM(shape, F32)
    return pl.pallas_call(
        wave_kernel,
        name="wave",
        grid=(24,),
        out_shape=outs,
        in_specs=[
            micro, pl.BlockSpec((1, 16, 2048), lambda t: (first(t) // CH, 0, 0)), whole(1, 2048), whole(2048, 1408), whole(8, 768), whole(8, 128), tile(128, ring), blk(1, 128, ring), whole(1, 512),
            whole(2, 64, 2048), whole(64, 2048), SMEM,
        ],
        out_specs=[
            micro, tile(512, first), tile(768, first), blk(Q + 8, 768, first), tile(128, first), tile(128, first),
            tile(512, last), tile(512, last), pl.BlockSpec((1, 2, 128, 512), lambda t: (last(t), 0, 0, 0)), whole(8, 8, 16, 128), tile(512, last), whole(8, 2, 16, 512), ANY, ANY,
        ],
        scratch_shapes=[
            V(8, 8, 16, 128), pltpu.VMEM((8, 2, 16, 512), BF16), pltpu.VMEM((2, 128, 512), BF16), pltpu.VMEM((2, 128, 512), BF16), V(TOK + 16, 1408), V(8, Q, 768), V(8, Q, 512), V(8, Q, 128), V(8, Q, 128), V(8, 128, 512), V(8, Q, 512), V(TOK, 512), V(128, 512), V(1, 128), V(Q + 8, 768),
            pltpu.VMEM((8, 2, 128, 512), BF16), pltpu.VMEM((8, 2, 64, 2048), BF16), pltpu.VMEM((8, 64, 2048), BF16), pltpu.VMEM((4, 2, 64, 2048), BF16),
            pltpu.SemaphoreType.DMA((64,)), pltpu.SemaphoreType.DMA((64,)), pltpu.SemaphoreType.DMA((2,)),
        ],
        compiler_params=pltpu.CompilerParams(collective_id=1, has_side_effects=True, vmem_limit_bytes=60 << 20),
        cost_estimate=pl.CostEstimate(flops=8 << 30, bytes_accessed=32 << 20, transcendentals=0),
    )(hid, halo, gain, w, conv, hp, flags, segrow, og, cot, outw, coef)


def entering(everyone, logs, coef, target, direction, micro, y):
    total = jnp.zeros((128, 512), F32)
    rows = [logs[q, micro].astype(F32) for q in range(8)]
    lt = [v[0:1] + v[1:2] + v[2:3] for v in rows]
    base = 160 * target + 80 * direction
    for k in range(4):
        q = 2 * k + y
        log = sum(coef[base + 8 * q + r] * lt[r] for r in range(8))
        total = total + jnp.exp(log) * coef[base + 64 + 8 * micro + q] * everyone[q, micro].astype(F32)
    return total


def same_mask(flags, segrow):
    return (flags[:, 5:6] == segrow) & (iota((Q, Q), 0) >= iota((Q, Q), 1))


def activations(pre):
    a = pre * sigmoid(pre)
    return a[:, :512], a[:, 512:640].astype(BF16), a[:, 640:768].astype(BF16)


def pair_halves(v):
    low_half = iota(v.shape, 1) < 64
    zero = jnp.zeros_like(v)
    return jnp.where(low_half, v, zero), jnp.where(low_half, zero, v)


def blk(a, b, at=lambda t: t):
    return pl.BlockSpec((1, a, b), lambda t: (at(t), 0, 0))


SMEM = pl.BlockSpec(memory_space=pltpu.SMEM)


def column(row):
    return jnp.concatenate([jnp.broadcast_to(row, (128, 128)).T] * 4, 1)


def back_at(t):
    return (t // CH) * CH + (CH - 1 - t % CH)


def pick_matrix(rows, start, count, shift, dtype=BF16):
    r, l = iota((rows, 128), 0), iota((rows, 128), 1)
    return ((r - start == l - shift) & (l >= shift) & (l < shift + count)).astype(dtype)


class Reduce:
    def __init__(self, n, key, a, b, a1, a2, pa, b1, b2, pb, b3):
        self.n, self.key, self.a, self.b = n, key, a, b
        self.a1, self.a2, self.pa, self.b1, self.b2, self.pb, self.b3 = a1, a2, pa, b1, b2, pb, b3
        self.half = a.shape[1] // 2

    def group(self, d, f):
        n = self.n
        return 2 * lax.rem(n.x + d, 4) + lax.rem(n.y + f, 2)

    def first_a(self, d, f):
        return self.n.copy((self.key, "a1", d, f), self.a.at[self.group(d, f)], self.a1.at[d - 1, f], self.n.at(dx=d))

    def first_b(self, d, e):
        n = self.n
        rep = lax.rem(n.ring + e, 4) // 2
        rows = pl.ds(pl.multiple_of(self.half * rep, self.half), self.half)
        return n.copy((self.key, "b1", d, e), self.b.at[self.group(d, e % 2), rows], self.b1.at[e - 1, lax.rem(n.x + d, 4)], n.at(dy=e))

    def send_a(self, d, f):
        if d:
            self.first_a(d, f).start()

    def send_b(self, d, f):
        for e in (1, 3) if f else (2,):
            self.first_b(d, e).start()

    def second_a(self, e):
        return self.n.copy((self.key, "a2", e), self.pa.at[e % 2], self.a2.at[e - 1], self.n.at(dy=e))

    def second_b(self, d):
        return self.n.copy((self.key, "b2", d), self.pb.at[lax.rem(self.n.x + d, 4)], self.b2.at[d - 1], self.n.at(dx=d))

    def third_b(self):
        return self.n.copy((self.key, "b3"), self.b3.at[self.n.rep], self.b3.at[self.n.rep], self.n.at(dy=2))

    def middle_a(self, f):
        for d in XS:
            self.first_a(d, f).wait_recv()
        self.pa[f] = add4(self.a[self.group(0, f)], self.a1[:, f]).astype(BF16)
        for e in (1, 3) if f else (2,):
            self.second_a(e).start()

    def middle_b(self):
        n = self.n
        rows = pl.ds(pl.multiple_of(self.half * n.rep, self.half), self.half)
        for d in (2, 1, 3, 0):
            for e in XS:
                self.first_b(d, e).wait_recv()
            k = lax.rem(n.x + d, 4)
            self.pb[k] = add4(self.b[2 * k + n.y, rows], self.b1[:, k]).astype(BF16)
            if d:
                self.second_b(d).start()

    def last_b(self):
        for d in XS:
            self.second_b(d).wait_recv()
        self.b3[self.n.rep] = add4(self.pb[self.n.x], self.b2).astype(self.b3.dtype)
        self.third_b().start()

    def last_a(self):
        for e in XS:
            self.second_a(e).wait_recv()
        return add4(self.pa[0], self.a2)

    def finish(self):
        for d in XS:
            for f in (0, 1):
                self.first_a(d, f).wait_send()
            self.second_b(d).wait_send()
        for e in XS:
            for d in range(4):
                self.first_b(d, e).wait_send()
            self.second_a(e).wait_send()
        self.third_b().wait_send()


def fetcher(sems):
    loads = {}

    def fetch(key, src, dst):
        loads[key] = pltpu.make_async_copy(src, dst, sems.at[len(loads)])
        loads[key].start()

    return loads, fetch


C1 = 256


def back_wave_kernel(
    mixed_h, carried_h, states_h, gate_h, dno_h, sums, pre_h, delta_h, logs_h, flags_h, segrow, og, hp, wout_h, cot, normed, endlog, coef,
    dgate, dpre_h, dbc, ddt, small_o, small_b, total, g_out, gate_rows,
    mixed, carried, states, gate, dno, pre, delta, logs, flags, wout, nout, dmix, tloc, dbi, starts, rsend, rrecv, tiles, part, near, far, gsw, oa, ob, oa1, oa2, opa, ob1, ob2, opb, ob3, oin,
    wa, wb, wa1, wa2, wpa, wb1, wb2, wpb, wb3, state, send, recv, load, tile_sem,
):
    eh = spread_matrix()
    n = Net(send, recv)
    g, m, core, z = n.g, n.m, n.c, n.z
    O = Reduce(n, "o", oa, ob, oa1, oa2, opa, ob1, ob2, opb, ob3)
    W = Reduce(n, "w", wa, wb, wa1, wa2, wpa, wb1, wb2, wpb, wb3)
    swap = n.copy("swap", gsw.at[:, 1 - core], oin, n.at(dc=1))
    loads, fetch = fetcher(load)
    for i in range(MICRO):
        some = pl.ds(CH * i, CH)
        for key, src, dst in (("mixed", mixed_h, mixed), ("gate", gate_h, gate), ("dno", dno_h, dno), ("pre", pre_h, pre), ("logs", logs_h, logs), ("flags", flags_h, flags)):
            fetch((key, i), src.at[some], dst.at[some])
    fetch("wout", wout_h, wout)
    for key, src, dst in (("delta", delta_h, delta), ("states", states_h, states), ("carried", carried_h, carried)):
        fetch(key, src, dst)

    def start_x(i, d):
        return n.copy(("sx", i, d), starts.at[g, i], starts.at[g, i], n.at(dx=d))

    def part_y(i):
        return n.copy(("r", i), rsend.at[i], rrecv.at[i], n.pair())

    def near_copy(d, i):
        return n.copy(("near", d, i), part.at[2 * lax.rem(z + d, 4) + 1 - core, i], near.at[d, i], n.at(dc=1))

    def far_copy(d, i):
        return n.copy(("far", d, i), near.at[d, i], far.at[d - 1, i], n.at(dz=d))

    n.meet([n.at(dz=a) for a in (1, 3, 2)] + [n.at(dc=1)] + [n.at(dx=d) for d in XS] + [n.at(dy=d) for d in XS])
    small_o[...] = jnp.zeros_like(small_o)
    small_b[...] = jnp.zeros_like(small_b)

    def outward(i, k):
        c = CH - 1 - k
        at = CH * i + c
        tot = sums[0, at]
        for q in range(1, 8):
            tot = tot + sums[q, at]
        r = column(lax.rsqrt(tot[0:1] / INNER + EPS))
        s2 = column(tot[8:9] / INNER)
        gt = gate[at]
        s = sigmoid(gt)
        sg = gt * s
        mix = mixed[at]
        gated = mix * sg
        dn = dno[at]
        n0 = gated * r
        rows = pl.ds(pl.multiple_of(Q * c, Q), Q)
        nout[i, rows] = (n0 * og[...]).astype(BF16)
        d_gated = r * (dn * og[...] - n0 * r * s2)
        dm = d_gated * sg
        dmix[at] = dm
        dgate[i, rows] = (d_gated * mix * (s * (1.0 + gt * (1.0 - s)))).astype(BF16)
        x = pre[at, :, :512]
        X = x * sigmoid(x)
        cc = pre[at, :, 640:768]
        C = (cc * sigmoid(cc)).astype(BF16)
        small_o[0:1] += jnp.sum(dn * n0, 0, keepdims=True)
        small_o[1:2] += jnp.sum(X * dm, 0, keepdims=True)
        E, _ = decays(logs[at], flags[at])
        Ex = heads_of(E, eh)
        G = right_parts(C, Ex * dm, 2, TN)
        tloc[at] = G
        state[...] = Ex[Q - 1 : Q] * state[...] + G

    for i in range(MICRO):
        for key in ("mixed", "gate", "dno", "pre", "logs", "flags"):
            loads[key, i].wait()
        state[...] = jnp.zeros_like(state)
        lax.fori_loop(0, CH, lambda k, carry, i=i: (outward(i, k), carry)[1], 0)
        starts[g, i] = state[...].astype(BF16)
        for d in XS:
            start_x(i, d).start()
        if i == 0:
            loads["wout"].wait()
        part[:, i] = bdot(nout[i], wout[...]).astype(BF16).reshape(8, 64, 2048)
        for d in (1, 3, 2, 0):
            near_copy(d, i).start()

    def bring(k):
        src, j = (cot, k) if k < 8 else (normed, W.group(*ORDER[k - 8]))
        return pltpu.make_async_copy(src.at[:, :, :, pl.ds(pl.multiple_of(256 * j, 256), 256)], tiles.at[k % 2], tile_sem.at[k % 2])

    def states_on(i):
        for d in XS:
            start_x(i, d).wait_recv()
        rsend[i] = entering(starts, endlog, coef, 1, 1, i, n.y).astype(BF16)
        part_y(i).start()

    def tokens_on(i):
        for d in (1, 3, 2, 0):
            near_copy(d, i).wait_recv()
            there = 2 * lax.rem(z + d, 4) + core
            near[d, i] = (part[there, i].astype(F32) + near[d, i].astype(F32)).astype(BF16)
            if d:
                far_copy(d, i).start()

    bring(0).start()
    for k in range(16):
        bring(k).wait()
        if k < 15:
            bring(k + 1).start()
        t = tiles.at[k % 2]
        if k < 8:
            v = sum(bdot(nout[i], t[:, i].reshape(TOK, 256), TN) for i in range(MICRO))
            gsw[:, :, :, 256 * k : 256 * k + 256] = v.astype(BF16).reshape(4, 2, 64, 256)
        else:
            d, f = ORDER[k - 8]
            q = W.group(d, f)
            v = sum(bdot(t[:, i].reshape(TOK, 256), dgate[i], TN) for i in range(MICRO))
            wa[q] = v[:, 0:C1].astype(BF16)
            wb[q] = v[:, C1:].astype(BF16)
            W.send_a(d, f)
            W.send_b(d, f)
        if k == 3:
            states_on(0)
            tokens_on(0)
        if k == 7:
            swap.start()
            for j in range(4):
                oa[4 * core + j] = gsw[j, core, :, 0:1024]
                ob[4 * core + j] = gsw[j, core, :, 1024:2048]
            states_on(1)
            tokens_on(1)

    swap.wait_recv()
    for j in range(4):
        oa[4 * (1 - core) + j] = oin[j, :, 0:1024]
        ob[4 * (1 - core) + j] = oin[j, :, 1024:2048]
    for d, f in ORDER:
        O.send_a(d, f)
        O.send_b(d, f)

    loads["delta"].wait()
    loads["states"].wait()
    loads["carried"].wait()

    def inside(at, carry):
        L = logs[at]
        f = flags[at]
        E, _ = decays(L, f)
        X, B, C = activations(pre[at])
        more = heads_of(jnp.concatenate([E, delta[at]], 0), eh)
        Ex, dx = more[:Q], more[Q:]
        Ub = (dx * X).astype(BF16)
        dm = dmix[at]
        dmb = dm.astype(BF16)
        psi = bdot(C, B, NT)
        keep = same_mask(f, segrow[at])
        LT = L.T
        dpsi = jnp.zeros((Q, Q), F32)
        for j in range(4):
            js = slice(128 * j, 128 * j + 128)
            u = pair_halves(Ub[:, js])
            y = pair_halves(dmb[:, js])
            acc = jnp.zeros((Q, 128), F32)
            for e in range(2):
                h = 2 * j + e
                K = jnp.where(keep, jnp.exp(L[:, h : h + 1] - LT[h : h + 1]), 0.0)
                acc = acc + bdot((psi * K).astype(BF16), y[e], TN)
                dpsi = dpsi + bdot(y[e], u[e], NT) * K
            dno[at, :, js] = acc
        dpb = dpsi.astype(BF16)
        dbi[at, 0:128] = bdot(C, dpb, TN)
        dbi[at, 128:256] = bdot(B, dpb, TT) + bdot(states[at, 0].astype(BF16), (Ex * dm).astype(BF16), NT)
        return carry

    lax.fori_loop(0, 8, inside, 0)
    for i in (0, 1):
        part_y(i).wait_recv()

    def inward(i, k):
        c = CH - 1 - k
        at = CH * i + c
        L = logs[at]
        d = delta[at]
        E, W_ = decays(L, flags[at])
        p = pre[at, :, 0:512]
        s = sigmoid(p)
        X = p * s
        bb = pre[at, :, 512:640]
        B = (bb * sigmoid(bb)).astype(BF16)
        more = heads_of(jnp.concatenate([E[Q - 8 :], W_, d, jnp.broadcast_to(hp[2:3], (8, 128))], 0), eh)
        Elast, Wx, dx, skip = more[7:8], more[8 : 8 + Q], more[8 + Q : 8 + 2 * Q], more[8 + 2 * Q : 9 + 2 * Q]
        U = dx * X
        dm = dmix[at]
        Yc = carried[at]
        Yi = mixed[at] - Yc - skip * X
        G = state[...]
        Gb = G.astype(BF16)
        dUi = dno[at]
        dUc = Wx * bdot(B, Gb)
        dU = dUi + dUc
        lanes = pl.ds(pl.multiple_of(Q * at, Q), Q)
        dbc[0:128, lanes] = (dbi[at, 0:128] + bdot(Gb, (Wx * U).astype(BF16), NT)).astype(BF16)
        dbc[128:256, lanes] = dbi[at, 128:256].astype(BF16)
        dL = sums_of(dm.astype(BF16).astype(F32) * Yi + dm * Yc - U.astype(BF16).astype(F32) * dUi - U * dUc, eh)
        end = sums_of(jnp.broadcast_to(jnp.sum(G * states[at, 1], 0, keepdims=True), (8, 512)), eh)[0:1]
        upper = (iota((Q, Q), 0) <= iota((Q, Q), 1)).astype(BF16)
        dstep = right_parts(upper, dL, 3) + end
        rate = hp[1:2]
        dr = (sums_of(dU * X, eh) + dstep * rate) * (1.0 - jnp.exp(-d))
        ddt[at] = dr.astype(BF16)
        small_b[0:1] += jnp.sum(dr, 0, keepdims=True)
        small_b[1:2] += jnp.sum(dstep * d * rate, 0, keepdims=True)
        gate[at] = (dx * dU + skip * dm) * (s * (1.0 + p * (1.0 - s)))
        state[...] = Elast * G + tloc[at]

    store = pltpu.make_async_copy(gate, dpre_h, load.at[0])
    for i in range(MICRO):
        state[...] = entering(starts, endlog, coef, 0, 1, i, n.y) + rrecv[i].astype(F32)
        lax.fori_loop(0, CH, lambda k, carry, i=i: (inward(i, k), carry)[1], 0)
    store.start()

    W.middle_b()
    W.middle_a(1)
    W.middle_a(0)
    O.middle_b()
    O.middle_a(1)
    O.middle_a(0)
    for i in range(MICRO):
        for d in XS:
            far_copy(d, i).wait_recv()
        total[i] = near[0, i].astype(F32) + far[0, i].astype(F32) + far[1, i].astype(F32) + far[2, i].astype(F32)
    W.last_b()
    O.last_b()
    gate_rows[:, 0:C1] = W.last_a().astype(BF16)
    g_out[:, 0:1024] = O.last_a()
    W.third_b().wait_recv()
    O.third_b().wait_recv()
    for h in range(2):
        g_out[32 * h : 32 * h + 32, 1024:2048] = ob3[h]
        gate_rows[128 * h : 128 * h + 128, C1:] = wb3[h]
    O.finish()
    W.finish()
    store.wait()
    swap.wait_send()
    for i in range(MICRO):
        part_y(i).wait_send()
        for d in XS:
            start_x(i, d).wait_send()
            far_copy(d, i).wait_send()
        for d in range(4):
            near_copy(d, i).wait_send()


def back_wave(mixed, carried, states, gate, dno, sums, pre, delta, logs, flags, segrow, og, hp, wout, cot, normed, endlog, coef):
    outs = [
        sds((2, TOK, 512), BF16), sds((8, Q, 512), F32), sds((256, T), BF16), sds((8, Q, 128), BF16), sds((8, 512), F32), sds((8, 128), F32), sds((2, 64, 2048), F32), sds((64, 2048), F32),
        sds((256, 512), BF16),
    ]
    V = lambda *s: pltpu.VMEM(s, BF16)
    R = lambda *s: pltpu.VMEM(s, F32)
    chunked = lambda v: v.reshape(8, Q, v.shape[-1])
    return pl.pallas_call(
        back_wave_kernel,
        name="back_wave",
        out_shape=outs,
        in_specs=[ANY] * 5 + [VM] + [ANY] * 4 + [VM] * 3 + [ANY] * 3 + [VM, SMEM],
        out_specs=[VM, ANY] + [VM] * 7,
        scratch_shapes=[
            R(8, Q, 512), R(8, Q, 512), R(8, 2, 128, 512), R(8, Q, 512), R(8, Q, 512), R(8, Q, 768), R(8, Q, 128), R(8, Q, 128), R(8, Q, 128), V(512, 2048),
            V(2, TOK, 512), R(8, Q, 512), R(8, 128, 512), R(8, 256, 128), V(8, 2, 128, 512), V(2, 128, 512), V(2, 128, 512), V(2, 8, 2, 64, 256), V(8, 2, 64, 2048),
            V(4, 2, 64, 2048), V(3, 2, 64, 2048), V(4, 2, 64, 2048),
            V(8, 64, 1024), V(8, 64, 1024), V(3, 2, 64, 1024), V(3, 64, 1024), V(2, 64, 1024), V(3, 4, 32, 1024), V(3, 32, 1024), V(4, 32, 1024), R(2, 32, 1024), V(4, 64, 2048),
            V(8, 256, C1), V(8, 256, C1), V(3, 2, 256, C1), V(3, 256, C1), V(2, 256, C1), V(3, 4, 128, C1), V(3, 128, C1), V(4, 128, C1), V(2, 128, C1), R(128, 512),
            pltpu.SemaphoreType.DMA((96,)), pltpu.SemaphoreType.DMA((96,)), pltpu.SemaphoreType.DMA((16,)), pltpu.SemaphoreType.DMA((2,)),
        ],
        compiler_params=pltpu.CompilerParams(collective_id=4, has_side_effects=True, vmem_limit_bytes=62 << 20),
        cost_estimate=pl.CostEstimate(flops=8 << 30, bytes_accessed=32 << 20, transcendentals=0),
    )(chunked(mixed), chunked(carried), states, chunked(gate), chunked(dno), sums, chunked(pre), chunked(delta), chunked(logs), chunked(flags), segrow, og, hp, wout, cot, normed, endlog, coef)


CB = 256
CA = 640 - CB


def tail_kernel(
    dbc, edge_x, gate_rows, dpre, pre, ext, flags, fnext, conv, ddt, dgate, w, hid, normed, small_o, small_b,
    gi, total, small_all,
    bc_s, ex_s, eb_src, eb_s, dps, pre_s, ext_s, fl_s, fn_s, ddt_s, dg_s, w_s, hid_s, nm_s, wt, e_s, dproj, part, near, far, conv_acc, gnorm,
    s0, s1, s2, sx, ga, gb, ga1, ga2, gpa, gb1, gb2, gpb, gb3, final, send, recv, load,
):
    n = Net(send, recv)
    x, y, z, c, m = n.x, n.y, n.z, n.c, n.m
    loads = {}

    def fetch(key, src, dst):
        loads[key] = pltpu.make_async_copy(src, dst, load.at[len(loads)])
        loads[key].start()

    fetch("pre", pre.at[:, :, pl.ds(512, 256)], pre_s)
    fetch("w", w, w_s)
    fetch("dpre", dpre, dps.at[:, pl.ds(0, TOK), pl.ds(0, 512)])
    fetch("ext", ext, ext_s)
    fetch("flags", flags, fl_s)
    fetch("fnext", fnext, fn_s)
    fetch("ddt", ddt, ddt_s)
    fetch("normed", normed, nm_s)
    fetch("dgate", dgate, dg_s)
    fetch("hid", hid, hid_s)
    n.meet([n.at(dz=a, dc=b) for a, b in OTHERS] + [n.at(dx=d) for d in XS] + [n.at(dy=d) for d in XS] + [n.group(1), n.group(7)])

    def bc_copy(a, b):
        return n.copy(("bc", a, b), dbc.at[n.member(a, b)], bc_s.at[m], n.at(dz=a, dc=b))

    edge1 = n.copy("edge1", edge_x, ex_s, n.group(7))
    edge2 = n.copy("edge2", eb_src, eb_s, n.group(7))

    def near_copy(d, i):
        return n.copy(("near", d, i), part.at[2 * lax.rem(z + d, 4) + 1 - c, i], near.at[d, i], n.at(dc=1))

    def far_copy(d, i):
        return n.copy(("far", d, i), near.at[d, i], far.at[d - 1, i], n.at(dz=d))

    def small_x(d):
        return n.copy(("sx", d), s0, s1.at[d - 1], n.at(dx=d))

    def small_y(d):
        return n.copy(("sy", d), sx, s2.at[d - 1], n.at(dy=d))

    def small_m(a, b):
        return n.copy(("sm", a, b), small_all.at[m], small_all.at[m], n.at(dz=a, dc=b))

    def rows_copy(a, b):
        return n.copy(("rows", a, b), final.at[n.member(a, b)], gi.at[m], n.at(dz=a, dc=b))

    W = Reduce(n, "w", ga, gb, ga1, ga2, gpa, gb1, gb2, gpb, gb3)

    for a, b in OTHERS:
        bc_copy(a, b).start()
    edge1.start()
    bc_s[m] = dbc[m]

    pick = pick_matrix(256, 32 * m, 32, 0)
    loads["w"].wait()
    wt[...] = (bdot(w_s[:, 1024:1280], pick) + bdot(w_s[:, 1280:1408], pick_matrix(128, 0, 8, 32))).astype(BF16)
    cw = jnp.concatenate([conv[:, 0:512], left_parts(conv[:, 512:768], pick, 3)], 1)
    for key in ("pre", "dpre"):
        loads[key].wait()
    for a, b in OTHERS:
        bc_copy(a, b).wait_recv()
    eye = pick_matrix(32, 0, 32, 0)

    def bc_chunk(i, k):
        t = CH * i + k
        tot = bc_s[0, :, Q * t : Q * t + Q].astype(F32)
        for q in range(1, 8):
            tot = tot + bc_s[q, :, Q * t : Q * t + Q].astype(F32)
        d = left_parts(tot, eye, 2, TN)
        p = left_parts(pre_s[t], pick, 2)
        s = sigmoid(p)
        dps[i, Q * k : Q * k + Q, 512:640] = d * (s * (1.0 + p * (1.0 - s)))

    for i in range(MICRO):
        bc_chunk(i, 0)
        eb_src[i] = dps[i, 0:8, 512:640]
    edge2.start()
    for i in range(MICRO):
        for k in range(1, CH):
            bc_chunk(i, k)
    for key in ("ext", "flags", "fnext", "ddt"):
        loads[key].wait()
    conv_acc[...] = jnp.zeros_like(conv_acc)
    pick_dt = pick_matrix(128, 0, 8, 32)

    def conv_chunk(i, k):
        t = CH * i + k
        e_s[:, 0:512] = ext_s[t, :, 0:512].astype(F32)
        e_s[:, 512:640] = bdot(ext_s[t, :, 512:768], pick)
        f, fn = fl_s[t], fn_s[t]
        dp = dps[i, Q * k : Q * k + Q]
        dx = cw[3:4] * dp
        conv_acc[3:4] += jnp.sum(dp * e_s[8 : 8 + Q], 0, keepdims=True)
        conv_acc[4:5] += jnp.sum(dp, 0, keepdims=True)
        for j in range(3):
            conv_acc[j : j + 1] += jnp.sum(dp * e_s[5 + j : 5 + j + Q] * f[:, j : j + 1], 0, keepdims=True)
            dx = dx + cw[j : j + 1] * dps[i, Q * k + 3 - j : Q * k + 3 - j + Q] * fn[:, j : j + 1]
        rows = slice(Q * k, Q * k + Q)
        dproj[i, rows, 0:512] = dx[:, 0:512].astype(BF16)
        dproj[i, rows, 512:640] = (dx[:, 512:640] + bdot(ddt_s[t], pick_dt)).astype(BF16)

    for i in range(MICRO):
        for k in range(CH - 1):
            conv_chunk(i, k)
    edge1.wait_recv()
    edge2.wait_recv()
    for i in range(MICRO):
        dps[i, TOK : TOK + 8, 0:512] = ex_s[i]
        dps[i, TOK : TOK + 8, 512:640] = eb_s[i]
        conv_chunk(i, CH - 1)

    loads["normed"].wait()
    for d, f in ORDER:
        q = W.group(d, f)
        at = pl.ds(pl.multiple_of(256 * q, 256), 256)
        v = sum(bdot(nm_s[:, i, :, at].reshape(TOK, 256), dproj[i], TN) for i in range(MICRO)).astype(BF16)
        gb[q] = v[:, 0:CB]
        ga[q] = v[:, CB:]
        W.send_a(d, f)
        W.send_b(d, f)

    loads["hid"].wait()
    loads["dgate"].wait()
    for i in range(MICRO):
        h = hid_s[:, i].reshape(TOK, 2048).astype(F32)
        scale = row_scale(h)
        first, main, rest = dg_s[i], dproj[i, :, 0:512], dproj[i, :, 512:640]

        def tile_of(j, carry, i=i, scale=scale, first=first, main=main, rest=rest):
            at = pl.ds(pl.multiple_of(256 * j, 256), 256)
            d = bdot(first, w_s[at, 0:512], NT) + bdot(main, w_s[at, 512:1024], NT) + bdot(rest, wt[at], NT)
            part[:, i, :, at] = d.astype(BF16).reshape(8, 64, 256)
            hv = hid_s[:, i, :, at].reshape(TOK, 256).astype(F32)
            s = jnp.sum(d * (hv * scale), 0, keepdims=True)
            gnorm[0:1, at] = s if i == 0 else gnorm[0:1, at] + s
            return carry

        lax.fori_loop(0, 8, tile_of, 0)
        for d in (1, 3, 2, 0):
            near_copy(d, i).start()
    for r in range(16):
        s0[r : r + 1] = gnorm[0:1, 128 * r : 128 * r + 128]
    for k in range(5):
        for r in range(5):
            s0[16 + 5 * k + r : 17 + 5 * k + r] = conv_acc[k : k + 1, 128 * r : 128 * r + 128]
    for r in range(4):
        s0[41 + r : 42 + r] = small_o[0:1, 128 * r : 128 * r + 128]
    s0[45:47] = small_b[0:2]
    s0[47:48] = sums_of(small_o[...], spread_matrix())[1:2]
    for d in XS:
        small_x(d).start()

    for i in range(MICRO):
        for d in (1, 3, 2, 0):
            near_copy(d, i).wait_recv()
            at = 2 * lax.rem(z + d, 4) + c
            near[d, i] = (part[at, i].astype(F32) + near[d, i].astype(F32)).astype(BF16)
            if d:
                far_copy(d, i).start()
    for d in XS:
        small_x(d).wait_recv()
    sx[...] = s0[...] + s1[0] + s1[1] + s1[2]
    for d in XS:
        small_y(d).start()
    W.middle_b()
    W.middle_a(1)
    W.middle_a(0)
    W.last_b()
    for d in XS:
        small_y(d).wait_recv()
    small_all[m] = sx[...] + s2[0] + s2[1] + s2[2]
    for a, b in OTHERS:
        small_m(a, b).start()
    for i in range(MICRO):
        for d in XS:
            far_copy(d, i).wait_recv()
        total[i] = near[0, i].astype(F32) + far[0, i].astype(F32) + far[1, i].astype(F32) + far[2, i].astype(F32)
    W.third_b().wait_recv()
    for h in range(2):
        final[4 * h : 4 * h + 4, :, 512 : 512 + CB] = gb3[h].reshape(4, 32, CB)
    final[:, :, 512 + CB :] = W.last_a().astype(BF16).reshape(8, 32, CA)
    final[:, :, 0:512] = gate_rows[...].reshape(8, 32, 512)
    for a, b in OTHERS:
        rows_copy(a, b).start()
    gi[m] = final[m]
    for a, b in OTHERS:
        rows_copy(a, b).wait_recv()
        small_m(a, b).wait_recv()
    W.finish()
    for a, b in OTHERS:
        bc_copy(a, b).wait_send()
        rows_copy(a, b).wait_send()
        small_m(a, b).wait_send()
    for d in XS:
        small_x(d).wait_send()
        small_y(d).wait_send()
        for i in range(MICRO):
            far_copy(d, i).wait_send()
    for d in range(4):
        for i in range(MICRO):
            near_copy(d, i).wait_send()
    edge1.wait_send()
    edge2.wait_send()


def tail_call(dbc, edge_x, gate_rows, dpre, pre, ext, flags, fnext, conv, ddt, dgate, w, hid, normed, small_o, small_b):
    outs = [sds((8, 32, 1152), BF16), sds((2, 64, 2048), F32), sds((8, 48, 128), F32)]
    V = lambda *s: pltpu.VMEM(s, BF16)
    R = lambda *s: pltpu.VMEM(s, F32)
    scratch = [
        V(8, 32, T), R(2, 8, 512), R(2, 8, 128), R(2, 8, 128), R(2, TOK + 8, 640), R(8, Q, 256), V(8, Q + 8, 768), R(8, Q, 128), R(8, Q, 128), V(8, Q, 128), V(2, TOK, 512), V(2048, 1408),
        V(8, 2, 64, 2048), V(8, 2, 64, 2048), V(2048, 128), R(Q + 8, 640), V(2, TOK, 640), V(8, 2, 64, 2048), V(4, 2, 64, 2048), V(3, 2, 64, 2048), R(8, 640), R(8, 2048),
        R(48, 128), R(3, 48, 128), R(3, 48, 128), R(48, 128),
        V(8, 256, CA), V(8, 256, CB), V(3, 2, 256, CA), V(3, 256, CA), V(2, 256, CA), V(3, 4, 128, CB), V(3, 128, CB), V(4, 128, CB), V(2, 128, CB),
        V(8, 32, 1152),
    ]
    return pl.pallas_call(
        tail_kernel,
        name="tail",
        out_shape=outs,
        in_specs=[VM, VM, VM] + [ANY] * 5 + [VM] + [ANY] * 5 + [VM] * 2,
        out_specs=[VM] * 3,
        scratch_shapes=[*scratch, pltpu.SemaphoreType.DMA((112,)), pltpu.SemaphoreType.DMA((112,)), pltpu.SemaphoreType.DMA((10,))],
        compiler_params=pltpu.CompilerParams(collective_id=5, has_side_effects=True, vmem_limit_bytes=62 << 20),
        cost_estimate=pl.CostEstimate(flops=8 << 30, bytes_accessed=32 << 20, transcendentals=0),
    )(dbc, edge_x, gate_rows, dpre, pre, ext, flags, fnext, conv, ddt, dgate, w, hid, normed, small_o, small_b)


def strips(v, zi, ci):
    r = v.shape[0]
    return lax.dynamic_slice(v.reshape(r, 2, 4, 4, 128), (0, ci, 0, zi, 0), (r, 1, 4, 1, 128)).reshape(r, 512)


def from_members(v):
    r = v.shape[1]
    return v.reshape(4, 2, r, 4, 128).transpose(2, 1, 3, 0, 4).reshape(r, 4096)


def from_heads(v):
    r = v.shape[1]
    return v.reshape(4, 2, r, 4, 2).transpose(2, 1, 3, 0, 4).reshape(r, 64)


def from_rows(v):
    return v.transpose(1, 0, 2).reshape(v.shape[1], 256)


def to_members(v):
    r = v.shape[0]
    return v.reshape(r, 2, 4, 4, 128).transpose(3, 1, 0, 2, 4).reshape(8, r, 512)


def xdot(a, b, dims=NN):
    return lax.dot_general(a, b, dims, preferred_element_type=F32)


def per_device(layer_in, cotangent, segment_ids, norm_gain, in_weight, conv_weight, conv_bias, dt_bias, a_log, skip_gain, out_gain, out_weight):
    xi, yi, zi, ci = (lax.axis_index(a) for a in SEQ)
    g = 2 * xi + yi
    m = 2 * zi + ci
    pack = jnp.concatenate([segment_ids[:, 0].astype(F32).reshape(-1), norm_gain, conv_weight.reshape(-1), conv_bias, dt_bias, a_log, skip_gain, out_gain, jnp.zeros((1024 - 567,), F32)]).reshape(8, 128)
    bc = jnp.broadcast_to(in_weight[None, :, 8192:8448], (8, 32, 256))
    dt_w = in_weight[:, 8448:].reshape(32, 2, 4, 4, 2).transpose(3, 1, 0, 2, 4).reshape(8, 32, 8)
    w_send = jnp.concatenate([to_members(in_weight[:, :4096]), to_members(in_weight[:, 4096:8192]), bc, dt_w, jnp.zeros((8, 32, 120), BF16)], 2)
    hid_all, w_in, small_all, halo = gather(layer_in[:, 0], w_send, pack)
    w_in = w_in.reshape(2048, 1408)
    full = small_all.reshape(64, 1024)
    seg_full = full[:, :128].reshape(64, 2, 64).transpose(1, 0, 2).reshape(2, 4096)
    full = full[:, 128:]
    norm_full = full[:, :32].reshape(1, 2048)
    conv_full = full[:, 32:372].reshape(64, 5, 68).transpose(1, 0, 2).reshape(5, CONV)
    conv = jnp.concatenate([strips(conv_full[:, :INNER], zi, ci), conv_full[:, INNER:]], 1)
    conv = jnp.pad(conv, ((0, 3), (0, 0)))
    hv = lax.dynamic_slice(full[:, 372:439].reshape(2, 4, 4, 2, 67), (ci, 0, zi, 0, 0), (1, 4, 1, 2, 67)).reshape(8, 67)
    og = hv[:, 3:].reshape(1, 512)
    hp = jnp.pad(jnp.stack([hv[:, 0], -jnp.exp(hv[:, 1]), hv[:, 2]]), ((0, 5), (0, 120)))

    padded = jnp.concatenate([jnp.full((MICRO, 8), -1.0, F32), seg_full, jnp.full((MICRO, 8), -2.0, F32)], 1)
    near = lax.dynamic_slice(padded, (0, g * TOK), (MICRO, TOK + 16))
    own = near[:, 8 : 8 + TOK]
    chunked = own.reshape(MICRO, CH, Q)
    before = jnp.concatenate([near[:, 7:8], chunked[:, :-1, -1]], 1)[:, :, None]
    lanes = [(near[:, 5 + k : 5 + k + TOK] == own).astype(F32).reshape(T) for k in range(3)]
    lanes += [(chunked == before).astype(F32).reshape(T), (chunked == chunked[:, :, -1:]).astype(F32).reshape(T), own.reshape(T)]
    flags = jnp.pad(jnp.stack(lanes, 1), ((0, 0), (0, 122)))
    fnext = jnp.pad(jnp.stack([(near[:, 11 - k : 11 - k + TOK] == own).astype(F32).reshape(T) for k in range(3)], 1), ((0, 0), (0, 125)))
    segrow = own.reshape(8, 1, Q)
    lasts = seg_full.reshape(MICRO, GROUPS, TOK)[:, :, -1]
    idx = jnp.arange(GROUPS)
    q, r = idx[:, None], idx[None, :]
    tables = []
    for target in (g, 2 * xi + 1 - yi):
        last_before = jnp.sum(jnp.where(idx == target - 1, lasts, 0.0), 1, keepdims=True)
        last_own = jnp.sum(jnp.where(idx == target, lasts, 0.0), 1, keepdims=True)
        ok_before = (idx < target) & (lasts == last_before)
        ok_after = (idx > target) & (jnp.roll(lasts, 1, axis=1) == last_own)
        tables += [(r > q) & (r < target), ok_before, (r > target) & (r < q), ok_after]
    coef = jnp.concatenate([v.astype(F32) for v in tables], 0).reshape(320)

    normed, gate, pre, ext, delta, logs, mixed, carried, states, sums, dno, ends_all, cot, w_out = wave(hid_all, halo, norm_full, w_in, conv, hp, flags, segrow, og, cotangent[:, 0], out_weight, coef)
    dgate, dpre, dbc, ddt, small_o, small_b, own_branch, g_out, gate_rows = back_wave(
        mixed, carried, states, gate, dno, sums, pre, delta, logs, flags, segrow, og, hp, w_out.reshape(512, 2048), cot, normed, ends_all, coef
    )
    split = lambda v: v.reshape(8, Q, v.shape[-1])
    dpre = dpre.reshape(MICRO, TOK, 512)
    gi, own_dn, small_sum = tail_call(
        dbc.reshape(8, 32, T), dpre[:, :8], gate_rows, dpre, split(pre), ext, split(flags), split(fnext), conv, ddt, dgate, w_in, hid_all, normed, small_o, small_b
    )
    gi = gi.astype(F32)
    hid_o = layer_in[:, 0].astype(F32)
    layer_out = (hid_o + own_branch).astype(BF16)
    ro = row_scale(hid_o)
    dg = own_dn * norm_full
    d_hid = ro * dg - hid_o * (ro * ro * ro) * jnp.mean(dg * hid_o, -1, keepdims=True)
    grad_in = (cotangent[:, 0].astype(F32) + d_hid).astype(BF16)
    g_in = jnp.concatenate([from_members(gi[:, :, :512]), from_members(gi[:, :, 512:1024]), from_rows(gi[:, :, 1024:1056]), from_heads(gi[:, :, 1056:1064])], 1)
    at = 8 * g + m
    g_norm = lax.dynamic_slice(small_sum[:, :16].sum(0).reshape(64, 32), (at, 0), (1, 32)).reshape(32)
    conv_s = small_sum[:, 16:41].reshape(8, 5, 640)
    conv_s = jnp.concatenate([from_members(conv_s[:, :, :512]), from_rows(conv_s[:, :, 512:544])], 1)
    conv_s = lax.dynamic_slice(conv_s, (0, 68 * at), (5, 68))
    og_s = from_members(small_sum[:, 41:45].reshape(8, 1, 512))[0]
    og_s = lax.dynamic_slice(og_s, (64 * at,), (64,))
    hd_s = from_heads(small_sum[:, 45:48, :8])
    hd_s = lax.dynamic_slice(hd_s, (0, at), (3, 1))
    return (layer_out[:, None], grad_in[:, None], g_norm, g_in, conv_s[:4], conv_s[4], hd_s[0], hd_s[1], hd_s[2], og_s, g_out)


def solution(mesh):
    fine = Mesh(mesh.devices.reshape(2, 4, 2, 4, 2), AXES)
    tok = P(None, "rep", SEQ, None)
    return jax.shard_map(
        per_device,
        mesh=fine,
        in_specs=(tok, tok, P(None, "rep", SEQ), P(SEQ), P(SEQ, None), P(None, SEQ), P(SEQ), P(SEQ), P(SEQ), P(SEQ), P(SEQ), P(SEQ, None)),
        out_specs=(tok, tok, P(SEQ), P(SEQ, None), P(None, SEQ), P(SEQ), P(SEQ), P(SEQ), P(SEQ), P(SEQ), P(SEQ, None)),
        check_vma=False,
    )
```

```python
import functools

import jax
import jax.numpy as jnp
from jax import lax
from jax.experimental import pallas as pl
from jax.experimental.pallas import tpu as pltpu
from jax.sharding import Mesh, PartitionSpec as P

EPS = 1e-05
INNER = 4096
MICRO = 2
CONV = 4352
F32 = jnp.float32
BF16 = jnp.bfloat16
AXES = ("rep", "x", "y", "z", "c")
SEQ = ("x", "y", "z", "c")
GROUPS = 8
TOK = 512
Q = 128
CH = TOK // Q

MESH = pl.DeviceIdType.MESH
ANY = pl.BlockSpec(memory_space=pl.ANY)
VM = pl.BlockSpec(memory_space=pltpu.VMEM)


class Net:
    def __init__(self, send, recv):
        self.send, self.recv, self.used, self.open = send, recv, 0, []
        self.keys = {}
        self.rep, self.x, self.y, self.z, self.c = (lax.axis_index(a) for a in AXES)
        self.ring = 2 * self.rep + self.y
        self.g = 2 * self.x + self.y
        self.m = 2 * self.z + self.c

    def at(self, dx=0, dy=0, dz=0, dc=0):
        ring = lax.rem(self.ring + dy, 4)
        return (ring // 2, lax.rem(self.x + dx, 4), lax.rem(ring, 2), lax.rem(self.z + dz, 4), lax.rem(self.c + dc, 2))

    def pair(self):
        return (self.rep, self.x, 1 - self.y, self.z, self.c)

    def across(self, dx):
        return (self.rep, lax.rem(self.x + dx, 4), 1 - self.y, self.z, self.c)

    def group(self, d):
        g = lax.rem(self.g + d, 8)
        return (self.rep, g // 2, lax.rem(g, 2), self.z, self.c)

    def member(self, dz, dc):
        return 2 * lax.rem(self.z + dz, 4) + lax.rem(self.c + dc, 2)

    def push(self, src, dst, where):
        i = self.used
        self.used += 1
        copy = pltpu.make_async_remote_copy(
            src_ref=src, dst_ref=dst, send_sem=self.send.at[i], recv_sem=self.recv.at[i], device_id=where, device_id_type=MESH
        )
        copy.start()
        self.open.append(copy)
        return copy

    def copy(self, key, src, dst, where):
        i = self.keys.setdefault(key, len(self.keys))
        return pltpu.make_async_remote_copy(
            src_ref=src, dst_ref=dst, send_sem=self.send.at[i], recv_sem=self.recv.at[i], device_id=where, device_id_type=MESH
        )

    def behind(self, d):
        return 2 * lax.rem(self.x + 4 - d, 4) + self.y

    def local(self, src, dst):
        i = self.used
        self.used += 1
        copy = pltpu.make_async_copy(src, dst, self.recv.at[i])
        copy.start()
        return copy

    def meet(self, peers):
        barrier = pltpu.get_barrier_semaphore()
        for peer in peers:
            pl.semaphore_signal(barrier, inc=1, device_id=peer, device_id_type=MESH)
        pl.semaphore_wait(barrier, len(peers))

    def finish(self):
        for copy in self.open:
            copy.wait_send()


OTHERS = [(dz, dc) for dz in (0, 1, 3, 2) for dc in (0, 1) if (dz, dc) != (0, 0)]
ZS = (0, 1, 3, 2)
XS = (1, 3, 2)
ORDER = [(d, f) for d in (2, 1, 3, 0) for f in (1, 0)]


def call(kernel, name, cid, outs, ins, spaces_in, spaces_out, sems, scratch=(), cost=1 << 20):
    return pl.pallas_call(
        kernel,
        name=name,
        out_shape=outs,
        in_specs=spaces_in,
        out_specs=spaces_out,
        scratch_shapes=[*scratch, pltpu.SemaphoreType.DMA((sems,)), pltpu.SemaphoreType.DMA((sems,))],
        compiler_params=pltpu.CompilerParams(collective_id=cid, has_side_effects=True, vmem_limit_bytes=60 << 20),
        cost_estimate=pl.CostEstimate(flops=0, bytes_accessed=cost, transcendentals=0),
    )(*ins)


def sds(shape, dtype):
    return jax.ShapeDtypeStruct(shape, dtype)


def add4(a, b):
    return a.astype(F32) + b[0].astype(F32) + b[1].astype(F32) + b[2].astype(F32)


NN = (((1,), (0,)), ((), ()))
NT = (((1,), (1,)), ((), ()))
TN = (((0,), (0,)), ((), ()))
TT = (((0,), (1,)), ((), ()))


def bdot(a, b, dims=NN):
    return lax.dot_general(a, b, dims, preferred_element_type=F32)


def parts(v, count):
    out = []
    for _ in range(count):
        p = v.astype(BF16)
        out.append(p)
        v = v - p.astype(F32)
    return out


def left_parts(v, w, count, dims=NN):
    return sum(bdot(p, w, dims) for p in parts(v, count))


def right_parts(w, v, count, dims=NN):
    return sum(bdot(w, p, dims) for p in parts(v, count))


def iota(shape, dim):
    return lax.broadcasted_iota(jnp.int32, shape, dim)


def spread_matrix():
    return (iota((128, 512), 0) == iota((128, 512), 1) // 64).astype(BF16)


def heads_of(v, eh):
    return left_parts(v, eh, 2)


def sums_of(v, eh):
    return left_parts(v, eh, 2, NT)


def lower_matrix():
    return (iota((Q, Q), 0) >= iota((Q, Q), 1)).astype(BF16)


def sigmoid(v):
    return 1.0 / (1.0 + jnp.exp(-v))


def softplus(v):
    return jnp.maximum(v, 0.0) + jnp.log1p(jnp.exp(-jnp.abs(v)))


def row_scale(h):
    return lax.rsqrt(jnp.mean(h * h, axis=-1, keepdims=True) + EPS)


def decays(L, flags):
    E = jnp.exp(L) * flags[:, 3:4]
    W = jnp.exp(L[Q - 1 : Q] - L) * flags[:, 4:5]
    return E, W


def wave_kernel(
    hid, wsend, pack, cot, outw,
    normed_h, hid_h, w_h, gate_h, pre_h, ext_h, delta_h, logs_h, flags_h, fnext_h, mixed_h, carried_h, states_h, dno_h, cot_h, wout_h,
    sums, endlog, conv, hp, og, gain, segrow,
    hid_s, halo, nrm, w_s, small, proj, pre, ext, delta, logs, flags, fnext, sloc, inner, carried, states, dno, ends, rsend, rrecv, cot_s, w_o, wo_s, convt, state, total, tail, send, recv, done,
):
    eh = spread_matrix()
    n = Net(send, recv)
    g, m, x, y, z, core = n.g, n.m, n.x, n.y, n.z, n.c
    ALLX = (0,) + XS
    copies = []

    def keyed(key, src, dst, where):
        cp = n.copy(key, src, dst, where)
        copies.append(cp)
        cp.start()
        return cp

    stores = []

    def store(src, dst):
        cp = pltpu.make_async_copy(src, dst, done.at[len(stores)])
        cp.start()
        stores.append(cp)

    n.meet([n.at(dz=a, dc=b) for a, b in OTHERS] + [n.at(dx=d) for d in XS] + [n.at(dy=1), n.at(dy=3), n.group(1), n.group(7)] + [n.across(d) for d in ALLX])

    wa, sa = {}, {}
    for a, b in OTHERS:
        wa[a, b] = keyed(("wa", a, b), wsend.at[n.member(a, b)], w_s.at[g, m], n.at(dz=a, dc=b))
        sa[a, b] = keyed(("sa", a, b), pack, small.at[g, m], n.at(dz=a, dc=b))
    w_s[g, m] = wsend[m]
    small[g, m] = pack[...]
    hid_s[m] = hid[...]
    wx, wy, sx, sy = {}, {}, {}, {}

    def along_y(d, k):
        first = pl.ds(2 * lax.rem(z + 4 - ZS[k], 4), 2)
        for half, dy in ((0, 1), (1, 3)):
            part = w_s.at[n.behind(d), first, pl.ds(16 * half, 16)]
            wy[d, k, half] = keyed(("wy", d, k, half), part, part, n.at(dy=dy))

    def issue(k):
        for b in (0, 1):
            if (ZS[k], b) != (0, 0):
                wa[ZS[k], b].wait_recv()
        block = w_s.at[g, pl.ds(2 * lax.rem(z + 4 - ZS[k], 4), 2)]
        for d in XS:
            wx[k, d] = keyed(("wx", k, d), block, block, n.at(dx=d))
        along_y(0, k)

    def forward(k):
        for d in XS:
            wx[k, d].wait_recv()
            along_y(d, k)

    issue(0)
    issue(1)
    hz = {a: keyed(("hz", a), hid_s.at[m], hid_s.at[m], n.at(dz=a)) for a in (1, 3, 2)}
    hn = [keyed("hn", hid_s.at[m], hid_s.at[m], n.at(dc=1))]
    for a, b in OTHERS:
        sa[a, b].wait_recv()
    for d in XS:
        sx[d] = keyed(("sx", d), small.at[g], small.at[g], n.at(dx=d))
    sy[0] = keyed(("sy", 0), small.at[g], small.at[g], n.pair())
    forward(0)
    issue(2)
    for d in XS:
        sx[d].wait_recv()
        mine = small.at[n.behind(d)]
        sy[d] = keyed(("sy", d), mine, mine, n.pair())
    forward(1)
    issue(3)
    for d in ALLX:
        sy[d].wait_recv()

    for q in range(16):
        v = small[q // 2, 4 * (q % 2), 2:3]
        for u in range(1, 4):
            v = v + small[q // 2, 4 * (q % 2) + u, 2:3]
        gain[0:1, 128 * q : 128 * q + 128] = v
    heads3 = jnp.zeros((3, 128), F32)
    for j in range(4):
        og[0:1, 128 * j : 128 * j + 128] = small[4 * core + j, 2 * z, 3:4] + small[4 * core + j, 2 * z + 1, 3:4]
        for e in range(2):
            heads3 = heads3 + small[4 * core + j, 2 * z + e, 4:7]
    hp[...] = jnp.zeros_like(hp)
    hp[0:1] = heads3[0:1]
    hp[1:2] = jnp.where(iota((1, 128), 1) < 8, -jnp.exp(heads3[1:2]), 0.0)
    hp[2:3] = heads3[2:3]
    for q in range(34):
        v = jnp.zeros((8, 128), F32)
        for i in range(64):
            if 68 * i // 128 == q:
                v = v + small[i // 8, i % 8, 8:16]
            elif 68 * i // 128 == q - 1:
                v = v + small[i // 8, i % 8, 16:24]
        convt[q] = v
    for j in range(4):
        conv[:, 128 * j : 128 * j + 128] = convt[4 * (4 * core + j) + z]
    conv[:, 512:640] = convt[32]
    conv[:, 640:768] = convt[33]

    forward(2)
    for a in (1, 3, 2):
        hz[a].wait_recv()
        theirs = hid_s.at[2 * lax.rem(z + 4 - a, 4) + core]
        hn.append(keyed(("hf", a), theirs, theirs, n.at(dc=1)))
    cot_s[m] = cot[...]
    cz = {a: keyed(("cz", a), cot_s.at[m], cot_s.at[m], n.at(dz=a)) for a in (1, 3, 2)}
    cn = [keyed("cn", cot_s.at[m], cot_s.at[m], n.at(dc=1))]

    lane = iota((8, 128), 1)

    def chunk_row(group, i, c):
        return jnp.broadcast_to(small[group, 2 * c, i : i + 1] + small[group, 2 * c + 1, i : i + 1], (8, 128))

    for i in range(MICRO):
        before = jnp.where(g > 0, chunk_row(lax.rem(g + 7, 8), i, CH - 1), -1.0)
        after = jnp.where(g < 7, chunk_row(lax.rem(g + 1, 8), i, 0), -2.0)
        rows = [before] + [chunk_row(g, i, c) for c in range(CH)] + [after]
        for c in range(CH):
            prv, cur, nxt = rows[c : c + 3]
            here, ahead = [], []
            for d in (3, 2, 1):
                back = jnp.where(lane < d, pltpu.roll(prv, d, 1), pltpu.roll(cur, d, 1))
                here.append((back == cur).astype(F32))
                on = jnp.where(lane >= 128 - d, pltpu.roll(nxt, 128 - d, 1), pltpu.roll(cur, 128 - d, 1))
                ahead.append((on == cur).astype(F32))
            here += [(cur == prv[:, 127:128]).astype(F32), (cur == cur[:, 127:128]).astype(F32), cur]
            sub = iota((128, 128), 0)
            for rows_of, to in ((here, flags), (ahead, fnext)):
                v = jnp.zeros((128, 128), F32)
                for r, row in enumerate(rows_of):
                    v = jnp.where(sub == r, jnp.broadcast_to(row[0:1], (128, 128)), v)
                to[CH * i + c] = v.T
            segrow[CH * i + c] = cur[0:1]

    forward(3)
    w_o[g] = outw[...]
    ox = {d: keyed(("ox", d), w_o.at[g], w_o.at[g], n.at(dx=d)) for d in XS}
    oy = {}

    def out_y(d):
        for half, dy in ((0, 1), (1, 3)):
            part = w_o.at[n.behind(d), pl.ds(32 * half, 32)]
            oy[d, half] = keyed(("oy", d, half), part, part, n.at(dy=dy))

    out_y(0)
    for cp in hn:
        cp.wait_recv()
    edge = keyed("edge", hid_s.at[7, :, pl.ds(48, 16)], halo, n.group(1))

    gv = gain[0:1]

    def norm(k, carry):
        for i in range(MICRO):
            h = hid_s[pl.ds(2 * k, 2), i].reshape(Q, 2048).astype(F32)
            nrm[i, pl.ds(pl.multiple_of(16 + Q * k, 16), Q)] = (h * row_scale(h) * gv).astype(BF16)
        return carry

    lax.fori_loop(0, CH, norm, 0)
    edge.wait_recv()
    for i in range(MICRO):
        h = halo[i].astype(F32)
        nrm[i, 0:16] = (h * row_scale(h) * gv).astype(BF16)
    for i in range(MICRO):
        store(nrm.at[i, pl.ds(16, TOK)], normed_h.at[i])

    def project(side, first):
        for i in range(MICRO):
            for lo in range(0, 1408, 256):
                hi = min(lo + 256, 1408)
                v = 0.0 if first else proj[i, :, lo:hi]
                for k in range(4):
                    q = 2 * k + side
                    v = v + bdot(nrm[i, :, pl.ds(pl.multiple_of(256 * q, 256), 256)], w_s[q, :, :, lo:hi].reshape(256, hi - lo))
                proj[i, :, lo:hi] = v

    project(y, True)
    for d in ALLX:
        for k in range(4):
            for half in (0, 1):
                wy[d, k, half].wait_recv()
    project(1 - y, False)
    for d in XS:
        ox[d].wait_recv()
        out_y(d)
    store(w_s, w_h)
    store(hid_s, hid_h)
    store(flags, flags_h)
    store(fnext, fnext_h)

    def front(i, c):
        at = CH * i + c
        rows = pl.ds(pl.multiple_of(16 + Q * c, 16), Q)
        f = flags[at]
        xbc = proj[i, rows, 512:1280].astype(BF16).astype(F32)
        tail[8:] = xbc
        acc = conv[4:5] + conv[3:4] * xbc
        for k in range(3):
            acc = acc + conv[k : k + 1] * tail[5 + k : 5 + k + Q] * f[:, k : k + 1]
        pre[at] = acc
        ext[at] = tail[...].astype(BF16)
        d = softplus(proj[i, rows, 1280:1408] + hp[0:1])
        delta[at] = d
        L = right_parts(lower_matrix(), d * hp[1:2], 3)
        logs[at] = L
        E, W = decays(L, f)
        xv = acc[:, :512]
        X = xv * sigmoid(xv)
        b = acc[:, 512:640]
        B = (b * sigmoid(b)).astype(BF16)
        S = right_parts(B, heads_of(W * d, eh) * X, 2, TN)
        sloc[at] = S
        last = heads_of(E[Q - 8 :], eh)
        state[...] = last[7:8] * state[...] + S
        tail[0:8] = tail[Q : Q + 8]
        total[...] = total[...] + L[Q - 1 : Q]

    ex, lx, ly = {}, {}, {}
    for i in range(MICRO):
        tail[0:8] = proj[i, 8:16, 512:1280].astype(BF16).astype(F32)
        state[...] = jnp.zeros_like(state)
        total[...] = jnp.zeros_like(total)
        lax.fori_loop(0, CH, lambda c, carry, i=i: (front(i, c), carry)[1], 0)
        ends[g, i] = state[...].astype(BF16)
        lt = parts(jnp.broadcast_to(heads_of(jnp.broadcast_to(total[...], (8, 128)), eh)[0:1], (16, 512)), 3)
        seg = jnp.broadcast_to(segrow[CH * i + CH - 1][:, 127:128], (16, 512))
        high = jnp.floor(seg * (1.0 / 64.0))
        r = iota((16, 512), 0)
        v = jnp.zeros((16, 512), BF16)
        for k, row in enumerate(lt + [high.astype(BF16), (seg - 64.0 * high).astype(BF16)]):
            v = jnp.where(r == k, row, v)
        endlog[g, i] = v
        for d in XS:
            lx[i, d] = keyed(("lx", i, d), endlog.at[g, i], endlog.at[g, i], n.at(dx=d))
        for d in ALLX:
            ly[i, d] = keyed(("ly", i, d), endlog.at[g, i], endlog.at[g, i], n.across(d))
        for d in XS:
            ex[i, d] = keyed(("ex", i, d), ends.at[g, i], ends.at[g, i], n.at(dx=d))
    store(pre, pre_h)
    store(ext, ext_h)
    store(delta, delta_h)
    store(logs, logs_h)
    for i in range(MICRO):
        store(proj.at[i, pl.ds(16, TOK), pl.ds(0, 512)], gate_h.at[i])

    def states_on(i):
        for d in XS:
            lx[i, d].wait_recv()
        for d in ALLX:
            ly[i, d].wait_recv()
        for d in XS:
            ex[i, d].wait_recv()
        rsend[i] = entering(n, ends, endlog, 1, 0, i).astype(BF16)
        return keyed(("r", i), rsend.at[i], rrecv.at[i], n.pair())

    def inside(at, carry):
        L = logs[at]
        X, B, C = activations(pre[at])
        U = (heads_of(delta[at], eh) * X).astype(BF16)
        psi = bdot(C, B, NT)
        keep = same_mask(flags[at], segrow[at])
        LT = L.T
        for j in range(4):
            u = pair_halves(U[:, 128 * j : 128 * j + 128])
            v = jnp.zeros((Q, 128), F32)
            for e in range(2):
                h = 2 * j + e
                K = jnp.where(keep, jnp.exp(L[:, h : h + 1] - LT[h : h + 1]), 0.0)
                v = v + bdot((psi * K).astype(BF16), u[e])
            inner[at, :, 128 * j : 128 * j + 128] = v
        return carry

    lax.fori_loop(0, 4, inside, 0)
    r0 = states_on(0)
    for d in ALLX:
        for half in (0, 1):
            oy[d, half].wait_recv()
    swap = keyed("swap", w_o.at[pl.ds(4 * (1 - core), 4)], wo_s.at[:, core], n.at(dc=1))
    for k in range(4):
        wo_s[k, core] = w_o[4 * core + k]
    for a in (1, 3, 2):
        cz[a].wait_recv()
        theirs = cot_s.at[2 * lax.rem(z + 4 - a, 4) + core]
        cn.append(keyed(("cf", a), theirs, theirs, n.at(dc=1)))
    lax.fori_loop(4, 8, inside, 0)
    r1 = states_on(1)
    swap.wait_recv()
    for cp in cn:
        cp.wait_recv()
    store(cot_s, cot_h)
    store(wo_s, wout_h)
    for i in range(MICRO):
        d = bdot(cot_s[:, i].reshape(TOK, 2048), wo_s[...].reshape(512, 2048), NT)
        for c in range(CH):
            dno[CH * i + c] = d[Q * c : Q * c + Q]
    store(dno, dno_h)

    def mix(i, c):
        at = CH * i + c
        E, _ = decays(logs[at], flags[at])
        X, _, C = activations(pre[at])
        more = heads_of(jnp.concatenate([E, jnp.broadcast_to(hp[2:3], (8, 128))], 0), eh)
        Ex, skip = more[:Q], more[Q : Q + 1]
        S = state[...]
        states[at, 0] = S
        Yc = Ex * bdot(C, S.astype(BF16))
        carried[at] = Yc
        mx = inner[at] + Yc + skip * X
        inner[at] = mx
        after = Ex[Q - 1 : Q] * S + sloc[at]
        state[...] = after
        states[at, 1] = after
        gt = proj[i, pl.ds(pl.multiple_of(16 + Q * c, 16), Q), 0:512]
        gated = mx * (gt * sigmoid(gt))
        ones = jnp.ones((8, 512), BF16)
        sums[m, at, 0:8] = right_parts(ones, gated * gated, 2, NT)
        sums[m, at, 8:16] = right_parts(ones, dno[at] * og[0:1] * gated, 2, NT)

    sm = []
    for i, r in ((0, r0), (1, r1)):
        r.wait_recv()
        state[...] = entering(n, ends, endlog, 0, 0, i) + rrecv[i].astype(F32)
        lax.fori_loop(0, CH, lambda c, carry, i=i: (mix(i, c), carry)[1], 0)
        mine = sums.at[m, pl.ds(CH * i, CH)]
        for a, b in OTHERS:
            sm.append(keyed(("sm", i, a, b), mine, mine, n.at(dz=a, dc=b)))
    store(inner, mixed_h)
    store(carried, carried_h)
    store(states, states_h)
    for cp in sm:
        cp.wait_recv()
    for cp in copies:
        cp.wait_send()
    for cp in stores:
        cp.wait()


def wave(hid, wsend, pack, cot, outw):
    V = lambda *s: pltpu.VMEM(s, BF16)
    R = lambda *s: pltpu.VMEM(s, F32)
    outs = [
        sds((2, TOK, 2048), BF16), sds((8, 2, 64, 2048), BF16), sds((8, 8, 32, 1408), BF16), sds((2, TOK, 512), F32), sds((8, Q, 768), F32), sds((8, Q + 8, 768), BF16), sds((8, Q, 128), F32), sds((8, Q, 128), F32),
        sds((8, Q, 128), F32), sds((8, Q, 128), F32), sds((8, Q, 512), F32), sds((8, Q, 512), F32), sds((8, 2, 128, 512), F32), sds((8, Q, 512), F32), sds((8, 2, 64, 2048), BF16), sds((4, 2, 64, 2048), BF16),
        sds((8, 8, 16, 128), F32), sds((8, 2, 16, 512), BF16), sds((8, 768), F32), sds((8, 128), F32), sds((8, 512), F32), sds((8, 2048), F32), sds((8, 1, 128), F32),
    ]
    scratch = [
        V(8, 2, 64, 2048), V(2, 16, 2048), V(2, TOK + 16, 2048), V(8, 8, 32, 1408), R(8, 8, 24, 128), R(2, TOK + 16, 1408), R(8, Q, 768), V(8, Q + 8, 768), R(8, Q, 128), R(8, Q, 128), R(8, Q, 128), R(8, Q, 128),
        R(8, 128, 512), R(8, Q, 512), R(8, Q, 512), R(8, 2, 128, 512), R(8, Q, 512), V(8, 2, 128, 512), V(2, 128, 512), V(2, 128, 512), V(8, 2, 64, 2048), V(8, 64, 2048), V(4, 2, 64, 2048),
        R(34, 8, 128), R(128, 512), R(1, 128), R(Q + 8, 768),
    ]
    return pl.pallas_call(
        wave_kernel,
        name="wave",
        out_shape=outs,
        in_specs=[VM] * 5,
        out_specs=[ANY] * 16 + [VM] * 7,
        scratch_shapes=[*scratch, pltpu.SemaphoreType.DMA((144,)), pltpu.SemaphoreType.DMA((144,)), pltpu.SemaphoreType.DMA((24,))],
        compiler_params=pltpu.CompilerParams(collective_id=1, has_side_effects=True, vmem_limit_bytes=64 * 1024 * 1024 - 65536),
        cost_estimate=pl.CostEstimate(flops=8 << 30, bytes_accessed=32 << 20, transcendentals=0),
    )(hid, wsend, pack, cot, outw)


def entering(n, everyone, logs, target, direction, micro):
    to = 2 * n.x + (1 - n.y if target else n.y)
    lt, last = [], []
    for q in range(8):
        v = logs[q, micro].astype(F32)
        lt.append(v[0:1] + v[1:2] + v[2:3])
        last.append(64.0 * v[3:4] + v[4:5])
    zero = jnp.zeros((1, 512), F32)
    edge = zero
    for r in range(8):
        edge = edge + jnp.where((r == to) if direction else (r == to - 1), last[r], zero)
    total = jnp.zeros((128, 512), F32)
    for k in range(4):
        q = 2 * k + n.y
        log = zero
        for r in range(8):
            between = (r > to) & (r < q) if direction else (r > q) & (r < to)
            log = log + jnp.where(between, lt[r], zero)
        if direction:
            there = jnp.where(n.y == 0, last[max(2 * k - 1, 0)], last[2 * k])
        else:
            there = jnp.where(n.y == 0, last[2 * k], last[2 * k + 1])
        reached = jnp.where((q > to) if direction else (q < to), 1.0, 0.0)
        total = total + jnp.where(there == edge, jnp.exp(log) * reached, zero) * everyone[q, micro].astype(F32)
    return total


def same_mask(flags, segrow):
    return (flags[:, 5:6] == segrow) & (iota((Q, Q), 0) >= iota((Q, Q), 1))


def activations(pre):
    a = pre * sigmoid(pre)
    return a[:, :512], a[:, 512:640].astype(BF16), a[:, 640:768].astype(BF16)


def pair_halves(v):
    low_half = iota(v.shape, 1) < 64
    zero = jnp.zeros_like(v)
    return jnp.where(low_half, v, zero), jnp.where(low_half, zero, v)


T = MICRO * TOK


def column(row):
    return jnp.concatenate([jnp.broadcast_to(row, (128, 128)).T] * 4, 1)


def pick_matrix(rows, start, count, shift, dtype=BF16):
    r, l = iota((rows, 128), 0), iota((rows, 128), 1)
    return ((r - start == l - shift) & (l >= shift) & (l < shift + count)).astype(dtype)


class Reduce:
    def __init__(self, n, key, a, b, a1, a2, pa, b1, b2, pb, b3):
        self.n, self.key, self.a, self.b = n, key, a, b
        self.a1, self.a2, self.pa, self.b1, self.b2, self.pb, self.b3 = a1, a2, pa, b1, b2, pb, b3
        self.half = a.shape[1] // 2

    def group(self, d, f):
        n = self.n
        return 2 * lax.rem(n.x + d, 4) + lax.rem(n.y + f, 2)

    def first_a(self, d, f):
        return self.n.copy((self.key, "a1", d, f), self.a.at[self.group(d, f)], self.a1.at[d - 1, f], self.n.at(dx=d))

    def first_b(self, d, e):
        n = self.n
        rep = lax.rem(n.ring + e, 4) // 2
        rows = pl.ds(pl.multiple_of(self.half * rep, self.half), self.half)
        return n.copy((self.key, "b1", d, e), self.b.at[self.group(d, e % 2), rows], self.b1.at[e - 1, lax.rem(n.x + d, 4)], n.at(dy=e))

    def send_a(self, d, f):
        if d:
            self.first_a(d, f).start()

    def send_b(self, d, f):
        for e in (1, 3) if f else (2,):
            self.first_b(d, e).start()

    def second_a(self, e):
        return self.n.copy((self.key, "a2", e), self.pa.at[e % 2], self.a2.at[e - 1], self.n.at(dy=e))

    def second_b(self, d):
        return self.n.copy((self.key, "b2", d), self.pb.at[lax.rem(self.n.x + d, 4)], self.b2.at[d - 1], self.n.at(dx=d))

    def third_b(self):
        return self.n.copy((self.key, "b3"), self.b3.at[self.n.rep], self.b3.at[self.n.rep], self.n.at(dy=2))

    def middle_a(self, f):
        for d in XS:
            self.first_a(d, f).wait_recv()
        self.pa[f] = add4(self.a[self.group(0, f)], self.a1[:, f]).astype(BF16)
        for e in (1, 3) if f else (2,):
            self.second_a(e).start()

    def middle_b(self):
        n = self.n
        rows = pl.ds(pl.multiple_of(self.half * n.rep, self.half), self.half)
        for d in (2, 1, 3, 0):
            for e in XS:
                self.first_b(d, e).wait_recv()
            k = lax.rem(n.x + d, 4)
            self.pb[k] = add4(self.b[2 * k + n.y, rows], self.b1[:, k]).astype(BF16)
            if d:
                self.second_b(d).start()

    def last_b(self):
        for d in XS:
            self.second_b(d).wait_recv()
        self.b3[self.n.rep] = add4(self.pb[self.n.x], self.b2).astype(self.b3.dtype)
        self.third_b().start()

    def last_a(self):
        for e in XS:
            self.second_a(e).wait_recv()
        return add4(self.pa[0], self.a2)

    def finish(self):
        for d in XS:
            for f in (0, 1):
                self.first_a(d, f).wait_send()
            self.second_b(d).wait_send()
        for e in XS:
            for d in range(4):
                self.first_b(d, e).wait_send()
            self.second_a(e).wait_send()
        self.third_b().wait_send()


def fetcher(sems):
    loads = {}

    def fetch(key, src, dst):
        loads[key] = pltpu.make_async_copy(src, dst, sems.at[len(loads)])
        loads[key].start()

    return loads, fetch


C1 = 256


def back_wave_kernel(
    mixed_h, carried_h, states_h, gate_h, dno_h, sums, pre_h, delta_h, logs_h, flags_h, segrow, og, hp, wout_h, cot, normed, endlog,
    dgate, dpre_h, dbc, ddt, small_o, small_b, total, g_out, gate_rows,
    mixed, carried, states, gate, dno, pre, delta, logs, flags, wout, nout, dmix, tloc, dbi, starts, rsend, rrecv, tiles, rows, part, near, far, gsw, oa, ob, oa1, oa2, opa, ob1, ob2, opb, ob3, oin,
    wa, wb, wa1, wa2, wpa, wb1, wb2, wpb, wb3, state, send, recv, load, tile_sem,
):
    eh = spread_matrix()
    n = Net(send, recv)
    g, m, core, z = n.g, n.m, n.c, n.z
    O = Reduce(n, "o", oa, ob, oa1, oa2, opa, ob1, ob2, opb, ob3)
    W = Reduce(n, "w", wa, wb, wa1, wa2, wpa, wb1, wb2, wpb, wb3)
    swap = n.copy("swap", gsw.at[:, 1 - core], oin, n.at(dc=1))
    loads, fetch = fetcher(load)
    for i in range(MICRO):
        some = pl.ds(CH * i, CH)
        for key, src, dst in (("mixed", mixed_h, mixed), ("gate", gate_h, gate), ("dno", dno_h, dno), ("pre", pre_h, pre), ("logs", logs_h, logs), ("flags", flags_h, flags)):
            fetch((key, i), src.at[some], dst.at[some])
    fetch("wout", wout_h, wout)
    for key, src, dst in (("delta", delta_h, delta), ("states", states_h, states), ("carried", carried_h, carried)):
        fetch(key, src, dst)

    def start_x(i, d):
        return n.copy(("sx", i, d), starts.at[g, i], starts.at[g, i], n.at(dx=d))

    def part_y(i):
        return n.copy(("r", i), rsend.at[i], rrecv.at[i], n.pair())

    def near_copy(d, i):
        return n.copy(("near", d, i), part.at[2 * lax.rem(z + d, 4) + 1 - core, i], near.at[d, i], n.at(dc=1))

    def far_copy(d, i):
        return n.copy(("far", d, i), near.at[d, i], far.at[d - 1, i], n.at(dz=d))

    n.meet([n.at(dz=a) for a in (1, 3, 2)] + [n.at(dc=1)] + [n.at(dx=d) for d in XS] + [n.at(dy=d) for d in XS])
    small_o[...] = jnp.zeros_like(small_o)
    small_b[...] = jnp.zeros_like(small_b)

    def outward(i, k):
        c = CH - 1 - k
        at = CH * i + c
        tot = sums[0, at]
        for q in range(1, 8):
            tot = tot + sums[q, at]
        r = column(lax.rsqrt(tot[0:1] / INNER + EPS))
        s2 = column(tot[8:9] / INNER)
        gt = gate[at]
        s = sigmoid(gt)
        sg = gt * s
        mix = mixed[at]
        gated = mix * sg
        dn = dno[at]
        n0 = gated * r
        rows = pl.ds(pl.multiple_of(Q * c, Q), Q)
        nout[i, rows] = (n0 * og[0:1]).astype(BF16)
        d_gated = r * (dn * og[0:1] - n0 * r * s2)
        dm = d_gated * sg
        dmix[at] = dm
        dgate[i, rows] = (d_gated * mix * (s * (1.0 + gt * (1.0 - s)))).astype(BF16)
        x = pre[at, :, :512]
        X = x * sigmoid(x)
        cc = pre[at, :, 640:768]
        C = (cc * sigmoid(cc)).astype(BF16)
        small_o[0:1] += jnp.sum(dn * n0, 0, keepdims=True)
        small_o[1:2] += jnp.sum(X * dm, 0, keepdims=True)
        E, _ = decays(logs[at], flags[at])
        Ex = heads_of(E, eh)
        G = right_parts(C, Ex * dm, 2, TN)
        tloc[at] = G
        state[...] = Ex[Q - 1 : Q] * state[...] + G

    for i in range(MICRO):
        for key in ("mixed", "gate", "dno", "pre", "logs", "flags"):
            loads[key, i].wait()
        state[...] = jnp.zeros_like(state)
        lax.fori_loop(0, CH, lambda k, carry, i=i: (outward(i, k), carry)[1], 0)
        starts[g, i] = state[...].astype(BF16)
        for d in XS:
            start_x(i, d).start()
        if i == 0:
            loads["wout"].wait()
        part[:, i] = bdot(nout[i], wout[...]).astype(BF16).reshape(8, 64, 2048)
        for d in (1, 3, 2, 0):
            near_copy(d, i).start()

    def bring(k):
        if k < 8:
            return pltpu.make_async_copy(cot.at[:, :, :, pl.ds(256 * k, 256)], tiles.at[k % 2], tile_sem.at[k % 2])
        at = pl.ds(pl.multiple_of(256 * W.group(*ORDER[k - 8]), 256), 256)
        return pltpu.make_async_copy(normed.at[:, :, at], rows.at[k % 2], tile_sem.at[k % 2])

    def states_on(i):
        for d in XS:
            start_x(i, d).wait_recv()
        rsend[i] = entering(n, starts, endlog, 1, 1, i).astype(BF16)
        part_y(i).start()

    def tokens_on(i):
        for d in (1, 3, 2, 0):
            near_copy(d, i).wait_recv()
            there = 2 * lax.rem(z + d, 4) + core
            near[d, i] = (part[there, i].astype(F32) + near[d, i].astype(F32)).astype(BF16)
            if d:
                far_copy(d, i).start()

    bring(0).start()
    for k in range(16):
        bring(k).wait()
        if k < 15:
            bring(k + 1).start()
        t = tiles.at[k % 2]
        if k < 8:
            v = sum(bdot(nout[i], t[:, i].reshape(TOK, 256), TN) for i in range(MICRO))
            gsw[:, :, :, 256 * k : 256 * k + 256] = v.astype(BF16).reshape(4, 2, 64, 256)
        else:
            d, f = ORDER[k - 8]
            q = W.group(d, f)
            v = sum(bdot(rows[k % 2, i], dgate[i], TN) for i in range(MICRO))
            wa[q] = v[:, 0:C1].astype(BF16)
            wb[q] = v[:, C1:].astype(BF16)
            W.send_a(d, f)
            W.send_b(d, f)
        if k == 3:
            states_on(0)
            tokens_on(0)
        if k == 7:
            swap.start()
            for j in range(4):
                oa[4 * core + j] = gsw[j, core, :, 0:1024]
                ob[4 * core + j] = gsw[j, core, :, 1024:2048]
            states_on(1)
            tokens_on(1)

    swap.wait_recv()
    for j in range(4):
        oa[4 * (1 - core) + j] = oin[j, :, 0:1024]
        ob[4 * (1 - core) + j] = oin[j, :, 1024:2048]
    for d, f in ORDER:
        O.send_a(d, f)
        O.send_b(d, f)

    loads["delta"].wait()
    loads["states"].wait()
    loads["carried"].wait()

    def inside(at, carry):
        L = logs[at]
        f = flags[at]
        E, _ = decays(L, f)
        X, B, C = activations(pre[at])
        more = heads_of(jnp.concatenate([E, delta[at]], 0), eh)
        Ex, dx = more[:Q], more[Q:]
        Ub = (dx * X).astype(BF16)
        dm = dmix[at]
        dmb = dm.astype(BF16)
        psi = bdot(C, B, NT)
        keep = same_mask(f, segrow[at])
        LT = L.T
        dpsi = jnp.zeros((Q, Q), F32)
        for j in range(4):
            js = slice(128 * j, 128 * j + 128)
            u = pair_halves(Ub[:, js])
            y = pair_halves(dmb[:, js])
            acc = jnp.zeros((Q, 128), F32)
            for e in range(2):
                h = 2 * j + e
                K = jnp.where(keep, jnp.exp(L[:, h : h + 1] - LT[h : h + 1]), 0.0)
                acc = acc + bdot((psi * K).astype(BF16), y[e], TN)
                dpsi = dpsi + bdot(y[e], u[e], NT) * K
            dno[at, :, js] = acc
        dpb = dpsi.astype(BF16)
        dbi[at, 0:128] = bdot(C, dpb, TN)
        dbi[at, 128:256] = bdot(B, dpb, TT) + bdot(states[at, 0].astype(BF16), (Ex * dm).astype(BF16), NT)
        return carry

    lax.fori_loop(0, 8, inside, 0)
    for i in (0, 1):
        part_y(i).wait_recv()

    def inward(i, k):
        c = CH - 1 - k
        at = CH * i + c
        L = logs[at]
        d = delta[at]
        E, W_ = decays(L, flags[at])
        p = pre[at, :, 0:512]
        s = sigmoid(p)
        X = p * s
        bb = pre[at, :, 512:640]
        B = (bb * sigmoid(bb)).astype(BF16)
        more = heads_of(jnp.concatenate([E[Q - 8 :], W_, d, jnp.broadcast_to(hp[2:3], (8, 128))], 0), eh)
        Elast, Wx, dx, skip = more[7:8], more[8 : 8 + Q], more[8 + Q : 8 + 2 * Q], more[8 + 2 * Q : 9 + 2 * Q]
        U = dx * X
        dm = dmix[at]
        Yc = carried[at]
        Yi = mixed[at] - Yc - skip * X
        G = state[...]
        Gb = G.astype(BF16)
        dUi = dno[at]
        dUc = Wx * bdot(B, Gb)
        dU = dUi + dUc
        lanes = pl.ds(pl.multiple_of(Q * at, Q), Q)
        dbc[0:128, lanes] = (dbi[at, 0:128] + bdot(Gb, (Wx * U).astype(BF16), NT)).astype(BF16)
        dbc[128:256, lanes] = dbi[at, 128:256].astype(BF16)
        dL = sums_of(dm.astype(BF16).astype(F32) * Yi + dm * Yc - U.astype(BF16).astype(F32) * dUi - U * dUc, eh)
        end = sums_of(jnp.broadcast_to(jnp.sum(G * states[at, 1], 0, keepdims=True), (8, 512)), eh)[0:1]
        upper = (iota((Q, Q), 0) <= iota((Q, Q), 1)).astype(BF16)
        dstep = right_parts(upper, dL, 3) + end
        rate = hp[1:2]
        dr = (sums_of(dU * X, eh) + dstep * rate) * (1.0 - jnp.exp(-d))
        ddt[at] = dr.astype(BF16)
        small_b[0:1] += jnp.sum(dr, 0, keepdims=True)
        small_b[1:2] += jnp.sum(dstep * d * rate, 0, keepdims=True)
        gate[at] = (dx * dU + skip * dm) * (s * (1.0 + p * (1.0 - s)))
        state[...] = Elast * G + tloc[at]

    store = pltpu.make_async_copy(gate, dpre_h, load.at[0])
    for i in range(MICRO):
        state[...] = entering(n, starts, endlog, 0, 1, i) + rrecv[i].astype(F32)
        lax.fori_loop(0, CH, lambda k, carry, i=i: (inward(i, k), carry)[1], 0)
    store.start()

    W.middle_b()
    W.middle_a(1)
    W.middle_a(0)
    O.middle_b()
    O.middle_a(1)
    O.middle_a(0)
    for i in range(MICRO):
        for d in XS:
            far_copy(d, i).wait_recv()
        total[i] = near[0, i].astype(F32) + far[0, i].astype(F32) + far[1, i].astype(F32) + far[2, i].astype(F32)
    W.last_b()
    O.last_b()
    gate_rows[:, 0:C1] = W.last_a().astype(BF16)
    g_out[:, 0:1024] = O.last_a()
    W.third_b().wait_recv()
    O.third_b().wait_recv()
    for h in range(2):
        g_out[32 * h : 32 * h + 32, 1024:2048] = ob3[h]
        gate_rows[128 * h : 128 * h + 128, C1:] = wb3[h]
    O.finish()
    W.finish()
    store.wait()
    swap.wait_send()
    for i in range(MICRO):
        part_y(i).wait_send()
        for d in XS:
            start_x(i, d).wait_send()
            far_copy(d, i).wait_send()
        for d in range(4):
            near_copy(d, i).wait_send()


def back_wave(mixed, carried, states, gate, dno, sums, pre, delta, logs, flags, segrow, og, hp, wout, cot, normed, endlog):
    outs = [
        sds((2, TOK, 512), BF16), sds((8, Q, 512), F32), sds((256, T), BF16), sds((8, Q, 128), BF16), sds((8, 512), F32), sds((8, 128), F32), sds((2, 64, 2048), F32), sds((64, 2048), F32),
        sds((256, 512), BF16),
    ]
    V = lambda *s: pltpu.VMEM(s, BF16)
    R = lambda *s: pltpu.VMEM(s, F32)
    return pl.pallas_call(
        back_wave_kernel,
        name="back_wave",
        out_shape=outs,
        in_specs=[ANY] * 5 + [VM] + [ANY] * 4 + [VM] * 3 + [ANY] * 3 + [VM],
        out_specs=[VM, ANY] + [VM] * 7,
        scratch_shapes=[
            R(8, Q, 512), R(8, Q, 512), R(8, 2, 128, 512), R(8, Q, 512), R(8, Q, 512), R(8, Q, 768), R(8, Q, 128), R(8, Q, 128), R(8, Q, 128), V(512, 2048),
            V(2, TOK, 512), R(8, Q, 512), R(8, 128, 512), R(8, 256, 128), V(8, 2, 128, 512), V(2, 128, 512), V(2, 128, 512), V(2, 8, 2, 64, 256), V(2, 2, TOK, 256), V(8, 2, 64, 2048),
            V(4, 2, 64, 2048), V(3, 2, 64, 2048), V(4, 2, 64, 2048),
            V(8, 64, 1024), V(8, 64, 1024), V(3, 2, 64, 1024), V(3, 64, 1024), V(2, 64, 1024), V(3, 4, 32, 1024), V(3, 32, 1024), V(4, 32, 1024), R(2, 32, 1024), V(4, 64, 2048),
            V(8, 256, C1), V(8, 256, C1), V(3, 2, 256, C1), V(3, 256, C1), V(2, 256, C1), V(3, 4, 128, C1), V(3, 128, C1), V(4, 128, C1), V(2, 128, C1), R(128, 512),
            pltpu.SemaphoreType.DMA((96,)), pltpu.SemaphoreType.DMA((96,)), pltpu.SemaphoreType.DMA((16,)), pltpu.SemaphoreType.DMA((2,)),
        ],
        compiler_params=pltpu.CompilerParams(collective_id=4, has_side_effects=True, vmem_limit_bytes=62 << 20),
        cost_estimate=pl.CostEstimate(flops=8 << 30, bytes_accessed=32 << 20, transcendentals=0),
    )(mixed, carried, states, gate.reshape(8, Q, 512), dno, sums, pre, delta, logs, flags, segrow, og, hp, wout, cot, normed, endlog)


CB = 256
CA = 640 - CB


def tail_kernel(
    dbc, edge_x, gate_rows, dpre, pre, ext, flags, fnext, conv, ddt, dgate, w, hid, normed, small_o, small_b,
    gi, total, small_all,
    bc_s, ex_s, eb_src, eb_s, dps, pre_s, ext_s, fl_s, fn_s, ddt_s, dg_s, w_s, hid_s, nm_s, wt, e_s, dproj, part, near, far, conv_acc, gnorm,
    s0, s1, s2, sx, ga, gb, ga1, ga2, gpa, gb1, gb2, gpb, gb3, final, send, recv, load,
):
    n = Net(send, recv)
    x, y, z, c, m = n.x, n.y, n.z, n.c, n.m
    loads = {}

    def fetch(key, src, dst):
        loads[key] = pltpu.make_async_copy(src, dst, load.at[len(loads)])
        loads[key].start()

    fetch("pre", pre.at[:, :, pl.ds(512, 256)], pre_s)
    fetch("w", w, w_s)
    fetch("dpre", dpre, dps.at[:, pl.ds(0, TOK), pl.ds(0, 512)])
    fetch("ext", ext, ext_s)
    fetch("flags", flags, fl_s)
    fetch("fnext", fnext, fn_s)
    fetch("ddt", ddt, ddt_s)
    fetch("normed", normed, nm_s)
    fetch("dgate", dgate, dg_s)
    fetch("hid", hid, hid_s)
    n.meet([n.at(dz=a, dc=b) for a, b in OTHERS] + [n.at(dx=d) for d in XS] + [n.at(dy=d) for d in XS] + [n.group(1), n.group(7)])

    def bc_copy(a, b):
        return n.copy(("bc", a, b), dbc.at[n.member(a, b)], bc_s.at[m], n.at(dz=a, dc=b))

    edge1 = n.copy("edge1", edge_x, ex_s, n.group(7))
    edge2 = n.copy("edge2", eb_src, eb_s, n.group(7))

    def near_copy(d, i):
        return n.copy(("near", d, i), part.at[2 * lax.rem(z + d, 4) + 1 - c, i], near.at[d, i], n.at(dc=1))

    def far_copy(d, i):
        return n.copy(("far", d, i), near.at[d, i], far.at[d - 1, i], n.at(dz=d))

    def small_x(d):
        return n.copy(("sx", d), s0, s1.at[d - 1], n.at(dx=d))

    def small_y(d):
        return n.copy(("sy", d), sx, s2.at[d - 1], n.at(dy=d))

    def small_m(a, b):
        return n.copy(("sm", a, b), small_all.at[m], small_all.at[m], n.at(dz=a, dc=b))

    def rows_copy(a, b):
        return n.copy(("rows", a, b), final.at[n.member(a, b)], gi.at[m], n.at(dz=a, dc=b))

    W = Reduce(n, "w", ga, gb, ga1, ga2, gpa, gb1, gb2, gpb, gb3)

    for a, b in OTHERS:
        bc_copy(a, b).start()
    edge1.start()
    bc_s[m] = dbc[m]

    pick = pick_matrix(256, 32 * m, 32, 0)
    loads["w"].wait()
    wt[...] = (bdot(w_s[:, 1024:1280], pick) + bdot(w_s[:, 1280:1408], pick_matrix(128, 0, 8, 32))).astype(BF16)
    cw = jnp.concatenate([conv[:, 0:512], left_parts(conv[:, 512:768], pick, 3)], 1)
    for key in ("pre", "dpre"):
        loads[key].wait()
    for a, b in OTHERS:
        bc_copy(a, b).wait_recv()
    eye = pick_matrix(32, 0, 32, 0)

    def bc_chunk(i, k):
        t = CH * i + k
        tot = bc_s[0, :, Q * t : Q * t + Q].astype(F32)
        for q in range(1, 8):
            tot = tot + bc_s[q, :, Q * t : Q * t + Q].astype(F32)
        d = left_parts(tot, eye, 2, TN)
        p = left_parts(pre_s[t], pick, 2)
        s = sigmoid(p)
        dps[i, Q * k : Q * k + Q, 512:640] = d * (s * (1.0 + p * (1.0 - s)))

    for i in range(MICRO):
        bc_chunk(i, 0)
        eb_src[i] = dps[i, 0:8, 512:640]
    edge2.start()
    for i in range(MICRO):
        for k in range(1, CH):
            bc_chunk(i, k)
    for key in ("ext", "flags", "fnext", "ddt"):
        loads[key].wait()
    conv_acc[...] = jnp.zeros_like(conv_acc)
    pick_dt = pick_matrix(128, 0, 8, 32)

    def conv_chunk(i, k):
        t = CH * i + k
        e_s[:, 0:512] = ext_s[t, :, 0:512].astype(F32)
        e_s[:, 512:640] = bdot(ext_s[t, :, 512:768], pick)
        f, fn = fl_s[t], fn_s[t]
        dp = dps[i, Q * k : Q * k + Q]
        dx = cw[3:4] * dp
        conv_acc[3:4] += jnp.sum(dp * e_s[8 : 8 + Q], 0, keepdims=True)
        conv_acc[4:5] += jnp.sum(dp, 0, keepdims=True)
        for j in range(3):
            conv_acc[j : j + 1] += jnp.sum(dp * e_s[5 + j : 5 + j + Q] * f[:, j : j + 1], 0, keepdims=True)
            dx = dx + cw[j : j + 1] * dps[i, Q * k + 3 - j : Q * k + 3 - j + Q] * fn[:, j : j + 1]
        rows = slice(Q * k, Q * k + Q)
        dproj[i, rows, 0:512] = dx[:, 0:512].astype(BF16)
        dproj[i, rows, 512:640] = (dx[:, 512:640] + bdot(ddt_s[t], pick_dt)).astype(BF16)

    for i in range(MICRO):
        for k in range(CH - 1):
            conv_chunk(i, k)
    edge1.wait_recv()
    edge2.wait_recv()
    for i in range(MICRO):
        dps[i, TOK : TOK + 8, 0:512] = ex_s[i]
        dps[i, TOK : TOK + 8, 512:640] = eb_s[i]
        conv_chunk(i, CH - 1)

    loads["normed"].wait()
    for d, f in ORDER:
        q = W.group(d, f)
        at = pl.ds(pl.multiple_of(256 * q, 256), 256)
        v = sum(bdot(nm_s[i, :, at], dproj[i], TN) for i in range(MICRO)).astype(BF16)
        gb[q] = v[:, 0:CB]
        ga[q] = v[:, CB:]
        W.send_a(d, f)
        W.send_b(d, f)

    loads["hid"].wait()
    loads["dgate"].wait()
    for i in range(MICRO):
        h = hid_s[:, i].reshape(TOK, 2048).astype(F32)
        scale = row_scale(h)
        first, main, rest = dg_s[i], dproj[i, :, 0:512], dproj[i, :, 512:640]

        def tile_of(j, carry, i=i, scale=scale, first=first, main=main, rest=rest):
            at = pl.ds(pl.multiple_of(256 * j, 256), 256)
            d = bdot(first, w_s[at, 0:512], NT) + bdot(main, w_s[at, 512:1024], NT) + bdot(rest, wt[at], NT)
            part[:, i, :, at] = d.astype(BF16).reshape(8, 64, 256)
            hv = hid_s[:, i, :, at].reshape(TOK, 256).astype(F32)
            s = jnp.sum(d * (hv * scale), 0, keepdims=True)
            gnorm[0:1, at] = s if i == 0 else gnorm[0:1, at] + s
            return carry

        lax.fori_loop(0, 8, tile_of, 0)
        for d in (1, 3, 2, 0):
            near_copy(d, i).start()
    for r in range(16):
        s0[r : r + 1] = gnorm[0:1, 128 * r : 128 * r + 128]
    for k in range(5):
        for r in range(5):
            s0[16 + 5 * k + r : 17 + 5 * k + r] = conv_acc[k : k + 1, 128 * r : 128 * r + 128]
    for r in range(4):
        s0[41 + r : 42 + r] = small_o[0:1, 128 * r : 128 * r + 128]
    s0[45:47] = small_b[0:2]
    s0[47:48] = sums_of(small_o[...], spread_matrix())[1:2]
    for d in XS:
        small_x(d).start()

    for i in range(MICRO):
        for d in (1, 3, 2, 0):
            near_copy(d, i).wait_recv()
            at = 2 * lax.rem(z + d, 4) + c
            near[d, i] = (part[at, i].astype(F32) + near[d, i].astype(F32)).astype(BF16)
            if d:
                far_copy(d, i).start()
    for d in XS:
        small_x(d).wait_recv()
    sx[...] = s0[...] + s1[0] + s1[1] + s1[2]
    for d in XS:
        small_y(d).start()
    W.middle_b()
    W.middle_a(1)
    W.middle_a(0)
    W.last_b()
    for d in XS:
        small_y(d).wait_recv()
    small_all[m] = sx[...] + s2[0] + s2[1] + s2[2]
    for a, b in OTHERS:
        small_m(a, b).start()
    for i in range(MICRO):
        for d in XS:
            far_copy(d, i).wait_recv()
        total[i] = near[0, i].astype(F32) + far[0, i].astype(F32) + far[1, i].astype(F32) + far[2, i].astype(F32)
    W.third_b().wait_recv()
    for h in range(2):
        final[4 * h : 4 * h + 4, :, 512 : 512 + CB] = gb3[h].reshape(4, 32, CB)
    final[:, :, 512 + CB :] = W.last_a().astype(BF16).reshape(8, 32, CA)
    final[:, :, 0:512] = gate_rows[...].reshape(8, 32, 512)
    for a, b in OTHERS:
        rows_copy(a, b).start()
    gi[m] = final[m]
    for a, b in OTHERS:
        rows_copy(a, b).wait_recv()
        small_m(a, b).wait_recv()
    W.finish()
    for a, b in OTHERS:
        bc_copy(a, b).wait_send()
        rows_copy(a, b).wait_send()
        small_m(a, b).wait_send()
    for d in XS:
        small_x(d).wait_send()
        small_y(d).wait_send()
        for i in range(MICRO):
            far_copy(d, i).wait_send()
    for d in range(4):
        for i in range(MICRO):
            near_copy(d, i).wait_send()
    edge1.wait_send()
    edge2.wait_send()


def tail_call(dbc, edge_x, gate_rows, dpre, pre, ext, flags, fnext, conv, ddt, dgate, w, hid, normed, small_o, small_b):
    outs = [sds((8, 32, 1152), BF16), sds((2, 64, 2048), F32), sds((8, 48, 128), F32)]
    V = lambda *s: pltpu.VMEM(s, BF16)
    R = lambda *s: pltpu.VMEM(s, F32)
    scratch = [
        V(8, 32, T), R(2, 8, 512), R(2, 8, 128), R(2, 8, 128), R(2, TOK + 8, 640), R(8, Q, 256), V(8, Q + 8, 768), R(8, Q, 128), R(8, Q, 128), V(8, Q, 128), V(2, TOK, 512), V(2048, 1408),
        V(8, 2, 64, 2048), V(2, TOK, 2048), V(2048, 128), R(Q + 8, 640), V(2, TOK, 640), V(8, 2, 64, 2048), V(4, 2, 64, 2048), V(3, 2, 64, 2048), R(8, 640), R(8, 2048),
        R(48, 128), R(3, 48, 128), R(3, 48, 128), R(48, 128),
        V(8, 256, CA), V(8, 256, CB), V(3, 2, 256, CA), V(3, 256, CA), V(2, 256, CA), V(3, 4, 128, CB), V(3, 128, CB), V(4, 128, CB), V(2, 128, CB),
        V(8, 32, 1152),
    ]
    return pl.pallas_call(
        tail_kernel,
        name="tail",
        out_shape=outs,
        in_specs=[VM, VM, VM] + [ANY] * 5 + [VM] + [ANY] * 5 + [VM] * 2,
        out_specs=[VM] * 3,
        scratch_shapes=[*scratch, pltpu.SemaphoreType.DMA((112,)), pltpu.SemaphoreType.DMA((112,)), pltpu.SemaphoreType.DMA((10,))],
        compiler_params=pltpu.CompilerParams(collective_id=5, has_side_effects=True, vmem_limit_bytes=62 << 20),
        cost_estimate=pl.CostEstimate(flops=8 << 30, bytes_accessed=32 << 20, transcendentals=0),
    )(dbc, edge_x, gate_rows, dpre, pre, ext, flags, fnext, conv, ddt, dgate, w, hid, normed, small_o, small_b)


def from_members(v):
    r = v.shape[1]
    return v.reshape(4, 2, r, 4, 128).transpose(2, 1, 3, 0, 4).reshape(r, 4096)


def from_heads(v):
    r = v.shape[1]
    return v.reshape(4, 2, r, 4, 2).transpose(2, 1, 3, 0, 4).reshape(r, 64)


def from_rows(v):
    return v.transpose(1, 0, 2).reshape(v.shape[1], 256)


def to_members(v):
    r = v.shape[0]
    return v.reshape(r, 2, 4, 4, 128).transpose(3, 1, 0, 2, 4).reshape(8, r, 512)


def xdot(a, b, dims=NN):
    return lax.dot_general(a, b, dims, preferred_element_type=F32)


def per_device(layer_in, cotangent, segment_ids, norm_gain, in_weight, conv_weight, conv_bias, dt_bias, a_log, skip_gain, out_gain, out_weight):
    xi, yi, zi, ci = (lax.axis_index(a) for a in SEQ)
    g = 2 * xi + yi
    m = 2 * zi + ci
    lane = jnp.arange(128)

    def placed(v, width, at):
        return jnp.where(lane // width == at, jnp.tile(v, 128 // width), 0.0)

    head = lane == 2 * (g % 4) + ci
    rows = [placed(segment_ids[i, 0].astype(F32), 64, ci) for i in range(MICRO)]
    rows += [placed(norm_gain, 32, m % 4), placed(out_gain, 64, ci)]
    rows += [jnp.where(head, v, 0.0) for v in (dt_bias, a_log, skip_gain)]
    window = jnp.pad(jnp.concatenate([conv_weight, conv_bias[None]], 0), ((0, 3), (0, 60)))
    window = lax.dynamic_update_slice(jnp.zeros((8, 256), F32), window, (0, 68 * (8 * g + m) % 128))
    pack = jnp.concatenate([jnp.stack(rows), jnp.zeros((1, 128), F32), window[:, :128], window[:, 128:]], 0)
    bc = jnp.broadcast_to(in_weight[None, :, 8192:8448], (8, 32, 256))
    dt_w = in_weight[:, 8448:].reshape(32, 2, 4, 4, 2).transpose(3, 1, 0, 2, 4).reshape(8, 32, 8)
    w_send = jnp.concatenate([to_members(in_weight[:, :4096]), to_members(in_weight[:, 4096:8192]), bc, dt_w, jnp.zeros((8, 32, 120), BF16)], 2)
    (
        normed, hid_all, w_in, gate, pre, ext, delta, logs, flags, fnext, mixed, carried, states, dno, cot, w_out,
        sums, ends_all, conv, hp, og, gain, segrow,
    ) = wave(layer_in[:, 0], w_send, pack, cotangent[:, 0], out_weight)
    w_in = w_in.reshape(2048, 1408)
    norm_full = gain[0:1]
    dgate, dpre, dbc, ddt, small_o, small_b, own_branch, g_out, gate_rows = back_wave(
        mixed, carried, states, gate, dno, sums, pre, delta, logs, flags, segrow, og, hp, w_out.reshape(512, 2048), cot, normed, ends_all
    )
    dpre = dpre.reshape(MICRO, TOK, 512)
    gi, own_dn, small_sum = tail_call(
        dbc.reshape(8, 32, T), dpre[:, :8], gate_rows, dpre, pre, ext, flags, fnext, conv, ddt, dgate, w_in, hid_all, normed, small_o, small_b
    )
    gi = gi.astype(F32)
    hid_o = layer_in[:, 0].astype(F32)
    layer_out = (hid_o + own_branch).astype(BF16)
    ro = row_scale(hid_o)
    dg = own_dn * norm_full
    d_hid = ro * dg - hid_o * (ro * ro * ro) * jnp.mean(dg * hid_o, -1, keepdims=True)
    grad_in = (cotangent[:, 0].astype(F32) + d_hid).astype(BF16)
    g_in = jnp.concatenate([from_members(gi[:, :, :512]), from_members(gi[:, :, 512:1024]), from_rows(gi[:, :, 1024:1056]), from_heads(gi[:, :, 1056:1064])], 1)
    at = 8 * g + m
    g_norm = lax.dynamic_slice(small_sum[:, :16].sum(0).reshape(64, 32), (at, 0), (1, 32)).reshape(32)
    conv_s = small_sum[:, 16:41].reshape(8, 5, 640)
    conv_s = jnp.concatenate([from_members(conv_s[:, :, :512]), from_rows(conv_s[:, :, 512:544])], 1)
    conv_s = lax.dynamic_slice(conv_s, (0, 68 * at), (5, 68))
    og_s = from_members(small_sum[:, 41:45].reshape(8, 1, 512))[0]
    og_s = lax.dynamic_slice(og_s, (64 * at,), (64,))
    hd_s = from_heads(small_sum[:, 45:48, :8])
    hd_s = lax.dynamic_slice(hd_s, (0, at), (3, 1))
    return (layer_out[:, None], grad_in[:, None], g_norm, g_in, conv_s[:4], conv_s[4], hd_s[0], hd_s[1], hd_s[2], og_s, g_out)


def solution(mesh):
    fine = Mesh(mesh.devices.reshape(2, 4, 2, 4, 2), AXES)
    tok = P(None, "rep", SEQ, None)
    return jax.shard_map(
        per_device,
        mesh=fine,
        in_specs=(tok, tok, P(None, "rep", SEQ), P(SEQ), P(SEQ, None), P(None, SEQ), P(SEQ), P(SEQ), P(SEQ), P(SEQ), P(SEQ), P(SEQ, None)),
        out_specs=(tok, tok, P(SEQ), P(SEQ, None), P(None, SEQ), P(SEQ), P(SEQ), P(SEQ), P(SEQ), P(SEQ), P(SEQ, None)),
        check_vma=False,
    )
```

```python
import functools

import jax
import jax.numpy as jnp
from jax import lax
from jax.experimental import pallas as pl
from jax.experimental.pallas import tpu as pltpu
from jax.sharding import Mesh, PartitionSpec as P

EPS = 1e-05
INNER = 4096
MICRO = 2
CONV = 4352
F32 = jnp.float32
BF16 = jnp.bfloat16
AXES = ("rep", "x", "y", "z", "c")
SEQ = ("x", "y", "z", "c")
GROUPS = 8
TOK = 512
Q = 128
CH = TOK // Q

MESH = pl.DeviceIdType.MESH
ANY = pl.BlockSpec(memory_space=pl.ANY)
VM = pl.BlockSpec(memory_space=pltpu.VMEM)


class Net:
    def __init__(self, send, recv):
        self.send, self.recv, self.used, self.open = send, recv, 0, []
        self.keys = {}
        self.rep, self.x, self.y, self.z, self.c = (lax.axis_index(a) for a in AXES)
        self.ring = 2 * self.rep + self.y
        self.g = 2 * self.x + self.y
        self.m = 2 * self.z + self.c

    def at(self, dx=0, dy=0, dz=0, dc=0):
        ring = lax.rem(self.ring + dy, 4)
        return (ring // 2, lax.rem(self.x + dx, 4), lax.rem(ring, 2), lax.rem(self.z + dz, 4), lax.rem(self.c + dc, 2))

    def pair(self):
        return (self.rep, self.x, 1 - self.y, self.z, self.c)

    def across(self, dx):
        return (self.rep, lax.rem(self.x + dx, 4), 1 - self.y, self.z, self.c)

    def group(self, d):
        g = lax.rem(self.g + d, 8)
        return (self.rep, g // 2, lax.rem(g, 2), self.z, self.c)

    def member(self, dz, dc):
        return 2 * lax.rem(self.z + dz, 4) + lax.rem(self.c + dc, 2)

    def push(self, src, dst, where):
        i = self.used
        self.used += 1
        copy = pltpu.make_async_remote_copy(
            src_ref=src, dst_ref=dst, send_sem=self.send.at[i], recv_sem=self.recv.at[i], device_id=where, device_id_type=MESH
        )
        copy.start()
        self.open.append(copy)
        return copy

    def copy(self, key, src, dst, where):
        i = self.keys.setdefault(key, len(self.keys))
        return pltpu.make_async_remote_copy(
            src_ref=src, dst_ref=dst, send_sem=self.send.at[i], recv_sem=self.recv.at[i], device_id=where, device_id_type=MESH
        )

    def behind(self, d):
        return 2 * lax.rem(self.x + 4 - d, 4) + self.y

    def local(self, src, dst):
        i = self.used
        self.used += 1
        copy = pltpu.make_async_copy(src, dst, self.recv.at[i])
        copy.start()
        return copy

    def meet(self, peers):
        barrier = pltpu.get_barrier_semaphore()
        for peer in peers:
            pl.semaphore_signal(barrier, inc=1, device_id=peer, device_id_type=MESH)
        pl.semaphore_wait(barrier, len(peers))

    def finish(self):
        for copy in self.open:
            copy.wait_send()


OTHERS = [(dz, dc) for dz in (0, 1, 3, 2) for dc in (0, 1) if (dz, dc) != (0, 0)]
ZS = (0, 1, 3, 2)
XS = (1, 3, 2)
ORDER = [(d, f) for d in (2, 1, 3, 0) for f in (1, 0)]


def call(kernel, name, cid, outs, ins, spaces_in, spaces_out, sems, scratch=(), cost=1 << 20):
    return pl.pallas_call(
        kernel,
        name=name,
        out_shape=outs,
        in_specs=spaces_in,
        out_specs=spaces_out,
        scratch_shapes=[*scratch, pltpu.SemaphoreType.DMA((sems,)), pltpu.SemaphoreType.DMA((sems,))],
        compiler_params=pltpu.CompilerParams(collective_id=cid, has_side_effects=True, vmem_limit_bytes=60 << 20),
        cost_estimate=pl.CostEstimate(flops=0, bytes_accessed=cost, transcendentals=0),
    )(*ins)


def sds(shape, dtype):
    return jax.ShapeDtypeStruct(shape, dtype)


def add4(a, b):
    return a.astype(F32) + b[0].astype(F32) + b[1].astype(F32) + b[2].astype(F32)


NN = (((1,), (0,)), ((), ()))
NT = (((1,), (1,)), ((), ()))
TN = (((0,), (0,)), ((), ()))
TT = (((0,), (1,)), ((), ()))


def bdot(a, b, dims=NN):
    return lax.dot_general(a, b, dims, preferred_element_type=F32)


def parts(v, count):
    out = []
    for _ in range(count):
        p = v.astype(BF16)
        out.append(p)
        v = v - p.astype(F32)
    return out


def left_parts(v, w, count, dims=NN):
    return sum(bdot(p, w, dims) for p in parts(v, count))


def right_parts(w, v, count, dims=NN):
    return sum(bdot(w, p, dims) for p in parts(v, count))


def iota(shape, dim):
    return lax.broadcasted_iota(jnp.int32, shape, dim)


def spread_matrix():
    return (iota((128, 512), 0) == iota((128, 512), 1) // 64).astype(BF16)


def heads_of(v, eh):
    return left_parts(v, eh, 2)


def sums_of(v, eh):
    return left_parts(v, eh, 2, NT)


def lower_matrix():
    return (iota((Q, Q), 0) >= iota((Q, Q), 1)).astype(BF16)


def sigmoid(v):
    return 1.0 / (1.0 + jnp.exp(-v))


def softplus(v):
    return jnp.maximum(v, 0.0) + jnp.log1p(jnp.exp(-jnp.abs(v)))


def row_scale(h):
    return lax.rsqrt(jnp.mean(h * h, axis=-1, keepdims=True) + EPS)


def decays(L, flags):
    E = jnp.exp(L) * flags[:, 3:4]
    W = jnp.exp(L[Q - 1 : Q] - L) * flags[:, 4:5]
    return E, W


def wave_kernel(
    hid, wsend, pack, cot, outw,
    normed_h, hid_h, w_h, gate_h, pre_h, ext_h, delta_h, logs_h, flags_h, fnext_h, mixed_h, carried_h, states_h, dno_h, cot_h, wout_h,
    sums, endlog, conv, hp, og, gain, segrow,
    hid_s, halo, nrm, turned, w_s, small, proj, pre, ext, delta, logs, flags, fnext, sloc, inner, carried, states, dno, ends, rsend, rrecv, cot_s, w_o, wo_s, convt, state, total, tail, send, recv, done,
):
    eh = spread_matrix()
    n = Net(send, recv)
    g, m, x, y, z, core = n.g, n.m, n.x, n.y, n.z, n.c
    ALLX = (0,) + XS
    copies = []

    def keyed(key, src, dst, where):
        cp = n.copy(key, src, dst, where)
        copies.append(cp)
        cp.start()
        return cp

    stores = []

    def store(src, dst):
        cp = pltpu.make_async_copy(src, dst, done.at[len(stores)])
        cp.start()
        stores.append(cp)

    n.meet([n.at(dz=a, dc=b) for a, b in OTHERS] + [n.at(dx=d) for d in XS] + [n.at(dy=1), n.at(dy=3), n.group(1), n.group(7)] + [n.across(d) for d in ALLX])

    wa, sa = {}, {}
    for a, b in OTHERS:
        wa[a, b] = keyed(("wa", a, b), wsend.at[n.member(a, b)], w_s.at[g, m], n.at(dz=a, dc=b))
        sa[a, b] = keyed(("sa", a, b), pack, small.at[g, m], n.at(dz=a, dc=b))
    w_s[g, m] = wsend[m]
    small[g, m] = pack[...]
    hid_s[m] = hid[...]
    wx, wy, sx, sy = {}, {}, {}, {}

    def along_y(d, k):
        first = pl.ds(2 * lax.rem(z + 4 - ZS[k], 4), 2)
        for half, dy in ((0, 1), (1, 3)):
            part = w_s.at[n.behind(d), first, pl.ds(16 * half, 16)]
            wy[d, k, half] = keyed(("wy", d, k, half), part, part, n.at(dy=dy))

    def issue(k):
        for b in (0, 1):
            if (ZS[k], b) != (0, 0):
                wa[ZS[k], b].wait_recv()
        block = w_s.at[g, pl.ds(2 * lax.rem(z + 4 - ZS[k], 4), 2)]
        for d in XS:
            wx[k, d] = keyed(("wx", k, d), block, block, n.at(dx=d))
        along_y(0, k)

    def forward(k):
        for d in XS:
            wx[k, d].wait_recv()
            along_y(d, k)

    issue(0)
    issue(1)
    hz = {a: keyed(("hz", a), hid_s.at[m], hid_s.at[m], n.at(dz=a)) for a in (1, 3, 2)}
    hn = [keyed("hn", hid_s.at[m], hid_s.at[m], n.at(dc=1))]
    for a, b in OTHERS:
        sa[a, b].wait_recv()
    for d in XS:
        sx[d] = keyed(("sx", d), small.at[g], small.at[g], n.at(dx=d))
    sy[0] = keyed(("sy", 0), small.at[g], small.at[g], n.pair())
    forward(0)
    issue(2)
    for d in XS:
        sx[d].wait_recv()
        mine = small.at[n.behind(d)]
        sy[d] = keyed(("sy", d), mine, mine, n.pair())
    forward(1)
    issue(3)
    for d in ALLX:
        sy[d].wait_recv()

    for q in range(16):
        v = small[q // 2, 4 * (q % 2), 2:3]
        for u in range(1, 4):
            v = v + small[q // 2, 4 * (q % 2) + u, 2:3]
        gain[0:1, 128 * q : 128 * q + 128] = v
    heads3 = jnp.zeros((3, 128), F32)
    for j in range(4):
        og[0:1, 128 * j : 128 * j + 128] = small[4 * core + j, 2 * z, 3:4] + small[4 * core + j, 2 * z + 1, 3:4]
        for e in range(2):
            heads3 = heads3 + small[4 * core + j, 2 * z + e, 4:7]
    hp[...] = jnp.zeros_like(hp)
    hp[0:1] = heads3[0:1]
    hp[1:2] = jnp.where(iota((1, 128), 1) < 8, -jnp.exp(heads3[1:2]), 0.0)
    hp[2:3] = heads3[2:3]
    for q in range(34):
        v = jnp.zeros((8, 128), F32)
        for i in range(64):
            if 68 * i // 128 == q:
                v = v + small[i // 8, i % 8, 8:16]
            elif 68 * i // 128 == q - 1:
                v = v + small[i // 8, i % 8, 16:24]
        convt[q] = v
    for j in range(4):
        conv[:, 128 * j : 128 * j + 128] = convt[4 * (4 * core + j) + z]
    conv[:, 512:640] = convt[32]
    conv[:, 640:768] = convt[33]

    forward(2)
    for a in (1, 3, 2):
        hz[a].wait_recv()
        theirs = hid_s.at[2 * lax.rem(z + 4 - a, 4) + core]
        hn.append(keyed(("hf", a), theirs, theirs, n.at(dc=1)))
    cot_s[m] = cot[...]
    cz = {a: keyed(("cz", a), cot_s.at[m], cot_s.at[m], n.at(dz=a)) for a in (1, 3, 2)}
    cn = [keyed("cn", cot_s.at[m], cot_s.at[m], n.at(dc=1))]

    lane = iota((8, 128), 1)

    def chunk_row(group, i, c):
        return jnp.broadcast_to(small[group, 2 * c, i : i + 1] + small[group, 2 * c + 1, i : i + 1], (8, 128))

    for i in range(MICRO):
        before = jnp.where(g > 0, chunk_row(lax.rem(g + 7, 8), i, CH - 1), -1.0)
        after = jnp.where(g < 7, chunk_row(lax.rem(g + 1, 8), i, 0), -2.0)
        rows = [before] + [chunk_row(g, i, c) for c in range(CH)] + [after]
        for c in range(CH):
            prv, cur, nxt = rows[c : c + 3]
            here, ahead = [], []
            for d in (3, 2, 1):
                back = jnp.where(lane < d, pltpu.roll(prv, d, 1), pltpu.roll(cur, d, 1))
                here.append((back == cur).astype(F32))
                on = jnp.where(lane >= 128 - d, pltpu.roll(nxt, 128 - d, 1), pltpu.roll(cur, 128 - d, 1))
                ahead.append((on == cur).astype(F32))
            here += [(cur == prv[:, 127:128]).astype(F32), (cur == cur[:, 127:128]).astype(F32), cur]
            sub = iota((128, 128), 0)
            for rows_of, to in ((here, flags), (ahead, fnext)):
                v = jnp.zeros((128, 128), F32)
                for r, row in enumerate(rows_of):
                    v = jnp.where(sub == r, jnp.broadcast_to(row[0:1], (128, 128)), v)
                to[CH * i + c] = v.T
            segrow[CH * i + c] = cur[0:1]

    forward(3)
    w_o[g] = outw[...]
    ox = {d: keyed(("ox", d), w_o.at[g], w_o.at[g], n.at(dx=d)) for d in XS}
    oy = {}

    def out_y(d):
        for half, dy in ((0, 1), (1, 3)):
            part = w_o.at[n.behind(d), pl.ds(32 * half, 32)]
            oy[d, half] = keyed(("oy", d, half), part, part, n.at(dy=dy))

    out_y(0)
    for cp in hn:
        cp.wait_recv()
    edge = keyed("edge", hid_s.at[7, :, pl.ds(48, 16)], halo, n.group(1))

    gv = gain[0:1]

    def norm(k, carry):
        for i in range(MICRO):
            h = hid_s[pl.ds(2 * k, 2), i].reshape(Q, 2048).astype(F32)
            v = h * row_scale(h) * gv
            nrm[i, pl.ds(pl.multiple_of(16 + Q * k, 16), Q)] = v.astype(BF16)
            turned[:, pl.ds(pl.multiple_of(TOK * i + Q * k, Q), Q)] = v.T.astype(BF16)
        return carry

    lax.fori_loop(0, CH, norm, 0)
    edge.wait_recv()
    for i in range(MICRO):
        h = halo[i].astype(F32)
        nrm[i, 0:16] = (h * row_scale(h) * gv).astype(BF16)
    store(turned, normed_h)

    def project(side, first):
        for i in range(MICRO):
            for lo in range(0, 1408, 256):
                hi = min(lo + 256, 1408)
                v = 0.0 if first else proj[i, :, lo:hi]
                for k in range(4):
                    q = 2 * k + side
                    v = v + bdot(nrm[i, :, pl.ds(pl.multiple_of(256 * q, 256), 256)], w_s[q, :, :, lo:hi].reshape(256, hi - lo))
                proj[i, :, lo:hi] = v

    project(y, True)
    for d in ALLX:
        for k in range(4):
            for half in (0, 1):
                wy[d, k, half].wait_recv()
    project(1 - y, False)
    for d in XS:
        ox[d].wait_recv()
        out_y(d)
    store(w_s, w_h)
    store(hid_s, hid_h)
    store(flags, flags_h)
    store(fnext, fnext_h)

    def front(i, c):
        at = CH * i + c
        rows = pl.ds(pl.multiple_of(16 + Q * c, 16), Q)
        f = flags[at]
        xbc = proj[i, rows, 512:1280].astype(BF16).astype(F32)
        tail[8:] = xbc
        acc = conv[4:5] + conv[3:4] * xbc
        for k in range(3):
            acc = acc + conv[k : k + 1] * tail[5 + k : 5 + k + Q] * f[:, k : k + 1]
        pre[at] = acc
        ext[at] = tail[...].astype(BF16)
        d = softplus(proj[i, rows, 1280:1408] + hp[0:1])
        delta[at] = d
        L = right_parts(lower_matrix(), d * hp[1:2], 3)
        logs[at] = L
        E, W = decays(L, f)
        xv = acc[:, :512]
        X = xv * sigmoid(xv)
        b = acc[:, 512:640]
        B = (b * sigmoid(b)).astype(BF16)
        S = right_parts(B, heads_of(W * d, eh) * X, 2, TN)
        sloc[at] = S
        last = heads_of(E[Q - 8 :], eh)
        state[...] = last[7:8] * state[...] + S
        tail[0:8] = tail[Q : Q + 8]
        total[...] = total[...] + L[Q - 1 : Q]

    ex, lx, ly = {}, {}, {}
    for i in range(MICRO):
        tail[0:8] = proj[i, 8:16, 512:1280].astype(BF16).astype(F32)
        state[...] = jnp.zeros_like(state)
        total[...] = jnp.zeros_like(total)
        lax.fori_loop(0, CH, lambda c, carry, i=i: (front(i, c), carry)[1], 0)
        ends[g, i] = state[...].astype(BF16)
        lt = parts(jnp.broadcast_to(heads_of(jnp.broadcast_to(total[...], (8, 128)), eh)[0:1], (16, 512)), 3)
        seg = jnp.broadcast_to(segrow[CH * i + CH - 1][:, 127:128], (16, 512))
        high = jnp.floor(seg * (1.0 / 64.0))
        r = iota((16, 512), 0)
        v = jnp.zeros((16, 512), BF16)
        for k, row in enumerate(lt + [high.astype(BF16), (seg - 64.0 * high).astype(BF16)]):
            v = jnp.where(r == k, row, v)
        endlog[g, i] = v
        for d in XS:
            lx[i, d] = keyed(("lx", i, d), endlog.at[g, i], endlog.at[g, i], n.at(dx=d))
        for d in ALLX:
            ly[i, d] = keyed(("ly", i, d), endlog.at[g, i], endlog.at[g, i], n.across(d))
        for d in XS:
            ex[i, d] = keyed(("ex", i, d), ends.at[g, i], ends.at[g, i], n.at(dx=d))
    store(pre, pre_h)
    store(ext, ext_h)
    store(delta, delta_h)
    store(logs, logs_h)
    for i in range(MICRO):
        store(proj.at[i, pl.ds(16, TOK), pl.ds(0, 512)], gate_h.at[i])

    def states_on(i):
        for d in XS:
            lx[i, d].wait_recv()
        for d in ALLX:
            ly[i, d].wait_recv()
        for d in XS:
            ex[i, d].wait_recv()
        rsend[i] = entering(n, ends, endlog, 1, 0, i).astype(BF16)
        return keyed(("r", i), rsend.at[i], rrecv.at[i], n.pair())

    def inside(at, carry):
        L = logs[at]
        X, B, C = activations(pre[at])
        U = (heads_of(delta[at], eh) * X).astype(BF16)
        psi = bdot(C, B, NT)
        keep = same_mask(flags[at], segrow[at])
        LT = L.T
        for j in range(4):
            u = pair_halves(U[:, 128 * j : 128 * j + 128])
            v = jnp.zeros((Q, 128), F32)
            for e in range(2):
                h = 2 * j + e
                K = jnp.where(keep, jnp.exp(L[:, h : h + 1] - LT[h : h + 1]), 0.0)
                v = v + bdot((psi * K).astype(BF16), u[e])
            inner[at, :, 128 * j : 128 * j + 128] = v
        return carry

    lax.fori_loop(0, 4, inside, 0)
    r0 = states_on(0)
    for d in ALLX:
        for half in (0, 1):
            oy[d, half].wait_recv()
    swap = keyed("swap", w_o.at[pl.ds(4 * (1 - core), 4)], wo_s.at[:, core], n.at(dc=1))
    for k in range(4):
        wo_s[k, core] = w_o[4 * core + k]
    for a in (1, 3, 2):
        cz[a].wait_recv()
        theirs = cot_s.at[2 * lax.rem(z + 4 - a, 4) + core]
        cn.append(keyed(("cf", a), theirs, theirs, n.at(dc=1)))
    lax.fori_loop(4, 8, inside, 0)
    r1 = states_on(1)
    swap.wait_recv()
    for cp in cn:
        cp.wait_recv()
    store(cot_s, cot_h)
    store(wo_s, wout_h)
    for i in range(MICRO):
        d = bdot(cot_s[:, i].reshape(TOK, 2048), wo_s[...].reshape(512, 2048), NT)
        for c in range(CH):
            dno[CH * i + c] = d[Q * c : Q * c + Q]
    store(dno, dno_h)

    def mix(i, c):
        at = CH * i + c
        E, _ = decays(logs[at], flags[at])
        X, _, C = activations(pre[at])
        more = heads_of(jnp.concatenate([E, jnp.broadcast_to(hp[2:3], (8, 128))], 0), eh)
        Ex, skip = more[:Q], more[Q : Q + 1]
        S = state[...]
        states[at, 0] = S
        Yc = Ex * bdot(C, S.astype(BF16))
        carried[at] = Yc
        mx = inner[at] + Yc + skip * X
        inner[at] = mx
        after = Ex[Q - 1 : Q] * S + sloc[at]
        state[...] = after
        states[at, 1] = after
        gt = proj[i, pl.ds(pl.multiple_of(16 + Q * c, 16), Q), 0:512]
        gated = mx * (gt * sigmoid(gt))
        ones = jnp.ones((8, 512), BF16)
        sums[m, at, 0:8] = right_parts(ones, gated * gated, 2, NT)
        sums[m, at, 8:16] = right_parts(ones, dno[at] * og[0:1] * gated, 2, NT)

    sm = []
    for i, r in ((0, r0), (1, r1)):
        r.wait_recv()
        state[...] = entering(n, ends, endlog, 0, 0, i) + rrecv[i].astype(F32)
        lax.fori_loop(0, CH, lambda c, carry, i=i: (mix(i, c), carry)[1], 0)
        mine = sums.at[m, pl.ds(CH * i, CH)]
        for a, b in OTHERS:
            sm.append(keyed(("sm", i, a, b), mine, mine, n.at(dz=a, dc=b)))
    store(inner, mixed_h)
    store(carried, carried_h)
    store(states, states_h)
    for cp in sm:
        cp.wait_recv()
    for cp in copies:
        cp.wait_send()
    for cp in stores:
        cp.wait()


def wave(hid, wsend, pack, cot, outw):
    V = lambda *s: pltpu.VMEM(s, BF16)
    R = lambda *s: pltpu.VMEM(s, F32)
    outs = [
        sds((2048, T), BF16), sds((8, 2, 64, 2048), BF16), sds((8, 8, 32, 1408), BF16), sds((2, TOK, 512), F32), sds((8, Q, 768), F32), sds((8, Q + 8, 768), BF16), sds((8, Q, 128), F32), sds((8, Q, 128), F32),
        sds((8, Q, 128), F32), sds((8, Q, 128), F32), sds((8, Q, 512), F32), sds((8, Q, 512), F32), sds((8, 2, 128, 512), F32), sds((8, Q, 512), F32), sds((8, 2, 64, 2048), BF16), sds((4, 2, 64, 2048), BF16),
        sds((8, 8, 16, 128), F32), sds((8, 2, 16, 512), BF16), sds((8, 768), F32), sds((8, 128), F32), sds((8, 512), F32), sds((8, 2048), F32), sds((8, 1, 128), F32),
    ]
    scratch = [
        V(8, 2, 64, 2048), V(2, 16, 2048), V(2, TOK + 16, 2048), V(2048, T), V(8, 8, 32, 1408), R(8, 8, 24, 128), R(2, TOK + 16, 1408), R(8, Q, 768), V(8, Q + 8, 768), R(8, Q, 128), R(8, Q, 128), R(8, Q, 128), R(8, Q, 128),
        R(8, 128, 512), R(8, Q, 512), R(8, Q, 512), R(8, 2, 128, 512), R(8, Q, 512), V(8, 2, 128, 512), V(2, 128, 512), V(2, 128, 512), V(8, 2, 64, 2048), V(8, 64, 2048), V(4, 2, 64, 2048),
        R(34, 8, 128), R(128, 512), R(1, 128), R(Q + 8, 768),
    ]
    return pl.pallas_call(
        wave_kernel,
        name="wave",
        out_shape=outs,
        in_specs=[VM] * 5,
        out_specs=[ANY] * 16 + [VM] * 7,
        scratch_shapes=[*scratch, pltpu.SemaphoreType.DMA((144,)), pltpu.SemaphoreType.DMA((144,)), pltpu.SemaphoreType.DMA((24,))],
        compiler_params=pltpu.CompilerParams(collective_id=1, has_side_effects=True, vmem_limit_bytes=64 * 1024 * 1024 - 65536),
        cost_estimate=pl.CostEstimate(flops=8 << 30, bytes_accessed=32 << 20, transcendentals=0),
    )(hid, wsend, pack, cot, outw)


def entering(n, everyone, logs, target, direction, micro):
    to = 2 * n.x + (1 - n.y if target else n.y)
    lt, last = [], []
    for q in range(8):
        v = logs[q, micro].astype(F32)
        lt.append(v[0:1] + v[1:2] + v[2:3])
        last.append(64.0 * v[3:4] + v[4:5])
    zero = jnp.zeros((1, 512), F32)
    edge = zero
    for r in range(8):
        edge = edge + jnp.where((r == to) if direction else (r == to - 1), last[r], zero)
    total = jnp.zeros((128, 512), F32)
    for k in range(4):
        q = 2 * k + n.y
        log = zero
        for r in range(8):
            between = (r > to) & (r < q) if direction else (r > q) & (r < to)
            log = log + jnp.where(between, lt[r], zero)
        if direction:
            there = jnp.where(n.y == 0, last[max(2 * k - 1, 0)], last[2 * k])
        else:
            there = jnp.where(n.y == 0, last[2 * k], last[2 * k + 1])
        reached = jnp.where((q > to) if direction else (q < to), 1.0, 0.0)
        total = total + jnp.where(there == edge, jnp.exp(log) * reached, zero) * everyone[q, micro].astype(F32)
    return total


def same_mask(flags, segrow):
    return (flags[:, 5:6] == segrow) & (iota((Q, Q), 0) >= iota((Q, Q), 1))


def activations(pre):
    a = pre * sigmoid(pre)
    return a[:, :512], a[:, 512:640].astype(BF16), a[:, 640:768].astype(BF16)


def pair_halves(v):
    low_half = iota(v.shape, 1) < 64
    zero = jnp.zeros_like(v)
    return jnp.where(low_half, v, zero), jnp.where(low_half, zero, v)


T = MICRO * TOK


def column(row):
    return jnp.concatenate([jnp.broadcast_to(row, (128, 128)).T] * 4, 1)


def pick_matrix(rows, start, count, shift, dtype=BF16):
    r, l = iota((rows, 128), 0), iota((rows, 128), 1)
    return ((r - start == l - shift) & (l >= shift) & (l < shift + count)).astype(dtype)


class Reduce:
    def __init__(self, n, key, a, b, a1, a2, pa, b1, b2, pb, b3):
        self.n, self.key, self.a, self.b = n, key, a, b
        self.a1, self.a2, self.pa, self.b1, self.b2, self.pb, self.b3 = a1, a2, pa, b1, b2, pb, b3
        self.half = a.shape[1] // 2

    def group(self, d, f):
        n = self.n
        return 2 * lax.rem(n.x + d, 4) + lax.rem(n.y + f, 2)

    def first_a(self, d, f):
        return self.n.copy((self.key, "a1", d, f), self.a.at[self.group(d, f)], self.a1.at[d - 1, f], self.n.at(dx=d))

    def first_b(self, d, e):
        n = self.n
        rep = lax.rem(n.ring + e, 4) // 2
        rows = pl.ds(pl.multiple_of(self.half * rep, self.half), self.half)
        return n.copy((self.key, "b1", d, e), self.b.at[self.group(d, e % 2), rows], self.b1.at[e - 1, lax.rem(n.x + d, 4)], n.at(dy=e))

    def send_a(self, d, f):
        if d:
            self.first_a(d, f).start()

    def send_b(self, d, f):
        for e in (1, 3) if f else (2,):
            self.first_b(d, e).start()

    def second_a(self, e):
        return self.n.copy((self.key, "a2", e), self.pa.at[e % 2], self.a2.at[e - 1], self.n.at(dy=e))

    def second_b(self, d):
        return self.n.copy((self.key, "b2", d), self.pb.at[lax.rem(self.n.x + d, 4)], self.b2.at[d - 1], self.n.at(dx=d))

    def third_b(self):
        return self.n.copy((self.key, "b3"), self.b3.at[self.n.rep], self.b3.at[self.n.rep], self.n.at(dy=2))

    def middle_a(self, f):
        for d in XS:
            self.first_a(d, f).wait_recv()
        self.pa[f] = add4(self.a[self.group(0, f)], self.a1[:, f]).astype(BF16)
        for e in (1, 3) if f else (2,):
            self.second_a(e).start()

    def middle_b(self):
        n = self.n
        rows = pl.ds(pl.multiple_of(self.half * n.rep, self.half), self.half)
        for d in (2, 1, 3, 0):
            for e in XS:
                self.first_b(d, e).wait_recv()
            k = lax.rem(n.x + d, 4)
            self.pb[k] = add4(self.b[2 * k + n.y, rows], self.b1[:, k]).astype(BF16)
            if d:
                self.second_b(d).start()

    def last_b(self):
        for d in XS:
            self.second_b(d).wait_recv()
        self.b3[self.n.rep] = add4(self.pb[self.n.x], self.b2).astype(self.b3.dtype)
        self.third_b().start()

    def last_a(self):
        for e in XS:
            self.second_a(e).wait_recv()
        return add4(self.pa[0], self.a2)

    def finish(self):
        for d in XS:
            for f in (0, 1):
                self.first_a(d, f).wait_send()
            self.second_b(d).wait_send()
        for e in XS:
            for d in range(4):
                self.first_b(d, e).wait_send()
            self.second_a(e).wait_send()
        self.third_b().wait_send()


def fetcher(sems):
    loads = {}

    def fetch(key, src, dst):
        loads[key] = pltpu.make_async_copy(src, dst, sems.at[len(loads)])
        loads[key].start()

    return loads, fetch


C1 = 256


def back_wave_kernel(
    mixed_h, carried_h, states_h, gate_h, dno_h, sums, pre_h, delta_h, logs_h, flags_h, segrow, og, hp, wout_h, normed, endlog,
    dgate, dpre_h, dbc, ddt, small_o, small_b, total, gate_rows, turned,
    mixed, carried, states, gate, dno, pre, delta, logs, flags, wout, nout, dmix, tloc, dbi, starts, rsend, rrecv, rows, part, near, far,
    wa, wb, wa1, wa2, wpa, wb1, wb2, wpb, wb3, state, send, recv, load, tile_sem,
):
    eh = spread_matrix()
    n = Net(send, recv)
    g, m, core, z = n.g, n.m, n.c, n.z
    W = Reduce(n, "w", wa, wb, wa1, wa2, wpa, wb1, wb2, wpb, wb3)
    loads, fetch = fetcher(load)
    for i in range(MICRO):
        some = pl.ds(CH * i, CH)
        for key, src, dst in (("mixed", mixed_h, mixed), ("gate", gate_h, gate), ("dno", dno_h, dno), ("pre", pre_h, pre), ("logs", logs_h, logs), ("flags", flags_h, flags)):
            fetch((key, i), src.at[some], dst.at[some])
    fetch("wout", wout_h, wout)
    for key, src, dst in (("delta", delta_h, delta), ("states", states_h, states), ("carried", carried_h, carried)):
        fetch(key, src, dst)

    def start_x(i, d):
        return n.copy(("sx", i, d), starts.at[g, i], starts.at[g, i], n.at(dx=d))

    def part_y(i):
        return n.copy(("r", i), rsend.at[i], rrecv.at[i], n.pair())

    def near_copy(d, i):
        return n.copy(("near", d, i), part.at[2 * lax.rem(z + d, 4) + 1 - core, i], near.at[d, i], n.at(dc=1))

    def far_copy(d, i):
        return n.copy(("far", d, i), near.at[d, i], far.at[d - 1, i], n.at(dz=d))

    n.meet([n.at(dz=a) for a in (1, 3, 2)] + [n.at(dc=1)] + [n.at(dx=d) for d in XS] + [n.at(dy=d) for d in XS])
    small_o[...] = jnp.zeros_like(small_o)
    small_b[...] = jnp.zeros_like(small_b)

    def outward(i, k):
        c = CH - 1 - k
        at = CH * i + c
        tot = sums[0, at]
        for q in range(1, 8):
            tot = tot + sums[q, at]
        r = column(lax.rsqrt(tot[0:1] / INNER + EPS))
        s2 = column(tot[8:9] / INNER)
        gt = gate[at]
        s = sigmoid(gt)
        sg = gt * s
        mix = mixed[at]
        gated = mix * sg
        dn = dno[at]
        n0 = gated * r
        rows = pl.ds(pl.multiple_of(Q * c, Q), Q)
        nb = n0 * og[0:1]
        nout[i, rows] = nb.astype(BF16)
        turned[:, pl.ds(pl.multiple_of(Q * at, Q), Q)] = nb.T.astype(BF16)
        d_gated = r * (dn * og[0:1] - n0 * r * s2)
        dm = d_gated * sg
        dmix[at] = dm
        dgate[i, rows] = (d_gated * mix * (s * (1.0 + gt * (1.0 - s)))).astype(BF16)
        x = pre[at, :, :512]
        X = x * sigmoid(x)
        cc = pre[at, :, 640:768]
        C = (cc * sigmoid(cc)).astype(BF16)
        small_o[0:1] += jnp.sum(dn * n0, 0, keepdims=True)
        small_o[1:2] += jnp.sum(X * dm, 0, keepdims=True)
        E, _ = decays(logs[at], flags[at])
        Ex = heads_of(E, eh)
        G = right_parts(C, Ex * dm, 2, TN)
        tloc[at] = G
        state[...] = Ex[Q - 1 : Q] * state[...] + G

    for i in range(MICRO):
        for key in ("mixed", "gate", "dno", "pre", "logs", "flags"):
            loads[key, i].wait()
        state[...] = jnp.zeros_like(state)
        lax.fori_loop(0, CH, lambda k, carry, i=i: (outward(i, k), carry)[1], 0)
        starts[g, i] = state[...].astype(BF16)
        for d in XS:
            start_x(i, d).start()
        if i == 0:
            loads["wout"].wait()
        part[:, i] = bdot(nout[i], wout[...]).astype(BF16).reshape(8, 64, 2048)
        for d in (1, 3, 2, 0):
            near_copy(d, i).start()

    def bring(k):
        at = pl.ds(pl.multiple_of(256 * W.group(*ORDER[k]), 256), 256)
        return pltpu.make_async_copy(normed.at[at], rows.at[k % 2], tile_sem.at[k % 2])

    def states_on(i):
        for d in XS:
            start_x(i, d).wait_recv()
        rsend[i] = entering(n, starts, endlog, 1, 1, i).astype(BF16)
        part_y(i).start()

    def tokens_on(i):
        for d in (1, 3, 2, 0):
            near_copy(d, i).wait_recv()
            there = 2 * lax.rem(z + d, 4) + core
            near[d, i] = (part[there, i].astype(F32) + near[d, i].astype(F32)).astype(BF16)
            if d:
                far_copy(d, i).start()

    bring(0).start()
    for k, (d, f) in enumerate(ORDER):
        bring(k).wait()
        if k < 7:
            bring(k + 1).start()
        q = W.group(d, f)
        v = bdot(rows[k % 2], dgate[...].reshape(T, 512))
        wa[q] = v[:, 0:C1].astype(BF16)
        wb[q] = v[:, C1:].astype(BF16)
        W.send_a(d, f)
        W.send_b(d, f)
        if k == 1:
            states_on(0)
            tokens_on(0)
        if k == 5:
            states_on(1)
            tokens_on(1)

    loads["delta"].wait()
    loads["states"].wait()
    loads["carried"].wait()

    def inside(at, carry):
        L = logs[at]
        f = flags[at]
        E, _ = decays(L, f)
        X, B, C = activations(pre[at])
        more = heads_of(jnp.concatenate([E, delta[at]], 0), eh)
        Ex, dx = more[:Q], more[Q:]
        Ub = (dx * X).astype(BF16)
        dm = dmix[at]
        dmb = dm.astype(BF16)
        psi = bdot(C, B, NT)
        keep = same_mask(f, segrow[at])
        LT = L.T
        dpsi = jnp.zeros((Q, Q), F32)
        for j in range(4):
            js = slice(128 * j, 128 * j + 128)
            u = pair_halves(Ub[:, js])
            y = pair_halves(dmb[:, js])
            acc = jnp.zeros((Q, 128), F32)
            for e in range(2):
                h = 2 * j + e
                K = jnp.where(keep, jnp.exp(L[:, h : h + 1] - LT[h : h + 1]), 0.0)
                acc = acc + bdot((psi * K).astype(BF16), y[e], TN)
                dpsi = dpsi + bdot(y[e], u[e], NT) * K
            dno[at, :, js] = acc
        dpb = dpsi.astype(BF16)
        dbi[at, 0:128] = bdot(C, dpb, TN)
        dbi[at, 128:256] = bdot(B, dpb, TT) + bdot(states[at, 0].astype(BF16), (Ex * dm).astype(BF16), NT)
        return carry

    lax.fori_loop(0, 8, inside, 0)
    for i in (0, 1):
        part_y(i).wait_recv()

    def inward(i, k):
        c = CH - 1 - k
        at = CH * i + c
        L = logs[at]
        d = delta[at]
        E, W_ = decays(L, flags[at])
        p = pre[at, :, 0:512]
        s = sigmoid(p)
        X = p * s
        bb = pre[at, :, 512:640]
        B = (bb * sigmoid(bb)).astype(BF16)
        more = heads_of(jnp.concatenate([E[Q - 8 :], W_, d, jnp.broadcast_to(hp[2:3], (8, 128))], 0), eh)
        Elast, Wx, dx, skip = more[7:8], more[8 : 8 + Q], more[8 + Q : 8 + 2 * Q], more[8 + 2 * Q : 9 + 2 * Q]
        U = dx * X
        dm = dmix[at]
        Yc = carried[at]
        Yi = mixed[at] - Yc - skip * X
        G = state[...]
        Gb = G.astype(BF16)
        dUi = dno[at]
        dUc = Wx * bdot(B, Gb)
        dU = dUi + dUc
        lanes = pl.ds(pl.multiple_of(Q * at, Q), Q)
        dbc[0:128, lanes] = (dbi[at, 0:128] + bdot(Gb, (Wx * U).astype(BF16), NT)).astype(BF16)
        dbc[128:256, lanes] = dbi[at, 128:256].astype(BF16)
        dL = sums_of(dm.astype(BF16).astype(F32) * Yi + dm * Yc - U.astype(BF16).astype(F32) * dUi - U * dUc, eh)
        end = sums_of(jnp.broadcast_to(jnp.sum(G * states[at, 1], 0, keepdims=True), (8, 512)), eh)[0:1]
        upper = (iota((Q, Q), 0) <= iota((Q, Q), 1)).astype(BF16)
        dstep = right_parts(upper, dL, 3) + end
        rate = hp[1:2]
        dr = (sums_of(dU * X, eh) + dstep * rate) * (1.0 - jnp.exp(-d))
        ddt[at] = dr.astype(BF16)
        small_b[0:1] += jnp.sum(dr, 0, keepdims=True)
        small_b[1:2] += jnp.sum(dstep * d * rate, 0, keepdims=True)
        gate[at] = (dx * dU + skip * dm) * (s * (1.0 + p * (1.0 - s)))
        state[...] = Elast * G + tloc[at]

    store = pltpu.make_async_copy(gate, dpre_h, load.at[0])
    for i in range(MICRO):
        state[...] = entering(n, starts, endlog, 0, 1, i) + rrecv[i].astype(F32)
        lax.fori_loop(0, CH, lambda k, carry, i=i: (inward(i, k), carry)[1], 0)
    store.start()

    W.middle_b()
    W.middle_a(1)
    W.middle_a(0)
    for i in range(MICRO):
        for d in XS:
            far_copy(d, i).wait_recv()
        total[i] = near[0, i].astype(F32) + far[0, i].astype(F32) + far[1, i].astype(F32) + far[2, i].astype(F32)
    W.last_b()
    gate_rows[:, 0:C1] = W.last_a().astype(BF16)
    W.third_b().wait_recv()
    for h in range(2):
        gate_rows[128 * h : 128 * h + 128, C1:] = wb3[h]
    W.finish()
    store.wait()
    for i in range(MICRO):
        part_y(i).wait_send()
        for d in XS:
            start_x(i, d).wait_send()
            far_copy(d, i).wait_send()
        for d in range(4):
            near_copy(d, i).wait_send()


def back_wave(mixed, carried, states, gate, dno, sums, pre, delta, logs, flags, segrow, og, hp, wout, normed, endlog):
    outs = [
        sds((2, TOK, 512), BF16), sds((8, Q, 512), F32), sds((256, T), BF16), sds((8, Q, 128), BF16), sds((8, 512), F32), sds((8, 128), F32), sds((2, 64, 2048), F32),
        sds((256, 512), BF16), sds((512, T), BF16),
    ]
    V = lambda *s: pltpu.VMEM(s, BF16)
    R = lambda *s: pltpu.VMEM(s, F32)
    return pl.pallas_call(
        back_wave_kernel,
        name="back_wave",
        out_shape=outs,
        in_specs=[ANY] * 5 + [VM] + [ANY] * 4 + [VM] * 3 + [ANY] * 2 + [VM],
        out_specs=[VM, ANY] + [VM] * 7,
        scratch_shapes=[
            R(8, Q, 512), R(8, Q, 512), R(8, 2, 128, 512), R(8, Q, 512), R(8, Q, 512), R(8, Q, 768), R(8, Q, 128), R(8, Q, 128), R(8, Q, 128), V(512, 2048),
            V(2, TOK, 512), R(8, Q, 512), R(8, 128, 512), R(8, 256, 128), V(8, 2, 128, 512), V(2, 128, 512), V(2, 128, 512), V(2, 256, T), V(8, 2, 64, 2048),
            V(4, 2, 64, 2048), V(3, 2, 64, 2048),
            V(8, 256, C1), V(8, 256, C1), V(3, 2, 256, C1), V(3, 256, C1), V(2, 256, C1), V(3, 4, 128, C1), V(3, 128, C1), V(4, 128, C1), V(2, 128, C1), R(128, 512),
            pltpu.SemaphoreType.DMA((96,)), pltpu.SemaphoreType.DMA((96,)), pltpu.SemaphoreType.DMA((16,)), pltpu.SemaphoreType.DMA((2,)),
        ],
        compiler_params=pltpu.CompilerParams(collective_id=4, has_side_effects=True, vmem_limit_bytes=62 << 20),
        cost_estimate=pl.CostEstimate(flops=8 << 30, bytes_accessed=32 << 20, transcendentals=0),
    )(mixed, carried, states, gate.reshape(8, Q, 512), dno, sums, pre, delta, logs, flags, segrow, og, hp, wout, normed, endlog)


CB = 256
CA = 640 - CB


def tail_kernel(
    dbc, edge_x, gate_rows, turned, cot, dpre, pre, ext, flags, fnext, conv, ddt, dgate, w, hid, normed, small_o, small_b,
    gi, g_out, total, small_all,
    bc_s, ex_s, eb_src, eb_s, dps, pre_s, ext_s, fl_s, fn_s, ddt_s, dg_s, w_s, hid_s, nm_s, wt, e_s, dproj, part, near, far, conv_acc, gnorm,
    s0, s1, s2, sx, ga, gb, ga1, ga2, gpa, gb1, gb2, gpb, gb3, cot_s, gsw, oa, ob, oa1, oa2, opa, ob1, ob2, opb, ob3, oin, final, send, recv, load, tile_sem,
):
    n = Net(send, recv)
    x, y, z, c, m = n.x, n.y, n.z, n.c, n.m
    loads = {}

    def fetch(key, src, dst):
        loads[key] = pltpu.make_async_copy(src, dst, load.at[len(loads)])
        loads[key].start()

    fetch("pre", pre.at[:, :, pl.ds(512, 256)], pre_s)
    fetch("w", w, w_s)
    fetch("dpre", dpre, dps.at[:, pl.ds(0, TOK), pl.ds(0, 512)])
    fetch("ext", ext, ext_s)
    fetch("flags", flags, fl_s)
    fetch("fnext", fnext, fn_s)
    fetch("ddt", ddt, ddt_s)
    fetch("normed", normed, nm_s)
    fetch("dgate", dgate, dg_s)
    fetch("hid", hid, hid_s)
    n.meet([n.at(dz=a, dc=b) for a, b in OTHERS] + [n.at(dx=d) for d in XS] + [n.at(dy=d) for d in XS] + [n.group(1), n.group(7)])

    def bc_copy(a, b):
        return n.copy(("bc", a, b), dbc.at[n.member(a, b)], bc_s.at[m], n.at(dz=a, dc=b))

    edge1 = n.copy("edge1", edge_x, ex_s, n.group(7))
    edge2 = n.copy("edge2", eb_src, eb_s, n.group(7))

    def near_copy(d, i):
        return n.copy(("near", d, i), part.at[2 * lax.rem(z + d, 4) + 1 - c, i], near.at[d, i], n.at(dc=1))

    def far_copy(d, i):
        return n.copy(("far", d, i), near.at[d, i], far.at[d - 1, i], n.at(dz=d))

    def small_x(d):
        return n.copy(("sx", d), s0, s1.at[d - 1], n.at(dx=d))

    def small_y(d):
        return n.copy(("sy", d), sx, s2.at[d - 1], n.at(dy=d))

    def small_m(a, b):
        return n.copy(("sm", a, b), small_all.at[m], small_all.at[m], n.at(dz=a, dc=b))

    def rows_copy(a, b):
        return n.copy(("rows", a, b), final.at[n.member(a, b)], gi.at[m], n.at(dz=a, dc=b))

    O = Reduce(n, "o", oa, ob, oa1, oa2, opa, ob1, ob2, opb, ob3)
    swap = n.copy("swap", gsw.at[:, 1 - c], oin, n.at(dc=1))
    W = Reduce(n, "w", ga, gb, ga1, ga2, gpa, gb1, gb2, gpb, gb3)

    for a, b in OTHERS:
        bc_copy(a, b).start()
    edge1.start()
    bc_s[m] = dbc[m]

    def bring(k):
        return pltpu.make_async_copy(cot.at[:, :, :, pl.ds(256 * k, 256)], cot_s.at[k % 2], tile_sem.at[k % 2])

    bring(0).start()
    for k in range(8):
        bring(k).wait()
        if k < 7:
            bring(k + 1).start()
        v = sum(bdot(turned[:, TOK * i : TOK * i + TOK], cot_s[k % 2, :, i].reshape(TOK, 256)) for i in range(MICRO))
        gsw[:, :, :, 256 * k : 256 * k + 256] = v.astype(BF16).reshape(4, 2, 64, 256)
    swap.start()
    for j in range(4):
        oa[4 * c + j] = gsw[j, c, :, 0:1024]
        ob[4 * c + j] = gsw[j, c, :, 1024:2048]

    pick = pick_matrix(256, 32 * m, 32, 0)
    loads["w"].wait()
    wt[...] = (bdot(w_s[:, 1024:1280], pick) + bdot(w_s[:, 1280:1408], pick_matrix(128, 0, 8, 32))).astype(BF16)
    cw = jnp.concatenate([conv[:, 0:512], left_parts(conv[:, 512:768], pick, 3)], 1)
    swap.wait_recv()
    for j in range(4):
        oa[4 * (1 - c) + j] = oin[j, :, 0:1024]
        ob[4 * (1 - c) + j] = oin[j, :, 1024:2048]
    for d, f in ORDER:
        O.send_a(d, f)
        O.send_b(d, f)

    for key in ("pre", "dpre"):
        loads[key].wait()
    for a, b in OTHERS:
        bc_copy(a, b).wait_recv()
    eye = pick_matrix(32, 0, 32, 0)

    def bc_chunk(i, k):
        t = CH * i + k
        tot = bc_s[0, :, Q * t : Q * t + Q].astype(F32)
        for q in range(1, 8):
            tot = tot + bc_s[q, :, Q * t : Q * t + Q].astype(F32)
        d = left_parts(tot, eye, 2, TN)
        p = left_parts(pre_s[t], pick, 2)
        s = sigmoid(p)
        dps[i, Q * k : Q * k + Q, 512:640] = d * (s * (1.0 + p * (1.0 - s)))

    for i in range(MICRO):
        bc_chunk(i, 0)
        eb_src[i] = dps[i, 0:8, 512:640]
    edge2.start()
    for i in range(MICRO):
        for k in range(1, CH):
            bc_chunk(i, k)
    for key in ("ext", "flags", "fnext", "ddt"):
        loads[key].wait()
    conv_acc[...] = jnp.zeros_like(conv_acc)
    pick_dt = pick_matrix(128, 0, 8, 32)

    def conv_chunk(i, k):
        t = CH * i + k
        e_s[:, 0:512] = ext_s[t, :, 0:512].astype(F32)
        e_s[:, 512:640] = bdot(ext_s[t, :, 512:768], pick)
        f, fn = fl_s[t], fn_s[t]
        dp = dps[i, Q * k : Q * k + Q]
        dx = cw[3:4] * dp
        conv_acc[3:4] += jnp.sum(dp * e_s[8 : 8 + Q], 0, keepdims=True)
        conv_acc[4:5] += jnp.sum(dp, 0, keepdims=True)
        for j in range(3):
            conv_acc[j : j + 1] += jnp.sum(dp * e_s[5 + j : 5 + j + Q] * f[:, j : j + 1], 0, keepdims=True)
            dx = dx + cw[j : j + 1] * dps[i, Q * k + 3 - j : Q * k + 3 - j + Q] * fn[:, j : j + 1]
        rows = slice(Q * k, Q * k + Q)
        dproj[i, rows, 0:512] = dx[:, 0:512].astype(BF16)
        dproj[i, rows, 512:640] = (dx[:, 512:640] + bdot(ddt_s[t], pick_dt)).astype(BF16)

    for i in range(MICRO):
        for k in range(CH - 1):
            conv_chunk(i, k)
    edge1.wait_recv()
    edge2.wait_recv()
    for i in range(MICRO):
        dps[i, TOK : TOK + 8, 0:512] = ex_s[i]
        dps[i, TOK : TOK + 8, 512:640] = eb_s[i]
        conv_chunk(i, CH - 1)

    loads["normed"].wait()
    for d, f in ORDER:
        q = W.group(d, f)
        at = pl.ds(pl.multiple_of(256 * q, 256), 256)
        v = bdot(nm_s[at], dproj[...].reshape(T, 640)).astype(BF16)
        gb[q] = v[:, 0:CB]
        ga[q] = v[:, CB:]
        W.send_a(d, f)
        W.send_b(d, f)

    O.middle_b()
    O.middle_a(1)
    O.middle_a(0)

    loads["hid"].wait()
    loads["dgate"].wait()
    for i in range(MICRO):
        h = hid_s[:, i].reshape(TOK, 2048).astype(F32)
        scale = row_scale(h)
        first, main, rest = dg_s[i], dproj[i, :, 0:512], dproj[i, :, 512:640]

        def tile_of(j, carry, i=i, scale=scale, first=first, main=main, rest=rest):
            at = pl.ds(pl.multiple_of(256 * j, 256), 256)
            d = bdot(first, w_s[at, 0:512], NT) + bdot(main, w_s[at, 512:1024], NT) + bdot(rest, wt[at], NT)
            part[:, i, :, at] = d.astype(BF16).reshape(8, 64, 256)
            hv = hid_s[:, i, :, at].reshape(TOK, 256).astype(F32)
            s = jnp.sum(d * (hv * scale), 0, keepdims=True)
            gnorm[0:1, at] = s if i == 0 else gnorm[0:1, at] + s
            return carry

        lax.fori_loop(0, 8, tile_of, 0)
        for d in (1, 3, 2, 0):
            near_copy(d, i).start()
    for r in range(16):
        s0[r : r + 1] = gnorm[0:1, 128 * r : 128 * r + 128]
    for k in range(5):
        for r in range(5):
            s0[16 + 5 * k + r : 17 + 5 * k + r] = conv_acc[k : k + 1, 128 * r : 128 * r + 128]
    for r in range(4):
        s0[41 + r : 42 + r] = small_o[0:1, 128 * r : 128 * r + 128]
    s0[45:47] = small_b[0:2]
    s0[47:48] = sums_of(small_o[...], spread_matrix())[1:2]
    for d in XS:
        small_x(d).start()

    for i in range(MICRO):
        for d in (1, 3, 2, 0):
            near_copy(d, i).wait_recv()
            at = 2 * lax.rem(z + d, 4) + c
            near[d, i] = (part[at, i].astype(F32) + near[d, i].astype(F32)).astype(BF16)
            if d:
                far_copy(d, i).start()
    for d in XS:
        small_x(d).wait_recv()
    sx[...] = s0[...] + s1[0] + s1[1] + s1[2]
    for d in XS:
        small_y(d).start()
    W.middle_b()
    W.middle_a(1)
    W.middle_a(0)
    O.last_b()
    g_out[:, 0:1024] = O.last_a()
    W.last_b()
    for d in XS:
        small_y(d).wait_recv()
    small_all[m] = sx[...] + s2[0] + s2[1] + s2[2]
    for a, b in OTHERS:
        small_m(a, b).start()
    for i in range(MICRO):
        for d in XS:
            far_copy(d, i).wait_recv()
        total[i] = near[0, i].astype(F32) + far[0, i].astype(F32) + far[1, i].astype(F32) + far[2, i].astype(F32)
    O.third_b().wait_recv()
    for h in range(2):
        g_out[32 * h : 32 * h + 32, 1024:2048] = ob3[h]
    W.third_b().wait_recv()
    for h in range(2):
        final[4 * h : 4 * h + 4, :, 512 : 512 + CB] = gb3[h].reshape(4, 32, CB)
    final[:, :, 512 + CB :] = W.last_a().astype(BF16).reshape(8, 32, CA)
    final[:, :, 0:512] = gate_rows[...].reshape(8, 32, 512)
    for a, b in OTHERS:
        rows_copy(a, b).start()
    gi[m] = final[m]
    for a, b in OTHERS:
        rows_copy(a, b).wait_recv()
        small_m(a, b).wait_recv()
    W.finish()
    O.finish()
    swap.wait_send()
    for a, b in OTHERS:
        bc_copy(a, b).wait_send()
        rows_copy(a, b).wait_send()
        small_m(a, b).wait_send()
    for d in XS:
        small_x(d).wait_send()
        small_y(d).wait_send()
        for i in range(MICRO):
            far_copy(d, i).wait_send()
    for d in range(4):
        for i in range(MICRO):
            near_copy(d, i).wait_send()
    edge1.wait_send()
    edge2.wait_send()


def tail_call(dbc, edge_x, gate_rows, turned, cot, dpre, pre, ext, flags, fnext, conv, ddt, dgate, w, hid, normed, small_o, small_b):
    outs = [sds((8, 32, 1152), BF16), sds((64, 2048), F32), sds((2, 64, 2048), F32), sds((8, 48, 128), F32)]
    V = lambda *s: pltpu.VMEM(s, BF16)
    R = lambda *s: pltpu.VMEM(s, F32)
    scratch = [
        V(8, 32, T), R(2, 8, 512), R(2, 8, 128), R(2, 8, 128), R(2, TOK + 8, 640), R(8, Q, 256), V(8, Q + 8, 768), R(8, Q, 128), R(8, Q, 128), V(8, Q, 128), V(2, TOK, 512), V(2048, 1408),
        V(8, 2, 64, 2048), V(2048, T), V(2048, 128), R(Q + 8, 640), V(2, TOK, 640), V(8, 2, 64, 2048), V(4, 2, 64, 2048), V(3, 2, 64, 2048), R(8, 640), R(8, 2048),
        R(48, 128), R(3, 48, 128), R(3, 48, 128), R(48, 128),
        V(8, 256, CA), V(8, 256, CB), V(3, 2, 256, CA), V(3, 256, CA), V(2, 256, CA), V(3, 4, 128, CB), V(3, 128, CB), V(4, 128, CB), V(2, 128, CB),
        V(2, 8, 2, 64, 256), V(4, 2, 64, 2048), V(8, 64, 1024), V(8, 64, 1024), V(3, 2, 64, 1024), V(3, 64, 1024), V(2, 64, 1024), V(3, 4, 32, 1024), V(3, 32, 1024), V(4, 32, 1024), R(2, 32, 1024), V(4, 64, 2048),
        V(8, 32, 1152),
    ]
    return pl.pallas_call(
        tail_kernel,
        name="tail",
        out_shape=outs,
        in_specs=[VM] * 4 + [ANY] * 6 + [VM] + [ANY] * 5 + [VM] * 2,
        out_specs=[VM] * 4,
        scratch_shapes=[*scratch, pltpu.SemaphoreType.DMA((112,)), pltpu.SemaphoreType.DMA((112,)), pltpu.SemaphoreType.DMA((10,)), pltpu.SemaphoreType.DMA((2,))],
        compiler_params=pltpu.CompilerParams(collective_id=5, has_side_effects=True, vmem_limit_bytes=62 << 20),
        cost_estimate=pl.CostEstimate(flops=8 << 30, bytes_accessed=32 << 20, transcendentals=0),
    )(dbc, edge_x, gate_rows, turned, cot, dpre, pre, ext, flags, fnext, conv, ddt, dgate, w, hid, normed, small_o, small_b)


def from_members(v):
    r = v.shape[1]
    return v.reshape(4, 2, r, 4, 128).transpose(2, 1, 3, 0, 4).reshape(r, 4096)


def from_heads(v):
    r = v.shape[1]
    return v.reshape(4, 2, r, 4, 2).transpose(2, 1, 3, 0, 4).reshape(r, 64)


def from_rows(v):
    return v.transpose(1, 0, 2).reshape(v.shape[1], 256)


def to_members(v):
    r = v.shape[0]
    return v.reshape(r, 2, 4, 4, 128).transpose(3, 1, 0, 2, 4).reshape(8, r, 512)


def xdot(a, b, dims=NN):
    return lax.dot_general(a, b, dims, preferred_element_type=F32)


def per_device(layer_in, cotangent, segment_ids, norm_gain, in_weight, conv_weight, conv_bias, dt_bias, a_log, skip_gain, out_gain, out_weight):
    xi, yi, zi, ci = (lax.axis_index(a) for a in SEQ)
    g = 2 * xi + yi
    m = 2 * zi + ci
    lane = jnp.arange(128)

    def placed(v, width, at):
        return jnp.where(lane // width == at, jnp.tile(v, 128 // width), 0.0)

    head = lane == 2 * (g % 4) + ci
    rows = [placed(segment_ids[i, 0].astype(F32), 64, ci) for i in range(MICRO)]
    rows += [placed(norm_gain, 32, m % 4), placed(out_gain, 64, ci)]
    rows += [jnp.where(head, v, 0.0) for v in (dt_bias, a_log, skip_gain)]
    window = jnp.pad(jnp.concatenate([conv_weight, conv_bias[None]], 0), ((0, 3), (0, 60)))
    window = lax.dynamic_update_slice(jnp.zeros((8, 256), F32), window, (0, 68 * (8 * g + m) % 128))
    pack = jnp.concatenate([jnp.stack(rows), jnp.zeros((1, 128), F32), window[:, :128], window[:, 128:]], 0)
    bc = jnp.broadcast_to(in_weight[None, :, 8192:8448], (8, 32, 256))
    dt_w = in_weight[:, 8448:].reshape(32, 2, 4, 4, 2).transpose(3, 1, 0, 2, 4).reshape(8, 32, 8)
    w_send = jnp.concatenate([to_members(in_weight[:, :4096]), to_members(in_weight[:, 4096:8192]), bc, dt_w, jnp.zeros((8, 32, 120), BF16)], 2)
    (
        normed, hid_all, w_in, gate, pre, ext, delta, logs, flags, fnext, mixed, carried, states, dno, cot, w_out,
        sums, ends_all, conv, hp, og, gain, segrow,
    ) = wave(layer_in[:, 0], w_send, pack, cotangent[:, 0], out_weight)
    w_in = w_in.reshape(2048, 1408)
    norm_full = gain[0:1]
    dgate, dpre, dbc, ddt, small_o, small_b, own_branch, gate_rows, turned = back_wave(
        mixed, carried, states, gate, dno, sums, pre, delta, logs, flags, segrow, og, hp, w_out.reshape(512, 2048), normed, ends_all
    )
    dpre = dpre.reshape(MICRO, TOK, 512)
    gi, g_out, own_dn, small_sum = tail_call(
        dbc.reshape(8, 32, T), dpre[:, :8], gate_rows, turned, cot, dpre, pre, ext, flags, fnext, conv, ddt, dgate, w_in, hid_all, normed, small_o, small_b
    )
    gi = gi.astype(F32)
    hid_o = layer_in[:, 0].astype(F32)
    layer_out = (hid_o + own_branch).astype(BF16)
    ro = row_scale(hid_o)
    dg = own_dn * norm_full
    d_hid = ro * dg - hid_o * (ro * ro * ro) * jnp.mean(dg * hid_o, -1, keepdims=True)
    grad_in = (cotangent[:, 0].astype(F32) + d_hid).astype(BF16)
    g_in = jnp.concatenate([from_members(gi[:, :, :512]), from_members(gi[:, :, 512:1024]), from_rows(gi[:, :, 1024:1056]), from_heads(gi[:, :, 1056:1064])], 1)
    at = 8 * g + m
    g_norm = lax.dynamic_slice(small_sum[:, :16].sum(0).reshape(64, 32), (at, 0), (1, 32)).reshape(32)
    conv_s = small_sum[:, 16:41].reshape(8, 5, 640)
    conv_s = jnp.concatenate([from_members(conv_s[:, :, :512]), from_rows(conv_s[:, :, 512:544])], 1)
    conv_s = lax.dynamic_slice(conv_s, (0, 68 * at), (5, 68))
    og_s = from_members(small_sum[:, 41:45].reshape(8, 1, 512))[0]
    og_s = lax.dynamic_slice(og_s, (64 * at,), (64,))
    hd_s = from_heads(small_sum[:, 45:48, :8])
    hd_s = lax.dynamic_slice(hd_s, (0, at), (3, 1))
    return (layer_out[:, None], grad_in[:, None], g_norm, g_in, conv_s[:4], conv_s[4], hd_s[0], hd_s[1], hd_s[2], og_s, g_out)


def solution(mesh):
    fine = Mesh(mesh.devices.reshape(2, 4, 2, 4, 2), AXES)
    tok = P(None, "rep", SEQ, None)
    return jax.shard_map(
        per_device,
        mesh=fine,
        in_specs=(tok, tok, P(None, "rep", SEQ), P(SEQ), P(SEQ, None), P(None, SEQ), P(SEQ), P(SEQ), P(SEQ), P(SEQ), P(SEQ), P(SEQ, None)),
        out_specs=(tok, tok, P(SEQ), P(SEQ, None), P(None, SEQ), P(SEQ), P(SEQ), P(SEQ), P(SEQ), P(SEQ), P(SEQ, None)),
        check_vma=False,
    )
```

```python
import functools

import jax
import jax.numpy as jnp
from jax import lax
from jax.experimental import pallas as pl
from jax.experimental.pallas import tpu as pltpu
from jax.sharding import Mesh, PartitionSpec as P

EPS = 1e-05
INNER = 4096
MICRO = 2
CONV = 4352
F32 = jnp.float32
BF16 = jnp.bfloat16
AXES = ("rep", "x", "y", "z", "c")
SEQ = ("x", "y", "z", "c")
GROUPS = 8
TOK = 512
Q = 128
CH = TOK // Q

MESH = pl.DeviceIdType.MESH
ANY = pl.BlockSpec(memory_space=pl.ANY)
VM = pl.BlockSpec(memory_space=pltpu.VMEM)


class Net:
    def __init__(self, send, recv):
        self.send, self.recv, self.used, self.open = send, recv, 0, []
        self.keys = {}
        self.rep, self.x, self.y, self.z, self.c = (lax.axis_index(a) for a in AXES)
        self.ring = 2 * self.rep + self.y
        self.g = 2 * self.x + self.y
        self.m = 2 * self.z + self.c

    def at(self, dx=0, dy=0, dz=0, dc=0):
        ring = lax.rem(self.ring + dy, 4)
        return (ring // 2, lax.rem(self.x + dx, 4), lax.rem(ring, 2), lax.rem(self.z + dz, 4), lax.rem(self.c + dc, 2))

    def pair(self):
        return (self.rep, self.x, 1 - self.y, self.z, self.c)

    def across(self, dx):
        return (self.rep, lax.rem(self.x + dx, 4), 1 - self.y, self.z, self.c)

    def group(self, d):
        g = lax.rem(self.g + d, 8)
        return (self.rep, g // 2, lax.rem(g, 2), self.z, self.c)

    def member(self, dz, dc):
        return 2 * lax.rem(self.z + dz, 4) + lax.rem(self.c + dc, 2)

    def push(self, src, dst, where):
        i = self.used
        self.used += 1
        copy = pltpu.make_async_remote_copy(
            src_ref=src, dst_ref=dst, send_sem=self.send.at[i], recv_sem=self.recv.at[i], device_id=where, device_id_type=MESH
        )
        copy.start()
        self.open.append(copy)
        return copy

    def copy(self, key, src, dst, where):
        i = self.keys.setdefault(key, len(self.keys))
        return pltpu.make_async_remote_copy(
            src_ref=src, dst_ref=dst, send_sem=self.send.at[i], recv_sem=self.recv.at[i], device_id=where, device_id_type=MESH
        )

    def behind(self, d):
        return 2 * lax.rem(self.x + 4 - d, 4) + self.y

    def local(self, src, dst):
        i = self.used
        self.used += 1
        copy = pltpu.make_async_copy(src, dst, self.recv.at[i])
        copy.start()
        return copy

    def meet(self, peers):
        barrier = pltpu.get_barrier_semaphore()
        for peer in peers:
            pl.semaphore_signal(barrier, inc=1, device_id=peer, device_id_type=MESH)
        pl.semaphore_wait(barrier, len(peers))

    def finish(self):
        for copy in self.open:
            copy.wait_send()


OTHERS = [(dz, dc) for dz in (0, 1, 3, 2) for dc in (0, 1) if (dz, dc) != (0, 0)]
ZS = (0, 1, 3, 2)
XS = (1, 3, 2)
ORDER = [(d, f) for d in (2, 1, 3, 0) for f in (1, 0)]


def call(kernel, name, cid, outs, ins, spaces_in, spaces_out, sems, scratch=(), cost=1 << 20):
    return pl.pallas_call(
        kernel,
        name=name,
        out_shape=outs,
        in_specs=spaces_in,
        out_specs=spaces_out,
        scratch_shapes=[*scratch, pltpu.SemaphoreType.DMA((sems,)), pltpu.SemaphoreType.DMA((sems,))],
        compiler_params=pltpu.CompilerParams(collective_id=cid, has_side_effects=True, vmem_limit_bytes=60 << 20),
        cost_estimate=pl.CostEstimate(flops=0, bytes_accessed=cost, transcendentals=0),
    )(*ins)


def sds(shape, dtype):
    return jax.ShapeDtypeStruct(shape, dtype)


def add4(a, b):
    return a.astype(F32) + b[0].astype(F32) + b[1].astype(F32) + b[2].astype(F32)


NN = (((1,), (0,)), ((), ()))
NT = (((1,), (1,)), ((), ()))
TN = (((0,), (0,)), ((), ()))
TT = (((0,), (1,)), ((), ()))


def bdot(a, b, dims=NN):
    return lax.dot_general(a, b, dims, preferred_element_type=F32)


def parts(v, count):
    out = []
    for _ in range(count):
        p = v.astype(BF16)
        out.append(p)
        v = v - p.astype(F32)
    return out


def left_parts(v, w, count, dims=NN):
    return sum(bdot(p, w, dims) for p in parts(v, count))


def right_parts(w, v, count, dims=NN):
    return sum(bdot(w, p, dims) for p in parts(v, count))


def iota(shape, dim):
    return lax.broadcasted_iota(jnp.int32, shape, dim)


def spread_matrix():
    return (iota((128, 512), 0) == iota((128, 512), 1) // 64).astype(BF16)


def heads_of(v, eh):
    return left_parts(v, eh, 2)


def sums_of(v, eh):
    return left_parts(v, eh, 2, NT)


def lower_matrix():
    return (iota((Q, Q), 0) >= iota((Q, Q), 1)).astype(BF16)


def sigmoid(v):
    return 1.0 / (1.0 + jnp.exp(-v))


def softplus(v):
    return jnp.maximum(v, 0.0) + jnp.log1p(jnp.exp(-jnp.abs(v)))


def row_scale(h):
    return lax.rsqrt(jnp.mean(h * h, axis=-1, keepdims=True) + EPS)


def decays(L, flags):
    E = jnp.exp(L) * flags[:, 3:4]
    W = jnp.exp(L[Q - 1 : Q] - L) * flags[:, 4:5]
    return E, W


def wave_kernel(
    hid, wsend, gsend, pack, cot, outw,
    normed_h, hid_h, w_h, wg_h, gate_h, pre_h, ext_h, delta_h, logs_h, flags_h, fnext_h, mixed_h, carried_h, states_h, dno_h, cot_h, wout_h,
    sums, endlog, conv, hp, og, gain, segrow,
    hid_s, halo, nrm, turned, w_s, g_s, small, proj, pre, ext, delta, logs, flags, fnext, sloc, inner, carried, states, dno, ends, rsend, rrecv, cot_s, w_o, wo_s, convt, state, total, tail, send, recv, done,
):
    eh = spread_matrix()
    n = Net(send, recv)
    g, m, x, y, z, core = n.g, n.m, n.x, n.y, n.z, n.c
    ALLX = (0,) + XS
    copies = []

    def keyed(key, src, dst, where):
        cp = n.copy(key, src, dst, where)
        copies.append(cp)
        cp.start()
        return cp

    stores = []

    def store(src, dst):
        cp = pltpu.make_async_copy(src, dst, done.at[len(stores)])
        cp.start()
        stores.append(cp)

    n.meet([n.at(dz=a, dc=b) for a, b in OTHERS] + [n.at(dx=d) for d in XS] + [n.at(dy=1), n.at(dy=3), n.group(1), n.group(7)] + [n.across(d) for d in ALLX])

    wa, sa = {}, {}
    sets = ((wsend, w_s), (gsend, g_s))
    for s, (src, dst) in enumerate(sets):
        for a, b in OTHERS:
            wa[s, a, b] = keyed(("wa", s, a, b), src.at[n.member(a, b)], dst.at[g, m], n.at(dz=a, dc=b))
            if s == 0:
                sa[a, b] = keyed(("sa", a, b), pack, small.at[g, m], n.at(dz=a, dc=b))
        dst[g, m] = src[m]
    small[g, m] = pack[...]
    hid_s[m] = hid[...]
    wx, wy, sx, sy = {}, {}, {}, {}

    def along_y(s, d, k):
        first = pl.ds(2 * lax.rem(z + 4 - ZS[k], 4), 2)
        for half, dy in ((0, 1), (1, 3)):
            part = sets[s][1].at[n.behind(d), first, pl.ds(16 * half, 16)]
            wy[s, d, k, half] = keyed(("wy", s, d, k, half), part, part, n.at(dy=dy))

    def issue(k, s=0):
        for b in (0, 1):
            if (ZS[k], b) != (0, 0):
                wa[s, ZS[k], b].wait_recv()
        block = sets[s][1].at[g, pl.ds(2 * lax.rem(z + 4 - ZS[k], 4), 2)]
        for d in XS:
            wx[s, k, d] = keyed(("wx", s, k, d), block, block, n.at(dx=d))
        along_y(s, 0, k)

    def forward(k, s=0):
        for d in XS:
            wx[s, k, d].wait_recv()
            along_y(s, d, k)

    def all_y(s):
        for d in ALLX:
            for k in range(4):
                for half in (0, 1):
                    wy[s, d, k, half].wait_recv()

    issue(0)
    issue(1)
    hz = {a: keyed(("hz", a), hid_s.at[m], hid_s.at[m], n.at(dz=a)) for a in (1, 3, 2)}
    hn = [keyed("hn", hid_s.at[m], hid_s.at[m], n.at(dc=1))]
    for a, b in OTHERS:
        sa[a, b].wait_recv()
    for d in XS:
        sx[d] = keyed(("sx", d), small.at[g], small.at[g], n.at(dx=d))
    sy[0] = keyed(("sy", 0), small.at[g], small.at[g], n.pair())
    forward(0)
    issue(2)
    for d in XS:
        sx[d].wait_recv()
        mine = small.at[n.behind(d)]
        sy[d] = keyed(("sy", d), mine, mine, n.pair())
    forward(1)
    issue(3)
    for d in ALLX:
        sy[d].wait_recv()

    for q in range(16):
        v = small[q // 2, 4 * (q % 2), 2:3]
        for u in range(1, 4):
            v = v + small[q // 2, 4 * (q % 2) + u, 2:3]
        gain[0:1, 128 * q : 128 * q + 128] = v
    heads3 = jnp.zeros((3, 128), F32)
    for j in range(4):
        og[0:1, 128 * j : 128 * j + 128] = small[4 * core + j, 2 * z, 3:4] + small[4 * core + j, 2 * z + 1, 3:4]
        for e in range(2):
            heads3 = heads3 + small[4 * core + j, 2 * z + e, 4:7]
    hp[...] = jnp.zeros_like(hp)
    hp[0:1] = heads3[0:1]
    hp[1:2] = jnp.where(iota((1, 128), 1) < 8, -jnp.exp(heads3[1:2]), 0.0)
    hp[2:3] = heads3[2:3]
    for q in range(34):
        v = jnp.zeros((8, 128), F32)
        for i in range(64):
            if 68 * i // 128 == q:
                v = v + small[i // 8, i % 8, 8:16]
            elif 68 * i // 128 == q - 1:
                v = v + small[i // 8, i % 8, 16:24]
        convt[q] = v
    for j in range(4):
        conv[:, 128 * j : 128 * j + 128] = convt[4 * (4 * core + j) + z]
    conv[:, 512:640] = convt[32]
    conv[:, 640:768] = convt[33]

    forward(2)
    for a in (1, 3, 2):
        hz[a].wait_recv()
        theirs = hid_s.at[2 * lax.rem(z + 4 - a, 4) + core]
        hn.append(keyed(("hf", a), theirs, theirs, n.at(dc=1)))
    cot_s[m] = cot[...]
    cz = {a: keyed(("cz", a), cot_s.at[m], cot_s.at[m], n.at(dz=a)) for a in (1, 3, 2)}
    cn = [keyed("cn", cot_s.at[m], cot_s.at[m], n.at(dc=1))]

    lane = iota((8, 128), 1)

    def chunk_row(group, i, c):
        return jnp.broadcast_to(small[group, 2 * c, i : i + 1] + small[group, 2 * c + 1, i : i + 1], (8, 128))

    for i in range(MICRO):
        before = jnp.where(g > 0, chunk_row(lax.rem(g + 7, 8), i, CH - 1), -1.0)
        after = jnp.where(g < 7, chunk_row(lax.rem(g + 1, 8), i, 0), -2.0)
        rows = [before] + [chunk_row(g, i, c) for c in range(CH)] + [after]
        for c in range(CH):
            prv, cur, nxt = rows[c : c + 3]
            here, ahead = [], []
            for d in (3, 2, 1):
                back = jnp.where(lane < d, pltpu.roll(prv, d, 1), pltpu.roll(cur, d, 1))
                here.append((back == cur).astype(F32))
                on = jnp.where(lane >= 128 - d, pltpu.roll(nxt, 128 - d, 1), pltpu.roll(cur, 128 - d, 1))
                ahead.append((on == cur).astype(F32))
            here += [(cur == prv[:, 127:128]).astype(F32), (cur == cur[:, 127:128]).astype(F32), cur]
            sub = iota((128, 128), 0)
            for rows_of, to in ((here, flags), (ahead, fnext)):
                v = jnp.zeros((128, 128), F32)
                for r, row in enumerate(rows_of):
                    v = jnp.where(sub == r, jnp.broadcast_to(row[0:1], (128, 128)), v)
                to[CH * i + c] = v.T
            segrow[CH * i + c] = cur[0:1]

    forward(3)
    for k in range(4):
        issue(k, 1)
    w_o[g] = outw[...]
    ox = {d: keyed(("ox", d), w_o.at[g], w_o.at[g], n.at(dx=d)) for d in XS}
    oy = {}

    def out_y(d):
        for half, dy in ((0, 1), (1, 3)):
            part = w_o.at[n.behind(d), pl.ds(32 * half, 32)]
            oy[d, half] = keyed(("oy", d, half), part, part, n.at(dy=dy))

    out_y(0)
    for cp in hn:
        cp.wait_recv()
    edge = keyed("edge", hid_s.at[7, :, pl.ds(48, 16)], halo, n.group(1))

    gv = gain[0:1]

    def norm(k, carry):
        for i in range(MICRO):
            h = hid_s[pl.ds(2 * k, 2), i].reshape(Q, 2048).astype(F32)
            v = h * row_scale(h) * gv
            nrm[i, pl.ds(pl.multiple_of(16 + Q * k, 16), Q)] = v.astype(BF16)
            turned[:, pl.ds(pl.multiple_of(TOK * i + Q * k, Q), Q)] = v.T.astype(BF16)
        return carry

    lax.fori_loop(0, CH, norm, 0)
    edge.wait_recv()
    for i in range(MICRO):
        h = halo[i].astype(F32)
        nrm[i, 0:16] = (h * row_scale(h) * gv).astype(BF16)
    store(turned, normed_h)

    def project(lo, hi, ref, off, sides, first):
        for i in range(MICRO):
            for at in range(lo, hi, 256):
                to = min(at + 256, hi)
                v = 0.0 if first else proj[i, :, at:to]
                for side in sides:
                    for k in range(4):
                        q = 2 * k + side
                        v = v + bdot(nrm[i, :, pl.ds(pl.multiple_of(256 * q, 256), 256)], ref[q, :, :, at - off : to - off].reshape(256, to - at))
                proj[i, :, at:to] = v

    project(512, 1408, w_s, 512, (y,), True)
    forward(0, 1)
    forward(1, 1)
    all_y(0)
    project(512, 1408, w_s, 512, (1 - y,), False)
    forward(2, 1)
    forward(3, 1)
    store(w_s, w_h)
    store(hid_s, hid_h)
    store(flags, flags_h)
    store(fnext, fnext_h)

    def front(i, c):
        at = CH * i + c
        rows = pl.ds(pl.multiple_of(16 + Q * c, 16), Q)
        f = flags[at]
        xbc = proj[i, rows, 512:1280].astype(BF16).astype(F32)
        tail[8:] = xbc
        acc = conv[4:5] + conv[3:4] * xbc
        for k in range(3):
            acc = acc + conv[k : k + 1] * tail[5 + k : 5 + k + Q] * f[:, k : k + 1]
        pre[at] = acc
        ext[at] = tail[...].astype(BF16)
        d = softplus(proj[i, rows, 1280:1408] + hp[0:1])
        delta[at] = d
        L = right_parts(lower_matrix(), d * hp[1:2], 3)
        logs[at] = L
        E, W = decays(L, f)
        xv = acc[:, :512]
        X = xv * sigmoid(xv)
        b = acc[:, 512:640]
        B = (b * sigmoid(b)).astype(BF16)
        S = right_parts(B, heads_of(W * d, eh) * X, 2, TN)
        sloc[at] = S
        last = heads_of(E[Q - 8 :], eh)
        state[...] = last[7:8] * state[...] + S
        tail[0:8] = tail[Q : Q + 8]
        total[...] = total[...] + L[Q - 1 : Q]

    ex, lx, ly = {}, {}, {}
    for i in range(MICRO):
        tail[0:8] = proj[i, 8:16, 512:1280].astype(BF16).astype(F32)
        state[...] = jnp.zeros_like(state)
        total[...] = jnp.zeros_like(total)
        lax.fori_loop(0, CH, lambda c, carry, i=i: (front(i, c), carry)[1], 0)
        ends[g, i] = state[...].astype(BF16)
        lt = parts(jnp.broadcast_to(heads_of(jnp.broadcast_to(total[...], (8, 128)), eh)[0:1], (16, 512)), 3)
        seg = jnp.broadcast_to(segrow[CH * i + CH - 1][:, 127:128], (16, 512))
        high = jnp.floor(seg * (1.0 / 64.0))
        r = iota((16, 512), 0)
        v = jnp.zeros((16, 512), BF16)
        for k, row in enumerate(lt + [high.astype(BF16), (seg - 64.0 * high).astype(BF16)]):
            v = jnp.where(r == k, row, v)
        endlog[g, i] = v
        for d in XS:
            lx[i, d] = keyed(("lx", i, d), endlog.at[g, i], endlog.at[g, i], n.at(dx=d))
        for d in ALLX:
            ly[i, d] = keyed(("ly", i, d), endlog.at[g, i], endlog.at[g, i], n.across(d))
        for d in XS:
            ex[i, d] = keyed(("ex", i, d), ends.at[g, i], ends.at[g, i], n.at(dx=d))
        if i == 0:
            for d in XS:
                ox[d].wait_recv()
                out_y(d)
    store(pre, pre_h)
    store(ext, ext_h)
    store(delta, delta_h)
    store(logs, logs_h)

    def states_on(i):
        for d in XS:
            lx[i, d].wait_recv()
        for d in ALLX:
            ly[i, d].wait_recv()
        for d in XS:
            ex[i, d].wait_recv()
        rsend[i] = entering(n, ends, endlog, 1, 0, i).astype(BF16)
        return keyed(("r", i), rsend.at[i], rrecv.at[i], n.pair())

    def inside(at, carry):
        L = logs[at]
        X, B, C = activations(pre[at])
        U = (heads_of(delta[at], eh) * X).astype(BF16)
        psi = bdot(C, B, NT)
        keep = same_mask(flags[at], segrow[at])
        LT = L.T
        for j in range(4):
            u = pair_halves(U[:, 128 * j : 128 * j + 128])
            v = jnp.zeros((Q, 128), F32)
            for e in range(2):
                h = 2 * j + e
                K = jnp.where(keep, jnp.exp(L[:, h : h + 1] - LT[h : h + 1]), 0.0)
                v = v + bdot((psi * K).astype(BF16), u[e])
            inner[at, :, 128 * j : 128 * j + 128] = v
        return carry

    lax.fori_loop(0, 4, inside, 0)
    r0 = states_on(0)
    for d in ALLX:
        for half in (0, 1):
            oy[d, half].wait_recv()
    swap = keyed("swap", w_o.at[pl.ds(4 * (1 - core), 4)], wo_s.at[:, core], n.at(dc=1))
    for k in range(4):
        wo_s[k, core] = w_o[4 * core + k]
    for a in (1, 3, 2):
        cz[a].wait_recv()
        theirs = cot_s.at[2 * lax.rem(z + 4 - a, 4) + core]
        cn.append(keyed(("cf", a), theirs, theirs, n.at(dc=1)))
    lax.fori_loop(4, 8, inside, 0)
    r1 = states_on(1)
    all_y(1)
    store(g_s, wg_h)
    project(0, 512, g_s, 0, (0, 1), True)
    for i in range(MICRO):
        store(proj.at[i, pl.ds(16, TOK), pl.ds(0, 512)], gate_h.at[i])
    swap.wait_recv()
    for cp in cn:
        cp.wait_recv()
    store(cot_s, cot_h)
    store(wo_s, wout_h)
    for i in range(MICRO):
        d = bdot(cot_s[:, i].reshape(TOK, 2048), wo_s[...].reshape(512, 2048), NT)
        for c in range(CH):
            dno[CH * i + c] = d[Q * c : Q * c + Q]
    store(dno, dno_h)

    def mix(i, c):
        at = CH * i + c
        E, _ = decays(logs[at], flags[at])
        X, _, C = activations(pre[at])
        more = heads_of(jnp.concatenate([E, jnp.broadcast_to(hp[2:3], (8, 128))], 0), eh)
        Ex, skip = more[:Q], more[Q : Q + 1]
        S = state[...]
        states[at, 0] = S
        Yc = Ex * bdot(C, S.astype(BF16))
        carried[at] = Yc
        mx = inner[at] + Yc + skip * X
        inner[at] = mx
        after = Ex[Q - 1 : Q] * S + sloc[at]
        state[...] = after
        states[at, 1] = after
        gt = proj[i, pl.ds(pl.multiple_of(16 + Q * c, 16), Q), 0:512]
        gated = mx * (gt * sigmoid(gt))
        ones = jnp.ones((8, 512), BF16)
        sums[m, at, 0:8] = right_parts(ones, gated * gated, 2, NT)
        sums[m, at, 8:16] = right_parts(ones, dno[at] * og[0:1] * gated, 2, NT)

    sm = []
    for i, r in ((0, r0), (1, r1)):
        r.wait_recv()
        state[...] = entering(n, ends, endlog, 0, 0, i) + rrecv[i].astype(F32)
        lax.fori_loop(0, CH, lambda c, carry, i=i: (mix(i, c), carry)[1], 0)
        mine = sums.at[m, pl.ds(CH * i, CH)]
        for a, b in OTHERS:
            sm.append(keyed(("sm", i, a, b), mine, mine, n.at(dz=a, dc=b)))
        some = pl.ds(CH * i, CH)
        store(inner.at[some], mixed_h.at[some])
        store(carried.at[some], carried_h.at[some])
        store(states.at[some], states_h.at[some])
    for cp in sm:
        cp.wait_recv()
    for cp in copies:
        cp.wait_send()
    for cp in stores:
        cp.wait()


def wave(hid, wsend, gsend, pack, cot, outw):
    V = lambda *s: pltpu.VMEM(s, BF16)
    R = lambda *s: pltpu.VMEM(s, F32)
    outs = [
        sds((2048, T), BF16), sds((8, 2, 64, 2048), BF16), sds((8, 8, 32, 896), BF16), sds((8, 8, 32, 512), BF16), sds((2, TOK, 512), F32), sds((8, Q, 768), F32), sds((8, Q + 8, 768), BF16), sds((8, Q, 128), F32), sds((8, Q, 128), F32),
        sds((8, Q, 128), F32), sds((8, Q, 128), F32), sds((8, Q, 512), F32), sds((8, Q, 512), F32), sds((8, 2, 128, 512), F32), sds((8, Q, 512), F32), sds((8, 2, 64, 2048), BF16), sds((4, 2, 64, 2048), BF16),
        sds((8, 8, 16, 128), F32), sds((8, 2, 16, 512), BF16), sds((8, 768), F32), sds((8, 128), F32), sds((8, 512), F32), sds((8, 2048), F32), sds((8, 1, 128), F32),
    ]
    scratch = [
        V(8, 2, 64, 2048), V(2, 16, 2048), V(2, TOK + 16, 2048), V(2048, T), V(8, 8, 32, 896), V(8, 8, 32, 512), R(8, 8, 24, 128), R(2, TOK + 16, 1408), R(8, Q, 768), V(8, Q + 8, 768), R(8, Q, 128), R(8, Q, 128), R(8, Q, 128), R(8, Q, 128),
        R(8, 128, 512), R(8, Q, 512), R(8, Q, 512), R(8, 2, 128, 512), R(8, Q, 512), V(8, 2, 128, 512), V(2, 128, 512), V(2, 128, 512), V(8, 2, 64, 2048), V(8, 64, 2048), V(4, 2, 64, 2048),
        R(34, 8, 128), R(128, 512), R(1, 128), R(Q + 8, 768),
    ]
    return pl.pallas_call(
        wave_kernel,
        name="wave",
        out_shape=outs,
        in_specs=[VM] * 6,
        out_specs=[ANY] * 17 + [VM] * 7,
        scratch_shapes=[*scratch, pltpu.SemaphoreType.DMA((192,)), pltpu.SemaphoreType.DMA((192,)), pltpu.SemaphoreType.DMA((24,))],
        compiler_params=pltpu.CompilerParams(collective_id=1, has_side_effects=True, vmem_limit_bytes=64 * 1024 * 1024 - 65536),
        cost_estimate=pl.CostEstimate(flops=8 << 30, bytes_accessed=32 << 20, transcendentals=0),
    )(hid, wsend, gsend, pack, cot, outw)


def entering(n, everyone, logs, target, direction, micro):
    to = 2 * n.x + (1 - n.y if target else n.y)
    lt, last = [], []
    for q in range(8):
        v = logs[q, micro].astype(F32)
        lt.append(v[0:1] + v[1:2] + v[2:3])
        last.append(64.0 * v[3:4] + v[4:5])
    zero = jnp.zeros((1, 512), F32)
    edge = zero
    for r in range(8):
        edge = edge + jnp.where((r == to) if direction else (r == to - 1), last[r], zero)
    total = jnp.zeros((128, 512), F32)
    for k in range(4):
        q = 2 * k + n.y
        log = zero
        for r in range(8):
            between = (r > to) & (r < q) if direction else (r > q) & (r < to)
            log = log + jnp.where(between, lt[r], zero)
        if direction:
            there = jnp.where(n.y == 0, last[max(2 * k - 1, 0)], last[2 * k])
        else:
            there = jnp.where(n.y == 0, last[2 * k], last[2 * k + 1])
        reached = jnp.where((q > to) if direction else (q < to), 1.0, 0.0)
        total = total + jnp.where(there == edge, jnp.exp(log) * reached, zero) * everyone[q, micro].astype(F32)
    return total


def same_mask(flags, segrow):
    return (flags[:, 5:6] == segrow) & (iota((Q, Q), 0) >= iota((Q, Q), 1))


def activations(pre):
    a = pre * sigmoid(pre)
    return a[:, :512], a[:, 512:640].astype(BF16), a[:, 640:768].astype(BF16)


def pair_halves(v):
    low_half = iota(v.shape, 1) < 64
    zero = jnp.zeros_like(v)
    return jnp.where(low_half, v, zero), jnp.where(low_half, zero, v)


T = MICRO * TOK


def column(row):
    return jnp.concatenate([jnp.broadcast_to(row, (128, 128)).T] * 4, 1)


def pick_matrix(rows, start, count, shift, dtype=BF16):
    r, l = iota((rows, 128), 0), iota((rows, 128), 1)
    return ((r - start == l - shift) & (l >= shift) & (l < shift + count)).astype(dtype)


class Reduce:
    def __init__(self, n, key, a, b, a1, a2, pa, b1, b2, pb, b3):
        self.n, self.key, self.a, self.b = n, key, a, b
        self.a1, self.a2, self.pa, self.b1, self.b2, self.pb, self.b3 = a1, a2, pa, b1, b2, pb, b3
        self.half = pb.shape[1]

    def group(self, d, f):
        n = self.n
        return 2 * lax.rem(n.x + d, 4) + lax.rem(n.y + f, 2)

    def first_a(self, d, f):
        return self.n.copy((self.key, "a1", d, f), self.a.at[self.group(d, f)], self.a1.at[d - 1, f], self.n.at(dx=d))

    def first_b(self, d, e):
        n = self.n
        rep = lax.rem(n.ring + e, 4) // 2
        rows = pl.ds(pl.multiple_of(self.half * rep, self.half), self.half)
        return n.copy((self.key, "b1", d, e), self.b.at[self.group(d, e % 2), rows], self.b1.at[e - 1, lax.rem(n.x + d, 4)], n.at(dy=e))

    def send_a(self, d, f):
        if d:
            self.first_a(d, f).start()

    def send_b(self, d, f):
        for e in (1, 3) if f else (2,):
            self.first_b(d, e).start()

    def second_a(self, e):
        return self.n.copy((self.key, "a2", e), self.pa.at[e % 2], self.a2.at[e - 1], self.n.at(dy=e))

    def second_b(self, d):
        return self.n.copy((self.key, "b2", d), self.pb.at[lax.rem(self.n.x + d, 4)], self.b2.at[d - 1], self.n.at(dx=d))

    def third_b(self):
        return self.n.copy((self.key, "b3"), self.b3.at[self.n.rep], self.b3.at[self.n.rep], self.n.at(dy=2))

    def middle_a(self, f):
        for d in XS:
            self.first_a(d, f).wait_recv()
        self.pa[f] = add4(self.a[self.group(0, f)], self.a1[:, f]).astype(BF16)

    def go_a(self, f):
        for e in (1, 3) if f else (2,):
            self.second_a(e).start()

    def go_b(self):
        for d in (2, 1, 3):
            self.second_b(d).start()

    def middle_b(self):
        n = self.n
        rows = pl.ds(pl.multiple_of(self.half * n.rep, self.half), self.half)
        for d in (2, 1, 3, 0):
            for e in XS:
                self.first_b(d, e).wait_recv()
            k = lax.rem(n.x + d, 4)
            self.pb[k] = add4(self.b[2 * k + n.y, rows], self.b1[:, k]).astype(BF16)

    def last_b(self):
        for d in XS:
            self.second_b(d).wait_recv()
        self.b3[self.n.rep] = add4(self.pb[self.n.x], self.b2).astype(self.b3.dtype)
        self.third_b().start()

    def last_a(self):
        for e in XS:
            self.second_a(e).wait_recv()
        return add4(self.pa[0], self.a2)

    def finish_first(self):
        for d in XS:
            for f in (0, 1):
                self.first_a(d, f).wait_send()
        for e in XS:
            for d in range(4):
                self.first_b(d, e).wait_send()

    def finish(self):
        for d in XS:
            self.second_b(d).wait_send()
            self.second_a(d).wait_send()
        self.third_b().wait_send()


def fetcher(sems):
    loads = {}

    def fetch(key, src, dst):
        loads[key] = pltpu.make_async_copy(src, dst, sems.at[len(loads)])
        loads[key].start()

    return loads, fetch


C1 = 256


def back_wave_kernel(
    mixed_h, carried_h, states_h, gate_h, dno_h, sums, pre_h, delta_h, logs_h, flags_h, segrow, og, hp, wout_h, normed, cot, endlog,
    dgate, dpre_h, bc_all, ddt, small_o, small_b, total, wpa, wpb, opa, opb, edges,
    mixed, carried, states, gate, dno, pre, delta, logs, flags, wout, nout, dmix, tloc, dbi, starts, rsend, rrecv, rows, part, near, far,
    wa, wb, wa1, wb1, turned, cot_s, gsw, oa, ob, oa1, ob1, oin, dbc, state, send, recv, load, tile_sem, cot_sem,
):
    eh = spread_matrix()
    n = Net(send, recv)
    g, m, core, z = n.g, n.m, n.c, n.z
    W = Reduce(n, "w", wa, wb, wa1, None, wpa, wb1, None, wpb, None)
    O = Reduce(n, "o", oa, ob, oa1, None, opa, ob1, None, opb, None)
    swap = n.copy("swap", gsw.at[:, 1 - core], oin, n.at(dc=1))
    loads, fetch = fetcher(load)
    for i in range(MICRO):
        some = pl.ds(CH * i, CH)
        for key, src, dst in (("mixed", mixed_h, mixed), ("gate", gate_h, gate), ("dno", dno_h, dno), ("pre", pre_h, pre), ("logs", logs_h, logs), ("flags", flags_h, flags)):
            fetch((key, i), src.at[some], dst.at[some])
    fetch("wout", wout_h, wout)
    for key, src, dst in (("delta", delta_h, delta), ("states", states_h, states), ("carried", carried_h, carried)):
        fetch(key, src, dst)

    def start_x(i, d):
        return n.copy(("sx", i, d), starts.at[g, i], starts.at[g, i], n.at(dx=d))

    def part_y(i):
        return n.copy(("r", i), rsend.at[i], rrecv.at[i], n.pair())

    def near_copy(d, i):
        return n.copy(("near", d, i), part.at[2 * lax.rem(z + d, 4) + 1 - core, i], near.at[d, i], n.at(dc=1))

    def far_copy(d, i):
        return n.copy(("far", d, i), near.at[d, i], far.at[d - 1, i], n.at(dz=d))

    def bc_copy(i, a, b):
        some = pl.ds(TOK * i, TOK)
        return n.copy(("bc", i, a, b), dbc.at[n.member(a, b), :, some], bc_all.at[m, :, some], n.at(dz=a, dc=b))

    def edge_copy(i):
        return n.copy(("edge", i), gate.at[CH * i, pl.ds(0, 8)], edges.at[i], n.group(7))

    n.meet([n.at(dz=a, dc=b) for a, b in OTHERS] + [n.at(dx=d) for d in XS] + [n.at(dy=d) for d in XS] + [n.group(1), n.group(7)])
    small_o[...] = jnp.zeros_like(small_o)
    small_b[...] = jnp.zeros_like(small_b)

    def outward(i, k):
        c = CH - 1 - k
        at = CH * i + c
        tot = sums[0, at]
        for q in range(1, 8):
            tot = tot + sums[q, at]
        r = column(lax.rsqrt(tot[0:1] / INNER + EPS))
        s2 = column(tot[8:9] / INNER)
        gt = gate[at]
        s = sigmoid(gt)
        sg = gt * s
        mix = mixed[at]
        gated = mix * sg
        dn = dno[at]
        n0 = gated * r
        rows = pl.ds(pl.multiple_of(Q * c, Q), Q)
        nb = n0 * og[0:1]
        nout[i, rows] = nb.astype(BF16)
        turned[:, pl.ds(pl.multiple_of(Q * at, Q), Q)] = nb.T.astype(BF16)
        d_gated = r * (dn * og[0:1] - n0 * r * s2)
        dm = d_gated * sg
        dmix[at] = dm
        dgate[i, rows] = (d_gated * mix * (s * (1.0 + gt * (1.0 - s)))).astype(BF16)
        x = pre[at, :, :512]
        X = x * sigmoid(x)
        cc = pre[at, :, 640:768]
        C = (cc * sigmoid(cc)).astype(BF16)
        small_o[0:1] += jnp.sum(dn * n0, 0, keepdims=True)
        small_o[1:2] += jnp.sum(X * dm, 0, keepdims=True)
        E, _ = decays(logs[at], flags[at])
        Ex = heads_of(E, eh)
        G = right_parts(C, Ex * dm, 2, TN)
        tloc[at] = G
        state[...] = Ex[Q - 1 : Q] * state[...] + G

    for i in range(MICRO):
        for key in ("mixed", "gate", "dno", "pre", "logs", "flags"):
            loads[key, i].wait()
        state[...] = jnp.zeros_like(state)
        lax.fori_loop(0, CH, lambda k, carry, i=i: (outward(i, k), carry)[1], 0)
        starts[g, i] = state[...].astype(BF16)
        for d in XS:
            start_x(i, d).start()
        if i == 0:
            loads["wout"].wait()
        part[:, i] = bdot(nout[i], wout[...]).astype(BF16).reshape(8, 64, 2048)
        for d in (1, 3, 2, 0):
            near_copy(d, i).start()

    def bring(k):
        at = pl.ds(pl.multiple_of(256 * W.group(*ORDER[k]), 256), 256)
        return pltpu.make_async_copy(normed.at[at], rows.at[k % 2], tile_sem.at[k % 2])

    def states_on(i):
        for d in XS:
            start_x(i, d).wait_recv()
        rsend[i] = entering(n, starts, endlog, 1, 1, i).astype(BF16)
        part_y(i).start()

    def tokens_on(i):
        for d in (1, 3, 2, 0):
            near_copy(d, i).wait_recv()
            there = 2 * lax.rem(z + d, 4) + core
            near[d, i] = (part[there, i].astype(F32) + near[d, i].astype(F32)).astype(BF16)
            if d:
                far_copy(d, i).start()

    bring(0).start()
    for k, (d, f) in enumerate(ORDER):
        bring(k).wait()
        if k < 7:
            bring(k + 1).start()
        q = W.group(d, f)
        v = bdot(rows[k % 2], dgate[...].reshape(T, 512))
        wa[q] = v[:, 0:C1].astype(BF16)
        wb[q] = v[:, C1:].astype(BF16)
        W.send_a(d, f)
        W.send_b(d, f)
        if k == 1:
            states_on(0)
            tokens_on(0)
        if k == 5:
            states_on(1)
            tokens_on(1)

    def bring_cot(k):
        return pltpu.make_async_copy(cot.at[:, :, :, pl.ds(256 * k, 256)], cot_s.at[k % 2], cot_sem.at[k % 2])

    bring_cot(0).start()
    for k in range(8):
        bring_cot(k).wait()
        if k < 7:
            bring_cot(k + 1).start()
        v = sum(bdot(turned[:, TOK * i : TOK * i + TOK], cot_s[k % 2, :, i].reshape(TOK, 256)) for i in range(MICRO))
        gsw[:, :, :, 256 * k : 256 * k + 256] = v.astype(BF16).reshape(4, 2, 64, 256)
    swap.start()
    for j in range(4):
        oa[4 * core + j] = gsw[j, core, :, 0:1024]
        ob[4 * core + j] = gsw[j, core, :, 1024:2048]

    loads["delta"].wait()
    loads["states"].wait()
    loads["carried"].wait()

    def inside(at, carry):
        L = logs[at]
        f = flags[at]
        E, _ = decays(L, f)
        X, B, C = activations(pre[at])
        more = heads_of(jnp.concatenate([E, delta[at]], 0), eh)
        Ex, dx = more[:Q], more[Q:]
        Ub = (dx * X).astype(BF16)
        dm = dmix[at]
        dmb = dm.astype(BF16)
        psi = bdot(C, B, NT)
        keep = same_mask(f, segrow[at])
        LT = L.T
        dpsi = jnp.zeros((Q, Q), F32)
        for j in range(4):
            js = slice(128 * j, 128 * j + 128)
            u = pair_halves(Ub[:, js])
            y = pair_halves(dmb[:, js])
            acc = jnp.zeros((Q, 128), F32)
            for e in range(2):
                h = 2 * j + e
                K = jnp.where(keep, jnp.exp(L[:, h : h + 1] - LT[h : h + 1]), 0.0)
                acc = acc + bdot((psi * K).astype(BF16), y[e], TN)
                dpsi = dpsi + bdot(y[e], u[e], NT) * K
            dno[at, :, js] = acc
        dpb = dpsi.astype(BF16)
        dbi[at, 0:128] = bdot(C, dpb, TN)
        dbi[at, 128:256] = bdot(B, dpb, TT) + bdot(states[at, 0].astype(BF16), (Ex * dm).astype(BF16), NT)
        return carry

    lax.fori_loop(0, 4, inside, 0)
    swap.wait_recv()
    for j in range(4):
        oa[4 * (1 - core) + j] = oin[j, :, 0:1024]
        ob[4 * (1 - core) + j] = oin[j, :, 1024:2048]
    for d, f in ORDER:
        O.send_a(d, f)
        O.send_b(d, f)
    lax.fori_loop(4, 8, inside, 0)
    for i in (0, 1):
        part_y(i).wait_recv()

    def inward(i, k):
        c = CH - 1 - k
        at = CH * i + c
        L = logs[at]
        d = delta[at]
        E, W_ = decays(L, flags[at])
        p = pre[at, :, 0:512]
        s = sigmoid(p)
        X = p * s
        bb = pre[at, :, 512:640]
        B = (bb * sigmoid(bb)).astype(BF16)
        more = heads_of(jnp.concatenate([E[Q - 8 :], W_, d, jnp.broadcast_to(hp[2:3], (8, 128))], 0), eh)
        Elast, Wx, dx, skip = more[7:8], more[8 : 8 + Q], more[8 + Q : 8 + 2 * Q], more[8 + 2 * Q : 9 + 2 * Q]
        U = dx * X
        dm = dmix[at]
        Yc = carried[at]
        Yi = mixed[at] - Yc - skip * X
        G = state[...]
        Gb = G.astype(BF16)
        dUi = dno[at]
        dUc = Wx * bdot(B, Gb)
        dU = dUi + dUc
        lanes = pl.ds(pl.multiple_of(Q * at, Q), Q)
        dbc[0:4, :, lanes] = (dbi[at, 0:128] + bdot(Gb, (Wx * U).astype(BF16), NT)).astype(BF16).reshape(4, 32, Q)
        dbc[4:8, :, lanes] = dbi[at, 128:256].astype(BF16).reshape(4, 32, Q)
        dL = sums_of(dm.astype(BF16).astype(F32) * Yi + dm * Yc - U.astype(BF16).astype(F32) * dUi - U * dUc, eh)
        end = sums_of(jnp.broadcast_to(jnp.sum(G * states[at, 1], 0, keepdims=True), (8, 512)), eh)[0:1]
        upper = (iota((Q, Q), 0) <= iota((Q, Q), 1)).astype(BF16)
        dstep = right_parts(upper, dL, 3) + end
        rate = hp[1:2]
        dr = (sums_of(dU * X, eh) + dstep * rate) * (1.0 - jnp.exp(-d))
        ddt[at] = dr.astype(BF16)
        small_b[0:1] += jnp.sum(dr, 0, keepdims=True)
        small_b[1:2] += jnp.sum(dstep * d * rate, 0, keepdims=True)
        gate[at] = (dx * dU + skip * dm) * (s * (1.0 + p * (1.0 - s)))
        state[...] = Elast * G + tloc[at]

    store = pltpu.make_async_copy(gate, dpre_h, load.at[0])
    for i in range(MICRO):
        state[...] = entering(n, starts, endlog, 0, 1, i) + rrecv[i].astype(F32)
        lax.fori_loop(0, CH, lambda k, carry, i=i: (inward(i, k), carry)[1], 0)
        edge_copy(i).start()
        for a, b in OTHERS:
            bc_copy(i, a, b).start()
    store.start()
    bc_all[m] = dbc[m]

    W.middle_b()
    W.middle_a(1)
    W.middle_a(0)
    for i in range(MICRO):
        for d in XS:
            far_copy(d, i).wait_recv()
        total[i] = near[0, i].astype(F32) + far[0, i].astype(F32) + far[1, i].astype(F32) + far[2, i].astype(F32)
    for i in range(MICRO):
        edge_copy(i).wait_recv()
        for a, b in OTHERS:
            bc_copy(i, a, b).wait_recv()
    O.middle_b()
    O.middle_a(1)
    O.middle_a(0)
    W.finish_first()
    O.finish_first()
    swap.wait_send()
    for i in range(MICRO):
        edge_copy(i).wait_send()
        for a, b in OTHERS:
            bc_copy(i, a, b).wait_send()
    store.wait()
    for i in range(MICRO):
        part_y(i).wait_send()
        for d in XS:
            start_x(i, d).wait_send()
            far_copy(d, i).wait_send()
        for d in range(4):
            near_copy(d, i).wait_send()


def back_wave(mixed, carried, states, gate, dno, sums, pre, delta, logs, flags, segrow, og, hp, wout, normed, cot, endlog):
    outs = [
        sds((2, TOK, 512), BF16), sds((8, Q, 512), F32), sds((8, 32, T), BF16), sds((8, Q, 128), BF16), sds((8, 512), F32), sds((8, 128), F32), sds((2, 64, 2048), F32),
        sds((2, 256, C1), BF16), sds((4, 128, C1), BF16), sds((2, 64, 1024), BF16), sds((4, 32, 1024), BF16), sds((2, 8, 512), F32),
    ]
    V = lambda *s: pltpu.VMEM(s, BF16)
    R = lambda *s: pltpu.VMEM(s, F32)
    return pl.pallas_call(
        back_wave_kernel,
        name="back_wave",
        out_shape=outs,
        in_specs=[ANY] * 5 + [VM] + [ANY] * 4 + [VM] * 3 + [ANY] * 3 + [VM],
        out_specs=[VM, ANY] + [VM] * 10,
        scratch_shapes=[
            R(8, Q, 512), R(8, Q, 512), R(8, 2, 128, 512), R(8, Q, 512), R(8, Q, 512), R(8, Q, 768), R(8, Q, 128), R(8, Q, 128), R(8, Q, 128), V(512, 2048),
            V(2, TOK, 512), R(8, Q, 512), R(8, 128, 512), R(8, 256, 128), V(8, 2, 128, 512), V(2, 128, 512), V(2, 128, 512), V(2, 256, T), V(8, 2, 64, 2048),
            V(4, 2, 64, 2048), V(3, 2, 64, 2048),
            V(8, 256, C1), V(8, 256, C1), V(3, 2, 256, C1), V(3, 4, 128, C1), V(512, T), V(2, 8, 2, 64, 256), V(4, 2, 64, 2048), V(8, 64, 1024), V(8, 64, 1024), V(3, 2, 64, 1024), V(3, 4, 32, 1024), V(4, 64, 2048), V(8, 32, T), R(128, 512),
            pltpu.SemaphoreType.DMA((96,)), pltpu.SemaphoreType.DMA((96,)), pltpu.SemaphoreType.DMA((16,)), pltpu.SemaphoreType.DMA((2,)), pltpu.SemaphoreType.DMA((2,)),
        ],
        compiler_params=pltpu.CompilerParams(collective_id=4, has_side_effects=True, vmem_limit_bytes=62 << 20),
        cost_estimate=pl.CostEstimate(flops=8 << 30, bytes_accessed=32 << 20, transcendentals=0),
    )(mixed, carried, states, gate.reshape(8, Q, 512), dno, sums, pre, delta, logs, flags, segrow, og, hp, wout, normed, cot, endlog)


CB = 256
CA = 640 - CB


def tail_kernel(
    bc_s, ex_s, wpa, wpb, opa, opb, branch, gain, cot, dpre, pre, ext, flags, fnext, conv, ddt, dgate, w, wg, hid, normed, small_o, small_b,
    gi, g_out, layer_out, grad_in, small_all,
    eb_src, eb_s, dps, pre_s, ext_s, fl_s, fn_s, ddt_s, dg_s, w_s, hid_s, nm_s, wt, e_s, dproj, part, near, far, conv_acc, gnorm,
    s0, s1, s2, sx, ga, gb, ga1, ga2, gpa, gb1, gb2, gpb, gb3, oa2, ob2, ob3, cot_own, ga2_, gb2_, gb3_, final, send, recv, load,
):
    n = Net(send, recv)
    x, y, z, c, m = n.x, n.y, n.z, n.c, n.m
    loads = {}

    def fetch(key, src, dst):
        loads[key] = pltpu.make_async_copy(src, dst, load.at[len(loads)])
        loads[key].start()

    fetch("pre", pre.at[:, :, pl.ds(512, 256)], pre_s)
    fetch("w", w, w_s.at[:, pl.ds(512, 896)])
    fetch("dpre", dpre, dps.at[:, pl.ds(0, TOK), pl.ds(0, 512)])
    fetch("ext", ext, ext_s)
    fetch("flags", flags, fl_s)
    fetch("fnext", fnext, fn_s)
    fetch("ddt", ddt, ddt_s)
    fetch("normed", normed, nm_s)
    fetch("dgate", dgate, dg_s)
    fetch("wg", wg, w_s.at[:, pl.ds(0, 512)])
    fetch("hid", hid, hid_s)
    fetch("cot", cot.at[m], cot_own)
    n.meet([n.at(dz=a, dc=b) for a, b in OTHERS] + [n.at(dx=d) for d in XS] + [n.at(dy=d) for d in XS] + [n.group(1), n.group(7)])
    G_ = Reduce(n, "g", None, None, None, ga2_, wpa, None, gb2_, wpb, gb3_)
    G_.go_a(1)
    G_.go_a(0)
    G_.go_b()
    O = Reduce(n, "o", None, None, None, oa2, opa, None, ob2, opb, ob3)
    O.go_a(1)
    O.go_a(0)
    O.go_b()

    edge2 = n.copy("edge2", eb_src, eb_s, n.group(7))

    def near_copy(d, i):
        return n.copy(("near", d, i), part.at[2 * lax.rem(z + d, 4) + 1 - c, i], near.at[d, i], n.at(dc=1))

    def far_copy(d, i):
        return n.copy(("far", d, i), near.at[d, i], far.at[d - 1, i], n.at(dz=d))

    def small_x(d):
        return n.copy(("sx", d), s0, s1.at[d - 1], n.at(dx=d))

    def small_y(d):
        return n.copy(("sy", d), sx, s2.at[d - 1], n.at(dy=d))

    def small_m(a, b):
        return n.copy(("sm", a, b), small_all.at[m], small_all.at[m], n.at(dz=a, dc=b))

    def rows_copy(a, b):
        return n.copy(("rows", a, b), final.at[n.member(a, b)], gi.at[m], n.at(dz=a, dc=b))

    W = Reduce(n, "w", ga, gb, ga1, ga2, gpa, gb1, gb2, gpb, gb3)

    pick = pick_matrix(256, 32 * m, 32, 0)
    loads["w"].wait()
    wt[...] = (bdot(w_s[:, 1024:1280], pick) + bdot(w_s[:, 1280:1408], pick_matrix(128, 0, 8, 32))).astype(BF16)
    cw = jnp.concatenate([conv[:, 0:512], left_parts(conv[:, 512:768], pick, 3)], 1)
    for key in ("pre", "dpre"):
        loads[key].wait()
    eye = pick_matrix(32, 0, 32, 0)

    def bc_chunk(i, k):
        t = CH * i + k
        tot = bc_s[0, :, Q * t : Q * t + Q].astype(F32)
        for q in range(1, 8):
            tot = tot + bc_s[q, :, Q * t : Q * t + Q].astype(F32)
        d = left_parts(tot, eye, 2, TN)
        p = left_parts(pre_s[t], pick, 2)
        s = sigmoid(p)
        dps[i, Q * k : Q * k + Q, 512:640] = d * (s * (1.0 + p * (1.0 - s)))

    for i in range(MICRO):
        bc_chunk(i, 0)
        eb_src[i] = dps[i, 0:8, 512:640]
    edge2.start()
    for i in range(MICRO):
        for k in range(1, CH):
            bc_chunk(i, k)
    for key in ("ext", "flags", "fnext", "ddt"):
        loads[key].wait()
    conv_acc[...] = jnp.zeros_like(conv_acc)
    pick_dt = pick_matrix(128, 0, 8, 32)

    def conv_chunk(i, k):
        t = CH * i + k
        e_s[:, 0:512] = ext_s[t, :, 0:512].astype(F32)
        e_s[:, 512:640] = bdot(ext_s[t, :, 512:768], pick)
        f, fn = fl_s[t], fn_s[t]
        dp = dps[i, Q * k : Q * k + Q]
        dx = cw[3:4] * dp
        conv_acc[3:4] += jnp.sum(dp * e_s[8 : 8 + Q], 0, keepdims=True)
        conv_acc[4:5] += jnp.sum(dp, 0, keepdims=True)
        for j in range(3):
            conv_acc[j : j + 1] += jnp.sum(dp * e_s[5 + j : 5 + j + Q] * f[:, j : j + 1], 0, keepdims=True)
            dx = dx + cw[j : j + 1] * dps[i, Q * k + 3 - j : Q * k + 3 - j + Q] * fn[:, j : j + 1]
        rows = slice(Q * k, Q * k + Q)
        dproj[i, rows, 0:512] = dx[:, 0:512].astype(BF16)
        dproj[i, rows, 512:640] = (dx[:, 512:640] + bdot(ddt_s[t], pick_dt)).astype(BF16)

    for i in range(MICRO):
        for k in range(CH - 1):
            conv_chunk(i, k)
    edge2.wait_recv()
    for i in range(MICRO):
        dps[i, TOK : TOK + 8, 0:512] = ex_s[i]
        dps[i, TOK : TOK + 8, 512:640] = eb_s[i]
        conv_chunk(i, CH - 1)

    loads["hid"].wait()
    loads["dgate"].wait()
    loads["wg"].wait()
    for i in range(MICRO):
        h = hid_s[:, i].reshape(TOK, 2048).astype(F32)
        scale = row_scale(h)
        first, main, rest = dg_s[i], dproj[i, :, 0:512], dproj[i, :, 512:640]

        def tile_of(j, carry, i=i, scale=scale, first=first, main=main, rest=rest):
            at = pl.ds(pl.multiple_of(256 * j, 256), 256)
            d = bdot(first, w_s[at, 0:512], NT) + bdot(main, w_s[at, 512:1024], NT) + bdot(rest, wt[at], NT)
            part[:, i, :, at] = d.astype(BF16).reshape(8, 64, 256)
            hv = hid_s[:, i, :, at].reshape(TOK, 256).astype(F32)
            s = jnp.sum(d * (hv * scale), 0, keepdims=True)
            gnorm[0:1, at] = s if i == 0 else gnorm[0:1, at] + s
            return carry

        lax.fori_loop(0, 8, tile_of, 0)
        for d in (1, 3, 2, 0):
            near_copy(d, i).start()
    for r in range(16):
        s0[r : r + 1] = gnorm[0:1, 128 * r : 128 * r + 128]
    for k in range(5):
        for r in range(5):
            s0[16 + 5 * k + r : 17 + 5 * k + r] = conv_acc[k : k + 1, 128 * r : 128 * r + 128]
    for r in range(4):
        s0[41 + r : 42 + r] = small_o[0:1, 128 * r : 128 * r + 128]
    s0[45:47] = small_b[0:2]
    s0[47:48] = sums_of(small_o[...], spread_matrix())[1:2]
    for d in XS:
        small_x(d).start()

    def tokens_on(i):
        for d in (1, 3, 2, 0):
            near_copy(d, i).wait_recv()
            there = 2 * lax.rem(z + d, 4) + c
            near[d, i] = (part[there, i].astype(F32) + near[d, i].astype(F32)).astype(BF16)
            if d:
                far_copy(d, i).start()

    loads["normed"].wait()
    for k, (d, f) in enumerate(ORDER):
        q = W.group(d, f)
        at = pl.ds(pl.multiple_of(256 * q, 256), 256)
        v = bdot(nm_s[at], dproj[...].reshape(T, 640)).astype(BF16)
        gb[q] = v[:, 0:CB]
        ga[q] = v[:, CB:]
        W.send_a(d, f)
        W.send_b(d, f)
        if k == 2:
            tokens_on(0)
        if k == 6:
            tokens_on(1)

    G_.last_b()
    O.last_b()
    g_out[:, 0:1024] = O.last_a()
    final[:, :, 0:C1] = G_.last_a().astype(BF16).reshape(8, 32, C1)
    for i in range(MICRO):
        layer_out[i] = (hid_s[m, i].astype(F32) + branch[i]).astype(BF16)
    for d in XS:
        small_x(d).wait_recv()
    sx[...] = s0[...] + s1[0] + s1[1] + s1[2]
    for d in XS:
        small_y(d).start()
    W.middle_b()
    W.go_b()
    W.middle_a(1)
    W.go_a(1)
    W.middle_a(0)
    W.go_a(0)
    W.last_b()
    for d in XS:
        small_y(d).wait_recv()
    small_all[m] = sx[...] + s2[0] + s2[1] + s2[2]
    for a, b in OTHERS:
        small_m(a, b).start()
    for i in range(MICRO):
        for d in XS:
            far_copy(d, i).wait_recv()
        dn = near[0, i].astype(F32) + far[0, i].astype(F32) + far[1, i].astype(F32) + far[2, i].astype(F32)
        if i == 0:
            loads["cot"].wait()
        h = hid_s[m, i].astype(F32)
        r = row_scale(h)
        dg = dn * gain[0:1]
        grad_in[i] = (cot_own[i].astype(F32) + r * dg - h * (r * r * r) * jnp.mean(dg * h, axis=-1, keepdims=True)).astype(BF16)
    O.third_b().wait_recv()
    for h in range(2):
        g_out[32 * h : 32 * h + 32, 1024:2048] = ob3[h]
    W.third_b().wait_recv()
    for h in range(2):
        final[4 * h : 4 * h + 4, :, 512 : 512 + CB] = gb3[h].reshape(4, 32, CB)
    final[:, :, 512 + CB :] = W.last_a().astype(BF16).reshape(8, 32, CA)
    G_.third_b().wait_recv()
    for h in range(2):
        final[4 * h : 4 * h + 4, :, C1:512] = gb3_[h].reshape(4, 32, C1)
    for a, b in OTHERS:
        rows_copy(a, b).start()
    gi[m] = final[m]
    for a, b in OTHERS:
        rows_copy(a, b).wait_recv()
        small_m(a, b).wait_recv()
    W.finish_first()
    W.finish()
    O.finish()
    G_.finish()
    for a, b in OTHERS:
        rows_copy(a, b).wait_send()
        small_m(a, b).wait_send()
    for d in XS:
        small_x(d).wait_send()
        small_y(d).wait_send()
        for i in range(MICRO):
            far_copy(d, i).wait_send()
    for d in range(4):
        for i in range(MICRO):
            near_copy(d, i).wait_send()
    edge2.wait_send()


def tail_call(bc_all, edges, wpa, wpb, opa, opb, branch, gain, cot, dpre, pre, ext, flags, fnext, conv, ddt, dgate, w, wg, hid, normed, small_o, small_b):
    outs = [sds((8, 32, 1152), BF16), sds((64, 2048), F32), sds((2, 64, 2048), BF16), sds((2, 64, 2048), BF16), sds((8, 48, 128), F32)]
    V = lambda *s: pltpu.VMEM(s, BF16)
    R = lambda *s: pltpu.VMEM(s, F32)
    scratch = [
        R(2, 8, 128), R(2, 8, 128), R(2, TOK + 8, 640), R(8, Q, 256), V(8, Q + 8, 768), R(8, Q, 128), R(8, Q, 128), V(8, Q, 128), V(2, TOK, 512), V(2048, 1408),
        V(8, 2, 64, 2048), V(2048, T), V(2048, 128), R(Q + 8, 640), V(2, TOK, 640), V(8, 2, 64, 2048), V(4, 2, 64, 2048), V(3, 2, 64, 2048), R(8, 640), R(8, 2048),
        R(48, 128), R(3, 48, 128), R(3, 48, 128), R(48, 128),
        V(8, 256, CA), V(8, 256, CB), V(3, 2, 256, CA), V(3, 256, CA), V(2, 256, CA), V(3, 4, 128, CB), V(3, 128, CB), V(4, 128, CB), V(2, 128, CB),
        V(3, 64, 1024), V(3, 32, 1024), R(2, 32, 1024), V(2, 64, 2048), V(3, 256, C1), V(3, 128, C1), V(2, 128, C1), V(8, 32, 1152),
    ]
    return pl.pallas_call(
        tail_kernel,
        name="tail",
        out_shape=outs,
        in_specs=[VM] * 8 + [ANY] * 6 + [VM] + [ANY] * 6 + [VM] * 2,
        out_specs=[VM] * 5,
        scratch_shapes=[*scratch, pltpu.SemaphoreType.DMA((112,)), pltpu.SemaphoreType.DMA((112,)), pltpu.SemaphoreType.DMA((12,))],
        compiler_params=pltpu.CompilerParams(collective_id=5, has_side_effects=True, vmem_limit_bytes=62 << 20),
        cost_estimate=pl.CostEstimate(flops=8 << 30, bytes_accessed=32 << 20, transcendentals=0),
    )(bc_all, edges, wpa, wpb, opa, opb, branch, gain, cot, dpre, pre, ext, flags, fnext, conv, ddt, dgate, w, wg, hid, normed, small_o, small_b)


def from_members(v):
    r = v.shape[1]
    return v.reshape(4, 2, r, 4, 128).transpose(2, 1, 3, 0, 4).reshape(r, 4096)


def from_heads(v):
    r = v.shape[1]
    return v.reshape(4, 2, r, 4, 2).transpose(2, 1, 3, 0, 4).reshape(r, 64)


def from_rows(v):
    return v.transpose(1, 0, 2).reshape(v.shape[1], 256)


def to_members(v):
    r = v.shape[0]
    return v.reshape(r, 2, 4, 4, 128).transpose(3, 1, 0, 2, 4).reshape(8, r, 512)


def xdot(a, b, dims=NN):
    return lax.dot_general(a, b, dims, preferred_element_type=F32)


def per_device(layer_in, cotangent, segment_ids, norm_gain, in_weight, conv_weight, conv_bias, dt_bias, a_log, skip_gain, out_gain, out_weight):
    xi, yi, zi, ci = (lax.axis_index(a) for a in SEQ)
    g = 2 * xi + yi
    m = 2 * zi + ci
    lane = jnp.arange(128)

    def placed(v, width, at):
        return jnp.where(lane // width == at, jnp.tile(v, 128 // width), 0.0)

    head = lane == 2 * (g % 4) + ci
    rows = [placed(segment_ids[i, 0].astype(F32), 64, ci) for i in range(MICRO)]
    rows += [placed(norm_gain, 32, m % 4), placed(out_gain, 64, ci)]
    rows += [jnp.where(head, v, 0.0) for v in (dt_bias, a_log, skip_gain)]
    window = jnp.pad(jnp.concatenate([conv_weight, conv_bias[None]], 0), ((0, 3), (0, 60)))
    window = lax.dynamic_update_slice(jnp.zeros((8, 256), F32), window, (0, 68 * (8 * g + m) % 128))
    pack = jnp.concatenate([jnp.stack(rows), jnp.zeros((1, 128), F32), window[:, :128], window[:, 128:]], 0)
    bc = jnp.broadcast_to(in_weight[None, :, 8192:8448], (8, 32, 256))
    dt_w = in_weight[:, 8448:].reshape(32, 2, 4, 4, 2).transpose(3, 1, 0, 2, 4).reshape(8, 32, 8)
    g_send = to_members(in_weight[:, :4096])
    w_send = jnp.concatenate([to_members(in_weight[:, 4096:8192]), bc, dt_w, jnp.zeros((8, 32, 120), BF16)], 2)
    (
        normed, hid_all, w_in, w_gate, gate, pre, ext, delta, logs, flags, fnext, mixed, carried, states, dno, cot, w_out,
        sums, ends_all, conv, hp, og, gain, segrow,
    ) = wave(layer_in[:, 0], w_send, g_send, pack, cotangent[:, 0], out_weight)
    w_in = w_in.reshape(2048, 896)
    w_gate = w_gate.reshape(2048, 512)
    dgate, dpre, bc_all, ddt, small_o, small_b, own_branch, wpa, wpb, opa, opb, edges = back_wave(
        mixed, carried, states, gate, dno, sums, pre, delta, logs, flags, segrow, og, hp, w_out.reshape(512, 2048), normed, cot, ends_all
    )
    dpre = dpre.reshape(MICRO, TOK, 512)
    gi, g_out, layer_out, grad_in, small_sum = tail_call(
        bc_all, edges, wpa, wpb, opa, opb, own_branch, gain, cot, dpre, pre, ext, flags, fnext, conv, ddt, dgate, w_in, w_gate, hid_all, normed, small_o, small_b
    )
    gi = gi.astype(F32)
    g_in = jnp.concatenate([from_members(gi[:, :, :512]), from_members(gi[:, :, 512:1024]), from_rows(gi[:, :, 1024:1056]), from_heads(gi[:, :, 1056:1064])], 1)
    at = 8 * g + m
    g_norm = lax.dynamic_slice(small_sum[:, :16].sum(0).reshape(64, 32), (at, 0), (1, 32)).reshape(32)
    conv_s = small_sum[:, 16:41].reshape(8, 5, 640)
    conv_s = jnp.concatenate([from_members(conv_s[:, :, :512]), from_rows(conv_s[:, :, 512:544])], 1)
    conv_s = lax.dynamic_slice(conv_s, (0, 68 * at), (5, 68))
    og_s = from_members(small_sum[:, 41:45].reshape(8, 1, 512))[0]
    og_s = lax.dynamic_slice(og_s, (64 * at,), (64,))
    hd_s = from_heads(small_sum[:, 45:48, :8])
    hd_s = lax.dynamic_slice(hd_s, (0, at), (3, 1))
    return (layer_out[:, None], grad_in[:, None], g_norm, g_in, conv_s[:4], conv_s[4], hd_s[0], hd_s[1], hd_s[2], og_s, g_out)


def solution(mesh):
    fine = Mesh(mesh.devices.reshape(2, 4, 2, 4, 2), AXES)
    tok = P(None, "rep", SEQ, None)
    return jax.shard_map(
        per_device,
        mesh=fine,
        in_specs=(tok, tok, P(None, "rep", SEQ), P(SEQ), P(SEQ, None), P(None, SEQ), P(SEQ), P(SEQ), P(SEQ), P(SEQ), P(SEQ), P(SEQ, None)),
        out_specs=(tok, tok, P(SEQ), P(SEQ, None), P(None, SEQ), P(SEQ), P(SEQ), P(SEQ), P(SEQ), P(SEQ), P(SEQ, None)),
        check_vma=False,
    )
```

```python
import functools

import jax
import jax.numpy as jnp
from jax import lax
from jax.experimental import pallas as pl
from jax.experimental.pallas import tpu as pltpu
from jax.sharding import Mesh, PartitionSpec as P

EPS = 1e-05
INNER = 4096
MICRO = 2
CONV = 4352
F32 = jnp.float32
BF16 = jnp.bfloat16
AXES = ("rep", "x", "y", "z", "c")
SEQ = ("x", "y", "z", "c")
GROUPS = 8
TOK = 512
Q = 128
CH = TOK // Q

MESH = pl.DeviceIdType.MESH
ANY = pl.BlockSpec(memory_space=pl.ANY)
VM = pl.BlockSpec(memory_space=pltpu.VMEM)


class Net:
    def __init__(self, send, recv):
        self.send, self.recv, self.used, self.open = send, recv, 0, []
        self.keys = {}
        self.rep, self.x, self.y, self.z, self.c = (lax.axis_index(a) for a in AXES)
        self.ring = 2 * self.rep + self.y
        self.g = 2 * self.x + self.y
        self.m = 2 * self.z + self.c

    def at(self, dx=0, dy=0, dz=0, dc=0):
        ring = lax.rem(self.ring + dy, 4)
        return (ring // 2, lax.rem(self.x + dx, 4), lax.rem(ring, 2), lax.rem(self.z + dz, 4), lax.rem(self.c + dc, 2))

    def pair(self):
        return (self.rep, self.x, 1 - self.y, self.z, self.c)

    def across(self, dx):
        return (self.rep, lax.rem(self.x + dx, 4), 1 - self.y, self.z, self.c)

    def group(self, d):
        g = lax.rem(self.g + d, 8)
        return (self.rep, g // 2, lax.rem(g, 2), self.z, self.c)

    def member(self, dz, dc):
        return 2 * lax.rem(self.z + dz, 4) + lax.rem(self.c + dc, 2)

    def push(self, src, dst, where):
        i = self.used
        self.used += 1
        copy = pltpu.make_async_remote_copy(
            src_ref=src, dst_ref=dst, send_sem=self.send.at[i], recv_sem=self.recv.at[i], device_id=where, device_id_type=MESH
        )
        copy.start()
        self.open.append(copy)
        return copy

    def copy(self, key, src, dst, where):
        i = self.keys.setdefault(key, len(self.keys))
        return pltpu.make_async_remote_copy(
            src_ref=src, dst_ref=dst, send_sem=self.send.at[i], recv_sem=self.recv.at[i], device_id=where, device_id_type=MESH
        )

    def behind(self, d):
        return 2 * lax.rem(self.x + 4 - d, 4) + self.y

    def local(self, src, dst):
        i = self.used
        self.used += 1
        copy = pltpu.make_async_copy(src, dst, self.recv.at[i])
        copy.start()
        return copy

    def meet(self, peers):
        barrier = pltpu.get_barrier_semaphore()
        for peer in peers:
            pl.semaphore_signal(barrier, inc=1, device_id=peer, device_id_type=MESH)
        pl.semaphore_wait(barrier, len(peers))

    def finish(self):
        for copy in self.open:
            copy.wait_send()


OTHERS = [(dz, dc) for dz in (0, 1, 3, 2) for dc in (0, 1) if (dz, dc) != (0, 0)]
ZS = (0, 1, 3, 2)
XS = (1, 3, 2)
ORDER = [(d, f) for d in (2, 1, 3, 0) for f in (1, 0)]


def call(kernel, name, cid, outs, ins, spaces_in, spaces_out, sems, scratch=(), cost=1 << 20):
    return pl.pallas_call(
        kernel,
        name=name,
        out_shape=outs,
        in_specs=spaces_in,
        out_specs=spaces_out,
        scratch_shapes=[*scratch, pltpu.SemaphoreType.DMA((sems,)), pltpu.SemaphoreType.DMA((sems,))],
        compiler_params=pltpu.CompilerParams(collective_id=cid, has_side_effects=True, vmem_limit_bytes=60 << 20),
        cost_estimate=pl.CostEstimate(flops=0, bytes_accessed=cost, transcendentals=0),
    )(*ins)


def sds(shape, dtype):
    return jax.ShapeDtypeStruct(shape, dtype)


def add4(a, b):
    return a.astype(F32) + b[0].astype(F32) + b[1].astype(F32) + b[2].astype(F32)


NN = (((1,), (0,)), ((), ()))
NT = (((1,), (1,)), ((), ()))
TN = (((0,), (0,)), ((), ()))
TT = (((0,), (1,)), ((), ()))


def bdot(a, b, dims=NN):
    return lax.dot_general(a, b, dims, preferred_element_type=F32)


def parts(v, count):
    out = []
    for _ in range(count):
        p = v.astype(BF16)
        out.append(p)
        v = v - p.astype(F32)
    return out


def left_parts(v, w, count, dims=NN):
    return sum(bdot(p, w, dims) for p in parts(v, count))


def right_parts(w, v, count, dims=NN):
    return sum(bdot(w, p, dims) for p in parts(v, count))


def iota(shape, dim):
    return lax.broadcasted_iota(jnp.int32, shape, dim)


def spread_matrix():
    return (iota((128, 512), 0) == iota((128, 512), 1) // 64).astype(BF16)


def heads_of(v, eh):
    return left_parts(v, eh, 2)


def sums_of(v, eh):
    return left_parts(v, eh, 2, NT)


def lower_matrix():
    return (iota((Q, Q), 0) >= iota((Q, Q), 1)).astype(BF16)


def sigmoid(v):
    return 1.0 / (1.0 + jnp.exp(-v))


def softplus(v):
    return jnp.maximum(v, 0.0) + jnp.log1p(jnp.exp(-jnp.abs(v)))


def row_scale(h):
    return lax.rsqrt(jnp.mean(h * h, axis=-1, keepdims=True) + EPS)


def decays(L, flags):
    E = jnp.exp(L) * flags[:, 3:4]
    W = jnp.exp(L[Q - 1 : Q] - L) * flags[:, 4:5]
    return E, W


def wave_kernel(
    hid, wsend, pack, cot, outw,
    normed_h, hid_h, w_h, gate_h, pre_h, ext_h, delta_h, logs_h, flags_h, fnext_h, mixed_h, carried_h, states_h, dno_h, cot_h, wout_h,
    sums, endlog, conv, hp, og, gain, segrow,
    hid_s, halo, nrm, turned, w_s, small, proj, pre, ext, delta, logs, flags, fnext, sloc, inner, carried, states, dno, ends, rsend, rrecv, cot_s, w_o, wo_s, convt, state, total, tail, send, recv, done, local,
):
    eh = spread_matrix()
    n = Net(send, recv)
    g, m, x, y, z, core = n.g, n.m, n.x, n.y, n.z, n.c
    ALLX = (0,) + XS
    copies = []

    def keyed(key, src, dst, where):
        cp = n.copy(key, src, dst, where)
        copies.append(cp)
        cp.start()
        return cp

    stores = []

    def store(src, dst):
        cp = pltpu.make_async_copy(src, dst, done.at[len(stores)])
        cp.start()
        stores.append(cp)

    n.meet([n.at(dz=a, dc=b) for a, b in OTHERS] + [n.at(dx=d) for d in XS] + [n.at(dy=1), n.at(dy=3), n.group(1), n.group(7)] + [n.across(d) for d in ALLX])

    wa, sa = {}, {}
    for a, b in OTHERS:
        wa[a, b] = keyed(("wa", a, b), wsend.at[n.member(a, b)], w_h.at[g, m], n.at(dz=a, dc=b))
        sa[a, b] = keyed(("sa", a, b), pack, small.at[g, m], n.at(dz=a, dc=b))
    own = [pltpu.make_async_copy(wsend.at[m], w_h.at[g, m], local.at[0]), pltpu.make_async_copy(hid, hid_h.at[m], local.at[1]), pltpu.make_async_copy(cot, cot_h.at[m], local.at[2])]
    for cp in own:
        cp.start()
    small[g, m] = pack[...]
    w_o[g] = outw[...]
    wx, wy, sx, sy = {}, {}, {}, {}

    def along_y(d, k):
        first = pl.ds(2 * lax.rem(z + 4 - ZS[k], 4), 2)
        for half, dy in ((0, 1), (1, 3)):
            part = w_h.at[n.behind(d), first, pl.ds(16 * half, 16)]
            wy[d, k, half] = keyed(("wy", d, k, half), part, part, n.at(dy=dy))

    def arrived(k):
        for b in (0, 1):
            if (ZS[k], b) in wa:
                wa.pop((ZS[k], b)).wait_recv()

    def issue(k):
        arrived(k)
        block = w_h.at[g, pl.ds(2 * lax.rem(z + 4 - ZS[k], 4), 2)]
        for d in XS:
            wx[k, d] = keyed(("wx", k, d), block, block, n.at(dx=d))
        along_y(0, k)

    def forward(k):
        for d in XS:
            wx[k, d].wait_recv()
            along_y(d, k)

    for cp in own:
        cp.wait()
    issue(0)
    issue(1)
    arrived(2)
    arrived(3)
    hz = {a: keyed(("hz", a), hid_h.at[m], hid_h.at[m], n.at(dz=a)) for a in (1, 3, 2)}
    hn = [keyed("hn", hid_h.at[m], hid_h.at[m], n.at(dc=1))]
    for a, b in OTHERS:
        sa[a, b].wait_recv()
    for d in XS:
        sx[d] = keyed(("sx", d), small.at[g], small.at[g], n.at(dx=d))
    sy[0] = keyed(("sy", 0), small.at[g], small.at[g], n.pair())
    forward(0)
    issue(2)
    for d in XS:
        sx[d].wait_recv()
        mine = small.at[n.behind(d)]
        sy[d] = keyed(("sy", d), mine, mine, n.pair())
    forward(1)
    issue(3)
    for d in ALLX:
        sy[d].wait_recv()

    for q in range(16):
        v = small[q // 2, 4 * (q % 2), 2:3]
        for u in range(1, 4):
            v = v + small[q // 2, 4 * (q % 2) + u, 2:3]
        gain[0:1, 128 * q : 128 * q + 128] = v
    heads3 = jnp.zeros((3, 128), F32)
    for j in range(4):
        og[0:1, 128 * j : 128 * j + 128] = small[4 * core + j, 2 * z, 3:4] + small[4 * core + j, 2 * z + 1, 3:4]
        for e in range(2):
            heads3 = heads3 + small[4 * core + j, 2 * z + e, 4:7]
    hp[...] = jnp.zeros_like(hp)
    hp[0:1] = heads3[0:1]
    hp[1:2] = jnp.where(iota((1, 128), 1) < 8, -jnp.exp(heads3[1:2]), 0.0)
    hp[2:3] = heads3[2:3]
    for q in range(34):
        v = jnp.zeros((8, 128), F32)
        for i in range(64):
            if 68 * i // 128 == q:
                v = v + small[i // 8, i % 8, 8:16]
            elif 68 * i // 128 == q - 1:
                v = v + small[i // 8, i % 8, 16:24]
        convt[q] = v
    for j in range(4):
        conv[:, 128 * j : 128 * j + 128] = convt[4 * (4 * core + j) + z]
    conv[:, 512:640] = convt[32]
    conv[:, 640:768] = convt[33]

    forward(2)
    for a in (1, 3, 2):
        hz[a].wait_recv()
        theirs = hid_h.at[2 * lax.rem(z + 4 - a, 4) + core]
        hn.append(keyed(("hf", a), theirs, theirs, n.at(dc=1)))
    cz = {a: keyed(("cz", a), cot_h.at[m], cot_h.at[m], n.at(dz=a)) for a in (1, 3, 2)}
    cn = [keyed("cn", cot_h.at[m], cot_h.at[m], n.at(dc=1))]

    lane = iota((8, 128), 1)

    def chunk_row(group, i, c):
        return jnp.broadcast_to(small[group, 2 * c, i : i + 1] + small[group, 2 * c + 1, i : i + 1], (8, 128))

    for i in range(MICRO):
        before = jnp.where(g > 0, chunk_row(lax.rem(g + 7, 8), i, CH - 1), -1.0)
        after = jnp.where(g < 7, chunk_row(lax.rem(g + 1, 8), i, 0), -2.0)
        rows = [before] + [chunk_row(g, i, c) for c in range(CH)] + [after]
        for c in range(CH):
            prv, cur, nxt = rows[c : c + 3]
            here, ahead = [], []
            for d in (3, 2, 1):
                back = jnp.where(lane < d, pltpu.roll(prv, d, 1), pltpu.roll(cur, d, 1))
                here.append((back == cur).astype(F32))
                on = jnp.where(lane >= 128 - d, pltpu.roll(nxt, 128 - d, 1), pltpu.roll(cur, 128 - d, 1))
                ahead.append((on == cur).astype(F32))
            here += [(cur == prv[:, 127:128]).astype(F32), (cur == cur[:, 127:128]).astype(F32), cur]
            sub = iota((128, 128), 0)
            for rows_of, to in ((here, flags), (ahead, fnext)):
                v = jnp.zeros((128, 128), F32)
                for r, row in enumerate(rows_of):
                    v = jnp.where(sub == r, jnp.broadcast_to(row[0:1], (128, 128)), v)
                to[CH * i + c] = v.T
            segrow[CH * i + c] = cur[0:1]

    forward(3)
    ox = {d: keyed(("ox", d), w_o.at[g], w_o.at[g], n.at(dx=d)) for d in XS}
    oy = {}

    def out_y(d):
        for half, dy in ((0, 1), (1, 3)):
            part = w_o.at[n.behind(d), pl.ds(32 * half, 32)]
            oy[d, half] = keyed(("oy", d, half), part, part, n.at(dy=dy))

    out_y(0)
    for cp in hn:
        cp.wait_recv()
    edge = keyed("edge", hid_h.at[7, :, pl.ds(48, 16)], halo, n.group(1))
    bring_h = pltpu.make_async_copy(hid_h, hid_s, local.at[0])
    bring_h.start()
    bring_w = [pltpu.make_async_copy(w_h.at[2 * k + y], w_s.at[2 * k + y], local.at[2 + k]) for k in range(4)]
    for cp in bring_w:
        cp.start()
    bring_h.wait()

    gv = gain[0:1]

    def norm(k, carry):
        for i in range(MICRO):
            h = hid_s[pl.ds(2 * k, 2), i].reshape(Q, 2048).astype(F32)
            v = h * row_scale(h) * gv
            nrm[i, pl.ds(pl.multiple_of(16 + Q * k, 16), Q)] = v.astype(BF16)
            turned[:, pl.ds(pl.multiple_of(TOK * i + Q * k, Q), Q)] = v.T.astype(BF16)
        return carry

    lax.fori_loop(0, CH, norm, 0)
    edge.wait_recv()
    for i in range(MICRO):
        h = halo[i].astype(F32)
        nrm[i, 0:16] = (h * row_scale(h) * gv).astype(BF16)
    store(turned, normed_h)

    def project(side, first):
        for i in range(MICRO):
            for lo in range(0, 1408, 256):
                hi = min(lo + 256, 1408)
                v = 0.0 if first else proj[i, :, lo:hi]
                for k in range(4):
                    q = 2 * k + side
                    v = v + bdot(nrm[i, :, pl.ds(pl.multiple_of(256 * q, 256), 256)], w_s[q, :, :, lo:hi].reshape(256, hi - lo))
                proj[i, :, lo:hi] = v

    for cp in bring_w:
        cp.wait()
    project(y, True)
    for d in ALLX:
        for k in range(4):
            for half in (0, 1):
                wy[d, k, half].wait_recv()
    bring_w = [pltpu.make_async_copy(w_h.at[2 * k + 1 - y], w_s.at[2 * k + 1 - y], local.at[2 + k]) for k in range(4)]
    for cp in bring_w:
        cp.start()
    for cp in bring_w:
        cp.wait()
    project(1 - y, False)
    for d in XS:
        ox[d].wait_recv()
        out_y(d)
    store(flags, flags_h)
    store(fnext, fnext_h)

    def front(i, c):
        at = CH * i + c
        rows = pl.ds(pl.multiple_of(16 + Q * c, 16), Q)
        f = flags[at]
        xbc = proj[i, rows, 512:1280].astype(BF16).astype(F32)
        tail[8:] = xbc
        acc = conv[4:5] + conv[3:4] * xbc
        for k in range(3):
            acc = acc + conv[k : k + 1] * tail[5 + k : 5 + k + Q] * f[:, k : k + 1]
        pre[at] = acc
        ext[at] = tail[...].astype(BF16)
        d = softplus(proj[i, rows, 1280:1408] + hp[0:1])
        delta[at] = d
        L = right_parts(lower_matrix(), d * hp[1:2], 3)
        logs[at] = L
        E, W = decays(L, f)
        xv = acc[:, :512]
        X = xv * sigmoid(xv)
        b = acc[:, 512:640]
        B = (b * sigmoid(b)).astype(BF16)
        S = right_parts(B, heads_of(W * d, eh) * X, 2, TN)
        sloc[at] = S
        last = heads_of(E[Q - 8 :], eh)
        state[...] = last[7:8] * state[...] + S
        tail[0:8] = tail[Q : Q + 8]
        total[...] = total[...] + L[Q - 1 : Q]

    ex, lx, ly = {}, {}, {}
    for i in range(MICRO):
        tail[0:8] = proj[i, 8:16, 512:1280].astype(BF16).astype(F32)
        state[...] = jnp.zeros_like(state)
        total[...] = jnp.zeros_like(total)
        lax.fori_loop(0, CH, lambda c, carry, i=i: (front(i, c), carry)[1], 0)
        ends[g, i] = state[...].astype(BF16)
        lt = parts(jnp.broadcast_to(heads_of(jnp.broadcast_to(total[...], (8, 128)), eh)[0:1], (16, 512)), 3)
        seg = jnp.broadcast_to(segrow[CH * i + CH - 1][:, 127:128], (16, 512))
        high = jnp.floor(seg * (1.0 / 64.0))
        r = iota((16, 512), 0)
        v = jnp.zeros((16, 512), BF16)
        for k, row in enumerate(lt + [high.astype(BF16), (seg - 64.0 * high).astype(BF16)]):
            v = jnp.where(r == k, row, v)
        endlog[g, i] = v
        for d in XS:
            lx[i, d] = keyed(("lx", i, d), endlog.at[g, i], endlog.at[g, i], n.at(dx=d))
        for d in ALLX:
            ly[i, d] = keyed(("ly", i, d), endlog.at[g, i], endlog.at[g, i], n.across(d))
        for d in XS:
            ex[i, d] = keyed(("ex", i, d), ends.at[g, i], ends.at[g, i], n.at(dx=d))
    store(pre, pre_h)
    store(ext, ext_h)
    store(delta, delta_h)
    store(logs, logs_h)
    for i in range(MICRO):
        store(proj.at[i, pl.ds(16, TOK), pl.ds(0, 512)], gate_h.at[i])

    def states_on(i):
        for d in XS:
            lx[i, d].wait_recv()
        for d in ALLX:
            ly[i, d].wait_recv()
        for d in XS:
            ex[i, d].wait_recv()
        rsend[i] = entering(n, ends, endlog, 1, 0, i).astype(BF16)
        return keyed(("r", i), rsend.at[i], rrecv.at[i], n.pair())

    def inside(at, carry):
        L = logs[at]
        X, B, C = activations(pre[at])
        U = (heads_of(delta[at], eh) * X).astype(BF16)
        psi = bdot(C, B, NT)
        keep = same_mask(flags[at], segrow[at])
        LT = L.T
        for j in range(4):
            u = pair_halves(U[:, 128 * j : 128 * j + 128])
            v = jnp.zeros((Q, 128), F32)
            for e in range(2):
                h = 2 * j + e
                K = jnp.where(keep, jnp.exp(L[:, h : h + 1] - LT[h : h + 1]), 0.0)
                v = v + bdot((psi * K).astype(BF16), u[e])
            inner[at, :, 128 * j : 128 * j + 128] = v
        return carry

    lax.fori_loop(0, 4, inside, 0)
    r0 = states_on(0)
    for d in ALLX:
        for half in (0, 1):
            oy[d, half].wait_recv()
    swap = keyed("swap", w_o.at[pl.ds(4 * (1 - core), 4)], wo_s.at[:, core], n.at(dc=1))
    for k in range(4):
        wo_s[k, core] = w_o[4 * core + k]
    for a in (1, 3, 2):
        cz[a].wait_recv()
        theirs = cot_h.at[2 * lax.rem(z + 4 - a, 4) + core]
        cn.append(keyed(("cf", a), theirs, theirs, n.at(dc=1)))
    lax.fori_loop(4, 8, inside, 0)
    r1 = states_on(1)
    swap.wait_recv()
    for cp in cn:
        cp.wait_recv()
    bring_c = pltpu.make_async_copy(cot_h, cot_s, local.at[0])
    bring_c.start()
    store(wo_s, wout_h)
    bring_c.wait()
    for i in range(MICRO):
        d = bdot(cot_s[:, i].reshape(TOK, 2048), wo_s[...].reshape(512, 2048), NT)
        for c in range(CH):
            dno[CH * i + c] = d[Q * c : Q * c + Q]
    store(dno, dno_h)

    def mix(i, c):
        at = CH * i + c
        E, _ = decays(logs[at], flags[at])
        X, _, C = activations(pre[at])
        more = heads_of(jnp.concatenate([E, jnp.broadcast_to(hp[2:3], (8, 128))], 0), eh)
        Ex, skip = more[:Q], more[Q : Q + 1]
        S = state[...]
        states[at, 0] = S
        Yc = Ex * bdot(C, S.astype(BF16))
        carried[at] = Yc
        mx = inner[at] + Yc + skip * X
        inner[at] = mx
        after = Ex[Q - 1 : Q] * S + sloc[at]
        state[...] = after
        states[at, 1] = after
        gt = proj[i, pl.ds(pl.multiple_of(16 + Q * c, 16), Q), 0:512]
        gated = mx * (gt * sigmoid(gt))
        ones = jnp.ones((8, 512), BF16)
        sums[m, at, 0:8] = right_parts(ones, gated * gated, 2, NT)
        sums[m, at, 8:16] = right_parts(ones, dno[at] * og[0:1] * gated, 2, NT)

    sm = []
    for i, r in ((0, r0), (1, r1)):
        r.wait_recv()
        state[...] = entering(n, ends, endlog, 0, 0, i) + rrecv[i].astype(F32)
        lax.fori_loop(0, CH, lambda c, carry, i=i: (mix(i, c), carry)[1], 0)
        mine = sums.at[m, pl.ds(CH * i, CH)]
        for a, b in OTHERS:
            sm.append(keyed(("sm", i, a, b), mine, mine, n.at(dz=a, dc=b)))
        some = pl.ds(CH * i, CH)
        store(inner.at[some], mixed_h.at[some])
        store(carried.at[some], carried_h.at[some])
        store(states.at[some], states_h.at[some])
    for cp in sm:
        cp.wait_recv()
    for cp in copies:
        cp.wait_send()
    for cp in stores:
        cp.wait()


def wave(hid, wsend, pack, cot, outw):
    V = lambda *s: pltpu.VMEM(s, BF16)
    R = lambda *s: pltpu.VMEM(s, F32)
    outs = [
        sds((2048, T), BF16), sds((8, 2, 64, 2048), BF16), sds((8, 8, 32, 1408), BF16), sds((2, TOK, 512), F32), sds((8, Q, 768), F32), sds((8, Q + 8, 768), BF16), sds((8, Q, 128), F32), sds((8, Q, 128), F32),
        sds((8, Q, 128), F32), sds((8, Q, 128), F32), sds((8, Q, 512), F32), sds((8, Q, 512), F32), sds((8, 2, 128, 512), F32), sds((8, Q, 512), F32), sds((8, 2, 64, 2048), BF16), sds((4, 2, 64, 2048), BF16),
        sds((8, 8, 16, 128), F32), sds((8, 2, 16, 512), BF16), sds((8, 768), F32), sds((8, 128), F32), sds((8, 512), F32), sds((8, 2048), F32), sds((8, 1, 128), F32),
    ]
    scratch = [
        V(8, 2, 64, 2048), V(2, 16, 2048), V(2, TOK + 16, 2048), V(2048, T), V(8, 8, 32, 1408), R(8, 8, 24, 128), R(2, TOK + 16, 1408), R(8, Q, 768), V(8, Q + 8, 768), R(8, Q, 128), R(8, Q, 128), R(8, Q, 128), R(8, Q, 128),
        R(8, 128, 512), R(8, Q, 512), R(8, Q, 512), R(8, 2, 128, 512), R(8, Q, 512), V(8, 2, 128, 512), V(2, 128, 512), V(2, 128, 512), V(8, 2, 64, 2048), V(8, 64, 2048), V(4, 2, 64, 2048),
        R(34, 8, 128), R(128, 512), R(1, 128), R(Q + 8, 768),
    ]
    return pl.pallas_call(
        wave_kernel,
        name="wave",
        out_shape=outs,
        in_specs=[VM] * 5,
        out_specs=[ANY] * 16 + [VM] * 7,
        scratch_shapes=[*scratch, pltpu.SemaphoreType.DMA((144,)), pltpu.SemaphoreType.DMA((144,)), pltpu.SemaphoreType.DMA((24,)), pltpu.SemaphoreType.DMA((6,))],
        compiler_params=pltpu.CompilerParams(collective_id=1, has_side_effects=True, vmem_limit_bytes=64 * 1024 * 1024 - 65536),
        cost_estimate=pl.CostEstimate(flops=8 << 30, bytes_accessed=32 << 20, transcendentals=0),
    )(hid, wsend, pack, cot, outw)


def entering(n, everyone, logs, target, direction, micro):
    to = 2 * n.x + (1 - n.y if target else n.y)
    lt, last = [], []
    for q in range(8):
        v = logs[q, micro].astype(F32)
        lt.append(v[0:1] + v[1:2] + v[2:3])
        last.append(64.0 * v[3:4] + v[4:5])
    zero = jnp.zeros((1, 512), F32)
    edge = zero
    for r in range(8):
        edge = edge + jnp.where((r == to) if direction else (r == to - 1), last[r], zero)
    total = jnp.zeros((128, 512), F32)
    for k in range(4):
        q = 2 * k + n.y
        log = zero
        for r in range(8):
            between = (r > to) & (r < q) if direction else (r > q) & (r < to)
            log = log + jnp.where(between, lt[r], zero)
        if direction:
            there = jnp.where(n.y == 0, last[max(2 * k - 1, 0)], last[2 * k])
        else:
            there = jnp.where(n.y == 0, last[2 * k], last[2 * k + 1])
        reached = jnp.where((q > to) if direction else (q < to), 1.0, 0.0)
        total = total + jnp.where(there == edge, jnp.exp(log) * reached, zero) * everyone[q, micro].astype(F32)
    return total


def same_mask(flags, segrow):
    return (flags[:, 5:6] == segrow) & (iota((Q, Q), 0) >= iota((Q, Q), 1))


def activations(pre):
    a = pre * sigmoid(pre)
    return a[:, :512], a[:, 512:640].astype(BF16), a[:, 640:768].astype(BF16)


def pair_halves(v):
    low_half = iota(v.shape, 1) < 64
    zero = jnp.zeros_like(v)
    return jnp.where(low_half, v, zero), jnp.where(low_half, zero, v)


T = MICRO * TOK


def column(row):
    return jnp.concatenate([jnp.broadcast_to(row, (128, 128)).T] * 4, 1)


def pick_matrix(rows, start, count, shift, dtype=BF16):
    r, l = iota((rows, 128), 0), iota((rows, 128), 1)
    return ((r - start == l - shift) & (l >= shift) & (l < shift + count)).astype(dtype)


class Reduce:
    def __init__(self, n, key, a, b, a1, a2, pa, b1, b2, pb, b3):
        self.n, self.key, self.a, self.b = n, key, a, b
        self.a1, self.a2, self.pa, self.b1, self.b2, self.pb, self.b3 = a1, a2, pa, b1, b2, pb, b3
        self.half = pb.shape[1]

    def group(self, d, f):
        n = self.n
        return 2 * lax.rem(n.x + d, 4) + lax.rem(n.y + f, 2)

    def first_a(self, d, f):
        return self.n.copy((self.key, "a1", d, f), self.a.at[self.group(d, f)], self.a1.at[d - 1, f], self.n.at(dx=d))

    def first_b(self, d, e):
        n = self.n
        rep = lax.rem(n.ring + e, 4) // 2
        rows = pl.ds(pl.multiple_of(self.half * rep, self.half), self.half)
        return n.copy((self.key, "b1", d, e), self.b.at[self.group(d, e % 2), rows], self.b1.at[e - 1, lax.rem(n.x + d, 4)], n.at(dy=e))

    def send_a(self, d, f):
        if d:
            self.first_a(d, f).start()

    def send_b(self, d, f):
        for e in (1, 3) if f else (2,):
            self.first_b(d, e).start()

    def second_a(self, e):
        return self.n.copy((self.key, "a2", e), self.pa.at[e % 2], self.a2.at[e - 1], self.n.at(dy=e))

    def second_b(self, d):
        return self.n.copy((self.key, "b2", d), self.pb.at[lax.rem(self.n.x + d, 4)], self.b2.at[d - 1], self.n.at(dx=d))

    def third_b(self):
        return self.n.copy((self.key, "b3"), self.b3.at[self.n.rep], self.b3.at[self.n.rep], self.n.at(dy=2))

    def middle_a(self, f):
        for d in XS:
            self.first_a(d, f).wait_recv()
        self.pa[f] = add4(self.a[self.group(0, f)], self.a1[:, f]).astype(BF16)

    def go_a(self, f):
        for e in (1, 3) if f else (2,):
            self.second_a(e).start()

    def go_b(self):
        for d in (2, 1, 3):
            self.second_b(d).start()

    def middle_b(self):
        n = self.n
        rows = pl.ds(pl.multiple_of(self.half * n.rep, self.half), self.half)
        for d in (2, 1, 3, 0):
            for e in XS:
                self.first_b(d, e).wait_recv()
            k = lax.rem(n.x + d, 4)
            self.pb[k] = add4(self.b[2 * k + n.y, rows], self.b1[:, k]).astype(BF16)

    def last_b(self):
        for d in XS:
            self.second_b(d).wait_recv()
        self.b3[self.n.rep] = add4(self.pb[self.n.x], self.b2).astype(self.b3.dtype)
        self.third_b().start()

    def last_a(self):
        for e in XS:
            self.second_a(e).wait_recv()
        return add4(self.pa[0], self.a2)

    def finish_first(self):
        for d in XS:
            for f in (0, 1):
                self.first_a(d, f).wait_send()
        for e in XS:
            for d in range(4):
                self.first_b(d, e).wait_send()

    def finish(self):
        for d in XS:
            self.second_b(d).wait_send()
            self.second_a(d).wait_send()
        self.third_b().wait_send()


def fetcher(sems):
    loads = {}

    def fetch(key, src, dst):
        loads[key] = pltpu.make_async_copy(src, dst, sems.at[len(loads)])
        loads[key].start()

    return loads, fetch


C1 = 256


def back_wave_kernel(
    mixed_h, carried_h, states_h, gate_h, dno_h, sums, pre_h, delta_h, logs_h, flags_h, segrow, og, hp, wout_h, normed, endlog,
    dgate, dpre_h, bc_all, ddt, small_o, small_b, total, wpa, wpb, turned, edges,
    mixed, carried, states, gate, dno, pre, delta, logs, flags, wout, nout, dmix, tloc, dbi, starts, rsend, rrecv, rows, part, near, far,
    wa, wb, wa1, wb1, dbc, state, send, recv, load, tile_sem,
):
    eh = spread_matrix()
    n = Net(send, recv)
    g, m, core, z = n.g, n.m, n.c, n.z
    W = Reduce(n, "w", wa, wb, wa1, None, wpa, wb1, None, wpb, None)
    loads, fetch = fetcher(load)
    for i in range(MICRO):
        some = pl.ds(CH * i, CH)
        for key, src, dst in (("mixed", mixed_h, mixed), ("gate", gate_h, gate), ("dno", dno_h, dno), ("pre", pre_h, pre), ("logs", logs_h, logs), ("flags", flags_h, flags)):
            fetch((key, i), src.at[some], dst.at[some])
    fetch("wout", wout_h, wout)
    for key, src, dst in (("delta", delta_h, delta), ("states", states_h, states), ("carried", carried_h, carried)):
        fetch(key, src, dst)

    def start_x(i, d):
        return n.copy(("sx", i, d), starts.at[g, i], starts.at[g, i], n.at(dx=d))

    def part_y(i):
        return n.copy(("r", i), rsend.at[i], rrecv.at[i], n.pair())

    def near_copy(d, i):
        return n.copy(("near", d, i), part.at[2 * lax.rem(z + d, 4) + 1 - core, i], near.at[d, i], n.at(dc=1))

    def far_copy(d, i):
        return n.copy(("far", d, i), near.at[d, i], far.at[d - 1, i], n.at(dz=d))

    def bc_copy(i, a, b):
        some = pl.ds(TOK * i, TOK)
        return n.copy(("bc", i, a, b), dbc.at[n.member(a, b), :, some], bc_all.at[m, :, some], n.at(dz=a, dc=b))

    def edge_copy(i):
        return n.copy(("edge", i), gate.at[CH * i, pl.ds(0, 8)], edges.at[i], n.group(7))

    n.meet([n.at(dz=a, dc=b) for a, b in OTHERS] + [n.at(dx=d) for d in XS] + [n.at(dy=d) for d in XS] + [n.group(1), n.group(7)])
    small_o[...] = jnp.zeros_like(small_o)
    small_b[...] = jnp.zeros_like(small_b)

    def outward(i, k):
        c = CH - 1 - k
        at = CH * i + c
        tot = sums[0, at]
        for q in range(1, 8):
            tot = tot + sums[q, at]
        r = column(lax.rsqrt(tot[0:1] / INNER + EPS))
        s2 = column(tot[8:9] / INNER)
        gt = gate[at]
        s = sigmoid(gt)
        sg = gt * s
        mix = mixed[at]
        gated = mix * sg
        dn = dno[at]
        n0 = gated * r
        rows = pl.ds(pl.multiple_of(Q * c, Q), Q)
        nb = n0 * og[0:1]
        nout[i, rows] = nb.astype(BF16)
        turned[:, pl.ds(pl.multiple_of(Q * at, Q), Q)] = nb.T.astype(BF16)
        d_gated = r * (dn * og[0:1] - n0 * r * s2)
        dm = d_gated * sg
        dmix[at] = dm
        dgate[i, rows] = (d_gated * mix * (s * (1.0 + gt * (1.0 - s)))).astype(BF16)
        x = pre[at, :, :512]
        X = x * sigmoid(x)
        cc = pre[at, :, 640:768]
        C = (cc * sigmoid(cc)).astype(BF16)
        small_o[0:1] += jnp.sum(dn * n0, 0, keepdims=True)
        small_o[1:2] += jnp.sum(X * dm, 0, keepdims=True)
        E, _ = decays(logs[at], flags[at])
        Ex = heads_of(E, eh)
        G = right_parts(C, Ex * dm, 2, TN)
        tloc[at] = G
        state[...] = Ex[Q - 1 : Q] * state[...] + G

    for i in range(MICRO):
        for key in ("mixed", "gate", "dno", "pre", "logs", "flags"):
            loads[key, i].wait()
        state[...] = jnp.zeros_like(state)
        lax.fori_loop(0, CH, lambda k, carry, i=i: (outward(i, k), carry)[1], 0)
        starts[g, i] = state[...].astype(BF16)
        for d in XS:
            start_x(i, d).start()
        if i == 0:
            loads["wout"].wait()
        part[:, i] = bdot(nout[i], wout[...]).astype(BF16).reshape(8, 64, 2048)
        for d in (1, 3, 2, 0):
            near_copy(d, i).start()

    def bring(k):
        at = pl.ds(pl.multiple_of(256 * W.group(*ORDER[k]), 256), 256)
        return pltpu.make_async_copy(normed.at[at], rows.at[k % 2], tile_sem.at[k % 2])

    def states_on(i):
        for d in XS:
            start_x(i, d).wait_recv()
        rsend[i] = entering(n, starts, endlog, 1, 1, i).astype(BF16)
        part_y(i).start()

    def tokens_on(i):
        for d in (1, 3, 2, 0):
            near_copy(d, i).wait_recv()
            there = 2 * lax.rem(z + d, 4) + core
            near[d, i] = (part[there, i].astype(F32) + near[d, i].astype(F32)).astype(BF16)
            if d:
                far_copy(d, i).start()

    bring(0).start()
    for k, (d, f) in enumerate(ORDER):
        bring(k).wait()
        if k < 7:
            bring(k + 1).start()
        q = W.group(d, f)
        v = bdot(rows[k % 2], dgate[...].reshape(T, 512))
        wa[q] = v[:, 0:C1].astype(BF16)
        wb[q] = v[:, C1:].astype(BF16)
        W.send_a(d, f)
        W.send_b(d, f)
        if k == 1:
            states_on(0)
            tokens_on(0)
        if k == 5:
            states_on(1)
            tokens_on(1)

    loads["delta"].wait()
    loads["states"].wait()
    loads["carried"].wait()

    def inside(at, carry):
        L = logs[at]
        f = flags[at]
        E, _ = decays(L, f)
        X, B, C = activations(pre[at])
        more = heads_of(jnp.concatenate([E, delta[at]], 0), eh)
        Ex, dx = more[:Q], more[Q:]
        Ub = (dx * X).astype(BF16)
        dm = dmix[at]
        dmb = dm.astype(BF16)
        psi = bdot(C, B, NT)
        keep = same_mask(f, segrow[at])
        LT = L.T
        dpsi = jnp.zeros((Q, Q), F32)
        for j in range(4):
            js = slice(128 * j, 128 * j + 128)
            u = pair_halves(Ub[:, js])
            y = pair_halves(dmb[:, js])
            acc = jnp.zeros((Q, 128), F32)
            for e in range(2):
                h = 2 * j + e
                K = jnp.where(keep, jnp.exp(L[:, h : h + 1] - LT[h : h + 1]), 0.0)
                acc = acc + bdot((psi * K).astype(BF16), y[e], TN)
                dpsi = dpsi + bdot(y[e], u[e], NT) * K
            dno[at, :, js] = acc
        dpb = dpsi.astype(BF16)
        dbi[at, 0:128] = bdot(C, dpb, TN)
        dbi[at, 128:256] = bdot(B, dpb, TT) + bdot(states[at, 0].astype(BF16), (Ex * dm).astype(BF16), NT)
        return carry

    lax.fori_loop(0, 8, inside, 0)
    for i in (0, 1):
        part_y(i).wait_recv()

    def inward(i, k):
        c = CH - 1 - k
        at = CH * i + c
        L = logs[at]
        d = delta[at]
        E, W_ = decays(L, flags[at])
        p = pre[at, :, 0:512]
        s = sigmoid(p)
        X = p * s
        bb = pre[at, :, 512:640]
        B = (bb * sigmoid(bb)).astype(BF16)
        more = heads_of(jnp.concatenate([E[Q - 8 :], W_, d, jnp.broadcast_to(hp[2:3], (8, 128))], 0), eh)
        Elast, Wx, dx, skip = more[7:8], more[8 : 8 + Q], more[8 + Q : 8 + 2 * Q], more[8 + 2 * Q : 9 + 2 * Q]
        U = dx * X
        dm = dmix[at]
        Yc = carried[at]
        Yi = mixed[at] - Yc - skip * X
        G = state[...]
        Gb = G.astype(BF16)
        dUi = dno[at]
        dUc = Wx * bdot(B, Gb)
        dU = dUi + dUc
        lanes = pl.ds(pl.multiple_of(Q * at, Q), Q)
        dbc[0:4, :, lanes] = (dbi[at, 0:128] + bdot(Gb, (Wx * U).astype(BF16), NT)).astype(BF16).reshape(4, 32, Q)
        dbc[4:8, :, lanes] = dbi[at, 128:256].astype(BF16).reshape(4, 32, Q)
        dL = sums_of(dm.astype(BF16).astype(F32) * Yi + dm * Yc - U.astype(BF16).astype(F32) * dUi - U * dUc, eh)
        end = sums_of(jnp.broadcast_to(jnp.sum(G * states[at, 1], 0, keepdims=True), (8, 512)), eh)[0:1]
        upper = (iota((Q, Q), 0) <= iota((Q, Q), 1)).astype(BF16)
        dstep = right_parts(upper, dL, 3) + end
        rate = hp[1:2]
        dr = (sums_of(dU * X, eh) + dstep * rate) * (1.0 - jnp.exp(-d))
        ddt[at] = dr.astype(BF16)
        small_b[0:1] += jnp.sum(dr, 0, keepdims=True)
        small_b[1:2] += jnp.sum(dstep * d * rate, 0, keepdims=True)
        gate[at] = (dx * dU + skip * dm) * (s * (1.0 + p * (1.0 - s)))
        state[...] = Elast * G + tloc[at]

    store = pltpu.make_async_copy(gate, dpre_h, load.at[0])
    for i in range(MICRO):
        state[...] = entering(n, starts, endlog, 0, 1, i) + rrecv[i].astype(F32)
        lax.fori_loop(0, CH, lambda k, carry, i=i: (inward(i, k), carry)[1], 0)
        edge_copy(i).start()
        for a, b in OTHERS:
            bc_copy(i, a, b).start()
    store.start()
    bc_all[m] = dbc[m]

    W.middle_b()
    W.middle_a(1)
    W.middle_a(0)
    for i in range(MICRO):
        for d in XS:
            far_copy(d, i).wait_recv()
        total[i] = near[0, i].astype(F32) + far[0, i].astype(F32) + far[1, i].astype(F32) + far[2, i].astype(F32)
    for i in range(MICRO):
        edge_copy(i).wait_recv()
        for a, b in OTHERS:
            bc_copy(i, a, b).wait_recv()
    W.finish_first()
    for i in range(MICRO):
        edge_copy(i).wait_send()
        for a, b in OTHERS:
            bc_copy(i, a, b).wait_send()
    store.wait()
    for i in range(MICRO):
        part_y(i).wait_send()
        for d in XS:
            start_x(i, d).wait_send()
            far_copy(d, i).wait_send()
        for d in range(4):
            near_copy(d, i).wait_send()


def back_wave(mixed, carried, states, gate, dno, sums, pre, delta, logs, flags, segrow, og, hp, wout, normed, endlog):
    outs = [
        sds((2, TOK, 512), BF16), sds((8, Q, 512), F32), sds((8, 32, T), BF16), sds((8, Q, 128), BF16), sds((8, 512), F32), sds((8, 128), F32), sds((2, 64, 2048), F32),
        sds((2, 256, C1), BF16), sds((4, 128, C1), BF16), sds((512, T), BF16), sds((2, 8, 512), F32),
    ]
    V = lambda *s: pltpu.VMEM(s, BF16)
    R = lambda *s: pltpu.VMEM(s, F32)
    return pl.pallas_call(
        back_wave_kernel,
        name="back_wave",
        out_shape=outs,
        in_specs=[ANY] * 5 + [VM] + [ANY] * 4 + [VM] * 3 + [ANY] * 2 + [VM],
        out_specs=[VM, ANY] + [VM] * 9,
        scratch_shapes=[
            R(8, Q, 512), R(8, Q, 512), R(8, 2, 128, 512), R(8, Q, 512), R(8, Q, 512), R(8, Q, 768), R(8, Q, 128), R(8, Q, 128), R(8, Q, 128), V(512, 2048),
            V(2, TOK, 512), R(8, Q, 512), R(8, 128, 512), R(8, 256, 128), V(8, 2, 128, 512), V(2, 128, 512), V(2, 128, 512), V(2, 256, T), V(8, 2, 64, 2048),
            V(4, 2, 64, 2048), V(3, 2, 64, 2048),
            V(8, 256, C1), V(8, 256, C1), V(3, 2, 256, C1), V(3, 4, 128, C1), V(8, 32, T), R(128, 512),
            pltpu.SemaphoreType.DMA((96,)), pltpu.SemaphoreType.DMA((96,)), pltpu.SemaphoreType.DMA((16,)), pltpu.SemaphoreType.DMA((2,)),
        ],
        compiler_params=pltpu.CompilerParams(collective_id=4, has_side_effects=True, vmem_limit_bytes=62 << 20),
        cost_estimate=pl.CostEstimate(flops=8 << 30, bytes_accessed=32 << 20, transcendentals=0),
    )(mixed, carried, states, gate.reshape(8, Q, 512), dno, sums, pre, delta, logs, flags, segrow, og, hp, wout, normed, endlog)


CB = 256
CA = 640 - CB


def tail_kernel(
    bc_s, ex_s, wpa, wpb, turned, branch, gain, cot, dpre, pre, ext, flags, fnext, conv, ddt, dgate, w, hid, normed, small_o, small_b,
    gi, g_out, layer_out, grad_in, small_all,
    eb_src, eb_s, dps, pre_s, ext_s, fl_s, fn_s, ddt_s, dg_s, w_s, hid_s, nm_s, wt, e_s, dproj, part, near, far, conv_acc, gnorm,
    s0, s1, s2, sx, ga, gb, ga1, ga2, gpa, gb1, gb2, gpb, gb3, cot_s, gsw, oa, ob, oa1, oa2, opa, ob1, ob2, opb, ob3, oin, cot_own, ga2_, gb2_, gb3_, final, send, recv, load, tile_sem,
):
    n = Net(send, recv)
    x, y, z, c, m = n.x, n.y, n.z, n.c, n.m
    loads = {}

    def fetch(key, src, dst):
        loads[key] = pltpu.make_async_copy(src, dst, load.at[len(loads)])
        loads[key].start()

    fetch("pre", pre.at[:, :, pl.ds(512, 256)], pre_s)
    fetch("w", w, w_s)
    fetch("dpre", dpre, dps.at[:, pl.ds(0, TOK), pl.ds(0, 512)])
    fetch("ext", ext, ext_s)
    fetch("flags", flags, fl_s)
    fetch("fnext", fnext, fn_s)
    fetch("ddt", ddt, ddt_s)
    fetch("normed", normed, nm_s)
    fetch("dgate", dgate, dg_s)
    fetch("hid", hid, hid_s)
    fetch("cot", cot.at[m], cot_own)
    n.meet([n.at(dz=a, dc=b) for a, b in OTHERS] + [n.at(dx=d) for d in XS] + [n.at(dy=d) for d in XS] + [n.group(1), n.group(7)])
    G_ = Reduce(n, "g", None, None, None, ga2_, wpa, None, gb2_, wpb, gb3_)
    G_.go_a(1)
    G_.go_a(0)
    G_.go_b()

    edge2 = n.copy("edge2", eb_src, eb_s, n.group(7))

    def near_copy(d, i):
        return n.copy(("near", d, i), part.at[2 * lax.rem(z + d, 4) + 1 - c, i], near.at[d, i], n.at(dc=1))

    def far_copy(d, i):
        return n.copy(("far", d, i), near.at[d, i], far.at[d - 1, i], n.at(dz=d))

    def small_x(d):
        return n.copy(("sx", d), s0, s1.at[d - 1], n.at(dx=d))

    def small_y(d):
        return n.copy(("sy", d), sx, s2.at[d - 1], n.at(dy=d))

    def small_m(a, b):
        return n.copy(("sm", a, b), small_all.at[m], small_all.at[m], n.at(dz=a, dc=b))

    def rows_copy(a, b):
        return n.copy(("rows", a, b), final.at[n.member(a, b)], gi.at[m], n.at(dz=a, dc=b))

    O = Reduce(n, "o", oa, ob, oa1, oa2, opa, ob1, ob2, opb, ob3)
    swap = n.copy("swap", gsw.at[:, 1 - c], oin, n.at(dc=1))
    W = Reduce(n, "w", ga, gb, ga1, ga2, gpa, gb1, gb2, gpb, gb3)

    pick = pick_matrix(256, 32 * m, 32, 0)
    loads["w"].wait()
    wt[...] = (bdot(w_s[:, 1024:1280], pick) + bdot(w_s[:, 1280:1408], pick_matrix(128, 0, 8, 32))).astype(BF16)
    cw = jnp.concatenate([conv[:, 0:512], left_parts(conv[:, 512:768], pick, 3)], 1)
    for key in ("pre", "dpre"):
        loads[key].wait()
    eye = pick_matrix(32, 0, 32, 0)

    def bc_chunk(i, k):
        t = CH * i + k
        tot = bc_s[0, :, Q * t : Q * t + Q].astype(F32)
        for q in range(1, 8):
            tot = tot + bc_s[q, :, Q * t : Q * t + Q].astype(F32)
        d = left_parts(tot, eye, 2, TN)
        p = left_parts(pre_s[t], pick, 2)
        s = sigmoid(p)
        dps[i, Q * k : Q * k + Q, 512:640] = d * (s * (1.0 + p * (1.0 - s)))

    for i in range(MICRO):
        bc_chunk(i, 0)
        eb_src[i] = dps[i, 0:8, 512:640]
    edge2.start()
    for i in range(MICRO):
        for k in range(1, CH):
            bc_chunk(i, k)
    def bring(k):
        return pltpu.make_async_copy(cot.at[:, :, :, pl.ds(256 * k, 256)], cot_s.at[k % 2], tile_sem.at[k % 2])

    bring(0).start()
    for k in range(8):
        bring(k).wait()
        if k < 7:
            bring(k + 1).start()
        v = sum(bdot(turned[:, TOK * i : TOK * i + TOK], cot_s[k % 2, :, i].reshape(TOK, 256)) for i in range(MICRO))
        gsw[:, :, :, 256 * k : 256 * k + 256] = v.astype(BF16).reshape(4, 2, 64, 256)
    swap.start()
    for j in range(4):
        oa[4 * c + j] = gsw[j, c, :, 0:1024]
        ob[4 * c + j] = gsw[j, c, :, 1024:2048]

    for key in ("ext", "flags", "fnext", "ddt"):
        loads[key].wait()
    conv_acc[...] = jnp.zeros_like(conv_acc)
    pick_dt = pick_matrix(128, 0, 8, 32)

    def conv_chunk(i, k):
        t = CH * i + k
        e_s[:, 0:512] = ext_s[t, :, 0:512].astype(F32)
        e_s[:, 512:640] = bdot(ext_s[t, :, 512:768], pick)
        f, fn = fl_s[t], fn_s[t]
        dp = dps[i, Q * k : Q * k + Q]
        dx = cw[3:4] * dp
        conv_acc[3:4] += jnp.sum(dp * e_s[8 : 8 + Q], 0, keepdims=True)
        conv_acc[4:5] += jnp.sum(dp, 0, keepdims=True)
        for j in range(3):
            conv_acc[j : j + 1] += jnp.sum(dp * e_s[5 + j : 5 + j + Q] * f[:, j : j + 1], 0, keepdims=True)
            dx = dx + cw[j : j + 1] * dps[i, Q * k + 3 - j : Q * k + 3 - j + Q] * fn[:, j : j + 1]
        rows = slice(Q * k, Q * k + Q)
        dproj[i, rows, 0:512] = dx[:, 0:512].astype(BF16)
        dproj[i, rows, 512:640] = (dx[:, 512:640] + bdot(ddt_s[t], pick_dt)).astype(BF16)

    for i in range(MICRO):
        for k in range(CH - 1):
            conv_chunk(i, k)
    swap.wait_recv()
    for j in range(4):
        oa[4 * (1 - c) + j] = oin[j, :, 0:1024]
        ob[4 * (1 - c) + j] = oin[j, :, 1024:2048]
    for d, f in ORDER:
        O.send_a(d, f)
        O.send_b(d, f)

    edge2.wait_recv()
    for i in range(MICRO):
        dps[i, TOK : TOK + 8, 0:512] = ex_s[i]
        dps[i, TOK : TOK + 8, 512:640] = eb_s[i]
        conv_chunk(i, CH - 1)

    loads["hid"].wait()
    loads["dgate"].wait()
    for i in range(MICRO):
        h = hid_s[:, i].reshape(TOK, 2048).astype(F32)
        scale = row_scale(h)
        first, main, rest = dg_s[i], dproj[i, :, 0:512], dproj[i, :, 512:640]

        def tile_of(j, carry, i=i, scale=scale, first=first, main=main, rest=rest):
            at = pl.ds(pl.multiple_of(256 * j, 256), 256)
            d = bdot(first, w_s[at, 0:512], NT) + bdot(main, w_s[at, 512:1024], NT) + bdot(rest, wt[at], NT)
            part[:, i, :, at] = d.astype(BF16).reshape(8, 64, 256)
            hv = hid_s[:, i, :, at].reshape(TOK, 256).astype(F32)
            s = jnp.sum(d * (hv * scale), 0, keepdims=True)
            gnorm[0:1, at] = s if i == 0 else gnorm[0:1, at] + s
            return carry

        lax.fori_loop(0, 8, tile_of, 0)
        for d in (1, 3, 2, 0):
            near_copy(d, i).start()
    for r in range(16):
        s0[r : r + 1] = gnorm[0:1, 128 * r : 128 * r + 128]
    for k in range(5):
        for r in range(5):
            s0[16 + 5 * k + r : 17 + 5 * k + r] = conv_acc[k : k + 1, 128 * r : 128 * r + 128]
    for r in range(4):
        s0[41 + r : 42 + r] = small_o[0:1, 128 * r : 128 * r + 128]
    s0[45:47] = small_b[0:2]
    s0[47:48] = sums_of(small_o[...], spread_matrix())[1:2]
    for d in XS:
        small_x(d).start()

    def tokens_on(i):
        for d in (1, 3, 2, 0):
            near_copy(d, i).wait_recv()
            there = 2 * lax.rem(z + d, 4) + c
            near[d, i] = (part[there, i].astype(F32) + near[d, i].astype(F32)).astype(BF16)
            if d:
                far_copy(d, i).start()

    loads["normed"].wait()
    for k, (d, f) in enumerate(ORDER):
        q = W.group(d, f)
        at = pl.ds(pl.multiple_of(256 * q, 256), 256)
        v = bdot(nm_s[at], dproj[...].reshape(T, 640)).astype(BF16)
        gb[q] = v[:, 0:CB]
        ga[q] = v[:, CB:]
        W.send_a(d, f)
        W.send_b(d, f)
        if k == 2:
            tokens_on(0)
        if k == 6:
            tokens_on(1)

    G_.last_b()
    final[:, :, 0:C1] = G_.last_a().astype(BF16).reshape(8, 32, C1)
    for i in range(MICRO):
        layer_out[i] = (hid_s[m, i].astype(F32) + branch[i]).astype(BF16)
    O.middle_b()
    O.go_b()
    O.middle_a(1)
    O.go_a(1)
    O.middle_a(0)
    O.go_a(0)

    for d in XS:
        small_x(d).wait_recv()
    sx[...] = s0[...] + s1[0] + s1[1] + s1[2]
    for d in XS:
        small_y(d).start()
    W.middle_b()
    W.go_b()
    W.middle_a(1)
    W.go_a(1)
    W.middle_a(0)
    W.go_a(0)
    O.last_b()
    g_out[:, 0:1024] = O.last_a()
    W.last_b()
    for d in XS:
        small_y(d).wait_recv()
    small_all[m] = sx[...] + s2[0] + s2[1] + s2[2]
    for a, b in OTHERS:
        small_m(a, b).start()
    for i in range(MICRO):
        for d in XS:
            far_copy(d, i).wait_recv()
        dn = near[0, i].astype(F32) + far[0, i].astype(F32) + far[1, i].astype(F32) + far[2, i].astype(F32)
        if i == 0:
            loads["cot"].wait()
        h = hid_s[m, i].astype(F32)
        r = row_scale(h)
        dg = dn * gain[0:1]
        grad_in[i] = (cot_own[i].astype(F32) + r * dg - h * (r * r * r) * jnp.mean(dg * h, axis=-1, keepdims=True)).astype(BF16)
    O.third_b().wait_recv()
    for h in range(2):
        g_out[32 * h : 32 * h + 32, 1024:2048] = ob3[h]
    W.third_b().wait_recv()
    for h in range(2):
        final[4 * h : 4 * h + 4, :, 512 : 512 + CB] = gb3[h].reshape(4, 32, CB)
    final[:, :, 512 + CB :] = W.last_a().astype(BF16).reshape(8, 32, CA)
    G_.third_b().wait_recv()
    for h in range(2):
        final[4 * h : 4 * h + 4, :, C1:512] = gb3_[h].reshape(4, 32, C1)
    for a, b in OTHERS:
        rows_copy(a, b).start()
    gi[m] = final[m]
    for a, b in OTHERS:
        rows_copy(a, b).wait_recv()
        small_m(a, b).wait_recv()
    W.finish_first()
    O.finish_first()
    W.finish()
    O.finish()
    G_.finish()
    swap.wait_send()
    for a, b in OTHERS:
        rows_copy(a, b).wait_send()
        small_m(a, b).wait_send()
    for d in XS:
        small_x(d).wait_send()
        small_y(d).wait_send()
        for i in range(MICRO):
            far_copy(d, i).wait_send()
    for d in range(4):
        for i in range(MICRO):
            near_copy(d, i).wait_send()
    edge2.wait_send()


def tail_call(bc_all, edges, wpa, wpb, turned, branch, gain, cot, dpre, pre, ext, flags, fnext, conv, ddt, dgate, w, hid, normed, small_o, small_b):
    outs = [sds((8, 32, 1152), BF16), sds((64, 2048), F32), sds((2, 64, 2048), BF16), sds((2, 64, 2048), BF16), sds((8, 48, 128), F32)]
    V = lambda *s: pltpu.VMEM(s, BF16)
    R = lambda *s: pltpu.VMEM(s, F32)
    scratch = [
        R(2, 8, 128), R(2, 8, 128), R(2, TOK + 8, 640), R(8, Q, 256), V(8, Q + 8, 768), R(8, Q, 128), R(8, Q, 128), V(8, Q, 128), V(2, TOK, 512), V(2048, 1408),
        V(8, 2, 64, 2048), V(2048, T), V(2048, 128), R(Q + 8, 640), V(2, TOK, 640), V(8, 2, 64, 2048), V(4, 2, 64, 2048), V(3, 2, 64, 2048), R(8, 640), R(8, 2048),
        R(48, 128), R(3, 48, 128), R(3, 48, 128), R(48, 128),
        V(8, 256, CA), V(8, 256, CB), V(3, 2, 256, CA), V(3, 256, CA), V(2, 256, CA), V(3, 4, 128, CB), V(3, 128, CB), V(4, 128, CB), V(2, 128, CB),
        V(2, 8, 2, 64, 256), V(4, 2, 64, 2048), V(8, 64, 1024), V(8, 64, 1024), V(3, 2, 64, 1024), V(3, 64, 1024), V(2, 64, 1024), V(3, 4, 32, 1024), V(3, 32, 1024), V(4, 32, 1024), R(2, 32, 1024), V(4, 64, 2048),
        V(2, 64, 2048), V(3, 256, C1), V(3, 128, C1), V(2, 128, C1), V(8, 32, 1152),
    ]
    return pl.pallas_call(
        tail_kernel,
        name="tail",
        out_shape=outs,
        in_specs=[VM] * 7 + [ANY] * 6 + [VM] + [ANY] * 5 + [VM] * 2,
        out_specs=[VM] * 5,
        scratch_shapes=[*scratch, pltpu.SemaphoreType.DMA((112,)), pltpu.SemaphoreType.DMA((112,)), pltpu.SemaphoreType.DMA((12,)), pltpu.SemaphoreType.DMA((2,))],
        compiler_params=pltpu.CompilerParams(collective_id=5, has_side_effects=True, vmem_limit_bytes=62 << 20),
        cost_estimate=pl.CostEstimate(flops=8 << 30, bytes_accessed=32 << 20, transcendentals=0),
    )(bc_all, edges, wpa, wpb, turned, branch, gain, cot, dpre, pre, ext, flags, fnext, conv, ddt, dgate, w, hid, normed, small_o, small_b)


def from_members(v):
    r = v.shape[1]
    return v.reshape(4, 2, r, 4, 128).transpose(2, 1, 3, 0, 4).reshape(r, 4096)


def from_heads(v):
    r = v.shape[1]
    return v.reshape(4, 2, r, 4, 2).transpose(2, 1, 3, 0, 4).reshape(r, 64)


def from_rows(v):
    return v.transpose(1, 0, 2).reshape(v.shape[1], 256)


def to_members(v):
    r = v.shape[0]
    return v.reshape(r, 2, 4, 4, 128).transpose(3, 1, 0, 2, 4).reshape(8, r, 512)


def xdot(a, b, dims=NN):
    return lax.dot_general(a, b, dims, preferred_element_type=F32)


def per_device(layer_in, cotangent, segment_ids, norm_gain, in_weight, conv_weight, conv_bias, dt_bias, a_log, skip_gain, out_gain, out_weight):
    xi, yi, zi, ci = (lax.axis_index(a) for a in SEQ)
    g = 2 * xi + yi
    m = 2 * zi + ci
    lane = jnp.arange(128)

    def placed(v, width, at):
        return jnp.where(lane // width == at, jnp.tile(v, 128 // width), 0.0)

    head = lane == 2 * (g % 4) + ci
    rows = [placed(segment_ids[i, 0].astype(F32), 64, ci) for i in range(MICRO)]
    rows += [placed(norm_gain, 32, m % 4), placed(out_gain, 64, ci)]
    rows += [jnp.where(head, v, 0.0) for v in (dt_bias, a_log, skip_gain)]
    window = jnp.pad(jnp.concatenate([conv_weight, conv_bias[None]], 0), ((0, 3), (0, 60)))
    window = lax.dynamic_update_slice(jnp.zeros((8, 256), F32), window, (0, 68 * (8 * g + m) % 128))
    pack = jnp.concatenate([jnp.stack(rows), jnp.zeros((1, 128), F32), window[:, :128], window[:, 128:]], 0)
    bc = jnp.broadcast_to(in_weight[None, :, 8192:8448], (8, 32, 256))
    dt_w = in_weight[:, 8448:].reshape(32, 2, 4, 4, 2).transpose(3, 1, 0, 2, 4).reshape(8, 32, 8)
    w_send = jnp.concatenate([to_members(in_weight[:, :4096]), to_members(in_weight[:, 4096:8192]), bc, dt_w, jnp.zeros((8, 32, 120), BF16)], 2)
    (
        normed, hid_all, w_in, gate, pre, ext, delta, logs, flags, fnext, mixed, carried, states, dno, cot, w_out,
        sums, ends_all, conv, hp, og, gain, segrow,
    ) = wave(layer_in[:, 0], w_send, pack, cotangent[:, 0], out_weight)
    w_in = w_in.reshape(2048, 1408)
    dgate, dpre, bc_all, ddt, small_o, small_b, own_branch, wpa, wpb, turned, edges = back_wave(
        mixed, carried, states, gate, dno, sums, pre, delta, logs, flags, segrow, og, hp, w_out.reshape(512, 2048), normed, ends_all
    )
    dpre = dpre.reshape(MICRO, TOK, 512)
    gi, g_out, layer_out, grad_in, small_sum = tail_call(
        bc_all, edges, wpa, wpb, turned, own_branch, gain, cot, dpre, pre, ext, flags, fnext, conv, ddt, dgate, w_in, hid_all, normed, small_o, small_b
    )
    gi = gi.astype(F32)
    g_in = jnp.concatenate([from_members(gi[:, :, :512]), from_members(gi[:, :, 512:1024]), from_rows(gi[:, :, 1024:1056]), from_heads(gi[:, :, 1056:1064])], 1)
    at = 8 * g + m
    g_norm = lax.dynamic_slice(small_sum[:, :16].sum(0).reshape(64, 32), (at, 0), (1, 32)).reshape(32)
    conv_s = small_sum[:, 16:41].reshape(8, 5, 640)
    conv_s = jnp.concatenate([from_members(conv_s[:, :, :512]), from_rows(conv_s[:, :, 512:544])], 1)
    conv_s = lax.dynamic_slice(conv_s, (0, 68 * at), (5, 68))
    og_s = from_members(small_sum[:, 41:45].reshape(8, 1, 512))[0]
    og_s = lax.dynamic_slice(og_s, (64 * at,), (64,))
    hd_s = from_heads(small_sum[:, 45:48, :8])
    hd_s = lax.dynamic_slice(hd_s, (0, at), (3, 1))
    return (layer_out[:, None], grad_in[:, None], g_norm, g_in, conv_s[:4], conv_s[4], hd_s[0], hd_s[1], hd_s[2], og_s, g_out)


def solution(mesh):
    fine = Mesh(mesh.devices.reshape(2, 4, 2, 4, 2), AXES)
    tok = P(None, "rep", SEQ, None)
    return jax.shard_map(
        per_device,
        mesh=fine,
        in_specs=(tok, tok, P(None, "rep", SEQ), P(SEQ), P(SEQ, None), P(None, SEQ), P(SEQ), P(SEQ), P(SEQ), P(SEQ), P(SEQ), P(SEQ, None)),
        out_specs=(tok, tok, P(SEQ), P(SEQ, None), P(None, SEQ), P(SEQ), P(SEQ), P(SEQ), P(SEQ), P(SEQ), P(SEQ, None)),
        check_vma=False,
    )
```

```python
import functools

import jax
import jax.numpy as jnp
from jax import lax
from jax.experimental import pallas as pl
from jax.experimental.pallas import tpu as pltpu
from jax.sharding import Mesh, PartitionSpec as P

EPS = 1e-05
INNER = 4096
MICRO = 2
CONV = 4352
F32 = jnp.float32
BF16 = jnp.bfloat16
AXES = ("rep", "x", "y", "z", "c")
SEQ = ("x", "y", "z", "c")
GROUPS = 8
TOK = 512
Q = 128
CH = TOK // Q

MESH = pl.DeviceIdType.MESH
ANY = pl.BlockSpec(memory_space=pl.ANY)
VM = pl.BlockSpec(memory_space=pltpu.VMEM)
SMEM = pl.BlockSpec(memory_space=pltpu.SMEM)


class Net:
    def __init__(self, send, recv):
        self.send, self.recv, self.used, self.open = send, recv, 0, []
        self.keys = {}
        self.rep, self.x, self.y, self.z, self.c = (lax.axis_index(a) for a in AXES)
        self.ring = 2 * self.rep + self.y
        self.g = 2 * self.x + self.y
        self.m = 2 * self.z + self.c

    def at(self, dx=0, dy=0, dz=0, dc=0):
        ring = lax.rem(self.ring + dy, 4)
        return (ring // 2, lax.rem(self.x + dx, 4), lax.rem(ring, 2), lax.rem(self.z + dz, 4), lax.rem(self.c + dc, 2))

    def pair(self):
        return (self.rep, self.x, 1 - self.y, self.z, self.c)

    def across(self, dx):
        return (self.rep, lax.rem(self.x + dx, 4), 1 - self.y, self.z, self.c)

    def group(self, d):
        g = lax.rem(self.g + d, 8)
        return (self.rep, g // 2, lax.rem(g, 2), self.z, self.c)

    def member(self, dz, dc):
        return 2 * lax.rem(self.z + dz, 4) + lax.rem(self.c + dc, 2)

    def push(self, src, dst, where):
        i = self.used
        self.used += 1
        copy = pltpu.make_async_remote_copy(
            src_ref=src, dst_ref=dst, send_sem=self.send.at[i], recv_sem=self.recv.at[i], device_id=where, device_id_type=MESH
        )
        copy.start()
        self.open.append(copy)
        return copy

    def copy(self, key, src, dst, where):
        i = self.keys.setdefault(key, len(self.keys))
        return pltpu.make_async_remote_copy(
            src_ref=src, dst_ref=dst, send_sem=self.send.at[i], recv_sem=self.recv.at[i], device_id=where, device_id_type=MESH
        )

    def behind(self, d):
        return 2 * lax.rem(self.x + 4 - d, 4) + self.y

    def local(self, src, dst):
        i = self.used
        self.used += 1
        copy = pltpu.make_async_copy(src, dst, self.recv.at[i])
        copy.start()
        return copy

    def greet(self, peers):
        for peer in peers:
            pl.semaphore_signal(pltpu.get_barrier_semaphore(), inc=1, device_id=peer, device_id_type=MESH)
        return len(peers)

    def meet(self, count):
        pl.semaphore_wait(pltpu.get_barrier_semaphore(), count)

    def finish(self):
        for copy in self.open:
            copy.wait_send()


OTHERS = [(dz, dc) for dz in (0, 1, 3, 2) for dc in (0, 1) if (dz, dc) != (0, 0)]
ZS = (0, 1, 3, 2)
XS = (1, 3, 2)
ORDER = [(d, f) for d in (2, 1, 3, 0) for f in (1, 0)]


def sds(shape, dtype):
    return jax.ShapeDtypeStruct(shape, dtype)


def add4(a, b):
    return a.astype(F32) + b[0].astype(F32) + b[1].astype(F32) + b[2].astype(F32)


NN = (((1,), (0,)), ((), ()))
NT = (((1,), (1,)), ((), ()))
TN = (((0,), (0,)), ((), ()))
TT = (((0,), (1,)), ((), ()))


def bdot(a, b, dims=NN):
    return lax.dot_general(a, b, dims, preferred_element_type=F32)


def parts(v, count):
    out = []
    for _ in range(count):
        p = v.astype(BF16)
        out.append(p)
        v = v - p.astype(F32)
    return out


def left_parts(v, w, count, dims=NN):
    return sum(bdot(p, w, dims) for p in parts(v, count))


def right_parts(w, v, count, dims=NN):
    return sum(bdot(w, p, dims) for p in parts(v, count))


def iota(shape, dim):
    return lax.broadcasted_iota(jnp.int32, shape, dim)


def spread_matrix():
    return (iota((128, 512), 0) == iota((128, 512), 1) // 64).astype(BF16)


def heads_of(v, eh):
    return left_parts(v, eh, 2)


def sums_of(v, eh):
    return left_parts(v, eh, 2, NT)


def lower_matrix():
    return (iota((Q, Q), 0) >= iota((Q, Q), 1)).astype(BF16)


def sigmoid(v):
    return 1.0 / (1.0 + jnp.exp(-v))


def softplus(v):
    return jnp.maximum(v, 0.0) + jnp.log1p(jnp.exp(-jnp.abs(v)))


def row_scale(h):
    return lax.rsqrt(jnp.mean(h * h, axis=-1, keepdims=True) + EPS)


def decays(L, flags):
    E = jnp.exp(L) * flags[:, 3:4]
    W = jnp.exp(L[Q - 1 : Q] - L) * flags[:, 4:5]
    return E, W


def wave_kernel(
    hid, inw, seg, gain_in, og_in, cw_in, cb_in, dtb_in, alog_in, skip_in, cot, outw,
    normed_h, hid_h, w_h, gate_h, pre_h, ext_h, delta_h, logs_h, flags_h, fnext_h, mixed_h, carried_h, states_h, dno_h, cot_h, wout_h,
    sums, endlog, conv, hp, og, gain, segrow,
    hid_s, halo, nrm, turned, w_s, small, proj, pre, ext, delta, logs, flags, fnext, sloc, inner, carried, states, dno, ends, rsend, rrecv, cot_s, w_o, wo_s, convt, state, total, tail, wsend, pack, window, send, recv, done,
):
    eh = spread_matrix()
    n = Net(send, recv)
    g, m, x, y, z, core = n.g, n.m, n.x, n.y, n.z, n.c
    ALLX = (0,) + XS
    copies = []

    def keyed(key, src, dst, where):
        cp = n.copy(key, src, dst, where)
        copies.append(cp)
        cp.start()
        return cp

    stores = []

    def store(src, dst):
        cp = pltpu.make_async_copy(src, dst, done.at[len(stores)])
        cp.start()
        stores.append(cp)

    peers = n.greet([n.at(dz=a, dc=b) for a, b in OTHERS] + [n.at(dx=d) for d in XS] + [n.at(dy=1), n.at(dy=3), n.group(1), n.group(7)] + [n.across(d) for d in ALLX])

    for q in range(8):
        zq, cq = q // 2, q % 2
        for j in range(4):
            at = 512 * (4 * cq + j) + 128 * zq
            wsend[q, :, 128 * j : 128 * j + 128] = inw[:, at : at + 128]
            wsend[q, :, 512 + 128 * j : 640 + 128 * j] = inw[:, 4096 + at : 4224 + at]
        wsend[q, :, 1024:1280] = inw[:, 8192:8448]
        r, k = iota((64, 128), 0), iota((64, 128), 1)
        take = ((r == 32 * cq + 8 * (k // 2) + 2 * zq + k % 2) & (k < 8)).astype(BF16)
        wsend[q, :, 1280:1408] = bdot(inw[:, 8448:8512], take).astype(BF16)
    pack[...] = jnp.zeros_like(pack)
    pack[0:2, 0:64] = seg[...].astype(F32)
    pack[3:4, 0:64] = og_in[...]
    first = pltpu.roll(pack[0:8], 64 * core, 1)
    pack[0:8] = jnp.zeros((8, 128), F32)
    pack[2:3, 0:32] = gain_in[...]
    first = first + pltpu.roll(pack[0:8], 32 * lax.rem(m, 4), 1)
    row, at = iota((8, 128), 0), iota((8, 128), 1) == 2 * lax.rem(g, 4) + core
    for k, ref in enumerate((dtb_in, alog_in, skip_in)):
        first = first + jnp.where(at & (row == 4 + k), ref[0], 0.0)
    pack[0:8] = first
    window[...] = jnp.zeros_like(window)
    window[0:4, 0:68] = cw_in[...]
    window[4:5, 0:68] = cb_in[...]
    moved = pltpu.roll(window[...], lax.rem(68 * (8 * g + m), 128), 1)
    pack[8:16] = moved[:, 0:128]
    pack[16:24] = moved[:, 128:256]

    n.meet(peers)
    wa, sa = {}, {}
    for a, b in OTHERS:
        wa[a, b] = keyed(("wa", a, b), wsend.at[n.member(a, b)], w_s.at[g, m], n.at(dz=a, dc=b))
        sa[a, b] = keyed(("sa", a, b), pack, small.at[g, m], n.at(dz=a, dc=b))
    w_s[g, m] = wsend[m]
    small[g, m] = pack[...]
    hid_s[m] = hid[...]
    wx, wy, sx, sy = {}, {}, {}, {}

    def along_y(d, k):
        first = pl.ds(2 * lax.rem(z + 4 - ZS[k], 4), 2)
        for half, dy in ((0, 1), (1, 3)):
            part = w_s.at[n.behind(d), first, pl.ds(16 * half, 16)]
            wy[d, k, half] = keyed(("wy", d, k, half), part, part, n.at(dy=dy))

    def issue(k):
        for b in (0, 1):
            if (ZS[k], b) != (0, 0):
                wa[ZS[k], b].wait_recv()
        block = w_s.at[g, pl.ds(2 * lax.rem(z + 4 - ZS[k], 4), 2)]
        for d in XS:
            wx[k, d] = keyed(("wx", k, d), block, block, n.at(dx=d))
        along_y(0, k)

    def forward(k):
        for d in XS:
            wx[k, d].wait_recv()
            along_y(d, k)

    issue(0)
    issue(1)
    hz = {a: keyed(("hz", a), hid_s.at[m], hid_s.at[m], n.at(dz=a)) for a in (1, 3, 2)}
    hn = [keyed("hn", hid_s.at[m], hid_s.at[m], n.at(dc=1))]
    for a, b in OTHERS:
        sa[a, b].wait_recv()
    for d in XS:
        sx[d] = keyed(("sx", d), small.at[g], small.at[g], n.at(dx=d))
    sy[0] = keyed(("sy", 0), small.at[g], small.at[g], n.pair())
    forward(0)
    issue(2)
    forward(1)
    issue(3)
    for d in XS:
        sx[d].wait_recv()
        mine = small.at[n.behind(d)]
        sy[d] = keyed(("sy", d), mine, mine, n.pair())
    forward(2)
    forward(3)
    w_o[g] = outw[...]
    ox = {d: keyed(("ox", d), w_o.at[g], w_o.at[g], n.at(dx=d)) for d in XS}
    oy = {}

    def out_y(d):
        for half, dy in ((0, 1), (1, 3)):
            part = w_o.at[n.behind(d), pl.ds(32 * half, 32)]
            oy[d, half] = keyed(("oy", d, half), part, part, n.at(dy=dy))

    out_y(0)
    for a in (1, 3, 2):
        hz[a].wait_recv()
        theirs = hid_s.at[2 * lax.rem(z + 4 - a, 4) + core]
        hn.append(keyed(("hf", a), theirs, theirs, n.at(dc=1)))
    cot_s[m] = cot[...]
    cz = {a: keyed(("cz", a), cot_s.at[m], cot_s.at[m], n.at(dz=a)) for a in (1, 3, 2)}
    cn = [keyed("cn", cot_s.at[m], cot_s.at[m], n.at(dc=1))]
    for d in ALLX:
        sy[d].wait_recv()

    for q in range(16):
        v = small[q // 2, 4 * (q % 2), 2:3]
        for u in range(1, 4):
            v = v + small[q // 2, 4 * (q % 2) + u, 2:3]
        gain[0:1, 128 * q : 128 * q + 128] = v
    heads3 = jnp.zeros((3, 128), F32)
    for j in range(4):
        og[0:1, 128 * j : 128 * j + 128] = small[4 * core + j, 2 * z, 3:4] + small[4 * core + j, 2 * z + 1, 3:4]
        for e in range(2):
            heads3 = heads3 + small[4 * core + j, 2 * z + e, 4:7]
    hp[...] = jnp.zeros_like(hp)
    hp[0:1] = heads3[0:1]
    hp[1:2] = jnp.where(iota((1, 128), 1) < 8, -jnp.exp(heads3[1:2]), 0.0)
    hp[2:3] = heads3[2:3]
    for q in range(34):
        v = jnp.zeros((8, 128), F32)
        for i in range(64):
            if 68 * i // 128 == q:
                v = v + small[i // 8, i % 8, 8:16]
            elif 68 * i // 128 == q - 1:
                v = v + small[i // 8, i % 8, 16:24]
        convt[q] = v
    for j in range(4):
        conv[:, 128 * j : 128 * j + 128] = convt[4 * (4 * core + j) + z]
    conv[:, 512:640] = convt[32]
    conv[:, 640:768] = convt[33]

    lane = iota((8, 128), 1)

    def chunk_row(group, i, c):
        return jnp.broadcast_to(small[group, 2 * c, i : i + 1] + small[group, 2 * c + 1, i : i + 1], (8, 128))

    for i in range(MICRO):
        before = jnp.where(g > 0, chunk_row(lax.rem(g + 7, 8), i, CH - 1), -1.0)
        after = jnp.where(g < 7, chunk_row(lax.rem(g + 1, 8), i, 0), -2.0)
        rows = [before] + [chunk_row(g, i, c) for c in range(CH)] + [after]
        for c in range(CH):
            prv, cur, nxt = rows[c : c + 3]
            here, ahead = [], []
            for d in (3, 2, 1):
                back = jnp.where(lane < d, pltpu.roll(prv, d, 1), pltpu.roll(cur, d, 1))
                here.append((back == cur).astype(F32))
                on = jnp.where(lane >= 128 - d, pltpu.roll(nxt, 128 - d, 1), pltpu.roll(cur, 128 - d, 1))
                ahead.append((on == cur).astype(F32))
            here += [(cur == prv[:, 127:128]).astype(F32), (cur == cur[:, 127:128]).astype(F32), cur]
            sub = iota((128, 128), 0)
            for rows_of, to in ((here, flags), (ahead, fnext)):
                v = jnp.zeros((128, 128), F32)
                for r, row in enumerate(rows_of):
                    v = jnp.where(sub == r, jnp.broadcast_to(row[0:1], (128, 128)), v)
                to[CH * i + c] = v.T
            segrow[CH * i + c] = cur[0:1]

    for cp in hn:
        cp.wait_recv()
    edge = keyed("edge", hid_s.at[7, :, pl.ds(48, 16)], halo, n.group(1))

    gv = gain[0:1]

    def norm(k, carry):
        for i in range(MICRO):
            h = hid_s[pl.ds(2 * k, 2), i].reshape(Q, 2048).astype(F32)
            v = h * row_scale(h) * gv
            nrm[i, pl.ds(pl.multiple_of(16 + Q * k, 16), Q)] = v.astype(BF16)
            turned[:, pl.ds(pl.multiple_of(TOK * i + Q * k, Q), Q)] = v.T.astype(BF16)
        return carry

    lax.fori_loop(0, CH, norm, 0)
    edge.wait_recv()
    for i in range(MICRO):
        h = halo[i].astype(F32)
        nrm[i, 0:16] = (h * row_scale(h) * gv).astype(BF16)
    store(turned, normed_h)

    def project(side, first):
        for i in range(MICRO):
            for lo in range(0, 1408, 256):
                hi = min(lo + 256, 1408)
                v = 0.0 if first else proj[i, :, lo:hi]
                for k in range(4):
                    q = 2 * k + side
                    v = v + bdot(nrm[i, :, pl.ds(pl.multiple_of(256 * q, 256), 256)], w_s[q, :, :, lo:hi].reshape(256, hi - lo))
                proj[i, :, lo:hi] = v

    project(y, True)
    for d in ALLX:
        for k in range(4):
            for half in (0, 1):
                wy[d, k, half].wait_recv()
    project(1 - y, False)
    for d in XS:
        ox[d].wait_recv()
        out_y(d)
    store(w_s, w_h)
    store(hid_s, hid_h)
    store(flags, flags_h)
    store(fnext, fnext_h)

    def front(i, c):
        at = CH * i + c
        rows = pl.ds(pl.multiple_of(16 + Q * c, 16), Q)
        f = flags[at]
        xbc = proj[i, rows, 512:1280].astype(BF16).astype(F32)
        tail[8:] = xbc
        acc = conv[4:5] + conv[3:4] * xbc
        for k in range(3):
            acc = acc + conv[k : k + 1] * tail[5 + k : 5 + k + Q] * f[:, k : k + 1]
        pre[at] = acc
        ext[at] = tail[...].astype(BF16)
        d = softplus(proj[i, rows, 1280:1408] + hp[0:1])
        delta[at] = d
        L = right_parts(lower_matrix(), d * hp[1:2], 3)
        logs[at] = L
        E, W = decays(L, f)
        xv = acc[:, :512]
        X = xv * sigmoid(xv)
        b = acc[:, 512:640]
        B = (b * sigmoid(b)).astype(BF16)
        S = right_parts(B, heads_of(W * d, eh) * X, 2, TN)
        sloc[at] = S
        last = heads_of(E[Q - 8 :], eh)
        state[...] = last[7:8] * state[...] + S
        tail[0:8] = tail[Q : Q + 8]
        total[...] = total[...] + L[Q - 1 : Q]

    ex, lx, ly = {}, {}, {}
    for i in range(MICRO):
        tail[0:8] = proj[i, 8:16, 512:1280].astype(BF16).astype(F32)
        state[...] = jnp.zeros_like(state)
        total[...] = jnp.zeros_like(total)
        lax.fori_loop(0, CH, lambda c, carry, i=i: (front(i, c), carry)[1], 0)
        ends[g, i] = state[...].astype(BF16)
        lt = parts(jnp.broadcast_to(heads_of(jnp.broadcast_to(total[...], (8, 128)), eh)[0:1], (16, 512)), 3)
        seg = jnp.broadcast_to(segrow[CH * i + CH - 1][:, 127:128], (16, 512))
        high = jnp.floor(seg * (1.0 / 64.0))
        r = iota((16, 512), 0)
        v = jnp.zeros((16, 512), BF16)
        for k, row in enumerate(lt + [high.astype(BF16), (seg - 64.0 * high).astype(BF16)]):
            v = jnp.where(r == k, row, v)
        endlog[g, i] = v
        for d in XS:
            lx[i, d] = keyed(("lx", i, d), endlog.at[g, i], endlog.at[g, i], n.at(dx=d))
        for d in ALLX:
            ly[i, d] = keyed(("ly", i, d), endlog.at[g, i], endlog.at[g, i], n.across(d))
        for d in XS:
            ex[i, d] = keyed(("ex", i, d), ends.at[g, i], ends.at[g, i], n.at(dx=d))
    store(pre, pre_h)
    store(ext, ext_h)
    store(delta, delta_h)
    store(logs, logs_h)
    for i in range(MICRO):
        store(proj.at[i, pl.ds(16, TOK), pl.ds(0, 512)], gate_h.at[i])

    def states_on(i):
        for d in XS:
            lx[i, d].wait_recv()
        for d in ALLX:
            ly[i, d].wait_recv()
        for d in XS:
            ex[i, d].wait_recv()
        rsend[i] = entering(n, ends, endlog, 1, 0, i).astype(BF16)
        return keyed(("r", i), rsend.at[i], rrecv.at[i], n.pair())

    def inside(at, carry):
        L = logs[at]
        X, B, C = activations(pre[at])
        U = (heads_of(delta[at], eh) * X).astype(BF16)
        psi = bdot(C, B, NT)
        keep = same_mask(flags[at], segrow[at])
        LT = L.T
        for j in range(4):
            u = pair_halves(U[:, 128 * j : 128 * j + 128])
            v = jnp.zeros((Q, 128), F32)
            for e in range(2):
                h = 2 * j + e
                K = jnp.where(keep, jnp.exp(L[:, h : h + 1] - LT[h : h + 1]), 0.0)
                v = v + bdot((psi * K).astype(BF16), u[e])
            inner[at, :, 128 * j : 128 * j + 128] = v
        return carry

    lax.fori_loop(0, 4, inside, 0)
    r0 = states_on(0)
    for d in ALLX:
        for half in (0, 1):
            oy[d, half].wait_recv()
    swap = keyed("swap", w_o.at[pl.ds(4 * (1 - core), 4)], wo_s.at[:, core], n.at(dc=1))
    for k in range(4):
        wo_s[k, core] = w_o[4 * core + k]
    for a in (1, 3, 2):
        cz[a].wait_recv()
        theirs = cot_s.at[2 * lax.rem(z + 4 - a, 4) + core]
        cn.append(keyed(("cf", a), theirs, theirs, n.at(dc=1)))
    lax.fori_loop(4, 8, inside, 0)
    r1 = states_on(1)
    swap.wait_recv()
    for cp in cn:
        cp.wait_recv()
    store(cot_s, cot_h)
    store(wo_s, wout_h)
    for i in range(MICRO):
        d = bdot(cot_s[:, i].reshape(TOK, 2048), wo_s[...].reshape(512, 2048), NT)
        for c in range(CH):
            dno[CH * i + c] = d[Q * c : Q * c + Q]
    store(dno, dno_h)

    def mix(i, c):
        at = CH * i + c
        E, _ = decays(logs[at], flags[at])
        X, _, C = activations(pre[at])
        more = heads_of(jnp.concatenate([E, jnp.broadcast_to(hp[2:3], (8, 128))], 0), eh)
        Ex, skip = more[:Q], more[Q : Q + 1]
        S = state[...]
        states[at, 0] = S
        Yc = Ex * bdot(C, S.astype(BF16))
        carried[at] = Yc
        mx = inner[at] + Yc + skip * X
        inner[at] = mx
        after = Ex[Q - 1 : Q] * S + sloc[at]
        state[...] = after
        states[at, 1] = after
        gt = proj[i, pl.ds(pl.multiple_of(16 + Q * c, 16), Q), 0:512]
        gated = mx * (gt * sigmoid(gt))
        ones = jnp.ones((8, 512), BF16)
        sums[m, at, 0:8] = right_parts(ones, gated * gated, 2, NT)
        sums[m, at, 8:16] = right_parts(ones, dno[at] * og[0:1] * gated, 2, NT)

    sm = []
    for i, r in ((0, r0), (1, r1)):
        r.wait_recv()
        state[...] = entering(n, ends, endlog, 0, 0, i) + rrecv[i].astype(F32)
        lax.fori_loop(0, CH, lambda c, carry, i=i: (mix(i, c), carry)[1], 0)
        mine = sums.at[m, pl.ds(CH * i, CH)]
        for a, b in OTHERS:
            sm.append(keyed(("sm", i, a, b), mine, mine, n.at(dz=a, dc=b)))
        some = pl.ds(CH * i, CH)
        store(inner.at[some], mixed_h.at[some])
        store(carried.at[some], carried_h.at[some])
        store(states.at[some], states_h.at[some])
    for cp in sm:
        cp.wait_recv()
    for cp in copies:
        cp.wait_send()
    for cp in stores:
        cp.wait()


def wave(hid, inw, seg, gain, og, cw, cb, dtb, alog, skip, cot, outw):
    V = lambda *s: pltpu.VMEM(s, BF16)
    R = lambda *s: pltpu.VMEM(s, F32)
    outs = [
        sds((2048, T), BF16), sds((8, 2, 64, 2048), BF16), sds((8, 8, 32, 1408), BF16), sds((2, TOK, 512), F32), sds((8, Q, 768), F32), sds((8, Q + 8, 768), BF16), sds((8, Q, 128), F32), sds((8, Q, 128), F32),
        sds((8, Q, 128), F32), sds((8, Q, 128), F32), sds((8, Q, 512), F32), sds((8, Q, 512), F32), sds((8, 2, 128, 512), F32), sds((8, Q, 512), F32), sds((8, 2, 64, 2048), BF16), sds((4, 2, 64, 2048), BF16),
        sds((8, 8, 16, 128), F32), sds((8, 2, 16, 512), BF16), sds((8, 768), F32), sds((8, 128), F32), sds((8, 512), F32), sds((8, 2048), F32), sds((8, 1, 128), F32),
    ]
    scratch = [
        V(8, 2, 64, 2048), V(2, 16, 2048), V(2, TOK + 16, 2048), V(2048, T), V(8, 8, 32, 1408), R(8, 8, 24, 128), R(2, TOK + 16, 1408), R(8, Q, 768), V(8, Q + 8, 768), R(8, Q, 128), R(8, Q, 128), R(8, Q, 128), R(8, Q, 128),
        R(8, 128, 512), R(8, Q, 512), R(8, Q, 512), R(8, 2, 128, 512), R(8, Q, 512), V(8, 2, 128, 512), V(2, 128, 512), V(2, 128, 512), V(8, 2, 64, 2048), V(8, 64, 2048), V(4, 2, 64, 2048),
        R(34, 8, 128), R(128, 512), R(1, 128), R(Q + 8, 768), V(8, 32, 1408), R(24, 128), R(8, 256),
    ]
    return pl.pallas_call(
        wave_kernel,
        name="wave",
        out_shape=outs,
        in_specs=[VM] * 7 + [SMEM] * 3 + [VM] * 2,
        out_specs=[ANY] * 16 + [VM] * 7,
        scratch_shapes=[*scratch, pltpu.SemaphoreType.DMA((144,)), pltpu.SemaphoreType.DMA((144,)), pltpu.SemaphoreType.DMA((24,))],
        compiler_params=pltpu.CompilerParams(collective_id=1, has_side_effects=True, vmem_limit_bytes=64 * 1024 * 1024 - 65536),
        cost_estimate=pl.CostEstimate(flops=8 << 30, bytes_accessed=32 << 20, transcendentals=0),
    )(hid, inw, seg, gain, og, cw, cb, dtb, alog, skip, cot, outw)


def entering(n, everyone, logs, target, direction, micro):
    to = 2 * n.x + (1 - n.y if target else n.y)
    lt, last = [], []
    for q in range(8):
        v = logs[q, micro].astype(F32)
        lt.append(v[0:1] + v[1:2] + v[2:3])
        last.append(64.0 * v[3:4] + v[4:5])
    zero = jnp.zeros((1, 512), F32)
    edge = zero
    for r in range(8):
        edge = edge + jnp.where((r == to) if direction else (r == to - 1), last[r], zero)
    total = jnp.zeros((128, 512), F32)
    for k in range(4):
        q = 2 * k + n.y
        log = zero
        for r in range(8):
            between = (r > to) & (r < q) if direction else (r > q) & (r < to)
            log = log + jnp.where(between, lt[r], zero)
        if direction:
            there = jnp.where(n.y == 0, last[max(2 * k - 1, 0)], last[2 * k])
        else:
            there = jnp.where(n.y == 0, last[2 * k], last[2 * k + 1])
        reached = jnp.where((q > to) if direction else (q < to), 1.0, 0.0)
        total = total + jnp.where(there == edge, jnp.exp(log) * reached, zero) * everyone[q, micro].astype(F32)
    return total


def same_mask(flags, segrow):
    return (flags[:, 5:6] == segrow) & (iota((Q, Q), 0) >= iota((Q, Q), 1))


def activations(pre):
    a = pre * sigmoid(pre)
    return a[:, :512], a[:, 512:640].astype(BF16), a[:, 640:768].astype(BF16)


def pair_halves(v):
    low_half = iota(v.shape, 1) < 64
    zero = jnp.zeros_like(v)
    return jnp.where(low_half, v, zero), jnp.where(low_half, zero, v)


T = MICRO * TOK


def column(row):
    return jnp.concatenate([jnp.broadcast_to(row, (128, 128)).T] * 4, 1)


def pick_matrix(rows, start, count, shift, dtype=BF16):
    r, l = iota((rows, 128), 0), iota((rows, 128), 1)
    return ((r - start == l - shift) & (l >= shift) & (l < shift + count)).astype(dtype)


class Reduce:
    def __init__(self, n, key, a, b, a1, a2, pa, b1, b2, pb, b3):
        self.n, self.key, self.a, self.b = n, key, a, b
        self.a1, self.a2, self.pa, self.b1, self.b2, self.pb, self.b3 = a1, a2, pa, b1, b2, pb, b3
        self.half = pb.shape[1]

    def group(self, d, f):
        n = self.n
        return 2 * lax.rem(n.x + d, 4) + lax.rem(n.y + f, 2)

    def first_a(self, d, f):
        return self.n.copy((self.key, "a1", d, f), self.a.at[self.group(d, f)], self.a1.at[d - 1, f], self.n.at(dx=d))

    def first_b(self, d, e):
        n = self.n
        rep = lax.rem(n.ring + e, 4) // 2
        rows = pl.ds(pl.multiple_of(self.half * rep, self.half), self.half)
        return n.copy((self.key, "b1", d, e), self.b.at[self.group(d, e % 2), rows], self.b1.at[e - 1, lax.rem(n.x + d, 4)], n.at(dy=e))

    def send_a(self, d, f):
        if d:
            self.first_a(d, f).start()

    def send_b(self, d, f):
        for e in (1, 3) if f else (2,):
            self.first_b(d, e).start()

    def second_a(self, e):
        return self.n.copy((self.key, "a2", e), self.pa.at[e % 2], self.a2.at[e - 1], self.n.at(dy=e))

    def second_b(self, d):
        return self.n.copy((self.key, "b2", d), self.pb.at[lax.rem(self.n.x + d, 4)], self.b2.at[d - 1], self.n.at(dx=d))

    def third_b(self):
        return self.n.copy((self.key, "b3"), self.b3.at[self.n.rep], self.b3.at[self.n.rep], self.n.at(dy=2))

    def middle_a(self, f):
        for d in XS:
            self.first_a(d, f).wait_recv()
        self.pa[f] = add4(self.a[self.group(0, f)], self.a1[:, f]).astype(BF16)

    def go_a(self, f):
        for e in (1, 3) if f else (2,):
            self.second_a(e).start()

    def go_b(self):
        for d in (2, 1, 3):
            self.second_b(d).start()

    def middle_b(self):
        n = self.n
        rows = pl.ds(pl.multiple_of(self.half * n.rep, self.half), self.half)
        for d in (2, 1, 3, 0):
            for e in XS:
                self.first_b(d, e).wait_recv()
            k = lax.rem(n.x + d, 4)
            self.pb[k] = add4(self.b[2 * k + n.y, rows], self.b1[:, k]).astype(BF16)

    def last_b(self):
        for d in XS:
            self.second_b(d).wait_recv()
        self.b3[self.n.rep] = add4(self.pb[self.n.x], self.b2).astype(self.b3.dtype)
        self.third_b().start()

    def last_a(self):
        for e in XS:
            self.second_a(e).wait_recv()
        return add4(self.pa[0], self.a2)

    def finish_first(self):
        for d in XS:
            for f in (0, 1):
                self.first_a(d, f).wait_send()
        for e in XS:
            for d in range(4):
                self.first_b(d, e).wait_send()

    def finish(self):
        for d in XS:
            self.second_b(d).wait_send()
            self.second_a(d).wait_send()
        self.third_b().wait_send()


def fetcher(sems):
    loads = {}

    def fetch(key, src, dst):
        loads[key] = pltpu.make_async_copy(src, dst, sems.at[len(loads)])
        loads[key].start()

    return loads, fetch


C1 = 256


def back_wave_kernel(
    mixed_h, carried_h, states_h, gate_h, dno_h, sums, pre_h, delta_h, logs_h, flags_h, segrow, og, hp, wout_h, normed, endlog,
    dgate, dpre_h, bc_all, ddt, small_o, small_b, total, wpa, wpb, turned, edges,
    mixed, carried, states, gate, dno, pre, delta, logs, flags, wout, nout, dmix, tloc, dbi, starts, rsend, rrecv, rows, part, near, far,
    wa, wb, wa1, wb1, dbc, state, send, recv, load, tile_sem,
):
    eh = spread_matrix()
    n = Net(send, recv)
    g, m, core, z = n.g, n.m, n.c, n.z
    W = Reduce(n, "w", wa, wb, wa1, None, wpa, wb1, None, wpb, None)
    loads, fetch = fetcher(load)
    peers = n.greet([n.at(dz=a, dc=b) for a, b in OTHERS] + [n.at(dx=d) for d in XS] + [n.at(dy=d) for d in XS] + [n.group(1), n.group(7)])
    for i in range(MICRO):
        some = pl.ds(CH * i, CH)
        for key, src, dst in (("mixed", mixed_h, mixed), ("gate", gate_h, gate), ("dno", dno_h, dno), ("pre", pre_h, pre), ("logs", logs_h, logs), ("flags", flags_h, flags)):
            fetch((key, i), src.at[some], dst.at[some])
    fetch("wout", wout_h, wout)
    for key, src, dst in (("delta", delta_h, delta), ("states", states_h, states), ("carried", carried_h, carried)):
        fetch(key, src, dst)

    def start_x(i, d):
        return n.copy(("sx", i, d), starts.at[g, i], starts.at[g, i], n.at(dx=d))

    def part_y(i):
        return n.copy(("r", i), rsend.at[i], rrecv.at[i], n.pair())

    def near_copy(d, i):
        return n.copy(("near", d, i), part.at[2 * lax.rem(z + d, 4) + 1 - core, i], near.at[d, i], n.at(dc=1))

    def far_copy(d, i):
        return n.copy(("far", d, i), near.at[d, i], far.at[d - 1, i], n.at(dz=d))

    def bc_copy(i, a, b):
        some = pl.ds(TOK * i, TOK)
        return n.copy(("bc", i, a, b), dbc.at[n.member(a, b), :, some], bc_all.at[m, :, some], n.at(dz=a, dc=b))

    def edge_copy(i):
        return n.copy(("edge", i), gate.at[CH * i, pl.ds(0, 8)], edges.at[i], n.group(7))

    small_o[...] = jnp.zeros_like(small_o)
    small_b[...] = jnp.zeros_like(small_b)

    def outward(i, k):
        c = CH - 1 - k
        at = CH * i + c
        tot = sums[0, at]
        for q in range(1, 8):
            tot = tot + sums[q, at]
        r = column(lax.rsqrt(tot[0:1] / INNER + EPS))
        s2 = column(tot[8:9] / INNER)
        gt = gate[at]
        s = sigmoid(gt)
        sg = gt * s
        mix = mixed[at]
        gated = mix * sg
        dn = dno[at]
        n0 = gated * r
        rows = pl.ds(pl.multiple_of(Q * c, Q), Q)
        nb = n0 * og[0:1]
        nout[i, rows] = nb.astype(BF16)
        turned[:, pl.ds(pl.multiple_of(Q * at, Q), Q)] = nb.T.astype(BF16)
        d_gated = r * (dn * og[0:1] - n0 * r * s2)
        dm = d_gated * sg
        dmix[at] = dm
        dgate[i, rows] = (d_gated * mix * (s * (1.0 + gt * (1.0 - s)))).astype(BF16)
        x = pre[at, :, :512]
        X = x * sigmoid(x)
        cc = pre[at, :, 640:768]
        C = (cc * sigmoid(cc)).astype(BF16)
        small_o[0:1] += jnp.sum(dn * n0, 0, keepdims=True)
        small_o[1:2] += jnp.sum(X * dm, 0, keepdims=True)
        E, _ = decays(logs[at], flags[at])
        Ex = heads_of(E, eh)
        G = right_parts(C, Ex * dm, 2, TN)
        tloc[at] = G
        state[...] = Ex[Q - 1 : Q] * state[...] + G

    for i in range(MICRO):
        for key in ("mixed", "gate", "dno", "pre", "logs", "flags"):
            loads[key, i].wait()
        state[...] = jnp.zeros_like(state)
        lax.fori_loop(0, CH, lambda k, carry, i=i: (outward(i, k), carry)[1], 0)
        starts[g, i] = state[...].astype(BF16)
        if i == 0:
            n.meet(peers)
        for d in XS:
            start_x(i, d).start()
        if i == 0:
            loads["wout"].wait()
        part[:, i] = bdot(nout[i], wout[...]).astype(BF16).reshape(8, 64, 2048)
        for d in (1, 3, 2, 0):
            near_copy(d, i).start()

    def bring(k):
        at = pl.ds(pl.multiple_of(256 * W.group(*ORDER[k]), 256), 256)
        return pltpu.make_async_copy(normed.at[at], rows.at[k % 2], tile_sem.at[k % 2])

    def states_on(i):
        for d in XS:
            start_x(i, d).wait_recv()
        rsend[i] = entering(n, starts, endlog, 1, 1, i).astype(BF16)
        part_y(i).start()

    def tokens_on(i):
        for d in (1, 3, 2, 0):
            near_copy(d, i).wait_recv()
            there = 2 * lax.rem(z + d, 4) + core
            near[d, i] = (part[there, i].astype(F32) + near[d, i].astype(F32)).astype(BF16)
            if d:
                far_copy(d, i).start()

    bring(0).start()
    for k, (d, f) in enumerate(ORDER):
        bring(k).wait()
        if k < 7:
            bring(k + 1).start()
        q = W.group(d, f)
        v = bdot(rows[k % 2], dgate[...].reshape(T, 512))
        wa[q] = v[:, 0:C1].astype(BF16)
        wb[q] = v[:, C1:].astype(BF16)
        W.send_a(d, f)
        W.send_b(d, f)
        if k == 1:
            states_on(0)
            tokens_on(0)
        if k == 5:
            states_on(1)
            tokens_on(1)

    loads["delta"].wait()
    loads["states"].wait()
    loads["carried"].wait()

    def inside(at, carry):
        L = logs[at]
        f = flags[at]
        E, _ = decays(L, f)
        X, B, C = activations(pre[at])
        more = heads_of(jnp.concatenate([E, delta[at]], 0), eh)
        Ex, dx = more[:Q], more[Q:]
        Ub = (dx * X).astype(BF16)
        dm = dmix[at]
        dmb = dm.astype(BF16)
        psi = bdot(C, B, NT)
        keep = same_mask(f, segrow[at])
        LT = L.T
        dpsi = jnp.zeros((Q, Q), F32)
        for j in range(4):
            js = slice(128 * j, 128 * j + 128)
            u = pair_halves(Ub[:, js])
            y = pair_halves(dmb[:, js])
            acc = jnp.zeros((Q, 128), F32)
            for e in range(2):
                h = 2 * j + e
                K = jnp.where(keep, jnp.exp(L[:, h : h + 1] - LT[h : h + 1]), 0.0)
                acc = acc + bdot((psi * K).astype(BF16), y[e], TN)
                dpsi = dpsi + bdot(y[e], u[e], NT) * K
            dno[at, :, js] = acc
        dpb = dpsi.astype(BF16)
        dbi[at, 0:128] = bdot(C, dpb, TN)
        dbi[at, 128:256] = bdot(B, dpb, TT) + bdot(states[at, 0].astype(BF16), (Ex * dm).astype(BF16), NT)
        return carry

    lax.fori_loop(0, 8, inside, 0)
    for i in (0, 1):
        part_y(i).wait_recv()

    def inward(i, k):
        c = CH - 1 - k
        at = CH * i + c
        L = logs[at]
        d = delta[at]
        E, W_ = decays(L, flags[at])
        p = pre[at, :, 0:512]
        s = sigmoid(p)
        X = p * s
        bb = pre[at, :, 512:640]
        B = (bb * sigmoid(bb)).astype(BF16)
        more = heads_of(jnp.concatenate([E[Q - 8 :], W_, d, jnp.broadcast_to(hp[2:3], (8, 128))], 0), eh)
        Elast, Wx, dx, skip = more[7:8], more[8 : 8 + Q], more[8 + Q : 8 + 2 * Q], more[8 + 2 * Q : 9 + 2 * Q]
        U = dx * X
        dm = dmix[at]
        Yc = carried[at]
        Yi = mixed[at] - Yc - skip * X
        G = state[...]
        Gb = G.astype(BF16)
        dUi = dno[at]
        dUc = Wx * bdot(B, Gb)
        dU = dUi + dUc
        lanes = pl.ds(pl.multiple_of(Q * at, Q), Q)
        dbc[0:4, :, lanes] = (dbi[at, 0:128] + bdot(Gb, (Wx * U).astype(BF16), NT)).astype(BF16).reshape(4, 32, Q)
        dbc[4:8, :, lanes] = dbi[at, 128:256].astype(BF16).reshape(4, 32, Q)
        dL = sums_of(dm.astype(BF16).astype(F32) * Yi + dm * Yc - U.astype(BF16).astype(F32) * dUi - U * dUc, eh)
        end = sums_of(jnp.broadcast_to(jnp.sum(G * states[at, 1], 0, keepdims=True), (8, 512)), eh)[0:1]
        upper = (iota((Q, Q), 0) <= iota((Q, Q), 1)).astype(BF16)
        dstep = right_parts(upper, dL, 3) + end
        rate = hp[1:2]
        dr = (sums_of(dU * X, eh) + dstep * rate) * (1.0 - jnp.exp(-d))
        ddt[at] = dr.astype(BF16)
        small_b[0:1] += jnp.sum(dr, 0, keepdims=True)
        small_b[1:2] += jnp.sum(dstep * d * rate, 0, keepdims=True)
        gate[at] = (dx * dU + skip * dm) * (s * (1.0 + p * (1.0 - s)))
        state[...] = Elast * G + tloc[at]

    store = pltpu.make_async_copy(gate, dpre_h, load.at[0])
    for i in range(MICRO):
        state[...] = entering(n, starts, endlog, 0, 1, i) + rrecv[i].astype(F32)
        lax.fori_loop(0, CH, lambda k, carry, i=i: (inward(i, k), carry)[1], 0)
        edge_copy(i).start()
        for a, b in OTHERS:
            bc_copy(i, a, b).start()
    store.start()
    bc_all[m] = dbc[m]

    W.middle_b()
    W.middle_a(1)
    W.middle_a(0)
    for i in range(MICRO):
        for d in XS:
            far_copy(d, i).wait_recv()
        total[i] = near[0, i].astype(F32) + far[0, i].astype(F32) + far[1, i].astype(F32) + far[2, i].astype(F32)
    for i in range(MICRO):
        edge_copy(i).wait_recv()
        for a, b in OTHERS:
            bc_copy(i, a, b).wait_recv()
    W.finish_first()
    for i in range(MICRO):
        edge_copy(i).wait_send()
        for a, b in OTHERS:
            bc_copy(i, a, b).wait_send()
    store.wait()
    for i in range(MICRO):
        part_y(i).wait_send()
        for d in XS:
            start_x(i, d).wait_send()
            far_copy(d, i).wait_send()
        for d in range(4):
            near_copy(d, i).wait_send()


def back_wave(mixed, carried, states, gate, dno, sums, pre, delta, logs, flags, segrow, og, hp, wout, normed, endlog):
    outs = [
        sds((2, TOK, 512), BF16), sds((8, Q, 512), F32), sds((8, 32, T), BF16), sds((8, Q, 128), BF16), sds((8, 512), F32), sds((8, 128), F32), sds((2, 64, 2048), F32),
        sds((2, 256, C1), BF16), sds((4, 128, C1), BF16), sds((512, T), BF16), sds((2, 8, 512), F32),
    ]
    V = lambda *s: pltpu.VMEM(s, BF16)
    R = lambda *s: pltpu.VMEM(s, F32)
    return pl.pallas_call(
        back_wave_kernel,
        name="back_wave",
        out_shape=outs,
        in_specs=[ANY] * 5 + [VM] + [ANY] * 4 + [VM] * 3 + [ANY] * 2 + [VM],
        out_specs=[VM, ANY] + [VM] * 9,
        scratch_shapes=[
            R(8, Q, 512), R(8, Q, 512), R(8, 2, 128, 512), R(8, Q, 512), R(8, Q, 512), R(8, Q, 768), R(8, Q, 128), R(8, Q, 128), R(8, Q, 128), V(512, 2048),
            V(2, TOK, 512), R(8, Q, 512), R(8, 128, 512), R(8, 256, 128), V(8, 2, 128, 512), V(2, 128, 512), V(2, 128, 512), V(2, 256, T), V(8, 2, 64, 2048),
            V(4, 2, 64, 2048), V(3, 2, 64, 2048),
            V(8, 256, C1), V(8, 256, C1), V(3, 2, 256, C1), V(3, 4, 128, C1), V(8, 32, T), R(128, 512),
            pltpu.SemaphoreType.DMA((96,)), pltpu.SemaphoreType.DMA((96,)), pltpu.SemaphoreType.DMA((16,)), pltpu.SemaphoreType.DMA((2,)),
        ],
        compiler_params=pltpu.CompilerParams(collective_id=4, has_side_effects=True, vmem_limit_bytes=62 << 20),
        cost_estimate=pl.CostEstimate(flops=8 << 30, bytes_accessed=32 << 20, transcendentals=0),
    )(mixed, carried, states, gate.reshape(8, Q, 512), dno, sums, pre, delta, logs, flags, segrow, og, hp, wout, normed, endlog)


CB = 256
CA = 640 - CB


def tail_kernel(
    bc_s, ex_s, wpa, wpb, turned, branch, gain, cot, dpre, pre, ext, flags, fnext, conv, ddt, dgate, w, hid, normed, small_o, small_b,
    g_in, g_out, layer_out, grad_in, small_out,
    eb_src, eb_s, dps, pre_s, ext_s, fl_s, fn_s, ddt_s, dg_s, w_s, hid_s, nm_s, wt, e_s, dproj, part, near, far, conv_acc, gnorm,
    s0, s1, s2, sx, ga, gb, ga1, ga2, gpa, gb1, gb2, gpb, gb3, cot_s, gsw, oa, ob, oa1, oa2, opa, ob1, ob2, opb, ob3, oin, cot_own, ga2_, gb2_, gb3_, gi, small_all, convt, final, send, recv, load, tile_sem,
):
    n = Net(send, recv)
    x, y, z, c, m = n.x, n.y, n.z, n.c, n.m
    loads = {}

    def fetch(key, src, dst):
        loads[key] = pltpu.make_async_copy(src, dst, load.at[len(loads)])
        loads[key].start()

    peers = n.greet([n.at(dz=a, dc=b) for a, b in OTHERS] + [n.at(dx=d) for d in XS] + [n.at(dy=d) for d in XS] + [n.group(1), n.group(7)])
    fetch("pre", pre.at[:, :, pl.ds(512, 256)], pre_s)
    fetch("w", w, w_s)
    fetch("dpre", dpre, dps.at[:, pl.ds(0, TOK), pl.ds(0, 512)])
    fetch("ext", ext, ext_s)
    fetch("flags", flags, fl_s)
    fetch("fnext", fnext, fn_s)
    fetch("ddt", ddt, ddt_s)
    fetch("normed", normed, nm_s)
    fetch("dgate", dgate, dg_s)
    fetch("hid", hid, hid_s)
    fetch("cot", cot.at[m], cot_own)
    n.meet(peers)
    G_ = Reduce(n, "g", None, None, None, ga2_, wpa, None, gb2_, wpb, gb3_)
    G_.go_a(1)
    G_.go_a(0)
    G_.go_b()

    edge2 = n.copy("edge2", eb_src, eb_s, n.group(7))

    def near_copy(d, i):
        return n.copy(("near", d, i), part.at[2 * lax.rem(z + d, 4) + 1 - c, i], near.at[d, i], n.at(dc=1))

    def far_copy(d, i):
        return n.copy(("far", d, i), near.at[d, i], far.at[d - 1, i], n.at(dz=d))

    def small_x(d):
        return n.copy(("sx", d), s0, s1.at[d - 1], n.at(dx=d))

    def small_y(d):
        return n.copy(("sy", d), sx, s2.at[d - 1], n.at(dy=d))

    def small_m(a, b):
        return n.copy(("sm", a, b), small_all.at[m], small_all.at[m], n.at(dz=a, dc=b))

    def rows_copy(a, b):
        return n.copy(("rows", a, b), final.at[n.member(a, b)], gi.at[m], n.at(dz=a, dc=b))

    O = Reduce(n, "o", oa, ob, oa1, oa2, opa, ob1, ob2, opb, ob3)
    swap = n.copy("swap", gsw.at[:, 1 - c], oin, n.at(dc=1))
    W = Reduce(n, "w", ga, gb, ga1, ga2, gpa, gb1, gb2, gpb, gb3)

    pick = pick_matrix(256, 32 * m, 32, 0)
    loads["w"].wait()
    wt[...] = (bdot(w_s[:, 1024:1280], pick) + bdot(w_s[:, 1280:1408], pick_matrix(128, 0, 8, 32))).astype(BF16)
    cw = jnp.concatenate([conv[:, 0:512], left_parts(conv[:, 512:768], pick, 3)], 1)
    for key in ("pre", "dpre"):
        loads[key].wait()
    eye = pick_matrix(32, 0, 32, 0)

    def bc_chunk(i, k):
        t = CH * i + k
        tot = bc_s[0, :, Q * t : Q * t + Q].astype(F32)
        for q in range(1, 8):
            tot = tot + bc_s[q, :, Q * t : Q * t + Q].astype(F32)
        d = left_parts(tot, eye, 2, TN)
        p = left_parts(pre_s[t], pick, 2)
        s = sigmoid(p)
        dps[i, Q * k : Q * k + Q, 512:640] = d * (s * (1.0 + p * (1.0 - s)))

    for i in range(MICRO):
        bc_chunk(i, 0)
        eb_src[i] = dps[i, 0:8, 512:640]
    edge2.start()
    for i in range(MICRO):
        for k in range(1, CH):
            bc_chunk(i, k)
    def bring(k):
        return pltpu.make_async_copy(cot.at[:, :, :, pl.ds(256 * k, 256)], cot_s.at[k % 2], tile_sem.at[k % 2])

    bring(0).start()
    for k in range(8):
        bring(k).wait()
        if k < 7:
            bring(k + 1).start()
        v = sum(bdot(turned[:, TOK * i : TOK * i + TOK], cot_s[k % 2, :, i].reshape(TOK, 256)) for i in range(MICRO))
        gsw[:, :, :, 256 * k : 256 * k + 256] = v.astype(BF16).reshape(4, 2, 64, 256)
    swap.start()
    for j in range(4):
        oa[4 * c + j] = gsw[j, c, :, 0:1024]
        ob[4 * c + j] = gsw[j, c, :, 1024:2048]

    for key in ("ext", "flags", "fnext", "ddt"):
        loads[key].wait()
    conv_acc[...] = jnp.zeros_like(conv_acc)
    pick_dt = pick_matrix(128, 0, 8, 32)

    def conv_chunk(i, k):
        t = CH * i + k
        e_s[:, 0:512] = ext_s[t, :, 0:512].astype(F32)
        e_s[:, 512:640] = bdot(ext_s[t, :, 512:768], pick)
        f, fn = fl_s[t], fn_s[t]
        dp = dps[i, Q * k : Q * k + Q]
        dx = cw[3:4] * dp
        conv_acc[3:4] += jnp.sum(dp * e_s[8 : 8 + Q], 0, keepdims=True)
        conv_acc[4:5] += jnp.sum(dp, 0, keepdims=True)
        for j in range(3):
            conv_acc[j : j + 1] += jnp.sum(dp * e_s[5 + j : 5 + j + Q] * f[:, j : j + 1], 0, keepdims=True)
            dx = dx + cw[j : j + 1] * dps[i, Q * k + 3 - j : Q * k + 3 - j + Q] * fn[:, j : j + 1]
        rows = slice(Q * k, Q * k + Q)
        dproj[i, rows, 0:512] = dx[:, 0:512].astype(BF16)
        dproj[i, rows, 512:640] = (dx[:, 512:640] + bdot(ddt_s[t], pick_dt)).astype(BF16)

    for i in range(MICRO):
        for k in range(CH - 1):
            conv_chunk(i, k)
    swap.wait_recv()
    for j in range(4):
        oa[4 * (1 - c) + j] = oin[j, :, 0:1024]
        ob[4 * (1 - c) + j] = oin[j, :, 1024:2048]
    for d, f in ORDER:
        O.send_a(d, f)
        O.send_b(d, f)

    edge2.wait_recv()
    for i in range(MICRO):
        dps[i, TOK : TOK + 8, 0:512] = ex_s[i]
        dps[i, TOK : TOK + 8, 512:640] = eb_s[i]
        conv_chunk(i, CH - 1)

    loads["hid"].wait()
    loads["dgate"].wait()
    for i in range(MICRO):
        h = hid_s[:, i].reshape(TOK, 2048).astype(F32)
        scale = row_scale(h)
        first, main, rest = dg_s[i], dproj[i, :, 0:512], dproj[i, :, 512:640]

        def tile_of(j, carry, i=i, scale=scale, first=first, main=main, rest=rest):
            at = pl.ds(pl.multiple_of(256 * j, 256), 256)
            d = bdot(first, w_s[at, 0:512], NT) + bdot(main, w_s[at, 512:1024], NT) + bdot(rest, wt[at], NT)
            part[:, i, :, at] = d.astype(BF16).reshape(8, 64, 256)
            hv = hid_s[:, i, :, at].reshape(TOK, 256).astype(F32)
            s = jnp.sum(d * (hv * scale), 0, keepdims=True)
            gnorm[0:1, at] = s if i == 0 else gnorm[0:1, at] + s
            return carry

        lax.fori_loop(0, 8, tile_of, 0)
        for d in (1, 3, 2, 0):
            near_copy(d, i).start()
    for r in range(16):
        s0[r : r + 1] = gnorm[0:1, 128 * r : 128 * r + 128]
    for k in range(5):
        for r in range(5):
            s0[16 + 5 * k + r : 17 + 5 * k + r] = conv_acc[k : k + 1, 128 * r : 128 * r + 128]
    for r in range(4):
        s0[41 + r : 42 + r] = small_o[0:1, 128 * r : 128 * r + 128]
    s0[45:47] = small_b[0:2]
    s0[47:48] = sums_of(small_o[...], spread_matrix())[1:2]
    for d in XS:
        small_x(d).start()

    def tokens_on(i):
        for d in (1, 3, 2, 0):
            near_copy(d, i).wait_recv()
            there = 2 * lax.rem(z + d, 4) + c
            near[d, i] = (part[there, i].astype(F32) + near[d, i].astype(F32)).astype(BF16)
            if d:
                far_copy(d, i).start()

    loads["normed"].wait()
    for k, (d, f) in enumerate(ORDER):
        q = W.group(d, f)
        at = pl.ds(pl.multiple_of(256 * q, 256), 256)
        v = bdot(nm_s[at], dproj[...].reshape(T, 640)).astype(BF16)
        gb[q] = v[:, 0:CB]
        ga[q] = v[:, CB:]
        W.send_a(d, f)
        W.send_b(d, f)
        if k == 2:
            tokens_on(0)
        if k == 6:
            tokens_on(1)

    G_.last_b()
    final[:, :, 0:C1] = G_.last_a().astype(BF16).reshape(8, 32, C1)
    for i in range(MICRO):
        layer_out[i] = (hid_s[m, i].astype(F32) + branch[i]).astype(BF16)
    O.middle_b()
    O.go_b()
    O.middle_a(1)
    O.go_a(1)
    O.middle_a(0)
    O.go_a(0)

    for d in XS:
        small_x(d).wait_recv()
    sx[...] = s0[...] + s1[0] + s1[1] + s1[2]
    for d in XS:
        small_y(d).start()
    W.middle_b()
    W.go_b()
    W.middle_a(1)
    W.go_a(1)
    W.middle_a(0)
    W.go_a(0)
    O.last_b()
    g_out[:, 0:1024] = O.last_a()
    W.last_b()
    for d in XS:
        small_y(d).wait_recv()
    small_all[m] = sx[...] + s2[0] + s2[1] + s2[2]
    for a, b in OTHERS:
        small_m(a, b).start()
    for i in range(MICRO):
        for d in XS:
            far_copy(d, i).wait_recv()
        dn = near[0, i].astype(F32) + far[0, i].astype(F32) + far[1, i].astype(F32) + far[2, i].astype(F32)
        if i == 0:
            loads["cot"].wait()
        h = hid_s[m, i].astype(F32)
        r = row_scale(h)
        dg = dn * gain[0:1]
        grad_in[i] = (cot_own[i].astype(F32) + r * dg - h * (r * r * r) * jnp.mean(dg * h, axis=-1, keepdims=True)).astype(BF16)
    O.third_b().wait_recv()
    for h in range(2):
        g_out[32 * h : 32 * h + 32, 1024:2048] = ob3[h]
    W.third_b().wait_recv()
    for h in range(2):
        final[4 * h : 4 * h + 4, :, 512 : 512 + CB] = gb3[h].reshape(4, 32, CB)
    final[:, :, 512 + CB :] = W.last_a().astype(BF16).reshape(8, 32, CA)
    G_.third_b().wait_recv()
    for h in range(2):
        final[4 * h : 4 * h + 4, :, C1:512] = gb3_[h].reshape(4, 32, C1)
    for a, b in OTHERS:
        rows_copy(a, b).start()
    gi[m] = final[m]
    for a, b in OTHERS:
        rows_copy(a, b).wait_recv()
        small_m(a, b).wait_recv()

    rest_cols = jnp.zeros((32, 384), F32)
    r, l = iota((128, 384), 0), iota((128, 384), 1)
    for q in range(8):
        zq, cq = q // 2, q % 2
        for j in range(4):
            at = 512 * (4 * cq + j) + 128 * zq
            g_in[:, at : at + 128] = gi[q, :, 128 * j : 128 * j + 128].astype(F32)
            g_in[:, 4096 + at : 4224 + at] = gi[q, :, 512 + 128 * j : 640 + 128 * j].astype(F32)
        k = r - 32
        put = ((r < 32) & (l == 32 * q + r)) | ((r >= 32) & (r < 40) & (l == 256 + 32 * cq + 8 * (k // 2) + 2 * zq + k % 2))
        rest_cols = rest_cols + bdot(gi[q, :, 1024:1152], put.astype(BF16))
    g_in[:, 8192:8512] = rest_cols[:, 0:320]

    g = n.g
    shard = 8 * g + m
    lane, row = iota((8, 128), 1), iota((8, 128), 0)

    def pick_row(v, at):
        return jnp.broadcast_to(jnp.sum(jnp.where(iota(v.shape, 0) == at, v, 0.0), 0, keepdims=True), (8, 128))

    norm_sum = small_all[0, 0:16]
    for q in range(1, 8):
        norm_sum = norm_sum + small_all[q, 0:16]
    norm_row = pltpu.roll(pick_row(norm_sum, shard // 4), lax.rem(128 - 32 * lax.rem(shard, 4), 128), 1)
    mine = small_all[2 * (m // 2) + g // 4]
    out_row = pltpu.roll(pick_row(mine[40:48], 1 + lax.rem(g, 4)), 64 * lax.rem(m, 2), 1)
    here = lane == 2 * lax.rem(g, 4) + lax.rem(m, 2)
    heads_row = jnp.zeros((8, 128), F32)
    for k in range(3):
        v = jnp.sum(jnp.where(here, pick_row(mine[40:48], 5 + k), 0.0), 1, keepdims=True)
        heads_row = heads_row + jnp.where(lane == k, v, 0.0)
    convt[...] = jnp.zeros_like(convt)
    for t in range(32):
        q, j = 2 * (t % 4) + t // 16, t // 4 % 4
        for k in range(5):
            convt[t, k : k + 1] = small_all[q, 16 + 5 * k + j : 17 + 5 * k + j]
    for q in range(8):
        for k in range(5):
            v = jnp.where(lane < 32, jnp.broadcast_to(small_all[q, 20 + 5 * k : 21 + 5 * k], (8, 128)), 0.0)
            convt[32 + q // 4, k : k + 1] += (pltpu.roll(v, 32 * (q % 4), 1) if q % 4 else v)[0:1]
    tile = 68 * shard // 128
    both = jnp.concatenate([convt[tile], convt[tile + 1]], 1)
    own = pltpu.roll(both, lax.rem(256 - lax.rem(68 * shard, 128), 256), 1)[:, 0:128]
    small_out[...] = jnp.where(row == 5, norm_row, jnp.where(row == 6, out_row, jnp.where(row == 7, heads_row, own)))
    W.finish_first()
    O.finish_first()
    W.finish()
    O.finish()
    G_.finish()
    swap.wait_send()
    for a, b in OTHERS:
        rows_copy(a, b).wait_send()
        small_m(a, b).wait_send()
    for d in XS:
        small_x(d).wait_send()
        small_y(d).wait_send()
        for i in range(MICRO):
            far_copy(d, i).wait_send()
    for d in range(4):
        for i in range(MICRO):
            near_copy(d, i).wait_send()
    edge2.wait_send()


def tail_call(bc_all, edges, wpa, wpb, turned, branch, gain, cot, dpre, pre, ext, flags, fnext, conv, ddt, dgate, w, hid, normed, small_o, small_b):
    outs = [sds((32, 8512), F32), sds((64, 2048), F32), sds((2, 64, 2048), BF16), sds((2, 64, 2048), BF16), sds((8, 128), F32)]
    V = lambda *s: pltpu.VMEM(s, BF16)
    R = lambda *s: pltpu.VMEM(s, F32)
    scratch = [
        R(2, 8, 128), R(2, 8, 128), R(2, TOK + 8, 640), R(8, Q, 256), V(8, Q + 8, 768), R(8, Q, 128), R(8, Q, 128), V(8, Q, 128), V(2, TOK, 512), V(2048, 1408),
        V(8, 2, 64, 2048), V(2048, T), V(2048, 128), R(Q + 8, 640), V(2, TOK, 640), V(8, 2, 64, 2048), V(4, 2, 64, 2048), V(3, 2, 64, 2048), R(8, 640), R(8, 2048),
        R(48, 128), R(3, 48, 128), R(3, 48, 128), R(48, 128),
        V(8, 256, CA), V(8, 256, CB), V(3, 2, 256, CA), V(3, 256, CA), V(2, 256, CA), V(3, 4, 128, CB), V(3, 128, CB), V(4, 128, CB), V(2, 128, CB),
        V(2, 8, 2, 64, 256), V(4, 2, 64, 2048), V(8, 64, 1024), V(8, 64, 1024), V(3, 2, 64, 1024), V(3, 64, 1024), V(2, 64, 1024), V(3, 4, 32, 1024), V(3, 32, 1024), V(4, 32, 1024), R(2, 32, 1024), V(4, 64, 2048),
        V(2, 64, 2048), V(3, 256, C1), V(3, 128, C1), V(2, 128, C1), V(8, 32, 1152), R(8, 48, 128), R(35, 8, 128), V(8, 32, 1152),
    ]
    return pl.pallas_call(
        tail_kernel,
        name="tail",
        out_shape=outs,
        in_specs=[VM] * 7 + [ANY] * 6 + [VM] + [ANY] * 5 + [VM] * 2,
        out_specs=[VM] * 5,
        scratch_shapes=[*scratch, pltpu.SemaphoreType.DMA((112,)), pltpu.SemaphoreType.DMA((112,)), pltpu.SemaphoreType.DMA((12,)), pltpu.SemaphoreType.DMA((2,))],
        compiler_params=pltpu.CompilerParams(collective_id=5, has_side_effects=True, vmem_limit_bytes=62 << 20),
        cost_estimate=pl.CostEstimate(flops=8 << 30, bytes_accessed=32 << 20, transcendentals=0),
    )(bc_all, edges, wpa, wpb, turned, branch, gain, cot, dpre, pre, ext, flags, fnext, conv, ddt, dgate, w, hid, normed, small_o, small_b)


def per_device(layer_in, cotangent, segment_ids, norm_gain, in_weight, conv_weight, conv_bias, dt_bias, a_log, skip_gain, out_gain, out_weight):
    (
        normed, hid_all, w_in, gate, pre, ext, delta, logs, flags, fnext, mixed, carried, states, dno, cot, w_out,
        sums, ends_all, conv, hp, og, gain, segrow,
    ) = wave(
        layer_in[:, 0], in_weight, segment_ids[:, 0], norm_gain[None], out_gain[None], conv_weight, conv_bias[None], dt_bias, a_log, skip_gain, cotangent[:, 0], out_weight
    )
    w_in = w_in.reshape(2048, 1408)
    dgate, dpre, bc_all, ddt, small_o, small_b, own_branch, wpa, wpb, turned, edges = back_wave(
        mixed, carried, states, gate, dno, sums, pre, delta, logs, flags, segrow, og, hp, w_out.reshape(512, 2048), normed, ends_all
    )
    dpre = dpre.reshape(MICRO, TOK, 512)
    g_in, g_out, layer_out, grad_in, small = tail_call(
        bc_all, edges, wpa, wpb, turned, own_branch, gain, cot, dpre, pre, ext, flags, fnext, conv, ddt, dgate, w_in, hid_all, normed, small_o, small_b
    )
    return (
        layer_out[:, None], grad_in[:, None], small[5, :32], g_in, small[:4, :68], small[4, :68], small[7, 0:1], small[7, 1:2], small[7, 2:3], small[6, :64], g_out,
    )


def solution(mesh):
    fine = Mesh(mesh.devices.reshape(2, 4, 2, 4, 2), AXES)
    tok = P(None, "rep", SEQ, None)
    return jax.shard_map(
        per_device,
        mesh=fine,
        in_specs=(tok, tok, P(None, "rep", SEQ), P(SEQ), P(SEQ, None), P(None, SEQ), P(SEQ), P(SEQ), P(SEQ), P(SEQ), P(SEQ), P(SEQ, None)),
        out_specs=(tok, tok, P(SEQ), P(SEQ, None), P(None, SEQ), P(SEQ), P(SEQ), P(SEQ), P(SEQ), P(SEQ), P(SEQ, None)),
        check_vma=False,
    )
```

```python
import functools

import jax
import jax.numpy as jnp
from jax import lax
from jax.experimental import pallas as pl
from jax.experimental.pallas import tpu as pltpu
from jax.sharding import Mesh, PartitionSpec as P

EPS = 1e-05
INNER = 4096
MICRO = 2
CONV = 4352
F32 = jnp.float32
BF16 = jnp.bfloat16
AXES = ("rep", "x", "y", "z", "c")
SEQ = ("x", "y", "z", "c")
GROUPS = 8
TOK = 512
Q = 128
CH = TOK // Q

MESH = pl.DeviceIdType.MESH
ANY = pl.BlockSpec(memory_space=pl.ANY)
VM = pl.BlockSpec(memory_space=pltpu.VMEM)
SMEM = pl.BlockSpec(memory_space=pltpu.SMEM)


class Net:
    def __init__(self, send, recv):
        self.send, self.recv, self.used, self.open = send, recv, 0, []
        self.keys = {}
        self.rep, self.x, self.y, self.z, self.c = (lax.axis_index(a) for a in AXES)
        self.ring = 2 * self.rep + self.y
        self.g = 2 * self.x + self.y
        self.m = 2 * self.z + self.c

    def at(self, dx=0, dy=0, dz=0, dc=0):
        ring = lax.rem(self.ring + dy, 4)
        return (ring // 2, lax.rem(self.x + dx, 4), lax.rem(ring, 2), lax.rem(self.z + dz, 4), lax.rem(self.c + dc, 2))

    def pair(self):
        return (self.rep, self.x, 1 - self.y, self.z, self.c)

    def across(self, dx):
        return (self.rep, lax.rem(self.x + dx, 4), 1 - self.y, self.z, self.c)

    def group(self, d):
        g = lax.rem(self.g + d, 8)
        return (self.rep, g // 2, lax.rem(g, 2), self.z, self.c)

    def member(self, dz, dc):
        return 2 * lax.rem(self.z + dz, 4) + lax.rem(self.c + dc, 2)

    def push(self, src, dst, where):
        i = self.used
        self.used += 1
        copy = pltpu.make_async_remote_copy(
            src_ref=src, dst_ref=dst, send_sem=self.send.at[i], recv_sem=self.recv.at[i], device_id=where, device_id_type=MESH
        )
        copy.start()
        self.open.append(copy)
        return copy

    def copy(self, key, src, dst, where):
        i = self.keys.setdefault(key, len(self.keys))
        return pltpu.make_async_remote_copy(
            src_ref=src, dst_ref=dst, send_sem=self.send.at[i], recv_sem=self.recv.at[i], device_id=where, device_id_type=MESH
        )

    def behind(self, d):
        return 2 * lax.rem(self.x + 4 - d, 4) + self.y

    def local(self, src, dst):
        i = self.used
        self.used += 1
        copy = pltpu.make_async_copy(src, dst, self.recv.at[i])
        copy.start()
        return copy

    def greet(self, peers):
        for peer in peers:
            pl.semaphore_signal(pltpu.get_barrier_semaphore(), inc=1, device_id=peer, device_id_type=MESH)
        return len(peers)

    def meet(self, count):
        pl.semaphore_wait(pltpu.get_barrier_semaphore(), count)

    def finish(self):
        for copy in self.open:
            copy.wait_send()


OTHERS = [(dz, dc) for dz in (0, 1, 3, 2) for dc in (0, 1) if (dz, dc) != (0, 0)]
ZS = (0, 1, 3, 2)
XS = (1, 3, 2)
ORDER = [(d, f) for d in (2, 1, 3, 0) for f in (1, 0)]


def sds(shape, dtype):
    return jax.ShapeDtypeStruct(shape, dtype)


def add4(a, b):
    return a.astype(F32) + b[0].astype(F32) + b[1].astype(F32) + b[2].astype(F32)


NN = (((1,), (0,)), ((), ()))
NT = (((1,), (1,)), ((), ()))
TN = (((0,), (0,)), ((), ()))
TT = (((0,), (1,)), ((), ()))


def bdot(a, b, dims=NN):
    return lax.dot_general(a, b, dims, preferred_element_type=F32)


def parts(v, count):
    out = []
    for _ in range(count):
        p = v.astype(BF16)
        out.append(p)
        v = v - p.astype(F32)
    return out


def left_parts(v, w, count, dims=NN):
    return sum(bdot(p, w, dims) for p in parts(v, count))


def right_parts(w, v, count, dims=NN):
    return sum(bdot(w, p, dims) for p in parts(v, count))


def iota(shape, dim):
    return lax.broadcasted_iota(jnp.int32, shape, dim)


def spread_matrix():
    return (iota((128, 512), 0) == iota((128, 512), 1) // 64).astype(BF16)


def heads_of(v, eh):
    return left_parts(v, eh, 2)


def sums_of(v, eh):
    return left_parts(v, eh, 2, NT)


def lower_matrix():
    return (iota((Q, Q), 0) >= iota((Q, Q), 1)).astype(BF16)


def sigmoid(v):
    return 1.0 / (1.0 + jnp.exp(-v))


def softplus(v):
    return jnp.maximum(v, 0.0) + jnp.log1p(jnp.exp(-jnp.abs(v)))


def row_scale(h):
    return lax.rsqrt(jnp.mean(h * h, axis=-1, keepdims=True) + EPS)


def decays(L, flags):
    E = jnp.exp(L) * flags[:, 3:4]
    W = jnp.exp(L[Q - 1 : Q] - L) * flags[:, 4:5]
    return E, W


def wave_kernel(
    hid, inw, seg, gain_in, og_in, cw_in, cb_in, dtb_in, alog_in, skip_in, cot, outw,
    normed_h, hid_h, w_h, gate_h, pre_h, ext_h, delta_h, logs_h, flags_h, fnext_h, mixed_h, carried_h, states_h, dno_h, cot_h, wout_h,
    sums, endlog, conv, hp, og, gain, segrow,
    hid_s, halo, nrm, turned, w_s, small, proj, pre, ext, delta, logs, flags, fnext, sloc, inner, carried, states, dno, ends, rsend, rrecv, cot_s, w_o, wo_s, convt, state, total, tail, wsend, pack, window, send, recv, done,
):
    eh = spread_matrix()
    n = Net(send, recv)
    g, m, x, y, z, core = n.g, n.m, n.x, n.y, n.z, n.c
    ALLX = (0,) + XS
    copies = []

    def keyed(key, src, dst, where):
        cp = n.copy(key, src, dst, where)
        copies.append(cp)
        cp.start()
        return cp

    stores = []

    def store(src, dst):
        cp = pltpu.make_async_copy(src, dst, done.at[len(stores)])
        cp.start()
        stores.append(cp)

    peers = n.greet([n.at(dz=a, dc=b) for a, b in OTHERS] + [n.at(dx=d) for d in XS] + [n.at(dy=1), n.at(dy=3), n.group(1), n.group(7)] + [n.across(d) for d in ALLX])

    for q in range(8):
        zq, cq = q // 2, q % 2
        for j in range(4):
            at = 512 * (4 * cq + j) + 128 * zq
            wsend[q, :, 128 * j : 128 * j + 128] = inw[:, at : at + 128]
            wsend[q, :, 512 + 128 * j : 640 + 128 * j] = inw[:, 4096 + at : 4224 + at]
        wsend[q, :, 1024:1280] = inw[:, 8192:8448]
        r, k = iota((64, 128), 0), iota((64, 128), 1)
        take = ((r == 32 * cq + 8 * (k // 2) + 2 * zq + k % 2) & (k < 8)).astype(BF16)
        wsend[q, :, 1280:1408] = bdot(inw[:, 8448:8512], take).astype(BF16)
    pack[...] = jnp.zeros_like(pack)
    pack[0:2, 0:64] = seg[...].astype(F32)
    pack[3:4, 0:64] = og_in[...]
    first = pltpu.roll(pack[0:8], 64 * core, 1)
    pack[0:8] = jnp.zeros((8, 128), F32)
    pack[2:3, 0:32] = gain_in[...]
    first = first + pltpu.roll(pack[0:8], 32 * lax.rem(m, 4), 1)
    row, at = iota((8, 128), 0), iota((8, 128), 1) == 2 * lax.rem(g, 4) + core
    for k, ref in enumerate((dtb_in, alog_in, skip_in)):
        first = first + jnp.where(at & (row == 4 + k), ref[0], 0.0)
    pack[0:8] = first
    window[...] = jnp.zeros_like(window)
    window[0:4, 0:68] = cw_in[...]
    window[4:5, 0:68] = cb_in[...]
    moved = pltpu.roll(window[...], lax.rem(68 * (8 * g + m), 128), 1)
    pack[8:16] = moved[:, 0:128]
    pack[16:24] = moved[:, 128:256]

    n.meet(peers)
    wa, sa = {}, {}

    def beside(a, b):
        zz = (z, z + 1 - 2 * lax.rem(z, 2), lax.rem(z + 2, 4), 3 - z)[a]
        cc = 1 - core if b else core
        return (n.rep, x, y, zz, cc), 2 * zz + cc

    PAIRS = [(a, b) for a in range(4) for b in (0, 1) if (a, b) != (0, 0)]
    for a, b in PAIRS:
        where, q = beside(a, b)
        wa[a, b] = keyed(("wa", a, b), wsend.at[q], w_s.at[g, m], where)
        sa[a, b] = keyed(("sa", a, b), pack, small.at[g, m], where)
    w_s[g, m] = wsend[m]
    small[g, m] = pack[...]
    hid_s[m] = hid[...]
    wx, wy, sx, sy = {}, {}, {}, {}

    def members(k):
        return pl.ds(4 * (z // 2 if k == 0 else 1 - z // 2), 4)

    def along_y(d, k):
        for half, dy in ((0, 1), (1, 3)):
            part = w_s.at[n.behind(d), members(k), pl.ds(16 * half, 16)]
            wy[d, k, half] = keyed(("wy", d, k, half), part, part, n.at(dy=dy))

    def issue(k):
        for a, b in PAIRS:
            if a // 2 == k:
                wa[a, b].wait_recv()
        block = w_s.at[g, members(k)]
        for d in XS:
            wx[k, d] = keyed(("wx", k, d), block, block, n.at(dx=d))
        along_y(0, k)

    def forward(k):
        for d in XS:
            wx[k, d].wait_recv()
            along_y(d, k)

    issue(0)
    issue(1)
    hz = {a: keyed(("hz", a), hid_s.at[m], hid_s.at[m], n.at(dz=a)) for a in (1, 3, 2)}
    hn = [keyed("hn", hid_s.at[m], hid_s.at[m], n.at(dc=1))]
    for a, b in PAIRS:
        sa[a, b].wait_recv()
    for d in XS:
        sx[d] = keyed(("sx", d), small.at[g], small.at[g], n.at(dx=d))
    sy[0] = keyed(("sy", 0), small.at[g], small.at[g], n.pair())
    forward(0)
    for d in XS:
        sx[d].wait_recv()
        mine = small.at[n.behind(d)]
        sy[d] = keyed(("sy", d), mine, mine, n.pair())
    forward(1)
    w_o[g] = outw[...]
    ox = {d: keyed(("ox", d), w_o.at[g], w_o.at[g], n.at(dx=d)) for d in XS}
    oy = {}

    def out_y(d):
        for half, dy in ((0, 1), (1, 3)):
            part = w_o.at[n.behind(d), pl.ds(32 * half, 32)]
            oy[d, half] = keyed(("oy", d, half), part, part, n.at(dy=dy))

    out_y(0)
    for a in (1, 3, 2):
        hz[a].wait_recv()
        theirs = hid_s.at[2 * lax.rem(z + 4 - a, 4) + core]
        hn.append(keyed(("hf", a), theirs, theirs, n.at(dc=1)))
    cot_s[m] = cot[...]
    cz = {a: keyed(("cz", a), cot_s.at[m], cot_s.at[m], n.at(dz=a)) for a in (1, 3, 2)}
    cn = [keyed("cn", cot_s.at[m], cot_s.at[m], n.at(dc=1))]
    for d in ALLX:
        sy[d].wait_recv()

    for q in range(16):
        v = small[q // 2, 4 * (q % 2), 2:3]
        for u in range(1, 4):
            v = v + small[q // 2, 4 * (q % 2) + u, 2:3]
        gain[0:1, 128 * q : 128 * q + 128] = v
    heads3 = jnp.zeros((3, 128), F32)
    for j in range(4):
        og[0:1, 128 * j : 128 * j + 128] = small[4 * core + j, 2 * z, 3:4] + small[4 * core + j, 2 * z + 1, 3:4]
        for e in range(2):
            heads3 = heads3 + small[4 * core + j, 2 * z + e, 4:7]
    hp[...] = jnp.zeros_like(hp)
    hp[0:1] = heads3[0:1]
    hp[1:2] = jnp.where(iota((1, 128), 1) < 8, -jnp.exp(heads3[1:2]), 0.0)
    hp[2:3] = heads3[2:3]
    for q in range(34):
        v = jnp.zeros((8, 128), F32)
        for i in range(64):
            if 68 * i // 128 == q:
                v = v + small[i // 8, i % 8, 8:16]
            elif 68 * i // 128 == q - 1:
                v = v + small[i // 8, i % 8, 16:24]
        convt[q] = v
    for j in range(4):
        conv[:, 128 * j : 128 * j + 128] = convt[4 * (4 * core + j) + z]
    conv[:, 512:640] = convt[32]
    conv[:, 640:768] = convt[33]

    lane = iota((8, 128), 1)

    def chunk_row(group, i, c):
        return jnp.broadcast_to(small[group, 2 * c, i : i + 1] + small[group, 2 * c + 1, i : i + 1], (8, 128))

    for i in range(MICRO):
        before = jnp.where(g > 0, chunk_row(lax.rem(g + 7, 8), i, CH - 1), -1.0)
        after = jnp.where(g < 7, chunk_row(lax.rem(g + 1, 8), i, 0), -2.0)
        rows = [before] + [chunk_row(g, i, c) for c in range(CH)] + [after]
        for c in range(CH):
            prv, cur, nxt = rows[c : c + 3]
            here, ahead = [], []
            for d in (3, 2, 1):
                back = jnp.where(lane < d, pltpu.roll(prv, d, 1), pltpu.roll(cur, d, 1))
                here.append((back == cur).astype(F32))
                on = jnp.where(lane >= 128 - d, pltpu.roll(nxt, 128 - d, 1), pltpu.roll(cur, 128 - d, 1))
                ahead.append((on == cur).astype(F32))
            here += [(cur == prv[:, 127:128]).astype(F32), (cur == cur[:, 127:128]).astype(F32), cur]
            sub = iota((128, 128), 0)
            for rows_of, to in ((here, flags), (ahead, fnext)):
                v = jnp.zeros((128, 128), F32)
                for r, row in enumerate(rows_of):
                    v = jnp.where(sub == r, jnp.broadcast_to(row[0:1], (128, 128)), v)
                to[CH * i + c] = v.T
            segrow[CH * i + c] = cur[0:1]

    for cp in hn:
        cp.wait_recv()
    edge = keyed("edge", hid_s.at[7, :, pl.ds(48, 16)], halo, n.group(1))

    gv = gain[0:1]

    def norm(k, carry):
        for i in range(MICRO):
            h = hid_s[pl.ds(2 * k, 2), i].reshape(Q, 2048).astype(F32)
            v = h * row_scale(h) * gv
            nrm[i, pl.ds(pl.multiple_of(16 + Q * k, 16), Q)] = v.astype(BF16)
            turned[:, pl.ds(pl.multiple_of(TOK * i + Q * k, Q), Q)] = v.T.astype(BF16)
        return carry

    lax.fori_loop(0, CH, norm, 0)
    edge.wait_recv()
    for i in range(MICRO):
        h = halo[i].astype(F32)
        nrm[i, 0:16] = (h * row_scale(h) * gv).astype(BF16)
    store(turned, normed_h)

    def project(side, first):
        for i in range(MICRO):
            for lo in range(0, 1408, 256):
                hi = min(lo + 256, 1408)
                v = 0.0 if first else proj[i, :, lo:hi]
                for k in range(4):
                    q = 2 * k + side
                    v = v + bdot(nrm[i, :, pl.ds(pl.multiple_of(256 * q, 256), 256)], w_s[q, :, :, lo:hi].reshape(256, hi - lo))
                proj[i, :, lo:hi] = v

    project(y, True)
    for d in ALLX:
        for k in range(2):
            for half in (0, 1):
                wy[d, k, half].wait_recv()
    project(1 - y, False)
    for d in XS:
        ox[d].wait_recv()
        out_y(d)
    store(w_s, w_h)
    store(hid_s, hid_h)
    store(flags, flags_h)
    store(fnext, fnext_h)

    def front(i, c):
        at = CH * i + c
        rows = pl.ds(pl.multiple_of(16 + Q * c, 16), Q)
        f = flags[at]
        xbc = proj[i, rows, 512:1280].astype(BF16).astype(F32)
        tail[8:] = xbc
        acc = conv[4:5] + conv[3:4] * xbc
        for k in range(3):
            acc = acc + conv[k : k + 1] * tail[5 + k : 5 + k + Q] * f[:, k : k + 1]
        pre[at] = acc
        ext[at] = tail[...].astype(BF16)
        d = softplus(proj[i, rows, 1280:1408] + hp[0:1])
        delta[at] = d
        L = right_parts(lower_matrix(), d * hp[1:2], 3)
        logs[at] = L
        E, W = decays(L, f)
        xv = acc[:, :512]
        X = xv * sigmoid(xv)
        b = acc[:, 512:640]
        B = (b * sigmoid(b)).astype(BF16)
        S = right_parts(B, heads_of(W * d, eh) * X, 2, TN)
        sloc[at] = S
        last = heads_of(E[Q - 8 :], eh)
        state[...] = last[7:8] * state[...] + S
        tail[0:8] = tail[Q : Q + 8]
        total[...] = total[...] + L[Q - 1 : Q]

    ex, lx, ly = {}, {}, {}
    for i in range(MICRO):
        tail[0:8] = proj[i, 8:16, 512:1280].astype(BF16).astype(F32)
        state[...] = jnp.zeros_like(state)
        total[...] = jnp.zeros_like(total)
        lax.fori_loop(0, CH, lambda c, carry, i=i: (front(i, c), carry)[1], 0)
        ends[g, i] = state[...].astype(BF16)
        lt = parts(jnp.broadcast_to(heads_of(jnp.broadcast_to(total[...], (8, 128)), eh)[0:1], (16, 512)), 3)
        seg = jnp.broadcast_to(segrow[CH * i + CH - 1][:, 127:128], (16, 512))
        high = jnp.floor(seg * (1.0 / 64.0))
        r = iota((16, 512), 0)
        v = jnp.zeros((16, 512), BF16)
        for k, row in enumerate(lt + [high.astype(BF16), (seg - 64.0 * high).astype(BF16)]):
            v = jnp.where(r == k, row, v)
        endlog[g, i] = v
        for d in XS:
            lx[i, d] = keyed(("lx", i, d), endlog.at[g, i], endlog.at[g, i], n.at(dx=d))
        for d in ALLX:
            ly[i, d] = keyed(("ly", i, d), endlog.at[g, i], endlog.at[g, i], n.across(d))
        for d in XS:
            ex[i, d] = keyed(("ex", i, d), ends.at[g, i], ends.at[g, i], n.at(dx=d))
    store(pre, pre_h)
    store(ext, ext_h)
    store(delta, delta_h)
    store(logs, logs_h)
    for i in range(MICRO):
        store(proj.at[i, pl.ds(16, TOK), pl.ds(0, 512)], gate_h.at[i])

    def states_on(i):
        for d in XS:
            lx[i, d].wait_recv()
        for d in ALLX:
            ly[i, d].wait_recv()
        for d in XS:
            ex[i, d].wait_recv()
        rsend[i] = entering(n, ends, endlog, 1, 0, i).astype(BF16)
        return keyed(("r", i), rsend.at[i], rrecv.at[i], n.pair())

    def inside(at, carry):
        L = logs[at]
        X, B, C = activations(pre[at])
        U = (heads_of(delta[at], eh) * X).astype(BF16)
        psi = bdot(C, B, NT)
        keep = same_mask(flags[at], segrow[at])
        LT = L.T
        for j in range(4):
            u = pair_halves(U[:, 128 * j : 128 * j + 128])
            v = jnp.zeros((Q, 128), F32)
            for e in range(2):
                h = 2 * j + e
                K = jnp.where(keep, jnp.exp(L[:, h : h + 1] - LT[h : h + 1]), 0.0)
                v = v + bdot((psi * K).astype(BF16), u[e])
            inner[at, :, 128 * j : 128 * j + 128] = v
        return carry

    lax.fori_loop(0, 4, inside, 0)
    r0 = states_on(0)
    for d in ALLX:
        for half in (0, 1):
            oy[d, half].wait_recv()
    swap = keyed("swap", w_o.at[pl.ds(4 * (1 - core), 4)], wo_s.at[:, core], n.at(dc=1))
    for k in range(4):
        wo_s[k, core] = w_o[4 * core + k]
    for a in (1, 3, 2):
        cz[a].wait_recv()
        theirs = cot_s.at[2 * lax.rem(z + 4 - a, 4) + core]
        cn.append(keyed(("cf", a), theirs, theirs, n.at(dc=1)))
    lax.fori_loop(4, 8, inside, 0)
    r1 = states_on(1)
    swap.wait_recv()
    for cp in cn:
        cp.wait_recv()
    store(cot_s, cot_h)
    store(wo_s, wout_h)
    for i in range(MICRO):
        d = bdot(cot_s[:, i].reshape(TOK, 2048), wo_s[...].reshape(512, 2048), NT)
        for c in range(CH):
            dno[CH * i + c] = d[Q * c : Q * c + Q]
    store(dno, dno_h)

    def mix(i, c):
        at = CH * i + c
        E, _ = decays(logs[at], flags[at])
        X, _, C = activations(pre[at])
        more = heads_of(jnp.concatenate([E, jnp.broadcast_to(hp[2:3], (8, 128))], 0), eh)
        Ex, skip = more[:Q], more[Q : Q + 1]
        S = state[...]
        states[at, 0] = S
        Yc = Ex * bdot(C, S.astype(BF16))
        carried[at] = Yc
        mx = inner[at] + Yc + skip * X
        inner[at] = mx
        after = Ex[Q - 1 : Q] * S + sloc[at]
        state[...] = after
        states[at, 1] = after
        gt = proj[i, pl.ds(pl.multiple_of(16 + Q * c, 16), Q), 0:512]
        gated = mx * (gt * sigmoid(gt))
        ones = jnp.ones((8, 512), BF16)
        sums[m, at, 0:8] = right_parts(ones, gated * gated, 2, NT)
        sums[m, at, 8:16] = right_parts(ones, dno[at] * og[0:1] * gated, 2, NT)

    sm = []
    for i, r in ((0, r0), (1, r1)):
        r.wait_recv()
        state[...] = entering(n, ends, endlog, 0, 0, i) + rrecv[i].astype(F32)
        lax.fori_loop(0, CH, lambda c, carry, i=i: (mix(i, c), carry)[1], 0)
        mine = sums.at[m, pl.ds(CH * i, CH)]
        for a, b in OTHERS:
            sm.append(keyed(("sm", i, a, b), mine, mine, n.at(dz=a, dc=b)))
        some = pl.ds(CH * i, CH)
        store(inner.at[some], mixed_h.at[some])
        store(carried.at[some], carried_h.at[some])
        store(states.at[some], states_h.at[some])
    for cp in sm:
        cp.wait_recv()
    for cp in copies:
        cp.wait_send()
    for cp in stores:
        cp.wait()


def wave(hid, inw, seg, gain, og, cw, cb, dtb, alog, skip, cot, outw):
    V = lambda *s: pltpu.VMEM(s, BF16)
    R = lambda *s: pltpu.VMEM(s, F32)
    outs = [
        sds((2048, T), BF16), sds((8, 2, 64, 2048), BF16), sds((8, 8, 32, 1408), BF16), sds((2, TOK, 512), F32), sds((8, Q, 768), F32), sds((8, Q + 8, 768), BF16), sds((8, Q, 128), F32), sds((8, Q, 128), F32),
        sds((8, Q, 128), F32), sds((8, Q, 128), F32), sds((8, Q, 512), F32), sds((8, Q, 512), F32), sds((8, 2, 128, 512), F32), sds((8, Q, 512), F32), sds((8, 2, 64, 2048), BF16), sds((4, 2, 64, 2048), BF16),
        sds((8, 8, 16, 128), F32), sds((8, 2, 16, 512), BF16), sds((8, 768), F32), sds((8, 128), F32), sds((8, 512), F32), sds((8, 2048), F32), sds((8, 1, 128), F32),
    ]
    scratch = [
        V(8, 2, 64, 2048), V(2, 16, 2048), V(2, TOK + 16, 2048), V(2048, T), V(8, 8, 32, 1408), R(8, 8, 24, 128), R(2, TOK + 16, 1408), R(8, Q, 768), V(8, Q + 8, 768), R(8, Q, 128), R(8, Q, 128), R(8, Q, 128), R(8, Q, 128),
        R(8, 128, 512), R(8, Q, 512), R(8, Q, 512), R(8, 2, 128, 512), R(8, Q, 512), V(8, 2, 128, 512), V(2, 128, 512), V(2, 128, 512), V(8, 2, 64, 2048), V(8, 64, 2048), V(4, 2, 64, 2048),
        R(34, 8, 128), R(128, 512), R(1, 128), R(Q + 8, 768), V(8, 32, 1408), R(24, 128), R(8, 256),
    ]
    return pl.pallas_call(
        wave_kernel,
        name="wave",
        out_shape=outs,
        in_specs=[VM] * 7 + [SMEM] * 3 + [VM] * 2,
        out_specs=[ANY] * 16 + [VM] * 7,
        scratch_shapes=[*scratch, pltpu.SemaphoreType.DMA((144,)), pltpu.SemaphoreType.DMA((144,)), pltpu.SemaphoreType.DMA((24,))],
        compiler_params=pltpu.CompilerParams(collective_id=1, has_side_effects=True, vmem_limit_bytes=64 * 1024 * 1024 - 65536),
        cost_estimate=pl.CostEstimate(flops=8 << 30, bytes_accessed=32 << 20, transcendentals=0),
    )(hid, inw, seg, gain, og, cw, cb, dtb, alog, skip, cot, outw)


def entering(n, everyone, logs, target, direction, micro):
    to = 2 * n.x + (1 - n.y if target else n.y)
    lt, last = [], []
    for q in range(8):
        v = logs[q, micro].astype(F32)
        lt.append(v[0:1] + v[1:2] + v[2:3])
        last.append(64.0 * v[3:4] + v[4:5])
    zero = jnp.zeros((1, 512), F32)
    edge = zero
    for r in range(8):
        edge = edge + jnp.where((r == to) if direction else (r == to - 1), last[r], zero)
    total = jnp.zeros((128, 512), F32)
    for k in range(4):
        q = 2 * k + n.y
        log = zero
        for r in range(8):
            between = (r > to) & (r < q) if direction else (r > q) & (r < to)
            log = log + jnp.where(between, lt[r], zero)
        if direction:
            there = jnp.where(n.y == 0, last[max(2 * k - 1, 0)], last[2 * k])
        else:
            there = jnp.where(n.y == 0, last[2 * k], last[2 * k + 1])
        reached = jnp.where((q > to) if direction else (q < to), 1.0, 0.0)
        total = total + jnp.where(there == edge, jnp.exp(log) * reached, zero) * everyone[q, micro].astype(F32)
    return total


def same_mask(flags, segrow):
    return (flags[:, 5:6] == segrow) & (iota((Q, Q), 0) >= iota((Q, Q), 1))


def activations(pre):
    a = pre * sigmoid(pre)
    return a[:, :512], a[:, 512:640].astype(BF16), a[:, 640:768].astype(BF16)


def pair_halves(v):
    low_half = iota(v.shape, 1) < 64
    zero = jnp.zeros_like(v)
    return jnp.where(low_half, v, zero), jnp.where(low_half, zero, v)


T = MICRO * TOK


def column(row):
    return jnp.concatenate([jnp.broadcast_to(row, (128, 128)).T] * 4, 1)


def pick_matrix(rows, start, count, shift, dtype=BF16):
    r, l = iota((rows, 128), 0), iota((rows, 128), 1)
    return ((r - start == l - shift) & (l >= shift) & (l < shift + count)).astype(dtype)


class Reduce:
    def __init__(self, n, key, a, b, a1, a2, pa, b1, b2, pb, b3):
        self.n, self.key, self.a, self.b = n, key, a, b
        self.a1, self.a2, self.pa, self.b1, self.b2, self.pb, self.b3 = a1, a2, pa, b1, b2, pb, b3
        self.half = pb.shape[1]

    def group(self, d, f):
        n = self.n
        return 2 * lax.rem(n.x + d, 4) + lax.rem(n.y + f, 2)

    def rows(self, e):
        rep = lax.rem(self.n.ring + e, 4) // 2
        return pl.ds(pl.multiple_of(self.half * rep, self.half), self.half)

    def first_a(self, d):
        return self.n.copy((self.key, "a1", d), self.a.at[pl.ds(2 * lax.rem(self.n.x + d, 4), 2)], self.a1.at[d - 1], self.n.at(dx=d))

    def first_b(self, e):
        return self.n.copy((self.key, "b1", e), self.b.at[lax.rem(self.n.y + e, 2), :, self.rows(e)], self.b1.at[e - 1], self.n.at(dy=e))

    def put(self, d, f, v, width):
        n = self.n
        self.b[lax.rem(n.y + f, 2), lax.rem(n.x + d, 4)] = v[:, 0:width]
        self.a[self.group(d, f)] = v[:, width:]

    def second_a(self, e):
        return self.n.copy((self.key, "a2", e), self.pa.at[e % 2], self.a2.at[e - 1], self.n.at(dy=e))

    def second_b(self, d):
        return self.n.copy((self.key, "b2", d), self.pb.at[lax.rem(self.n.x + d, 4)], self.b2.at[d - 1], self.n.at(dx=d))

    def third_b(self):
        return self.n.copy((self.key, "b3"), self.b3.at[self.n.rep], self.b3.at[self.n.rep], self.n.at(dy=2))

    def middle_a(self):
        for d in XS:
            self.first_a(d).wait_recv()
        for f in (0, 1):
            k = lax.rem(self.n.y + f, 2)
            self.pa[f] = add4(self.a[self.group(0, f)], [self.a1[d, k] for d in range(3)]).astype(BF16)

    def go_a(self, f):
        for e in (1, 3) if f else (2,):
            self.second_a(e).start()

    def go_b(self):
        for d in (2, 1, 3):
            self.second_b(d).start()

    def middle_b(self):
        for e in XS:
            self.first_b(e).wait_recv()
        for k in range(4):
            self.pb[k] = add4(self.b[self.n.y, k, self.rows(0)], self.b1[:, k]).astype(BF16)

    def last_b(self):
        for d in XS:
            self.second_b(d).wait_recv()
        self.b3[self.n.rep] = add4(self.pb[self.n.x], self.b2).astype(self.b3.dtype)
        self.third_b().start()

    def last_a(self):
        for e in XS:
            self.second_a(e).wait_recv()
        return add4(self.pa[0], self.a2)

    def finish_first(self):
        for d in XS:
            self.first_a(d).wait_send()
            self.first_b(d).wait_send()

    def finish(self):
        for d in XS:
            self.second_b(d).wait_send()
            self.second_a(d).wait_send()
        self.third_b().wait_send()


def fetcher(sems):
    loads = {}

    def fetch(key, src, dst):
        loads[key] = pltpu.make_async_copy(src, dst, sems.at[len(loads)])
        loads[key].start()

    return loads, fetch


C1 = 256


def back_wave_kernel(
    mixed_h, carried_h, states_h, gate_h, dno_h, sums, pre_h, delta_h, logs_h, flags_h, segrow, og, hp, wout_h, normed, endlog,
    dgate, dpre_h, bc_all, ddt, small_o, small_b, total, wpa, wpb, turned, edges,
    mixed, carried, states, gate, dno, pre, delta, logs, flags, wout, nout, dmix, tloc, dbi, starts, rsend, rrecv, rows, part, near, far,
    wa, wb, wa1, wb1, dbc, state, send, recv, load, tile_sem,
):
    eh = spread_matrix()
    n = Net(send, recv)
    g, m, core, z = n.g, n.m, n.c, n.z
    W = Reduce(n, "w", wa, wb, wa1, None, wpa, wb1, None, wpb, None)
    loads, fetch = fetcher(load)
    peers = n.greet([n.at(dz=a, dc=b) for a, b in OTHERS] + [n.at(dx=d) for d in XS] + [n.at(dy=d) for d in XS] + [n.group(1), n.group(7)])
    for i in range(MICRO):
        some = pl.ds(CH * i, CH)
        for key, src, dst in (("mixed", mixed_h, mixed), ("gate", gate_h, gate), ("dno", dno_h, dno), ("pre", pre_h, pre), ("logs", logs_h, logs), ("flags", flags_h, flags)):
            fetch((key, i), src.at[some], dst.at[some])
    fetch("wout", wout_h, wout)
    for key, src, dst in (("delta", delta_h, delta), ("states", states_h, states), ("carried", carried_h, carried)):
        fetch(key, src, dst)

    def start_x(i, d):
        return n.copy(("sx", i, d), starts.at[g, i], starts.at[g, i], n.at(dx=d))

    def part_y(i):
        return n.copy(("r", i), rsend.at[i], rrecv.at[i], n.pair())

    def near_copy(i):
        return n.copy(("near", i), part.at[:, 1 - core, i], near.at[:, i], n.at(dc=1))

    def far_copy(d, i):
        return n.copy(("far", d, i), near.at[lax.rem(z + d, 4), i], far.at[d - 1, i], n.at(dz=d))

    def bc_copy(i, a, b):
        some = pl.ds(TOK * i, TOK)
        return n.copy(("bc", i, a, b), dbc.at[n.member(a, b), :, some], bc_all.at[m, :, some], n.at(dz=a, dc=b))

    def edge_copy(i):
        return n.copy(("edge", i), gate.at[CH * i, pl.ds(0, 8)], edges.at[i], n.group(7))

    small_o[...] = jnp.zeros_like(small_o)
    small_b[...] = jnp.zeros_like(small_b)

    def outward(i, k):
        c = CH - 1 - k
        at = CH * i + c
        tot = sums[0, at]
        for q in range(1, 8):
            tot = tot + sums[q, at]
        r = column(lax.rsqrt(tot[0:1] / INNER + EPS))
        s2 = column(tot[8:9] / INNER)
        gt = gate[at]
        s = sigmoid(gt)
        sg = gt * s
        mix = mixed[at]
        gated = mix * sg
        dn = dno[at]
        n0 = gated * r
        rows = pl.ds(pl.multiple_of(Q * c, Q), Q)
        nb = n0 * og[0:1]
        nout[i, rows] = nb.astype(BF16)
        turned[:, pl.ds(pl.multiple_of(Q * at, Q), Q)] = nb.T.astype(BF16)
        d_gated = r * (dn * og[0:1] - n0 * r * s2)
        dm = d_gated * sg
        dmix[at] = dm
        dgate[i, rows] = (d_gated * mix * (s * (1.0 + gt * (1.0 - s)))).astype(BF16)
        x = pre[at, :, :512]
        X = x * sigmoid(x)
        cc = pre[at, :, 640:768]
        C = (cc * sigmoid(cc)).astype(BF16)
        small_o[0:1] += jnp.sum(dn * n0, 0, keepdims=True)
        small_o[1:2] += jnp.sum(X * dm, 0, keepdims=True)
        E, _ = decays(logs[at], flags[at])
        Ex = heads_of(E, eh)
        G = right_parts(C, Ex * dm, 2, TN)
        tloc[at] = G
        state[...] = Ex[Q - 1 : Q] * state[...] + G

    for i in range(MICRO):
        for key in ("mixed", "gate", "dno", "pre", "logs", "flags"):
            loads[key, i].wait()
        state[...] = jnp.zeros_like(state)
        lax.fori_loop(0, CH, lambda k, carry, i=i: (outward(i, k), carry)[1], 0)
        starts[g, i] = state[...].astype(BF16)
        if i == 0:
            n.meet(peers)
        for d in XS:
            start_x(i, d).start()
        if i == 0:
            loads["wout"].wait()
        part[:, :, i] = bdot(nout[i], wout[...]).astype(BF16).reshape(4, 2, 64, 2048)
        near_copy(i).start()

    def bring(k):
        at = pl.ds(pl.multiple_of(256 * W.group(*ORDER[k]), 256), 256)
        return pltpu.make_async_copy(normed.at[at], rows.at[k % 2], tile_sem.at[k % 2])

    def states_on(i):
        for d in XS:
            start_x(i, d).wait_recv()
        rsend[i] = entering(n, starts, endlog, 1, 1, i).astype(BF16)
        part_y(i).start()

    def tokens_on(i):
        near_copy(i).wait_recv()
        for d in (1, 3, 2, 0):
            there = lax.rem(z + d, 4)
            near[there, i] = (part[there, core, i].astype(F32) + near[there, i].astype(F32)).astype(BF16)
            if d:
                far_copy(d, i).start()

    bring(0).start()
    for k, (d, f) in enumerate(ORDER):
        bring(k).wait()
        if k < 7:
            bring(k + 1).start()
        W.put(d, f, bdot(rows[k % 2], dgate[...].reshape(T, 512)).astype(BF16), C1)
        if f == 0 and d:
            W.first_a(d).start()
        if k == 1:
            states_on(0)
            tokens_on(0)
        if k == 5:
            states_on(1)
            tokens_on(1)
    for e in (2, 1, 3):
        W.first_b(e).start()

    loads["delta"].wait()
    loads["states"].wait()
    loads["carried"].wait()

    def inside(at, carry):
        L = logs[at]
        f = flags[at]
        E, _ = decays(L, f)
        X, B, C = activations(pre[at])
        more = heads_of(jnp.concatenate([E, delta[at]], 0), eh)
        Ex, dx = more[:Q], more[Q:]
        Ub = (dx * X).astype(BF16)
        dm = dmix[at]
        dmb = dm.astype(BF16)
        psi = bdot(C, B, NT)
        keep = same_mask(f, segrow[at])
        LT = L.T
        dpsi = jnp.zeros((Q, Q), F32)
        for j in range(4):
            js = slice(128 * j, 128 * j + 128)
            u = pair_halves(Ub[:, js])
            y = pair_halves(dmb[:, js])
            acc = jnp.zeros((Q, 128), F32)
            for e in range(2):
                h = 2 * j + e
                K = jnp.where(keep, jnp.exp(L[:, h : h + 1] - LT[h : h + 1]), 0.0)
                acc = acc + bdot((psi * K).astype(BF16), y[e], TN)
                dpsi = dpsi + bdot(y[e], u[e], NT) * K
            dno[at, :, js] = acc
        dpb = dpsi.astype(BF16)
        dbi[at, 0:128] = bdot(C, dpb, TN)
        dbi[at, 128:256] = bdot(B, dpb, TT) + bdot(states[at, 0].astype(BF16), (Ex * dm).astype(BF16), NT)
        return carry

    lax.fori_loop(0, 8, inside, 0)
    for i in (0, 1):
        part_y(i).wait_recv()

    def inward(i, k):
        c = CH - 1 - k
        at = CH * i + c
        L = logs[at]
        d = delta[at]
        E, W_ = decays(L, flags[at])
        p = pre[at, :, 0:512]
        s = sigmoid(p)
        X = p * s
        bb = pre[at, :, 512:640]
        B = (bb * sigmoid(bb)).astype(BF16)
        more = heads_of(jnp.concatenate([E[Q - 8 :], W_, d, jnp.broadcast_to(hp[2:3], (8, 128))], 0), eh)
        Elast, Wx, dx, skip = more[7:8], more[8 : 8 + Q], more[8 + Q : 8 + 2 * Q], more[8 + 2 * Q : 9 + 2 * Q]
        U = dx * X
        dm = dmix[at]
        Yc = carried[at]
        Yi = mixed[at] - Yc - skip * X
        G = state[...]
        Gb = G.astype(BF16)
        dUi = dno[at]
        dUc = Wx * bdot(B, Gb)
        dU = dUi + dUc
        lanes = pl.ds(pl.multiple_of(Q * at, Q), Q)
        dbc[0:4, :, lanes] = (dbi[at, 0:128] + bdot(Gb, (Wx * U).astype(BF16), NT)).astype(BF16).reshape(4, 32, Q)
        dbc[4:8, :, lanes] = dbi[at, 128:256].astype(BF16).reshape(4, 32, Q)
        dL = sums_of(dm.astype(BF16).astype(F32) * Yi + dm * Yc - U.astype(BF16).astype(F32) * dUi - U * dUc, eh)
        end = sums_of(jnp.broadcast_to(jnp.sum(G * states[at, 1], 0, keepdims=True), (8, 512)), eh)[0:1]
        upper = (iota((Q, Q), 0) <= iota((Q, Q), 1)).astype(BF16)
        dstep = right_parts(upper, dL, 3) + end
        rate = hp[1:2]
        dr = (sums_of(dU * X, eh) + dstep * rate) * (1.0 - jnp.exp(-d))
        ddt[at] = dr.astype(BF16)
        small_b[0:1] += jnp.sum(dr, 0, keepdims=True)
        small_b[1:2] += jnp.sum(dstep * d * rate, 0, keepdims=True)
        gate[at] = (dx * dU + skip * dm) * (s * (1.0 + p * (1.0 - s)))
        state[...] = Elast * G + tloc[at]

    store = pltpu.make_async_copy(gate, dpre_h, load.at[0])
    for i in range(MICRO):
        state[...] = entering(n, starts, endlog, 0, 1, i) + rrecv[i].astype(F32)
        lax.fori_loop(0, CH, lambda k, carry, i=i: (inward(i, k), carry)[1], 0)
        edge_copy(i).start()
        for a, b in OTHERS:
            bc_copy(i, a, b).start()
    store.start()
    bc_all[m] = dbc[m]

    W.middle_b()
    W.middle_a()
    for i in range(MICRO):
        for d in XS:
            far_copy(d, i).wait_recv()
        total[i] = near[z, i].astype(F32) + far[0, i].astype(F32) + far[1, i].astype(F32) + far[2, i].astype(F32)
    for i in range(MICRO):
        edge_copy(i).wait_recv()
        for a, b in OTHERS:
            bc_copy(i, a, b).wait_recv()
    W.finish_first()
    for i in range(MICRO):
        edge_copy(i).wait_send()
        for a, b in OTHERS:
            bc_copy(i, a, b).wait_send()
    store.wait()
    for i in range(MICRO):
        part_y(i).wait_send()
        for d in XS:
            start_x(i, d).wait_send()
            far_copy(d, i).wait_send()
        near_copy(i).wait_send()


def back_wave(mixed, carried, states, gate, dno, sums, pre, delta, logs, flags, segrow, og, hp, wout, normed, endlog):
    outs = [
        sds((2, TOK, 512), BF16), sds((8, Q, 512), F32), sds((8, 32, T), BF16), sds((8, Q, 128), BF16), sds((8, 512), F32), sds((8, 128), F32), sds((2, 64, 2048), F32),
        sds((2, 256, C1), BF16), sds((4, 128, C1), BF16), sds((512, T), BF16), sds((2, 8, 512), F32),
    ]
    V = lambda *s: pltpu.VMEM(s, BF16)
    R = lambda *s: pltpu.VMEM(s, F32)
    return pl.pallas_call(
        back_wave_kernel,
        name="back_wave",
        out_shape=outs,
        in_specs=[ANY] * 5 + [VM] + [ANY] * 4 + [VM] * 3 + [ANY] * 2 + [VM],
        out_specs=[VM, ANY] + [VM] * 9,
        scratch_shapes=[
            R(8, Q, 512), R(8, Q, 512), R(8, 2, 128, 512), R(8, Q, 512), R(8, Q, 512), R(8, Q, 768), R(8, Q, 128), R(8, Q, 128), R(8, Q, 128), V(512, 2048),
            V(2, TOK, 512), R(8, Q, 512), R(8, 128, 512), R(8, 256, 128), V(8, 2, 128, 512), V(2, 128, 512), V(2, 128, 512), V(2, 256, T), V(4, 2, 2, 64, 2048),
            V(4, 2, 64, 2048), V(3, 2, 64, 2048),
            V(8, 256, C1), V(2, 4, 256, C1), V(3, 2, 256, C1), V(3, 4, 128, C1), V(8, 32, T), R(128, 512),
            pltpu.SemaphoreType.DMA((96,)), pltpu.SemaphoreType.DMA((96,)), pltpu.SemaphoreType.DMA((16,)), pltpu.SemaphoreType.DMA((2,)),
        ],
        compiler_params=pltpu.CompilerParams(collective_id=4, has_side_effects=True, vmem_limit_bytes=62 << 20),
        cost_estimate=pl.CostEstimate(flops=8 << 30, bytes_accessed=32 << 20, transcendentals=0),
    )(mixed, carried, states, gate.reshape(8, Q, 512), dno, sums, pre, delta, logs, flags, segrow, og, hp, wout, normed, endlog)


CB = 256
CA = 640 - CB


def tail_kernel(
    bc_s, ex_s, wpa, wpb, turned, branch, gain, cot, dpre, pre, ext, flags, fnext, conv, ddt, dgate, w, hid, normed, small_o, small_b,
    g_in, g_out, layer_out, grad_in, small_out,
    eb_src, eb_s, dps, pre_s, ext_s, fl_s, fn_s, ddt_s, dg_s, w_s, hid_s, nm_s, wt, e_s, dproj, part, near, far, conv_acc, gnorm,
    s0, s1, s2, sx, ga, gb, ga1, ga2, gpa, gb1, gb2, gpb, gb3, cot_s, gsw, oa, ob, oa1, oa2, opa, ob1, ob2, opb, ob3, oin, cot_own, ga2_, gb2_, gb3_, gi, small_all, convt, final, send, recv, load, tile_sem,
):
    n = Net(send, recv)
    x, y, z, c, m = n.x, n.y, n.z, n.c, n.m
    loads = {}

    def fetch(key, src, dst):
        loads[key] = pltpu.make_async_copy(src, dst, load.at[len(loads)])
        loads[key].start()

    peers = n.greet([n.at(dz=a, dc=b) for a, b in OTHERS] + [n.at(dx=d) for d in XS] + [n.at(dy=d) for d in XS] + [n.group(1), n.group(7)])
    fetch("pre", pre.at[:, :, pl.ds(512, 256)], pre_s)
    fetch("w", w, w_s)
    fetch("dpre", dpre, dps.at[:, pl.ds(0, TOK), pl.ds(0, 512)])
    fetch("ext", ext, ext_s)
    fetch("flags", flags, fl_s)
    fetch("fnext", fnext, fn_s)
    fetch("ddt", ddt, ddt_s)
    fetch("normed", normed, nm_s)
    fetch("dgate", dgate, dg_s)
    fetch("hid", hid, hid_s)
    fetch("cot", cot.at[m], cot_own)
    n.meet(peers)
    G_ = Reduce(n, "g", None, None, None, ga2_, wpa, None, gb2_, wpb, gb3_)
    G_.go_a(1)
    G_.go_a(0)
    G_.go_b()

    edge2 = n.copy("edge2", eb_src, eb_s, n.group(7))

    def near_copy(i):
        return n.copy(("near", i), part.at[:, 1 - c, i], near.at[:, i], n.at(dc=1))

    def far_copy(d, i):
        return n.copy(("far", d, i), near.at[lax.rem(z + d, 4), i], far.at[d - 1, i], n.at(dz=d))

    def small_x(d):
        return n.copy(("sx", d), s0, s1.at[d - 1], n.at(dx=d))

    def small_y(d):
        return n.copy(("sy", d), sx, s2.at[d - 1], n.at(dy=d))

    def small_m(a, b):
        return n.copy(("sm", a, b), small_all.at[m], small_all.at[m], n.at(dz=a, dc=b))

    def rows_copy(a, b):
        return n.copy(("rows", a, b), final.at[n.member(a, b)], gi.at[m], n.at(dz=a, dc=b))

    O = Reduce(n, "o", oa, ob, oa1, oa2, opa, ob1, ob2, opb, ob3)
    swap = n.copy("swap", gsw.at[:, 1 - c], oin, n.at(dc=1))
    W = Reduce(n, "w", ga, gb, ga1, ga2, gpa, gb1, gb2, gpb, gb3)

    pick = pick_matrix(256, 32 * m, 32, 0)
    loads["w"].wait()
    wt[...] = (bdot(w_s[:, 1024:1280], pick) + bdot(w_s[:, 1280:1408], pick_matrix(128, 0, 8, 32))).astype(BF16)
    cw = jnp.concatenate([conv[:, 0:512], left_parts(conv[:, 512:768], pick, 3)], 1)
    for key in ("pre", "dpre"):
        loads[key].wait()
    eye = pick_matrix(32, 0, 32, 0)

    def bc_chunk(i, k):
        t = CH * i + k
        tot = bc_s[0, :, Q * t : Q * t + Q].astype(F32)
        for q in range(1, 8):
            tot = tot + bc_s[q, :, Q * t : Q * t + Q].astype(F32)
        d = left_parts(tot, eye, 2, TN)
        p = left_parts(pre_s[t], pick, 2)
        s = sigmoid(p)
        dps[i, Q * k : Q * k + Q, 512:640] = d * (s * (1.0 + p * (1.0 - s)))

    for i in range(MICRO):
        bc_chunk(i, 0)
        eb_src[i] = dps[i, 0:8, 512:640]
    edge2.start()
    for i in range(MICRO):
        for k in range(1, CH):
            bc_chunk(i, k)
    def bring(k):
        return pltpu.make_async_copy(cot.at[:, :, :, pl.ds(256 * k, 256)], cot_s.at[k % 2], tile_sem.at[k % 2])

    bring(0).start()
    for k in range(8):
        bring(k).wait()
        if k < 7:
            bring(k + 1).start()
        v = sum(bdot(turned[:, TOK * i : TOK * i + TOK], cot_s[k % 2, :, i].reshape(TOK, 256)) for i in range(MICRO))
        gsw[:, :, :, 256 * k : 256 * k + 256] = v.astype(BF16).reshape(4, 2, 64, 256)
    swap.start()
    for j in range(4):
        oa[4 * c + j] = gsw[j, c, :, 0:1024]
        ob[j % 2, 2 * c + j // 2] = gsw[j, c, :, 1024:2048]

    for key in ("ext", "flags", "fnext", "ddt"):
        loads[key].wait()
    conv_acc[...] = jnp.zeros_like(conv_acc)
    pick_dt = pick_matrix(128, 0, 8, 32)

    def conv_chunk(i, k):
        t = CH * i + k
        e_s[:, 0:512] = ext_s[t, :, 0:512].astype(F32)
        e_s[:, 512:640] = bdot(ext_s[t, :, 512:768], pick)
        f, fn = fl_s[t], fn_s[t]
        dp = dps[i, Q * k : Q * k + Q]
        dx = cw[3:4] * dp
        conv_acc[3:4] += jnp.sum(dp * e_s[8 : 8 + Q], 0, keepdims=True)
        conv_acc[4:5] += jnp.sum(dp, 0, keepdims=True)
        for j in range(3):
            conv_acc[j : j + 1] += jnp.sum(dp * e_s[5 + j : 5 + j + Q] * f[:, j : j + 1], 0, keepdims=True)
            dx = dx + cw[j : j + 1] * dps[i, Q * k + 3 - j : Q * k + 3 - j + Q] * fn[:, j : j + 1]
        rows = slice(Q * k, Q * k + Q)
        dproj[i, rows, 0:512] = dx[:, 0:512].astype(BF16)
        dproj[i, rows, 512:640] = (dx[:, 512:640] + bdot(ddt_s[t], pick_dt)).astype(BF16)

    for i in range(MICRO):
        for k in range(CH - 1):
            conv_chunk(i, k)
    swap.wait_recv()
    for j in range(4):
        oa[4 * (1 - c) + j] = oin[j, :, 0:1024]
        ob[j % 2, 2 * (1 - c) + j // 2] = oin[j, :, 1024:2048]
    for d in (2, 1, 3):
        O.first_a(d).start()
        O.first_b(d).start()

    edge2.wait_recv()
    for i in range(MICRO):
        dps[i, TOK : TOK + 8, 0:512] = ex_s[i]
        dps[i, TOK : TOK + 8, 512:640] = eb_s[i]
        conv_chunk(i, CH - 1)

    loads["hid"].wait()
    loads["dgate"].wait()
    for i in range(MICRO):
        h = hid_s[:, i].reshape(TOK, 2048).astype(F32)
        scale = row_scale(h)
        first, main, rest = dg_s[i], dproj[i, :, 0:512], dproj[i, :, 512:640]

        def tile_of(j, carry, i=i, scale=scale, first=first, main=main, rest=rest):
            at = pl.ds(pl.multiple_of(256 * j, 256), 256)
            d = bdot(first, w_s[at, 0:512], NT) + bdot(main, w_s[at, 512:1024], NT) + bdot(rest, wt[at], NT)
            part[:, :, i, :, at] = d.astype(BF16).reshape(4, 2, 64, 256)
            hv = hid_s[:, i, :, at].reshape(TOK, 256).astype(F32)
            s = jnp.sum(d * (hv * scale), 0, keepdims=True)
            gnorm[0:1, at] = s if i == 0 else gnorm[0:1, at] + s
            return carry

        lax.fori_loop(0, 8, tile_of, 0)
        near_copy(i).start()
    for r in range(16):
        s0[r : r + 1] = gnorm[0:1, 128 * r : 128 * r + 128]
    for k in range(5):
        for r in range(5):
            s0[16 + 5 * k + r : 17 + 5 * k + r] = conv_acc[k : k + 1, 128 * r : 128 * r + 128]
    for r in range(4):
        s0[41 + r : 42 + r] = small_o[0:1, 128 * r : 128 * r + 128]
    s0[45:47] = small_b[0:2]
    s0[47:48] = sums_of(small_o[...], spread_matrix())[1:2]
    for d in XS:
        small_x(d).start()

    def tokens_on(i):
        near_copy(i).wait_recv()
        for d in (1, 3, 2, 0):
            there = lax.rem(z + d, 4)
            near[there, i] = (part[there, c, i].astype(F32) + near[there, i].astype(F32)).astype(BF16)
            if d:
                far_copy(d, i).start()

    loads["normed"].wait()
    for k, (d, f) in enumerate(ORDER):
        q = W.group(d, f)
        at = pl.ds(pl.multiple_of(256 * q, 256), 256)
        v = bdot(nm_s[at], dproj[...].reshape(T, 640)).astype(BF16)
        W.put(d, f, v, CB)
        if f == 0 and d:
            W.first_a(d).start()
        if k == 2:
            tokens_on(0)
        if k == 6:
            tokens_on(1)
    for e in (2, 1, 3):
        W.first_b(e).start()

    G_.last_b()
    final[:, :, C1:512] = G_.last_a().astype(BF16).reshape(8, 32, C1)
    for i in range(MICRO):
        layer_out[i] = (hid_s[m, i].astype(F32) + branch[i]).astype(BF16)
    O.middle_b()
    O.go_b()
    O.middle_a()
    O.go_a(1)
    O.go_a(0)

    for d in XS:
        small_x(d).wait_recv()
    sx[...] = s0[...] + s1[0] + s1[1] + s1[2]
    for d in XS:
        small_y(d).start()
    W.middle_b()
    W.go_b()
    W.middle_a()
    W.go_a(1)
    W.go_a(0)
    O.last_b()
    g_out[:, 0:1024] = O.last_a()
    W.last_b()
    for d in XS:
        small_y(d).wait_recv()
    small_all[m] = sx[...] + s2[0] + s2[1] + s2[2]
    for a, b in OTHERS:
        small_m(a, b).start()
    for i in range(MICRO):
        for d in XS:
            far_copy(d, i).wait_recv()
        dn = near[z, i].astype(F32) + far[0, i].astype(F32) + far[1, i].astype(F32) + far[2, i].astype(F32)
        if i == 0:
            loads["cot"].wait()
        h = hid_s[m, i].astype(F32)
        r = row_scale(h)
        dg = dn * gain[0:1]
        grad_in[i] = (cot_own[i].astype(F32) + r * dg - h * (r * r * r) * jnp.mean(dg * h, axis=-1, keepdims=True)).astype(BF16)
    O.third_b().wait_recv()
    for h in range(2):
        g_out[32 * h : 32 * h + 32, 1024:2048] = ob3[h]
    W.third_b().wait_recv()
    for h in range(2):
        final[4 * h : 4 * h + 4, :, 512 : 512 + CB] = gb3[h].reshape(4, 32, CB)
    final[:, :, 512 + CB :] = W.last_a().astype(BF16).reshape(8, 32, CA)
    G_.third_b().wait_recv()
    for h in range(2):
        final[4 * h : 4 * h + 4, :, 0:C1] = gb3_[h].reshape(4, 32, C1)
    for a, b in OTHERS:
        rows_copy(a, b).start()
    gi[m] = final[m]
    for a, b in OTHERS:
        rows_copy(a, b).wait_recv()
        small_m(a, b).wait_recv()

    rest_cols = jnp.zeros((32, 384), F32)
    r, l = iota((128, 384), 0), iota((128, 384), 1)
    for q in range(8):
        zq, cq = q // 2, q % 2
        for j in range(4):
            at = 512 * (4 * cq + j) + 128 * zq
            g_in[:, at : at + 128] = gi[q, :, 128 * j : 128 * j + 128].astype(F32)
            g_in[:, 4096 + at : 4224 + at] = gi[q, :, 512 + 128 * j : 640 + 128 * j].astype(F32)
        k = r - 32
        put = ((r < 32) & (l == 32 * q + r)) | ((r >= 32) & (r < 40) & (l == 256 + 32 * cq + 8 * (k // 2) + 2 * zq + k % 2))
        rest_cols = rest_cols + bdot(gi[q, :, 1024:1152], put.astype(BF16))
    g_in[:, 8192:8512] = rest_cols[:, 0:320]

    g = n.g
    shard = 8 * g + m
    lane, row = iota((8, 128), 1), iota((8, 128), 0)

    def pick_row(v, at):
        return jnp.broadcast_to(jnp.sum(jnp.where(iota(v.shape, 0) == at, v, 0.0), 0, keepdims=True), (8, 128))

    norm_sum = small_all[0, 0:16]
    for q in range(1, 8):
        norm_sum = norm_sum + small_all[q, 0:16]
    norm_row = pltpu.roll(pick_row(norm_sum, shard // 4), lax.rem(128 - 32 * lax.rem(shard, 4), 128), 1)
    mine = small_all[2 * (m // 2) + g // 4]
    out_row = pltpu.roll(pick_row(mine[40:48], 1 + lax.rem(g, 4)), 64 * lax.rem(m, 2), 1)
    here = lane == 2 * lax.rem(g, 4) + lax.rem(m, 2)
    heads_row = jnp.zeros((8, 128), F32)
    for k in range(3):
        v = jnp.sum(jnp.where(here, pick_row(mine[40:48], 5 + k), 0.0), 1, keepdims=True)
        heads_row = heads_row + jnp.where(lane == k, v, 0.0)
    convt[...] = jnp.zeros_like(convt)
    for t in range(32):
        q, j = 2 * (t % 4) + t // 16, t // 4 % 4
        for k in range(5):
            convt[t, k : k + 1] = small_all[q, 16 + 5 * k + j : 17 + 5 * k + j]
    for q in range(8):
        for k in range(5):
            v = jnp.where(lane < 32, jnp.broadcast_to(small_all[q, 20 + 5 * k : 21 + 5 * k], (8, 128)), 0.0)
            convt[32 + q // 4, k : k + 1] += (pltpu.roll(v, 32 * (q % 4), 1) if q % 4 else v)[0:1]
    tile = 68 * shard // 128
    both = jnp.concatenate([convt[tile], convt[tile + 1]], 1)
    own = pltpu.roll(both, lax.rem(256 - lax.rem(68 * shard, 128), 256), 1)[:, 0:128]
    small_out[...] = jnp.where(row == 5, norm_row, jnp.where(row == 6, out_row, jnp.where(row == 7, heads_row, own)))
    W.finish_first()
    O.finish_first()
    W.finish()
    O.finish()
    G_.finish()
    swap.wait_send()
    for a, b in OTHERS:
        rows_copy(a, b).wait_send()
        small_m(a, b).wait_send()
    for d in XS:
        small_x(d).wait_send()
        small_y(d).wait_send()
        for i in range(MICRO):
            far_copy(d, i).wait_send()
    for i in range(MICRO):
        near_copy(i).wait_send()
    edge2.wait_send()


def tail_call(bc_all, edges, wpa, wpb, turned, branch, gain, cot, dpre, pre, ext, flags, fnext, conv, ddt, dgate, w, hid, normed, small_o, small_b):
    outs = [sds((32, 8512), F32), sds((64, 2048), F32), sds((2, 64, 2048), BF16), sds((2, 64, 2048), BF16), sds((8, 128), F32)]
    V = lambda *s: pltpu.VMEM(s, BF16)
    R = lambda *s: pltpu.VMEM(s, F32)
    scratch = [
        R(2, 8, 128), R(2, 8, 128), R(2, TOK + 8, 640), R(8, Q, 256), V(8, Q + 8, 768), R(8, Q, 128), R(8, Q, 128), V(8, Q, 128), V(2, TOK, 512), V(2048, 1408),
        V(8, 2, 64, 2048), V(2048, T), V(2048, 128), R(Q + 8, 640), V(2, TOK, 640), V(4, 2, 2, 64, 2048), V(4, 2, 64, 2048), V(3, 2, 64, 2048), R(8, 640), R(8, 2048),
        R(48, 128), R(3, 48, 128), R(3, 48, 128), R(48, 128),
        V(8, 256, CA), V(2, 4, 256, CB), V(3, 2, 256, CA), V(3, 256, CA), V(2, 256, CA), V(3, 4, 128, CB), V(3, 128, CB), V(4, 128, CB), V(2, 128, CB),
        V(2, 8, 2, 64, 256), V(4, 2, 64, 2048), V(8, 64, 1024), V(2, 4, 64, 1024), V(3, 2, 64, 1024), V(3, 64, 1024), V(2, 64, 1024), V(3, 4, 32, 1024), V(3, 32, 1024), V(4, 32, 1024), R(2, 32, 1024), V(4, 64, 2048),
        V(2, 64, 2048), V(3, 256, C1), V(3, 128, C1), V(2, 128, C1), V(8, 32, 1152), R(8, 48, 128), R(35, 8, 128), V(8, 32, 1152),
    ]
    return pl.pallas_call(
        tail_kernel,
        name="tail",
        out_shape=outs,
        in_specs=[VM] * 7 + [ANY] * 6 + [VM] + [ANY] * 5 + [VM] * 2,
        out_specs=[VM] * 5,
        scratch_shapes=[*scratch, pltpu.SemaphoreType.DMA((112,)), pltpu.SemaphoreType.DMA((112,)), pltpu.SemaphoreType.DMA((12,)), pltpu.SemaphoreType.DMA((2,))],
        compiler_params=pltpu.CompilerParams(collective_id=5, has_side_effects=True, vmem_limit_bytes=62 << 20),
        cost_estimate=pl.CostEstimate(flops=8 << 30, bytes_accessed=32 << 20, transcendentals=0),
    )(bc_all, edges, wpa, wpb, turned, branch, gain, cot, dpre, pre, ext, flags, fnext, conv, ddt, dgate, w, hid, normed, small_o, small_b)


def per_device(layer_in, cotangent, segment_ids, norm_gain, in_weight, conv_weight, conv_bias, dt_bias, a_log, skip_gain, out_gain, out_weight):
    (
        normed, hid_all, w_in, gate, pre, ext, delta, logs, flags, fnext, mixed, carried, states, dno, cot, w_out,
        sums, ends_all, conv, hp, og, gain, segrow,
    ) = wave(
        layer_in[:, 0], in_weight, segment_ids[:, 0], norm_gain[None], out_gain[None], conv_weight, conv_bias[None], dt_bias, a_log, skip_gain, cotangent[:, 0], out_weight
    )
    w_in = w_in.reshape(2048, 1408)
    dgate, dpre, bc_all, ddt, small_o, small_b, own_branch, wpa, wpb, turned, edges = back_wave(
        mixed, carried, states, gate, dno, sums, pre, delta, logs, flags, segrow, og, hp, w_out.reshape(512, 2048), normed, ends_all
    )
    dpre = dpre.reshape(MICRO, TOK, 512)
    g_in, g_out, layer_out, grad_in, small = tail_call(
        bc_all, edges, wpa, wpb, turned, own_branch, gain, cot, dpre, pre, ext, flags, fnext, conv, ddt, dgate, w_in, hid_all, normed, small_o, small_b
    )
    return (
        layer_out[:, None], grad_in[:, None], small[5, :32], g_in, small[:4, :68], small[4, :68], small[7, 0:1], small[7, 1:2], small[7, 2:3], small[6, :64], g_out,
    )


def solution(mesh):
    fine = Mesh(mesh.devices.reshape(2, 4, 2, 4, 2), AXES)
    tok = P(None, "rep", SEQ, None)
    return jax.shard_map(
        per_device,
        mesh=fine,
        in_specs=(tok, tok, P(None, "rep", SEQ), P(SEQ), P(SEQ, None), P(None, SEQ), P(SEQ), P(SEQ), P(SEQ), P(SEQ), P(SEQ), P(SEQ, None)),
        out_specs=(tok, tok, P(SEQ), P(SEQ, None), P(None, SEQ), P(SEQ), P(SEQ), P(SEQ), P(SEQ), P(SEQ), P(SEQ, None)),
        check_vma=False,
    )
```

```python
import functools

import jax
import jax.numpy as jnp
from jax import lax
from jax.experimental import pallas as pl
from jax.experimental.pallas import tpu as pltpu
from jax.sharding import Mesh, PartitionSpec as P

EPS = 1e-05
INNER = 4096
MICRO = 2
CONV = 4352
F32 = jnp.float32
BF16 = jnp.bfloat16
AXES = ("rep", "x", "y", "z", "c")
SEQ = ("x", "y", "z", "c")
GROUPS = 8
TOK = 512
Q = 128
CH = TOK // Q

MESH = pl.DeviceIdType.MESH
ANY = pl.BlockSpec(memory_space=pl.ANY)
VM = pl.BlockSpec(memory_space=pltpu.VMEM)
SMEM = pl.BlockSpec(memory_space=pltpu.SMEM)


class Net:
    def __init__(self, send, recv):
        self.send, self.recv, self.used, self.open = send, recv, 0, []
        self.keys = {}
        self.rep, self.x, self.y, self.z, self.c = (lax.axis_index(a) for a in AXES)
        self.ring = 2 * self.rep + self.y
        self.g = 2 * self.x + self.y
        self.m = 2 * self.z + self.c

    def at(self, dx=0, dy=0, dz=0, dc=0):
        ring = lax.rem(self.ring + dy, 4)
        return (ring // 2, lax.rem(self.x + dx, 4), lax.rem(ring, 2), lax.rem(self.z + dz, 4), lax.rem(self.c + dc, 2))

    def pair(self):
        return (self.rep, self.x, 1 - self.y, self.z, self.c)

    def across(self, dx):
        return (self.rep, lax.rem(self.x + dx, 4), 1 - self.y, self.z, self.c)

    def group(self, d):
        g = lax.rem(self.g + d, 8)
        return (self.rep, g // 2, lax.rem(g, 2), self.z, self.c)

    def member(self, dz, dc):
        return 2 * lax.rem(self.z + dz, 4) + lax.rem(self.c + dc, 2)

    def push(self, src, dst, where):
        i = self.used
        self.used += 1
        copy = pltpu.make_async_remote_copy(
            src_ref=src, dst_ref=dst, send_sem=self.send.at[i], recv_sem=self.recv.at[i], device_id=where, device_id_type=MESH
        )
        copy.start()
        self.open.append(copy)
        return copy

    def copy(self, key, src, dst, where):
        i = self.keys.setdefault(key, len(self.keys))
        return pltpu.make_async_remote_copy(
            src_ref=src, dst_ref=dst, send_sem=self.send.at[i], recv_sem=self.recv.at[i], device_id=where, device_id_type=MESH
        )

    def behind(self, d):
        return 2 * lax.rem(self.x + 4 - d, 4) + self.y

    def local(self, src, dst):
        i = self.used
        self.used += 1
        copy = pltpu.make_async_copy(src, dst, self.recv.at[i])
        copy.start()
        return copy

    def greet(self, peers):
        for peer in peers:
            pl.semaphore_signal(pltpu.get_barrier_semaphore(), inc=1, device_id=peer, device_id_type=MESH)
        return len(peers)

    def meet(self, count):
        pl.semaphore_wait(pltpu.get_barrier_semaphore(), count)

    def finish(self):
        for copy in self.open:
            copy.wait_send()


OTHERS = [(dz, dc) for dz in (0, 1, 3, 2) for dc in (0, 1) if (dz, dc) != (0, 0)]
ZS = (0, 1, 3, 2)
XS = (1, 3, 2)
ORDER = [(d, f) for f in (1, 0) for d in (2, 1, 3, 0)]


def sds(shape, dtype):
    return jax.ShapeDtypeStruct(shape, dtype)


def add4(a, b):
    return a.astype(F32) + b[0].astype(F32) + b[1].astype(F32) + b[2].astype(F32)


NN = (((1,), (0,)), ((), ()))
NT = (((1,), (1,)), ((), ()))
TN = (((0,), (0,)), ((), ()))
TT = (((0,), (1,)), ((), ()))


def bdot(a, b, dims=NN):
    return lax.dot_general(a, b, dims, preferred_element_type=F32)


def parts(v, count):
    out = []
    for _ in range(count):
        p = v.astype(BF16)
        out.append(p)
        v = v - p.astype(F32)
    return out


def left_parts(v, w, count, dims=NN):
    return sum(bdot(p, w, dims) for p in parts(v, count))


def right_parts(w, v, count, dims=NN):
    return sum(bdot(w, p, dims) for p in parts(v, count))


def iota(shape, dim):
    return lax.broadcasted_iota(jnp.int32, shape, dim)


def spread_matrix():
    r = iota((128, 512), 0)
    return ((r % 8 == iota((128, 512), 1) // 64) & (r < 16)).astype(BF16)


def heads_of(v, eh):
    high = v.astype(BF16).astype(F32)
    both = jnp.where(iota(v.shape, 1) < 8, high, pltpu.roll(v - high, 8, 1))
    return bdot(both.astype(BF16), eh)


def sums_of(v, eh):
    return left_parts(v, eh, 2, NT)


def lower_matrix():
    return (iota((Q, Q), 0) >= iota((Q, Q), 1)).astype(BF16)


def sigmoid(v):
    return 1.0 / (1.0 + jnp.exp(-v))


def softplus(v):
    return jnp.maximum(v, 0.0) + jnp.log1p(jnp.exp(-jnp.abs(v)))


def row_scale(h):
    return lax.rsqrt(jnp.mean(h * h, axis=-1, keepdims=True) + EPS)


def decays(L, flags):
    E = jnp.exp(L) * flags[:, 3:4]
    W = jnp.exp(L[Q - 1 : Q] - L) * flags[:, 4:5]
    return E, W


def wave_kernel(
    hid, inw, seg, gain_in, og_in, cw_in, cb_in, dtb_in, alog_in, skip_in, cot, outw,
    normed_h, hid_h, w_h, gate_h, pre_h, ext_h, delta_h, logs_h, flags_h, fnext_h, mixed_h, carried_h, states_h, dno_h, cot_h, wout_h,
    sums, endlog, conv, hp, og, gain, segrow,
    hid_s, halo, nrm, turned, w_s, small, proj, pre, ext, delta, logs, flags, fnext, sloc, inner, carried, states, dno, ends, rsend, rrecv, cot_s, w_o, wo_s, convt, state, total, tail, wsend, pack, window, send, recv, done,
):
    eh = spread_matrix()
    n = Net(send, recv)
    g, m, x, y, z, core = n.g, n.m, n.x, n.y, n.z, n.c
    ALLX = (0,) + XS
    copies = []

    def keyed(key, src, dst, where):
        cp = n.copy(key, src, dst, where)
        copies.append(cp)
        cp.start()
        return cp

    stores = []

    def store(src, dst):
        cp = pltpu.make_async_copy(src, dst, done.at[len(stores)])
        cp.start()
        stores.append(cp)

    peers = n.greet([n.at(dz=a, dc=b) for a, b in OTHERS] + [n.at(dx=d) for d in XS] + [n.at(dy=1), n.at(dy=3), n.group(1), n.group(7)] + [n.across(d) for d in ALLX])

    for q in range(8):
        zq, cq = q // 2, q % 2
        for j in range(4):
            at = 512 * (4 * cq + j) + 128 * zq
            wsend[q, :, 128 * j : 128 * j + 128] = inw[:, at : at + 128]
            wsend[q, :, 512 + 128 * j : 640 + 128 * j] = inw[:, 4096 + at : 4224 + at]
        wsend[q, :, 1024:1280] = inw[:, 8192:8448]
        r, k = iota((64, 128), 0), iota((64, 128), 1)
        take = ((r == 32 * cq + 8 * (k // 2) + 2 * zq + k % 2) & (k < 8)).astype(BF16)
        wsend[q, :, 1280:1408] = bdot(inw[:, 8448:8512], take).astype(BF16)
    pack[...] = jnp.zeros_like(pack)
    pack[0:2, 0:64] = seg[...].astype(F32)
    pack[3:4, 0:64] = og_in[...]
    first = pltpu.roll(pack[0:8], 64 * core, 1)
    pack[0:8] = jnp.zeros((8, 128), F32)
    pack[2:3, 0:32] = gain_in[...]
    first = first + pltpu.roll(pack[0:8], 32 * lax.rem(m, 4), 1)
    row, at = iota((8, 128), 0), iota((8, 128), 1) == 2 * lax.rem(g, 4) + core
    for k, ref in enumerate((dtb_in, alog_in, skip_in)):
        first = first + jnp.where(at & (row == 4 + k), ref[0], 0.0)
    pack[0:8] = first
    window[...] = jnp.zeros_like(window)
    window[0:4, 0:68] = cw_in[...]
    window[4:5, 0:68] = cb_in[...]
    moved = pltpu.roll(window[...], lax.rem(68 * (8 * g + m), 128), 1)
    pack[8:16] = moved[:, 0:128]
    pack[16:24] = moved[:, 128:256]

    n.meet(peers)
    wa, sa = {}, {}
    for a, b in OTHERS:
        wa[a, b] = keyed(("wa", a, b), wsend.at[n.member(a, b)], w_s.at[g, m], n.at(dz=a, dc=b))
        sa[a, b] = keyed(("sa", a, b), pack, small.at[g, m], n.at(dz=a, dc=b))
    w_s[g, m] = wsend[m]
    small[g, m] = pack[...]
    hid_s[m] = hid[...]
    wx, wy, sx, sy = {}, {}, {}, {}

    def source(k):
        return n.member(4 - ZS[k // 2], k % 2)

    def along_y(d, k):
        for half, dy in ((0, 1), (1, 3)):
            part = w_s.at[n.behind(d), source(k), pl.ds(16 * half, 16)]
            wy[d, k, half] = keyed(("wy", d, k, half), part, part, n.at(dy=dy))

    def issue(k):
        if k:
            wa[ZS[k // 2], k % 2].wait_recv()
        block = w_s.at[g, source(k)]
        for d in XS:
            wx[k, d] = keyed(("wx", k, d), block, block, n.at(dx=d))
        along_y(0, k)

    def forward(k):
        for d in XS:
            wx[k, d].wait_recv()
            along_y(d, k)

    for k in range(4):
        issue(k)
    hz = {a: keyed(("hz", a), hid_s.at[m], hid_s.at[m], n.at(dz=a)) for a in (1, 3, 2)}
    hn = [keyed("hn", hid_s.at[m], hid_s.at[m], n.at(dc=1))]
    for a, b in OTHERS:
        sa[a, b].wait_recv()
    for d in XS:
        sx[d] = keyed(("sx", d), small.at[g], small.at[g], n.at(dx=d))
    sy[0] = keyed(("sy", 0), small.at[g], small.at[g], n.pair())
    for k in range(4):
        forward(k)
        issue(k + 4)
    for d in XS:
        sx[d].wait_recv()
        mine = small.at[n.behind(d)]
        sy[d] = keyed(("sy", d), mine, mine, n.pair())
    for k in range(4, 8):
        forward(k)
    w_o[g] = outw[...]
    ox = {d: keyed(("ox", d), w_o.at[g], w_o.at[g], n.at(dx=d)) for d in XS}
    oy = {}

    def out_y(d):
        for half, dy in ((0, 1), (1, 3)):
            part = w_o.at[n.behind(d), pl.ds(32 * half, 32)]
            oy[d, half] = keyed(("oy", d, half), part, part, n.at(dy=dy))

    out_y(0)
    for a in (1, 3, 2):
        hz[a].wait_recv()
        theirs = hid_s.at[2 * lax.rem(z + 4 - a, 4) + core]
        hn.append(keyed(("hf", a), theirs, theirs, n.at(dc=1)))
    cot_s[m] = cot[...]
    cz = {a: keyed(("cz", a), cot_s.at[m], cot_s.at[m], n.at(dz=a)) for a in (1, 3, 2)}
    cn = [keyed("cn", cot_s.at[m], cot_s.at[m], n.at(dc=1))]
    for d in ALLX:
        sy[d].wait_recv()

    for q in range(16):
        v = small[q // 2, 4 * (q % 2), 2:3]
        for u in range(1, 4):
            v = v + small[q // 2, 4 * (q % 2) + u, 2:3]
        gain[0:1, 128 * q : 128 * q + 128] = v
    heads3 = jnp.zeros((3, 128), F32)
    for j in range(4):
        og[0:1, 128 * j : 128 * j + 128] = small[4 * core + j, 2 * z, 3:4] + small[4 * core + j, 2 * z + 1, 3:4]
        for e in range(2):
            heads3 = heads3 + small[4 * core + j, 2 * z + e, 4:7]
    hp[...] = jnp.zeros_like(hp)
    hp[0:1] = heads3[0:1]
    hp[1:2] = jnp.where(iota((1, 128), 1) < 8, -jnp.exp(heads3[1:2]), 0.0)
    hp[2:3] = heads3[2:3]
    for q in range(34):
        v = jnp.zeros((8, 128), F32)
        for i in range(64):
            if 68 * i // 128 == q:
                v = v + small[i // 8, i % 8, 8:16]
            elif 68 * i // 128 == q - 1:
                v = v + small[i // 8, i % 8, 16:24]
        convt[q] = v
    for j in range(4):
        conv[:, 128 * j : 128 * j + 128] = convt[4 * (4 * core + j) + z]
    conv[:, 512:640] = convt[32]
    conv[:, 640:768] = convt[33]

    lane = iota((8, 128), 1)

    def chunk_row(group, i, c):
        return jnp.broadcast_to(small[group, 2 * c, i : i + 1] + small[group, 2 * c + 1, i : i + 1], (8, 128))

    for i in range(MICRO):
        before = jnp.where(g > 0, chunk_row(lax.rem(g + 7, 8), i, CH - 1), -1.0)
        after = jnp.where(g < 7, chunk_row(lax.rem(g + 1, 8), i, 0), -2.0)
        rows = [before] + [chunk_row(g, i, c) for c in range(CH)] + [after]
        for c in range(CH):
            prv, cur, nxt = rows[c : c + 3]
            here, ahead = [], []
            for d in (3, 2, 1):
                back = jnp.where(lane < d, pltpu.roll(prv, d, 1), pltpu.roll(cur, d, 1))
                here.append((back == cur).astype(F32))
                on = jnp.where(lane >= 128 - d, pltpu.roll(nxt, 128 - d, 1), pltpu.roll(cur, 128 - d, 1))
                ahead.append((on == cur).astype(F32))
            here += [(cur == prv[:, 127:128]).astype(F32), (cur == cur[:, 127:128]).astype(F32), cur]
            sub = iota((128, 128), 0)
            for rows_of, to in ((here, flags), (ahead, fnext)):
                v = jnp.zeros((128, 128), F32)
                for r, row in enumerate(rows_of):
                    v = jnp.where(sub == r, jnp.broadcast_to(row[0:1], (128, 128)), v)
                to[CH * i + c] = v.T
            segrow[CH * i + c] = cur[0:1]

    for cp in hn:
        cp.wait_recv()
    edge = keyed("edge", hid_s.at[7, :, pl.ds(48, 16)], halo, n.group(1))

    gv = gain[0:1]

    def norm(k, carry):
        for i in range(MICRO):
            h = hid_s[pl.ds(2 * k, 2), i].reshape(Q, 2048).astype(F32)
            v = h * row_scale(h) * gv
            nrm[i, pl.ds(pl.multiple_of(16 + Q * k, 16), Q)] = v.astype(BF16)
            turned[:, pl.ds(pl.multiple_of(TOK * i + Q * k, Q), Q)] = v.T.astype(BF16)
        return carry

    lax.fori_loop(0, CH, norm, 0)
    edge.wait_recv()
    for i in range(MICRO):
        h = halo[i].astype(F32)
        nrm[i, 0:16] = (h * row_scale(h) * gv).astype(BF16)
    store(turned, normed_h)

    def project(side, first):
        for i in range(MICRO):
            for lo in range(0, 1408, 256):
                hi = min(lo + 256, 1408)
                v = 0.0 if first else proj[i, :, lo:hi]
                for k in range(4):
                    q = 2 * k + side
                    v = v + bdot(nrm[i, :, pl.ds(pl.multiple_of(256 * q, 256), 256)], w_s[q, :, :, lo:hi].reshape(256, hi - lo))
                proj[i, :, lo:hi] = v

    project(y, True)
    for d in ALLX:
        for k in range(8):
            for half in (0, 1):
                wy[d, k, half].wait_recv()
    project(1 - y, False)
    for d in XS:
        ox[d].wait_recv()
        out_y(d)
    store(w_s, w_h)
    store(hid_s, hid_h)
    store(flags, flags_h)
    store(fnext, fnext_h)

    def front(i, c):
        at = CH * i + c
        rows = pl.ds(pl.multiple_of(16 + Q * c, 16), Q)
        f = flags[at]
        xbc = proj[i, rows, 512:1280].astype(BF16).astype(F32)
        tail[8:] = xbc
        acc = conv[4:5] + conv[3:4] * xbc
        for k in range(3):
            acc = acc + conv[k : k + 1] * tail[5 + k : 5 + k + Q] * f[:, k : k + 1]
        pre[at] = acc
        ext[at] = tail[...].astype(BF16)
        d = softplus(proj[i, rows, 1280:1408] + hp[0:1])
        delta[at] = d
        L = right_parts(lower_matrix(), d * hp[1:2], 3)
        logs[at] = L
        E, W = decays(L, f)
        xv = acc[:, :512]
        X = xv * sigmoid(xv)
        b = acc[:, 512:640]
        B = (b * sigmoid(b)).astype(BF16)
        S = right_parts(B, heads_of(W * d, eh) * X, 2, TN)
        sloc[at] = S
        last = heads_of(E[Q - 8 :], eh)
        state[...] = last[7:8] * state[...] + S
        tail[0:8] = tail[Q : Q + 8]
        total[...] = total[...] + L[Q - 1 : Q]

    ex, lx, ly = {}, {}, {}
    for i in range(MICRO):
        tail[0:8] = proj[i, 8:16, 512:1280].astype(BF16).astype(F32)
        state[...] = jnp.zeros_like(state)
        total[...] = jnp.zeros_like(total)
        lax.fori_loop(0, CH, lambda c, carry, i=i: (front(i, c), carry)[1], 0)
        ends[g, i] = state[...].astype(BF16)
        lt = parts(jnp.broadcast_to(heads_of(jnp.broadcast_to(total[...], (8, 128)), eh)[0:1], (16, 512)), 3)
        seg = jnp.broadcast_to(segrow[CH * i + CH - 1][:, 127:128], (16, 512))
        high = jnp.floor(seg * (1.0 / 64.0))
        r = iota((16, 512), 0)
        v = jnp.zeros((16, 512), BF16)
        for k, row in enumerate(lt + [high.astype(BF16), (seg - 64.0 * high).astype(BF16)]):
            v = jnp.where(r == k, row, v)
        endlog[g, i] = v
        for d in XS:
            lx[i, d] = keyed(("lx", i, d), endlog.at[g, i], endlog.at[g, i], n.at(dx=d))
        for d in ALLX:
            ly[i, d] = keyed(("ly", i, d), endlog.at[g, i], endlog.at[g, i], n.across(d))
        for d in XS:
            ex[i, d] = keyed(("ex", i, d), ends.at[g, i], ends.at[g, i], n.at(dx=d))
    store(pre, pre_h)
    store(ext, ext_h)
    store(delta, delta_h)
    store(logs, logs_h)
    for i in range(MICRO):
        store(proj.at[i, pl.ds(16, TOK), pl.ds(0, 512)], gate_h.at[i])

    def states_on(i):
        for d in XS:
            lx[i, d].wait_recv()
        for d in ALLX:
            ly[i, d].wait_recv()
        for d in XS:
            ex[i, d].wait_recv()
        rsend[i] = entering(n, ends, endlog, 1, 0, i).astype(BF16)
        return keyed(("r", i), rsend.at[i], rrecv.at[i], n.pair())

    def inside(at, carry):
        L = logs[at]
        X, B, C = activations(pre[at])
        U = (heads_of(delta[at], eh) * X).astype(BF16)
        psi = bdot(C, B, NT)
        keep = same_mask(flags[at], segrow[at])
        LT = L.T
        for j in range(4):
            u = pair_halves(U[:, 128 * j : 128 * j + 128])
            v = jnp.zeros((Q, 128), F32)
            for e in range(2):
                h = 2 * j + e
                K = jnp.where(keep, jnp.exp(L[:, h : h + 1] - LT[h : h + 1]), 0.0)
                v = v + bdot((psi * K).astype(BF16), u[e])
            inner[at, :, 128 * j : 128 * j + 128] = v
        return carry

    lax.fori_loop(0, 4, inside, 0)
    r0 = states_on(0)
    for d in ALLX:
        for half in (0, 1):
            oy[d, half].wait_recv()
    swap = keyed("swap", w_o.at[pl.ds(4 * (1 - core), 4)], wo_s.at[:, core], n.at(dc=1))
    for k in range(4):
        wo_s[k, core] = w_o[4 * core + k]
    for a in (1, 3, 2):
        cz[a].wait_recv()
        theirs = cot_s.at[2 * lax.rem(z + 4 - a, 4) + core]
        cn.append(keyed(("cf", a), theirs, theirs, n.at(dc=1)))
    lax.fori_loop(4, 8, inside, 0)
    r1 = states_on(1)
    swap.wait_recv()
    for cp in cn:
        cp.wait_recv()
    store(cot_s, cot_h)
    store(wo_s, wout_h)
    for i in range(MICRO):
        d = bdot(cot_s[:, i].reshape(TOK, 2048), wo_s[...].reshape(512, 2048), NT)
        for c in range(CH):
            dno[CH * i + c] = d[Q * c : Q * c + Q]
    store(dno, dno_h)

    def mix(i, c):
        at = CH * i + c
        E, _ = decays(logs[at], flags[at])
        X, _, C = activations(pre[at])
        more = heads_of(jnp.concatenate([E, jnp.broadcast_to(hp[2:3], (8, 128))], 0), eh)
        Ex, skip = more[:Q], more[Q : Q + 1]
        S = state[...]
        states[at, 0] = S
        Yc = Ex * bdot(C, S.astype(BF16))
        carried[at] = Yc
        mx = inner[at] + Yc + skip * X
        inner[at] = mx
        after = Ex[Q - 1 : Q] * S + sloc[at]
        state[...] = after
        states[at, 1] = after
        gt = proj[i, pl.ds(pl.multiple_of(16 + Q * c, 16), Q), 0:512]
        gated = mx * (gt * sigmoid(gt))
        ones = jnp.ones((8, 512), BF16)
        sums[m, at, 0:8] = right_parts(ones, gated * gated, 2, NT)
        sums[m, at, 8:16] = right_parts(ones, dno[at] * og[0:1] * gated, 2, NT)

    sm = []
    for i, r in ((0, r0), (1, r1)):
        r.wait_recv()
        state[...] = entering(n, ends, endlog, 0, 0, i) + rrecv[i].astype(F32)
        lax.fori_loop(0, CH, lambda c, carry, i=i: (mix(i, c), carry)[1], 0)
        mine = sums.at[m, pl.ds(CH * i, CH)]
        for a, b in OTHERS:
            sm.append(keyed(("sm", i, a, b), mine, mine, n.at(dz=a, dc=b)))
        some = pl.ds(CH * i, CH)
        store(inner.at[some], mixed_h.at[some])
        store(carried.at[some], carried_h.at[some])
        store(states.at[some], states_h.at[some])
    for cp in sm:
        cp.wait_recv()
    for cp in copies:
        cp.wait_send()
    for cp in stores:
        cp.wait()


def wave(hid, inw, seg, gain, og, cw, cb, dtb, alog, skip, cot, outw):
    V = lambda *s: pltpu.VMEM(s, BF16)
    R = lambda *s: pltpu.VMEM(s, F32)
    outs = [
        sds((2048, T), BF16), sds((8, 2, 64, 2048), BF16), sds((8, 8, 32, 1408), BF16), sds((2, TOK, 512), F32), sds((8, Q, 768), F32), sds((8, Q + 8, 768), BF16), sds((8, Q, 128), F32), sds((8, Q, 128), F32),
        sds((8, Q, 128), F32), sds((8, Q, 128), F32), sds((8, Q, 512), F32), sds((8, Q, 512), F32), sds((8, 2, 128, 512), F32), sds((8, Q, 512), F32), sds((8, 2, 64, 2048), BF16), sds((4, 2, 64, 2048), BF16),
        sds((8, 8, 16, 128), F32), sds((8, 2, 16, 512), BF16), sds((8, 768), F32), sds((8, 128), F32), sds((8, 512), F32), sds((8, 2048), F32), sds((8, 1, 128), F32),
    ]
    scratch = [
        V(8, 2, 64, 2048), V(2, 16, 2048), V(2, TOK + 16, 2048), V(2048, T), V(8, 8, 32, 1408), R(8, 8, 24, 128), R(2, TOK + 16, 1408), R(8, Q, 768), V(8, Q + 8, 768), R(8, Q, 128), R(8, Q, 128), R(8, Q, 128), R(8, Q, 128),
        R(8, 128, 512), R(8, Q, 512), R(8, Q, 512), R(8, 2, 128, 512), R(8, Q, 512), V(8, 2, 128, 512), V(2, 128, 512), V(2, 128, 512), V(8, 2, 64, 2048), V(8, 64, 2048), V(4, 2, 64, 2048),
        R(34, 8, 128), R(128, 512), R(1, 128), R(Q + 8, 768), V(8, 32, 1408), R(24, 128), R(8, 256),
    ]
    return pl.pallas_call(
        wave_kernel,
        name="wave",
        out_shape=outs,
        in_specs=[VM] * 7 + [SMEM] * 3 + [VM] * 2,
        out_specs=[ANY] * 16 + [VM] * 7,
        scratch_shapes=[*scratch, pltpu.SemaphoreType.DMA((192,)), pltpu.SemaphoreType.DMA((192,)), pltpu.SemaphoreType.DMA((24,))],
        compiler_params=pltpu.CompilerParams(collective_id=1, has_side_effects=True, vmem_limit_bytes=64 * 1024 * 1024 - 65536),
        cost_estimate=pl.CostEstimate(flops=8 << 30, bytes_accessed=32 << 20, transcendentals=0),
    )(hid, inw, seg, gain, og, cw, cb, dtb, alog, skip, cot, outw)


def entering(n, everyone, logs, target, direction, micro):
    to = 2 * n.x + (1 - n.y if target else n.y)
    lt, last = [], []
    for q in range(8):
        v = logs[q, micro].astype(F32)
        lt.append(v[0:1] + v[1:2] + v[2:3])
        last.append(64.0 * v[3:4] + v[4:5])
    zero = jnp.zeros((1, 512), F32)
    edge = zero
    for r in range(8):
        edge = edge + jnp.where((r == to) if direction else (r == to - 1), last[r], zero)
    total = jnp.zeros((128, 512), F32)
    for k in range(4):
        q = 2 * k + n.y
        log = zero
        for r in range(8):
            between = (r > to) & (r < q) if direction else (r > q) & (r < to)
            log = log + jnp.where(between, lt[r], zero)
        if direction:
            there = jnp.where(n.y == 0, last[max(2 * k - 1, 0)], last[2 * k])
        else:
            there = jnp.where(n.y == 0, last[2 * k], last[2 * k + 1])
        reached = jnp.where((q > to) if direction else (q < to), 1.0, 0.0)
        total = total + jnp.where(there == edge, jnp.exp(log) * reached, zero) * everyone[q, micro].astype(F32)
    return total


def same_mask(flags, segrow):
    return (flags[:, 5:6] == segrow) & (iota((Q, Q), 0) >= iota((Q, Q), 1))


def activations(pre):
    a = pre * sigmoid(pre)
    return a[:, :512], a[:, 512:640].astype(BF16), a[:, 640:768].astype(BF16)


def pair_halves(v):
    low_half = iota(v.shape, 1) < 64
    zero = jnp.zeros_like(v)
    return jnp.where(low_half, v, zero), jnp.where(low_half, zero, v)


T = MICRO * TOK


def column(row):
    return jnp.concatenate([jnp.broadcast_to(row, (128, 128)).T] * 4, 1)


def pick_matrix(rows, start, count, shift, dtype=BF16):
    r, l = iota((rows, 128), 0), iota((rows, 128), 1)
    return ((r - start == l - shift) & (l >= shift) & (l < shift + count)).astype(dtype)


class Reduce:
    def __init__(self, n, key, a, b, a1, a2, pa, b1, b2, pb, b3):
        self.n, self.key, self.a, self.b = n, key, a, b
        self.a1, self.a2, self.pa, self.b1, self.b2, self.pb, self.b3 = a1, a2, pa, b1, b2, pb, b3
        self.half = pb.shape[1]

    def group(self, d, f):
        n = self.n
        return 2 * lax.rem(n.x + d, 4) + lax.rem(n.y + f, 2)

    def first_a(self, d, f):
        return self.n.copy((self.key, "a1", d, f), self.a.at[self.group(d, f)], self.a1.at[d - 1, f], self.n.at(dx=d))

    def first_b(self, d, e):
        n = self.n
        rep = lax.rem(n.ring + e, 4) // 2
        rows = pl.ds(pl.multiple_of(self.half * rep, self.half), self.half)
        return n.copy((self.key, "b1", d, e), self.b.at[self.group(d, e % 2), rows], self.b1.at[e - 1, lax.rem(n.x + d, 4)], n.at(dy=e))

    def send_a(self, d, f):
        if d:
            self.first_a(d, f).start()

    def send_b(self, d, f):
        for e in (1, 3) if f else (2,):
            self.first_b(d, e).start()

    def second_a(self, e):
        return self.n.copy((self.key, "a2", e), self.pa.at[e % 2], self.a2.at[e - 1], self.n.at(dy=e))

    def second_b(self, d):
        return self.n.copy((self.key, "b2", d), self.pb.at[lax.rem(self.n.x + d, 4)], self.b2.at[d - 1], self.n.at(dx=d))

    def third_b(self):
        return self.n.copy((self.key, "b3"), self.b3.at[self.n.rep], self.b3.at[self.n.rep], self.n.at(dy=2))

    def middle_a(self, f):
        for d in XS:
            self.first_a(d, f).wait_recv()
        self.pa[f] = add4(self.a[self.group(0, f)], self.a1[:, f]).astype(BF16)

    def go_a(self, f):
        for e in (1, 3) if f else (2,):
            self.second_a(e).start()

    def go_b(self):
        for d in (2, 1, 3):
            self.second_b(d).start()

    def middle_b(self):
        n = self.n
        rows = pl.ds(pl.multiple_of(self.half * n.rep, self.half), self.half)
        for d in (2, 1, 3, 0):
            for e in XS:
                self.first_b(d, e).wait_recv()
            k = lax.rem(n.x + d, 4)
            self.pb[k] = add4(self.b[2 * k + n.y, rows], self.b1[:, k]).astype(BF16)

    def last_b(self):
        for d in XS:
            self.second_b(d).wait_recv()
        self.b3[self.n.rep] = add4(self.pb[self.n.x], self.b2).astype(self.b3.dtype)
        self.third_b().start()

    def last_a(self):
        for e in XS:
            self.second_a(e).wait_recv()
        return add4(self.pa[0], self.a2)

    def finish_first(self):
        for d in XS:
            for f in (0, 1):
                self.first_a(d, f).wait_send()
        for e in XS:
            for d in range(4):
                self.first_b(d, e).wait_send()

    def finish(self):
        for d in XS:
            self.second_b(d).wait_send()
            self.second_a(d).wait_send()
        self.third_b().wait_send()


def fetcher(sems):
    loads = {}

    def fetch(key, src, dst):
        loads[key] = pltpu.make_async_copy(src, dst, sems.at[len(loads)])
        loads[key].start()

    return loads, fetch


C1 = 256


def back_wave_kernel(
    mixed_h, carried_h, states_h, gate_h, dno_h, sums, pre_h, delta_h, logs_h, flags_h, segrow, og, hp, wout_h, normed, endlog,
    dgate, dpre_h, bc_all, ddt, small_o, small_b, total, wpa, wpb, turned, edges,
    mixed, carried, states, gate, dno, pre, delta, logs, flags, wout, nout, dmix, tloc, dbi, starts, rsend, rrecv, rows, part, near, far,
    wa, wb, wa1, wb1, dbc, state, send, recv, load, tile_sem,
):
    eh = spread_matrix()
    n = Net(send, recv)
    g, m, core, z = n.g, n.m, n.c, n.z
    W = Reduce(n, "w", wa, wb, wa1, None, wpa, wb1, None, wpb, None)
    loads, fetch = fetcher(load)
    peers = n.greet([n.at(dz=a, dc=b) for a, b in OTHERS] + [n.at(dx=d) for d in XS] + [n.at(dy=d) for d in XS] + [n.group(1), n.group(7)])
    for i in range(MICRO):
        some = pl.ds(CH * i, CH)
        for key, src, dst in (("mixed", mixed_h, mixed), ("gate", gate_h, gate), ("dno", dno_h, dno), ("pre", pre_h, pre), ("logs", logs_h, logs), ("flags", flags_h, flags)):
            fetch((key, i), src.at[some], dst.at[some])
    fetch("wout", wout_h, wout)
    for key, src, dst in (("delta", delta_h, delta), ("states", states_h, states), ("carried", carried_h, carried)):
        fetch(key, src, dst)

    def start_x(i, d):
        return n.copy(("sx", i, d), starts.at[g, i], starts.at[g, i], n.at(dx=d))

    def part_y(i):
        return n.copy(("r", i), rsend.at[i], rrecv.at[i], n.pair())

    def near_copy(d, i):
        return n.copy(("near", d, i), part.at[2 * lax.rem(z + d, 4) + 1 - core, i], near.at[d, i], n.at(dc=1))

    def far_copy(d, i):
        return n.copy(("far", d, i), near.at[d, i], far.at[d - 1, i], n.at(dz=d))

    def bc_copy(i, a, b):
        some = pl.ds(TOK * i, TOK)
        return n.copy(("bc", i, a, b), dbc.at[n.member(a, b), :, some], bc_all.at[m, :, some], n.at(dz=a, dc=b))

    def edge_copy(i):
        return n.copy(("edge", i), gate.at[CH * i, pl.ds(0, 8)], edges.at[i], n.group(7))

    small_o[...] = jnp.zeros_like(small_o)
    small_b[...] = jnp.zeros_like(small_b)

    def outward(i, k):
        c = CH - 1 - k
        at = CH * i + c
        tot = sums[0, at]
        for q in range(1, 8):
            tot = tot + sums[q, at]
        r = column(lax.rsqrt(tot[0:1] / INNER + EPS))
        s2 = column(tot[8:9] / INNER)
        gt = gate[at]
        s = sigmoid(gt)
        sg = gt * s
        mix = mixed[at]
        gated = mix * sg
        dn = dno[at]
        n0 = gated * r
        rows = pl.ds(pl.multiple_of(Q * c, Q), Q)
        nb = n0 * og[0:1]
        nout[i, rows] = nb.astype(BF16)
        turned[:, pl.ds(pl.multiple_of(Q * at, Q), Q)] = nb.T.astype(BF16)
        d_gated = r * (dn * og[0:1] - n0 * r * s2)
        dm = d_gated * sg
        dmix[at] = dm
        dgate[i, rows] = (d_gated * mix * (s * (1.0 + gt * (1.0 - s)))).astype(BF16)
        x = pre[at, :, :512]
        X = x * sigmoid(x)
        cc = pre[at, :, 640:768]
        C = (cc * sigmoid(cc)).astype(BF16)
        small_o[0:1] += jnp.sum(dn * n0, 0, keepdims=True)
        small_o[1:2] += jnp.sum(X * dm, 0, keepdims=True)
        E, _ = decays(logs[at], flags[at])
        Ex = heads_of(E, eh)
        G = right_parts(C, Ex * dm, 2, TN)
        tloc[at] = G
        state[...] = Ex[Q - 1 : Q] * state[...] + G

    for i in range(MICRO):
        for key in ("mixed", "gate", "dno", "pre", "logs", "flags"):
            loads[key, i].wait()
        state[...] = jnp.zeros_like(state)
        lax.fori_loop(0, CH, lambda k, carry, i=i: (outward(i, k), carry)[1], 0)
        starts[g, i] = state[...].astype(BF16)
        if i == 0:
            n.meet(peers)
        for d in XS:
            start_x(i, d).start()
        if i == 0:
            loads["wout"].wait()
        part[:, i] = bdot(nout[i], wout[...]).astype(BF16).reshape(8, 64, 2048)
        for d in (1, 3, 2, 0):
            near_copy(d, i).start()

    def bring(k):
        at = pl.ds(pl.multiple_of(256 * W.group(*ORDER[k]), 256), 256)
        return pltpu.make_async_copy(normed.at[at], rows.at[k % 2], tile_sem.at[k % 2])

    def states_on(i):
        for d in XS:
            start_x(i, d).wait_recv()
        rsend[i] = entering(n, starts, endlog, 1, 1, i).astype(BF16)
        part_y(i).start()

    def tokens_on(i):
        for d in (1, 3, 2, 0):
            near_copy(d, i).wait_recv()
            there = 2 * lax.rem(z + d, 4) + core
            near[d, i] = (part[there, i].astype(F32) + near[d, i].astype(F32)).astype(BF16)
            if d:
                far_copy(d, i).start()

    bring(0).start()
    for k, (d, f) in enumerate(ORDER):
        bring(k).wait()
        if k < 7:
            bring(k + 1).start()
        q = W.group(d, f)
        v = bdot(rows[k % 2], dgate[...].reshape(T, 512))
        wa[q] = v[:, 0:C1].astype(BF16)
        wb[q] = v[:, C1:].astype(BF16)
        W.send_a(d, f)
        W.send_b(d, f)
        if k == 1:
            states_on(0)
            tokens_on(0)
        if k == 5:
            states_on(1)
            tokens_on(1)

    loads["delta"].wait()
    loads["states"].wait()
    loads["carried"].wait()

    def inside(at, carry):
        L = logs[at]
        f = flags[at]
        E, _ = decays(L, f)
        X, B, C = activations(pre[at])
        more = heads_of(jnp.concatenate([E, delta[at]], 0), eh)
        Ex, dx = more[:Q], more[Q:]
        Ub = (dx * X).astype(BF16)
        dm = dmix[at]
        dmb = dm.astype(BF16)
        psi = bdot(C, B, NT)
        keep = same_mask(f, segrow[at])
        LT = L.T
        dpsi = jnp.zeros((Q, Q), F32)
        for j in range(4):
            js = slice(128 * j, 128 * j + 128)
            u = pair_halves(Ub[:, js])
            y = pair_halves(dmb[:, js])
            acc = jnp.zeros((Q, 128), F32)
            for e in range(2):
                h = 2 * j + e
                K = jnp.where(keep, jnp.exp(L[:, h : h + 1] - LT[h : h + 1]), 0.0)
                acc = acc + bdot((psi * K).astype(BF16), y[e], TN)
                dpsi = dpsi + bdot(y[e], u[e], NT) * K
            dno[at, :, js] = acc
        dpb = dpsi.astype(BF16)
        dbi[at, 0:128] = bdot(C, dpb, TN)
        dbi[at, 128:256] = bdot(B, dpb, TT) + bdot(states[at, 0].astype(BF16), (Ex * dm).astype(BF16), NT)
        return carry

    lax.fori_loop(0, 8, inside, 0)
    for i in (0, 1):
        part_y(i).wait_recv()

    def inward(i, k):
        c = CH - 1 - k
        at = CH * i + c
        L = logs[at]
        d = delta[at]
        E, W_ = decays(L, flags[at])
        p = pre[at, :, 0:512]
        s = sigmoid(p)
        X = p * s
        bb = pre[at, :, 512:640]
        B = (bb * sigmoid(bb)).astype(BF16)
        more = heads_of(jnp.concatenate([E[Q - 8 :], W_, d, jnp.broadcast_to(hp[2:3], (8, 128))], 0), eh)
        Elast, Wx, dx, skip = more[7:8], more[8 : 8 + Q], more[8 + Q : 8 + 2 * Q], more[8 + 2 * Q : 9 + 2 * Q]
        U = dx * X
        dm = dmix[at]
        Yc = carried[at]
        Yi = mixed[at] - Yc - skip * X
        G = state[...]
        Gb = G.astype(BF16)
        dUi = dno[at]
        dUc = Wx * bdot(B, Gb)
        dU = dUi + dUc
        lanes = pl.ds(pl.multiple_of(Q * at, Q), Q)
        dbc[0:4, :, lanes] = (dbi[at, 0:128] + bdot(Gb, (Wx * U).astype(BF16), NT)).astype(BF16).reshape(4, 32, Q)
        dbc[4:8, :, lanes] = dbi[at, 128:256].astype(BF16).reshape(4, 32, Q)
        dL = sums_of(dm.astype(BF16).astype(F32) * Yi + dm * Yc - U.astype(BF16).astype(F32) * dUi - U * dUc, eh)
        end = sums_of(jnp.broadcast_to(jnp.sum(G * states[at, 1], 0, keepdims=True), (8, 512)), eh)[0:1]
        upper = (iota((Q, Q), 0) <= iota((Q, Q), 1)).astype(BF16)
        dstep = right_parts(upper, dL, 3) + end
        rate = hp[1:2]
        dr = (sums_of(dU * X, eh) + dstep * rate) * (1.0 - jnp.exp(-d))
        ddt[at] = dr.astype(BF16)
        small_b[0:1] += jnp.sum(dr, 0, keepdims=True)
        small_b[1:2] += jnp.sum(dstep * d * rate, 0, keepdims=True)
        gate[at] = (dx * dU + skip * dm) * (s * (1.0 + p * (1.0 - s)))
        state[...] = Elast * G + tloc[at]

    store = pltpu.make_async_copy(gate, dpre_h, load.at[0])
    for i in range(MICRO):
        state[...] = entering(n, starts, endlog, 0, 1, i) + rrecv[i].astype(F32)
        lax.fori_loop(0, CH, lambda k, carry, i=i: (inward(i, k), carry)[1], 0)
        edge_copy(i).start()
        for a, b in OTHERS:
            bc_copy(i, a, b).start()
    store.start()
    bc_all[m] = dbc[m]

    W.middle_b()
    W.middle_a(1)
    W.middle_a(0)
    for i in range(MICRO):
        for d in XS:
            far_copy(d, i).wait_recv()
        total[i] = near[0, i].astype(F32) + far[0, i].astype(F32) + far[1, i].astype(F32) + far[2, i].astype(F32)
    for i in range(MICRO):
        edge_copy(i).wait_recv()
        for a, b in OTHERS:
            bc_copy(i, a, b).wait_recv()
    W.finish_first()
    for i in range(MICRO):
        edge_copy(i).wait_send()
        for a, b in OTHERS:
            bc_copy(i, a, b).wait_send()
    store.wait()
    for i in range(MICRO):
        part_y(i).wait_send()
        for d in XS:
            start_x(i, d).wait_send()
            far_copy(d, i).wait_send()
        for d in range(4):
            near_copy(d, i).wait_send()


def back_wave(mixed, carried, states, gate, dno, sums, pre, delta, logs, flags, segrow, og, hp, wout, normed, endlog):
    outs = [
        sds((2, TOK, 512), BF16), sds((8, Q, 512), F32), sds((8, 32, T), BF16), sds((8, Q, 128), BF16), sds((8, 512), F32), sds((8, 128), F32), sds((2, 64, 2048), F32),
        sds((2, 256, C1), BF16), sds((4, 128, C1), BF16), sds((512, T), BF16), sds((2, 8, 512), F32),
    ]
    V = lambda *s: pltpu.VMEM(s, BF16)
    R = lambda *s: pltpu.VMEM(s, F32)
    return pl.pallas_call(
        back_wave_kernel,
        name="back_wave",
        out_shape=outs,
        in_specs=[ANY] * 5 + [VM] + [ANY] * 4 + [VM] * 3 + [ANY] * 2 + [VM],
        out_specs=[VM, ANY] + [VM] * 9,
        scratch_shapes=[
            R(8, Q, 512), R(8, Q, 512), R(8, 2, 128, 512), R(8, Q, 512), R(8, Q, 512), R(8, Q, 768), R(8, Q, 128), R(8, Q, 128), R(8, Q, 128), V(512, 2048),
            V(2, TOK, 512), R(8, Q, 512), R(8, 128, 512), R(8, 256, 128), V(8, 2, 128, 512), V(2, 128, 512), V(2, 128, 512), V(2, 256, T), V(8, 2, 64, 2048),
            V(4, 2, 64, 2048), V(3, 2, 64, 2048),
            V(8, 256, C1), V(8, 256, C1), V(3, 2, 256, C1), V(3, 4, 128, C1), V(8, 32, T), R(128, 512),
            pltpu.SemaphoreType.DMA((96,)), pltpu.SemaphoreType.DMA((96,)), pltpu.SemaphoreType.DMA((16,)), pltpu.SemaphoreType.DMA((2,)),
        ],
        compiler_params=pltpu.CompilerParams(collective_id=4, has_side_effects=True, vmem_limit_bytes=62 << 20),
        cost_estimate=pl.CostEstimate(flops=8 << 30, bytes_accessed=32 << 20, transcendentals=0),
    )(mixed, carried, states, gate.reshape(8, Q, 512), dno, sums, pre, delta, logs, flags, segrow, og, hp, wout, normed, endlog)


CB = 384
CA = 640 - CB


def tail_kernel(
    bc_s, ex_s, wpa, wpb, turned, branch, gain, cot, dpre, pre, ext, flags, fnext, conv, ddt, dgate, w, hid, normed, small_o, small_b,
    g_in, g_out, layer_out, grad_in, conv_out, bias_out, norm_out, gain_out, dtb_out, alog_out, skip_out,
    eb_src, eb_s, dps, pre_s, ext_s, fl_s, fn_s, ddt_s, dg_s, w_s, hid_s, nm_s, wt, e_s, dproj, part, near, far, conv_acc, gnorm,
    s0, s1, s2, sx, ga, gb, ga1, ga2, gpa, gb1, gb2, gpb, gb3, cot_s, gsw, oa, ob, oa1, oa2, opa, ob1, ob2, opb, ob3, oin, cot_own, ga2_, gb2_, gb3_, gi, small_all, convt, final, send, recv, load, tile_sem,
):
    n = Net(send, recv)
    x, y, z, c, m = n.x, n.y, n.z, n.c, n.m
    loads = {}

    def fetch(key, src, dst):
        loads[key] = pltpu.make_async_copy(src, dst, load.at[len(loads)])
        loads[key].start()

    peers = n.greet([n.at(dz=a, dc=b) for a, b in OTHERS] + [n.at(dx=d) for d in XS] + [n.at(dy=d) for d in XS] + [n.group(1), n.group(7)])
    fetch("pre", pre.at[:, :, pl.ds(512, 256)], pre_s)
    fetch("w", w, w_s)
    fetch("dpre", dpre, dps.at[:, pl.ds(0, TOK), pl.ds(0, 512)])
    fetch("ext", ext, ext_s)
    fetch("flags", flags, fl_s)
    fetch("fnext", fnext, fn_s)
    fetch("ddt", ddt, ddt_s)
    fetch("normed", normed, nm_s)
    fetch("dgate", dgate, dg_s)
    fetch("hid", hid, hid_s)
    fetch("cot", cot.at[m], cot_own)
    n.meet(peers)
    G_ = Reduce(n, "g", None, None, None, ga2_, wpa, None, gb2_, wpb, gb3_)
    G_.go_a(1)
    G_.go_a(0)
    G_.go_b()

    edge2 = n.copy("edge2", eb_src, eb_s, n.group(7))

    def near_copy(d, i):
        return n.copy(("near", d, i), part.at[2 * lax.rem(z + d, 4) + 1 - c, i], near.at[d, i], n.at(dc=1))

    def far_copy(d, i):
        return n.copy(("far", d, i), near.at[d, i], far.at[d - 1, i], n.at(dz=d))

    def small_x(d):
        return n.copy(("sx", d), s0, s1.at[d - 1], n.at(dx=d))

    def small_y(d):
        return n.copy(("sy", d), sx, s2.at[d - 1], n.at(dy=d))

    def small_m(a, b):
        return n.copy(("sm", a, b), small_all.at[m], small_all.at[m], n.at(dz=a, dc=b))

    def rows_copy(a, b):
        return n.copy(("rows", a, b), final.at[n.member(a, b)], gi.at[m], n.at(dz=a, dc=b))

    O = Reduce(n, "o", oa, ob, oa1, oa2, opa, ob1, ob2, opb, ob3)
    swap = n.copy("swap", gsw.at[:, 1 - c], oin, n.at(dc=1))
    W = Reduce(n, "w", ga, gb, ga1, ga2, gpa, gb1, gb2, gpb, gb3)

    pick = pick_matrix(256, 32 * m, 32, 0)
    loads["w"].wait()
    wt[...] = (bdot(w_s[:, 1024:1280], pick) + bdot(w_s[:, 1280:1408], pick_matrix(128, 0, 8, 32))).astype(BF16)
    cw = jnp.concatenate([conv[:, 0:512], left_parts(conv[:, 512:768], pick, 3)], 1)
    for key in ("pre", "dpre"):
        loads[key].wait()
    eye = pick_matrix(32, 0, 32, 0)

    def bc_chunk(i, k):
        t = CH * i + k
        tot = bc_s[0, :, Q * t : Q * t + Q].astype(F32)
        for q in range(1, 8):
            tot = tot + bc_s[q, :, Q * t : Q * t + Q].astype(F32)
        d = left_parts(tot, eye, 2, TN)
        p = left_parts(pre_s[t], pick, 2)
        s = sigmoid(p)
        dps[i, Q * k : Q * k + Q, 512:640] = d * (s * (1.0 + p * (1.0 - s)))

    for i in range(MICRO):
        bc_chunk(i, 0)
        eb_src[i] = dps[i, 0:8, 512:640]
    edge2.start()
    for i in range(MICRO):
        for k in range(1, CH):
            bc_chunk(i, k)
    def bring(k):
        return pltpu.make_async_copy(cot.at[:, :, :, pl.ds(256 * k, 256)], cot_s.at[k % 2], tile_sem.at[k % 2])

    bring(0).start()
    for k in range(8):
        bring(k).wait()
        if k < 7:
            bring(k + 1).start()
        v = sum(bdot(turned[:, TOK * i : TOK * i + TOK], cot_s[k % 2, :, i].reshape(TOK, 256)) for i in range(MICRO))
        gsw[:, :, :, 256 * k : 256 * k + 256] = v.astype(BF16).reshape(4, 2, 64, 256)
    swap.start()
    for j in range(4):
        oa[4 * c + j] = gsw[j, c, :, 0:1024]
        ob[4 * c + j] = gsw[j, c, :, 1024:2048]

    for key in ("ext", "flags", "fnext", "ddt"):
        loads[key].wait()
    conv_acc[...] = jnp.zeros_like(conv_acc)
    pick_dt = pick_matrix(128, 0, 8, 32)

    def conv_chunk(i, k):
        t = CH * i + k
        e_s[:, 0:512] = ext_s[t, :, 0:512].astype(F32)
        e_s[:, 512:640] = bdot(ext_s[t, :, 512:768], pick)
        f, fn = fl_s[t], fn_s[t]
        dp = dps[i, Q * k : Q * k + Q]
        dx = cw[3:4] * dp
        conv_acc[3:4] += jnp.sum(dp * e_s[8 : 8 + Q], 0, keepdims=True)
        conv_acc[4:5] += jnp.sum(dp, 0, keepdims=True)
        for j in range(3):
            conv_acc[j : j + 1] += jnp.sum(dp * e_s[5 + j : 5 + j + Q] * f[:, j : j + 1], 0, keepdims=True)
            dx = dx + cw[j : j + 1] * dps[i, Q * k + 3 - j : Q * k + 3 - j + Q] * fn[:, j : j + 1]
        rows = slice(Q * k, Q * k + Q)
        dproj[i, rows, 0:512] = dx[:, 0:512].astype(BF16)
        dproj[i, rows, 512:640] = (dx[:, 512:640] + bdot(ddt_s[t], pick_dt)).astype(BF16)

    for i in range(MICRO):
        for k in range(CH - 1):
            conv_chunk(i, k)
    swap.wait_recv()
    for j in range(4):
        oa[4 * (1 - c) + j] = oin[j, :, 0:1024]
        ob[4 * (1 - c) + j] = oin[j, :, 1024:2048]
    for d, f in ORDER:
        O.send_a(d, f)
        O.send_b(d, f)

    edge2.wait_recv()
    for i in range(MICRO):
        dps[i, TOK : TOK + 8, 0:512] = ex_s[i]
        dps[i, TOK : TOK + 8, 512:640] = eb_s[i]
        conv_chunk(i, CH - 1)

    loads["hid"].wait()
    loads["dgate"].wait()
    for i in range(MICRO):
        h = hid_s[:, i].reshape(TOK, 2048).astype(F32)
        scale = row_scale(h)
        first, main, rest = dg_s[i], dproj[i, :, 0:512], dproj[i, :, 512:640]

        def tile_of(j, carry, i=i, scale=scale, first=first, main=main, rest=rest):
            at = pl.ds(pl.multiple_of(256 * j, 256), 256)
            d = bdot(first, w_s[at, 0:512], NT) + bdot(main, w_s[at, 512:1024], NT) + bdot(rest, wt[at], NT)
            part[:, i, :, at] = d.astype(BF16).reshape(8, 64, 256)
            hv = hid_s[:, i, :, at].reshape(TOK, 256).astype(F32)
            s = jnp.sum(d * (hv * scale), 0, keepdims=True)
            gnorm[0:1, at] = s if i == 0 else gnorm[0:1, at] + s
            return carry

        lax.fori_loop(0, 8, tile_of, 0)
        for d in (1, 3, 2, 0):
            near_copy(d, i).start()
    for r in range(16):
        s0[r : r + 1] = gnorm[0:1, 128 * r : 128 * r + 128]
    for k in range(5):
        for r in range(5):
            s0[16 + 5 * k + r : 17 + 5 * k + r] = conv_acc[k : k + 1, 128 * r : 128 * r + 128]
    for r in range(4):
        s0[41 + r : 42 + r] = small_o[0:1, 128 * r : 128 * r + 128]
    s0[45:47] = small_b[0:2]
    s0[47:48] = sums_of(small_o[...], spread_matrix())[1:2]
    for d in XS:
        small_x(d).start()

    def tokens_on(i):
        for d in (1, 3, 2, 0):
            near_copy(d, i).wait_recv()
            there = 2 * lax.rem(z + d, 4) + c
            near[d, i] = (part[there, i].astype(F32) + near[d, i].astype(F32)).astype(BF16)
            if d:
                far_copy(d, i).start()

    loads["normed"].wait()
    for k, (d, f) in enumerate(ORDER):
        q = W.group(d, f)
        at = pl.ds(pl.multiple_of(256 * q, 256), 256)
        v = bdot(nm_s[at], dproj[...].reshape(T, 640)).astype(BF16)
        gb[q] = v[:, 0:CB]
        ga[q] = v[:, CB:]
        W.send_a(d, f)
        W.send_b(d, f)
        if k == 2:
            tokens_on(0)
        if k == 6:
            tokens_on(1)

    G_.last_b()
    final[:, :, 0:C1] = G_.last_a().astype(BF16).reshape(8, 32, C1)
    for i in range(MICRO):
        layer_out[i] = (hid_s[m, i].astype(F32) + branch[i]).astype(BF16)
    O.middle_a(1)
    O.go_a(1)
    O.middle_b()
    O.go_b()
    O.middle_a(0)
    O.go_a(0)

    for d in XS:
        small_x(d).wait_recv()
    sx[...] = s0[...] + s1[0] + s1[1] + s1[2]
    for d in XS:
        small_y(d).start()
    W.middle_a(1)
    W.go_a(1)
    W.middle_b()
    W.go_b()
    W.middle_a(0)
    W.go_a(0)
    O.last_b()
    g_out[:, 0:1024] = O.last_a()
    W.last_b()
    for d in XS:
        small_y(d).wait_recv()
    small_all[m] = sx[...] + s2[0] + s2[1] + s2[2]
    for a, b in OTHERS:
        small_m(a, b).start()
    for i in range(MICRO):
        for d in XS:
            far_copy(d, i).wait_recv()
        dn = near[0, i].astype(F32) + far[0, i].astype(F32) + far[1, i].astype(F32) + far[2, i].astype(F32)
        if i == 0:
            loads["cot"].wait()
        h = hid_s[m, i].astype(F32)
        r = row_scale(h)
        dg = dn * gain[0:1]
        grad_in[i] = (cot_own[i].astype(F32) + r * dg - h * (r * r * r) * jnp.mean(dg * h, axis=-1, keepdims=True)).astype(BF16)
    O.third_b().wait_recv()
    for h in range(2):
        g_out[32 * h : 32 * h + 32, 1024:2048] = ob3[h]
    W.third_b().wait_recv()
    for h in range(2):
        final[4 * h : 4 * h + 4, :, 512 : 512 + CB] = gb3[h].reshape(4, 32, CB)
    final[:, :, 512 + CB :] = W.last_a().astype(BF16).reshape(8, 32, CA)
    G_.third_b().wait_recv()
    for h in range(2):
        final[4 * h : 4 * h + 4, :, C1:512] = gb3_[h].reshape(4, 32, C1)
    for a, b in OTHERS:
        rows_copy(a, b).start()
    gi[m] = final[m]
    for a, b in OTHERS:
        rows_copy(a, b).wait_recv()
        small_m(a, b).wait_recv()

    rest_cols = jnp.zeros((32, 384), F32)
    r, l = iota((128, 384), 0), iota((128, 384), 1)
    for q in range(8):
        zq, cq = q // 2, q % 2
        for j in range(4):
            at = 512 * (4 * cq + j) + 128 * zq
            g_in[:, at : at + 128] = gi[q, :, 128 * j : 128 * j + 128].astype(F32)
            g_in[:, 4096 + at : 4224 + at] = gi[q, :, 512 + 128 * j : 640 + 128 * j].astype(F32)
        k = r - 32
        put = ((r < 32) & (l == 32 * q + r)) | ((r >= 32) & (r < 40) & (l == 256 + 32 * cq + 8 * (k // 2) + 2 * zq + k % 2))
        rest_cols = rest_cols + bdot(gi[q, :, 1024:1152], put.astype(BF16))
    g_in[:, 8192:8512] = rest_cols[:, 0:320]

    g = n.g
    shard = 8 * g + m
    lane = iota((8, 128), 1)

    def pick_row(v, at):
        return jnp.broadcast_to(jnp.sum(jnp.where(iota(v.shape, 0) == at, v, 0.0), 0, keepdims=True), (8, 128))

    norm_sum = small_all[0, 0:16]
    for q in range(1, 8):
        norm_sum = norm_sum + small_all[q, 0:16]
    norm_row = pltpu.roll(pick_row(norm_sum, shard // 4), lax.rem(128 - 32 * lax.rem(shard, 4), 128), 1)
    mine = small_all[2 * (m // 2) + g // 4]
    out_row = pltpu.roll(pick_row(mine[40:48], 1 + lax.rem(g, 4)), 64 * lax.rem(m, 2), 1)
    here = lane == 2 * lax.rem(g, 4) + lax.rem(m, 2)
    for k, ref in enumerate((dtb_out, alog_out, skip_out)):
        ref[...] = jnp.sum(jnp.where(here, pick_row(mine[40:48], 5 + k), 0.0), 1, keepdims=True)[0:1]
    convt[...] = jnp.zeros_like(convt)
    for t in range(32):
        q, j = 2 * (t % 4) + t // 16, t // 4 % 4
        for k in range(5):
            convt[t, k : k + 1] = small_all[q, 16 + 5 * k + j : 17 + 5 * k + j]
    for q in range(8):
        for k in range(5):
            v = jnp.where(lane < 32, jnp.broadcast_to(small_all[q, 20 + 5 * k : 21 + 5 * k], (8, 128)), 0.0)
            convt[32 + q // 4, k : k + 1] += (pltpu.roll(v, 32 * (q % 4), 1) if q % 4 else v)[0:1]
    tile = 68 * shard // 128
    both = jnp.concatenate([convt[tile], convt[tile + 1]], 1)
    own = pltpu.roll(both, lax.rem(256 - lax.rem(68 * shard, 128), 256), 1)[:, 0:128]
    conv_out[...] = own[0:4, 0:68]
    bias_out[...] = own[4:5, 0:68]
    norm_out[...] = norm_row[0:1, 0:32]
    gain_out[...] = out_row[0:1, 0:64]
    W.finish_first()
    O.finish_first()
    W.finish()
    O.finish()
    G_.finish()
    swap.wait_send()
    for a, b in OTHERS:
        rows_copy(a, b).wait_send()
        small_m(a, b).wait_send()
    for d in XS:
        small_x(d).wait_send()
        small_y(d).wait_send()
        for i in range(MICRO):
            far_copy(d, i).wait_send()
    for d in range(4):
        for i in range(MICRO):
            near_copy(d, i).wait_send()
    edge2.wait_send()


def tail_call(bc_all, edges, wpa, wpb, turned, branch, gain, cot, dpre, pre, ext, flags, fnext, conv, ddt, dgate, w, hid, normed, small_o, small_b):
    outs = [sds((32, 8512), F32), sds((64, 2048), F32), sds((2, 64, 2048), BF16), sds((2, 64, 2048), BF16)] + [sds(v, F32) for v in ((4, 68), (1, 68), (1, 32), (1, 64), (1, 1), (1, 1), (1, 1))]
    V = lambda *s: pltpu.VMEM(s, BF16)
    R = lambda *s: pltpu.VMEM(s, F32)
    scratch = [
        R(2, 8, 128), R(2, 8, 128), R(2, TOK + 8, 640), R(8, Q, 256), V(8, Q + 8, 768), R(8, Q, 128), R(8, Q, 128), V(8, Q, 128), V(2, TOK, 512), V(2048, 1408),
        V(8, 2, 64, 2048), V(2048, T), V(2048, 128), R(Q + 8, 640), V(2, TOK, 640), V(8, 2, 64, 2048), V(4, 2, 64, 2048), V(3, 2, 64, 2048), R(8, 640), R(8, 2048),
        R(48, 128), R(3, 48, 128), R(3, 48, 128), R(48, 128),
        V(8, 256, CA), V(8, 256, CB), V(3, 2, 256, CA), V(3, 256, CA), V(2, 256, CA), V(3, 4, 128, CB), V(3, 128, CB), V(4, 128, CB), V(2, 128, CB),
        V(2, 8, 2, 64, 256), V(4, 2, 64, 2048), V(8, 64, 1024), V(8, 64, 1024), V(3, 2, 64, 1024), V(3, 64, 1024), V(2, 64, 1024), V(3, 4, 32, 1024), V(3, 32, 1024), V(4, 32, 1024), R(2, 32, 1024), V(4, 64, 2048),
        V(2, 64, 2048), V(3, 256, C1), V(3, 128, C1), V(2, 128, C1), V(8, 32, 1152), R(8, 48, 128), R(35, 8, 128), V(8, 32, 1152),
    ]
    return pl.pallas_call(
        tail_kernel,
        name="tail",
        out_shape=outs,
        in_specs=[VM] * 7 + [ANY] * 6 + [VM] + [ANY] * 5 + [VM] * 2,
        out_specs=[VM] * 11,
        scratch_shapes=[*scratch, pltpu.SemaphoreType.DMA((112,)), pltpu.SemaphoreType.DMA((112,)), pltpu.SemaphoreType.DMA((12,)), pltpu.SemaphoreType.DMA((2,))],
        compiler_params=pltpu.CompilerParams(collective_id=5, has_side_effects=True, vmem_limit_bytes=62 << 20),
        cost_estimate=pl.CostEstimate(flops=8 << 30, bytes_accessed=32 << 20, transcendentals=0),
    )(bc_all, edges, wpa, wpb, turned, branch, gain, cot, dpre, pre, ext, flags, fnext, conv, ddt, dgate, w, hid, normed, small_o, small_b)


def per_device(layer_in, cotangent, segment_ids, norm_gain, in_weight, conv_weight, conv_bias, dt_bias, a_log, skip_gain, out_gain, out_weight):
    (
        normed, hid_all, w_in, gate, pre, ext, delta, logs, flags, fnext, mixed, carried, states, dno, cot, w_out,
        sums, ends_all, conv, hp, og, gain, segrow,
    ) = wave(
        layer_in[:, 0], in_weight, segment_ids[:, 0], norm_gain[None], out_gain[None], conv_weight, conv_bias[None], dt_bias, a_log, skip_gain, cotangent[:, 0], out_weight
    )
    w_in = w_in.reshape(2048, 1408)
    dgate, dpre, bc_all, ddt, small_o, small_b, own_branch, wpa, wpb, turned, edges = back_wave(
        mixed, carried, states, gate, dno, sums, pre, delta, logs, flags, segrow, og, hp, w_out.reshape(512, 2048), normed, ends_all
    )
    dpre = dpre.reshape(MICRO, TOK, 512)
    g_in, g_out, layer_out, grad_in, conv_g, bias_g, norm_g, gain_g, dtb_g, alog_g, skip_g = tail_call(
        bc_all, edges, wpa, wpb, turned, own_branch, gain, cot, dpre, pre, ext, flags, fnext, conv, ddt, dgate, w_in, hid_all, normed, small_o, small_b
    )
    return (
        layer_out[:, None], grad_in[:, None], norm_g[0], g_in, conv_g, bias_g[0], dtb_g[0], alog_g[0], skip_g[0], gain_g[0], g_out,
    )


def solution(mesh):
    fine = Mesh(mesh.devices.reshape(2, 4, 2, 4, 2), AXES)
    tok = P(None, "rep", SEQ, None)
    return jax.shard_map(
        per_device,
        mesh=fine,
        in_specs=(tok, tok, P(None, "rep", SEQ), P(SEQ), P(SEQ, None), P(None, SEQ), P(SEQ), P(SEQ), P(SEQ), P(SEQ), P(SEQ), P(SEQ, None)),
        out_specs=(tok, tok, P(SEQ), P(SEQ, None), P(None, SEQ), P(SEQ), P(SEQ), P(SEQ), P(SEQ), P(SEQ), P(SEQ, None)),
        check_vma=False,
    )
```
